32 devices in a mesh: ka: 16 (over z, x, core), ga: 2 (over y).
Axes of the slice: x: 2, y: 2, z: 4, core: 2. Of those that a mesh axis runs over, the one named last changes fastest.
Arguments:
- orbitals: bfloat16 [32, 1024, 256], P('ka', 'ga'), may hold values from -1.5 to 1.5
- minus_table: int32 [2, 32], replicated, may hold values from 0 to 31, as said below
- points: int32 [512], replicated, may hold values from 0 to 1023, as said below
Outputs:
- pair_matrix: float32 [512, 2, 2, 1024], P('ka', None, None, 'ga')
The draws below stay inside these ranges and needn't reach their ends.
Inputs may be any that keep to these rules, and one draw needn't show every extreme that they name: `minus_table`: row q holds (k - s) mod 32 for every k, with one shift s for the row that is a nonzero multiple of 2; the two rows have different shifts. `points`: distinct grid indices; 0 and 1023 are among them.
All inputs are finite; a program needn't handle non-finite values.
Results may differ from the reference program's by a relative error of at most 0.0012.
Values may be sent and summed in bfloat16 or wider, within the bound.
No kernel may reach another device: no remote copies, remote signals or barrier semaphores. Data moves between devices by JAX's collectives and lax.ppermute only.
A program may use at most 64 MiB of HBM per device.

```python
import math
import jax
import jax.numpy as jnp
from jax import lax

NB = 128
NPTS = 512
K_DEV = 2
NK = 32
NGRID = 1024
N_KA = 16


def draw_minus_table(key, part):
    key = jax.random.fold_in(key, 12)
    first_key, second_key = jax.random.split(key)
    first_shift = jax.random.randint(first_key, (), 1, N_KA)
    offset = jax.random.randint(second_key, (), 1, N_KA - 1)
    second_shift = 1 + (first_shift - 1 + offset) % (N_KA - 1)
    shifts = jnp.stack([first_shift, second_shift]) * K_DEV
    kpoints = jnp.arange(NK, dtype=jnp.int32)
    return ((kpoints[None, :] - shifts[:, None]) % NK).astype(jnp.int32)


def draw_points(key, part):
    key = jax.random.fold_in(key, 11)
    inner = jax.random.permutation(key, NGRID - 2)[:NPTS - 2] + 1
    ends = jnp.array([0, NGRID - 1], dtype=jnp.int32)
    return jnp.concatenate([ends[:1], inner.astype(jnp.int32), ends[1:]]).astype(jnp.int32)


def level_of(rng, shape, cuts, least, largest):
    level, own = 1.0, jax.random.fold_in(rng, 6)
    for dim, parts in cuts:
        heights = jnp.exp(jax.random.uniform(jax.random.fold_in(own, dim), (parts,), jnp.float32, least / len(cuts), largest / len(cuts)))
        level = level * jnp.repeat(heights, shape[dim] // parts).reshape([-1 if axis == dim else 1 for axis in range(len(shape))])
    return level


def scatter_about(rng, shape, width, reach, cuts=(), held_as=jnp.bfloat16):
    entries = jax.random.normal(rng, shape, jnp.float32) * width
    if len(cuts) > 0:
        entries = level_of(rng, shape, cuts, -0.22, 0.18) * entries
    return jnp.clip(entries, min=-reach, max=reach).astype(held_as)


def setup_inputs(seed: int = 0) -> dict:
    splits = jax.random.split(jax.random.key(seed), 4)
    return {
        "orbitals": scatter_about(splits[0], (NK, NGRID, 2 * NB), ((2 * NB) ** -0.25), 1.5, ((0, 16), (1, 2))),
        "minus_table": draw_minus_table(jax.random.fold_in(splits[3], 71), 0),
        "points": draw_points(jax.random.fold_in(splits[3], 71), 0),
    }


def pair_field(field_rows, collected):
    halfway = collected.shape[1] // 2
    rotated = jnp.concatenate([-collected[:, halfway:], collected[:, :halfway]], axis=1)
    stacked = jnp.concatenate([collected, rotated], axis=0)
    product = lax.dot_general(stacked, field_rows, (((1,), (1,)), ((), ())), preferred_element_type=jnp.float32)
    rounded = lax.optimization_barrier(product.astype(jnp.bfloat16))
    return rounded.astype(jnp.float32)

def reference(orbitals, minus_table, points):
    npoints = points.shape[0]

    def advance(total, kpoint):
        own_field = pair_field(orbitals[kpoint], orbitals[kpoint][points])
        pieces = []
        for transfer in range(minus_table.shape[0]):
            other_k = minus_table[transfer, kpoint]
            other_rows = orbitals[other_k]
            other_field = pair_field(other_rows, other_rows[points])
            real_part = own_field[:npoints] * other_field[:npoints] + own_field[npoints:] * other_field[npoints:]
            imag_part = own_field[npoints:] * other_field[:npoints] - own_field[:npoints] * other_field[npoints:]
            pieces.append(jnp.stack([real_part, imag_part], axis=1))
        return (total + jnp.stack(pieces, axis=1), None)
    initial = jnp.zeros((npoints, minus_table.shape[0], 2, orbitals.shape[1]), jnp.float32)
    total, unused = lax.scan(advance, initial, jnp.arange(orbitals.shape[0], dtype=jnp.int32))
    return total * (1.0 / math.sqrt(NK))
```

```python
import functools
import math

import jax
import jax.numpy as jnp
from jax import lax
from jax.experimental import pallas as pl
from jax.experimental.pallas import tpu as pltpu
from jax.sharding import Mesh
from jax.sharding import PartitionSpec as P

VMEM_LIMIT = 40 * 1024 * 1024
SPLIT = 2
ALL = ("half", "inner", "hi", "lo")


def swap(block, cut, other):
    half, inner, hi, lo = (lax.axis_size(name) for name in ALL)
    slabs = hi * lo
    size = half * inner * slabs
    route = []
    for place in range(size):
        kplace, slab = divmod(place, slabs)
        kplace = (kplace + cut * inner) % (half * inner)
        route.append((place, kplace * slabs + (slab ^ other)))
    return lax.ppermute(block, ALL, route)


def field_kernel(count, lo_ref, rows_ref, *refs):
    slab_refs, (out_ref, picked_ref) = refs[:count], refs[count:]
    slab_size, channels = slab_refs[0].shape
    npoints = rows_ref.shape[0]
    half = channels // 2
    groups, _, _, length, _ = out_ref.shape
    place = pl.program_id(0)

    @pl.when(place == 0)
    def _():
        spot = lax.broadcasted_iota(jnp.int32, (npoints, slab_size), 1)
        picked = jnp.zeros((npoints, channels), jnp.float32)
        for number, slab_ref in enumerate(slab_refs):
            chosen = (rows_ref[:, number : number + 1] == spot).astype(jnp.float32)
            picked += jnp.dot(
                chosen.astype(jnp.bfloat16), slab_ref[...], preferred_element_type=jnp.float32
            )
        rotated = jnp.concatenate([-picked[:, half:], picked[:, :half]], axis=1)
        picked_ref[0] = picked.astype(jnp.bfloat16)
        picked_ref[1] = rotated.astype(jnp.bfloat16)

    for number in range(SPLIT):

        @pl.when(place == number)
        def _(number=number):
            for part in range(2):
                product = lax.dot_general(
                    picked_ref[part],
                    slab_refs[number][...],
                    (((1,), (1,)), ((), ())),
                    preferred_element_type=jnp.float32,
                )
                pieces = product.reshape(groups, length, slab_size)
                out_ref[:, 0, part] = pieces.astype(jnp.bfloat16)


def make_fields(slabs, rows, groups, lo):
    slab_size, channels = slabs[0].shape
    npoints = rows.shape[0]
    length = npoints // groups
    whole = lambda place, lo: (0, 0)
    return pl.pallas_call(
        functools.partial(field_kernel, len(slabs)),
        grid_spec=pltpu.PrefetchScalarGridSpec(
            num_scalar_prefetch=1,
            grid=(SPLIT,),
            in_specs=[pl.BlockSpec(rows.shape, whole)]
            + [pl.BlockSpec((slab_size, channels), whole) for _ in slabs],
            out_specs=pl.BlockSpec(
                (groups, 1, 2, length, slab_size), lambda place, lo: (0, lo[0] ^ place, 0, 0, 0)
            ),
            scratch_shapes=[pltpu.VMEM((2, npoints, channels), jnp.bfloat16)],
        ),
        out_shape=jax.ShapeDtypeStruct((groups, SPLIT, 2, length, slab_size), jnp.bfloat16),
        compiler_params=pltpu.CompilerParams(vmem_limit_bytes=VMEM_LIMIT),
        name="fields",
    )(lo, rows, *slabs)


def pair_kernel(scale, table_ref, near_ref, far_ref, out_ref, held_ref):
    total_k, _, length, width = held_ref.shape
    transfers = table_ref.shape[0]
    held_ref[: total_k // 2] = near_ref[...].astype(jnp.float32)
    held_ref[total_k // 2 :] = far_ref[...].astype(jnp.float32)

    def load(k, part, start, count):
        return held_ref[k, part, pl.ds(start, count), :]

    count = min(16, length)
    for start in range(0, length, count):

        def step(k, sums):
            real, imag = load(k, 0, start, count), load(k, 1, start, count)
            after = []
            for transfer in range(transfers):
                other = table_ref[transfer, k]
                other_real = load(other, 0, start, count)
                other_imag = load(other, 1, start, count)
                after.append(sums[2 * transfer] + (real * other_real + imag * other_imag))
                after.append(sums[2 * transfer + 1] + (imag * other_real - real * other_imag))
            return tuple(after)

        zero = jnp.zeros((count, width), jnp.float32)
        sums = lax.fori_loop(0, total_k, step, (zero,) * (2 * transfers), unroll=4)
        for place, value in enumerate(sums):
            out_ref[pl.ds(start, count), place // 2, place % 2, :] = value * scale


def make_pairs(near, far, table):
    half_k, _, length, slab_size = near.shape
    transfers = table.shape[0]
    width = 256
    fields = pl.BlockSpec((half_k, 2, length, width), lambda r, table: (0, 0, 0, r))
    return pl.pallas_call(
        functools.partial(pair_kernel, 1.0 / math.sqrt(2 * half_k)),
        grid_spec=pltpu.PrefetchScalarGridSpec(
            num_scalar_prefetch=1,
            grid=(slab_size // width,),
            in_specs=[fields, fields],
            out_specs=pl.BlockSpec((length, transfers, 2, width), lambda r, table: (0, 0, 0, r)),
            scratch_shapes=[pltpu.VMEM((2 * half_k, 2, length, width), jnp.float32)],
        ),
        out_shape=jax.ShapeDtypeStruct((length, transfers, 2, slab_size), jnp.float32),
        compiler_params=pltpu.CompilerParams(vmem_limit_bytes=VMEM_LIMIT),
        name="pairs",
    )(table, near, far)


def on_device(orbitals, minus_table, points):
    kdevice, slab_size, channels = orbitals.shape
    half = lax.axis_index("half")
    groups = lax.axis_size("inner")
    slabs = lax.axis_size("hi") * lax.axis_size("lo")
    lo = lax.axis_index("lo")
    here = lax.axis_index("hi") * SPLIT + lo
    total_k = 2 * groups * kdevice

    mine = lax.dynamic_index_in_dim(orbitals, lo, 0, keepdims=False)
    other = lax.dynamic_index_in_dim(orbitals, 1 - lo, 0, keepdims=False)
    near = [mine] + [swap(other if x & 1 else mine, 0, x) for x in range(1, slabs)]
    far = [swap(other if x & 1 else mine, 1, x) for x in range(slabs)]

    half_points = points.shape[0] // 2
    wanted = lax.dynamic_slice_in_dim(points, half * half_points, half_points)
    starts = jnp.stack([(here ^ x) * slab_size for x in range(slabs)])
    rows = wanted[:, None] - starts[None, :]

    def share(held):
        fields = make_fields(held, rows, groups, lo.reshape(1))
        fields = fields.reshape((groups * SPLIT,) + fields.shape[2:])
        return lax.all_to_all(fields, ("inner", "lo"), split_axis=0, concat_axis=0, tiled=True)

    near_fields = share(near)
    far_fields = share(far)

    turn = half * (total_k // 2)
    table = (jnp.roll(minus_table, -turn, axis=1) - turn) % total_k
    return make_pairs(near_fields, far_fields, table)


def solution(mesh):
    kplaces, slabs = mesh.shape["ka"], mesh.shape["ga"]
    devices = mesh.devices.reshape(2, kplaces // 2, slabs // SPLIT, SPLIT)
    finer = Mesh(devices, ALL)
    return jax.shard_map(
        on_device,
        mesh=finer,
        in_specs=(P(("half", "inner"), ("hi", "lo"), None), P(), P()),
        out_specs=P(("half", "inner"), None, None, ("hi", "lo")),
        check_vma=False,
    )
```

```python
import functools
import math

import jax
import jax.numpy as jnp
from jax import lax
from jax.experimental import pallas as pl
from jax.experimental.pallas import tpu as pltpu
from jax.sharding import Mesh
from jax.sharding import PartitionSpec as P

VMEM_LIMIT = 40 * 1024 * 1024
SPLIT = 2
ALL = ("half", "inner", "hi", "lo")


def swap(block, cut, other):
    half, inner, hi, lo = (lax.axis_size(name) for name in ALL)
    slabs = hi * lo
    size = half * inner * slabs
    route = []
    for place in range(size):
        kplace, slab = divmod(place, slabs)
        kplace = (kplace + cut * inner) % (half * inner)
        route.append((place, kplace * slabs + (slab ^ other)))
    return lax.ppermute(block, ALL, route)


def field_kernel(count, lo_ref, rows_ref, *refs):
    slab_refs, (out_ref, picked_ref) = refs[:count], refs[count:]
    slab_size, channels = slab_refs[0].shape
    npoints = rows_ref.shape[0]
    half = channels // 2
    groups, _, _, length, _ = out_ref.shape
    place = pl.program_id(0)

    @pl.when(place == 0)
    def _():
        spot = lax.broadcasted_iota(jnp.int32, (npoints, slab_size), 1)
        picked = jnp.zeros((npoints, channels), jnp.float32)
        for number, slab_ref in enumerate(slab_refs):
            chosen = (rows_ref[:, number : number + 1] == spot).astype(jnp.float32)
            picked += jnp.dot(
                chosen.astype(jnp.bfloat16), slab_ref[...], preferred_element_type=jnp.float32
            )
        rotated = jnp.concatenate([-picked[:, half:], picked[:, :half]], axis=1)
        picked_ref[0] = picked.astype(jnp.bfloat16)
        picked_ref[1] = rotated.astype(jnp.bfloat16)

    for number in range(SPLIT):

        @pl.when(place == number)
        def _(number=number):
            for part in range(2):
                product = lax.dot_general(
                    picked_ref[part],
                    slab_refs[number][...],
                    (((1,), (1,)), ((), ())),
                    preferred_element_type=jnp.float32,
                )
                pieces = product.reshape(groups, length, slab_size)
                out_ref[:, 0, part] = pieces.astype(jnp.bfloat16)


def make_fields(slabs, rows, groups, lo):
    slab_size, channels = slabs[0].shape
    npoints = rows.shape[0]
    length = npoints // groups
    whole = lambda place, lo: (0, 0)
    return pl.pallas_call(
        functools.partial(field_kernel, len(slabs)),
        grid_spec=pltpu.PrefetchScalarGridSpec(
            num_scalar_prefetch=1,
            grid=(SPLIT,),
            in_specs=[pl.BlockSpec(rows.shape, whole)]
            + [pl.BlockSpec((slab_size, channels), whole) for _ in slabs],
            out_specs=pl.BlockSpec(
                (groups, 1, 2, length, slab_size), lambda place, lo: (0, lo[0] ^ place, 0, 0, 0)
            ),
            scratch_shapes=[pltpu.VMEM((2, npoints, channels), jnp.bfloat16)],
        ),
        out_shape=jax.ShapeDtypeStruct((groups, SPLIT, 2, length, slab_size), jnp.bfloat16),
        compiler_params=pltpu.CompilerParams(vmem_limit_bytes=VMEM_LIMIT),
        name="fields",
    )(lo, rows, *slabs)


def pair_kernel(scale, table_ref, near_ref, far_ref, out_ref, held_ref):
    total_k, _, length, width = held_ref.shape
    transfers = table_ref.shape[0]
    held_ref[: total_k // 2] = near_ref[...].astype(jnp.float32)
    held_ref[total_k // 2 :] = far_ref[...].astype(jnp.float32)

    def load(k, part, start, count):
        return held_ref[k, part, pl.ds(start, count), :]

    count = min(16, length)
    for start in range(0, length, count):

        def step(k, sums):
            real, imag = load(k, 0, start, count), load(k, 1, start, count)
            after = []
            for transfer in range(transfers):
                other = table_ref[transfer, k]
                other_real = load(other, 0, start, count)
                other_imag = load(other, 1, start, count)
                after.append(sums[2 * transfer] + (real * other_real + imag * other_imag))
                after.append(sums[2 * transfer + 1] + (imag * other_real - real * other_imag))
            return tuple(after)

        zero = jnp.zeros((count, width), jnp.float32)
        sums = lax.fori_loop(0, total_k, step, (zero,) * (2 * transfers), unroll=4)
        for place, value in enumerate(sums):
            out_ref[pl.ds(start, count), place // 2, place % 2, :] = value * scale


def make_pairs(near, far, table):
    half_k, _, length, slab_size = near.shape
    transfers = table.shape[0]
    width = 256
    fields = pl.BlockSpec((half_k, 2, length, width), lambda r, table: (0, 0, 0, r))
    return pl.pallas_call(
        functools.partial(pair_kernel, 1.0 / math.sqrt(2 * half_k)),
        grid_spec=pltpu.PrefetchScalarGridSpec(
            num_scalar_prefetch=1,
            grid=(slab_size // width,),
            in_specs=[fields, fields],
            out_specs=pl.BlockSpec((length, transfers, 2, width), lambda r, table: (0, 0, 0, r)),
            scratch_shapes=[pltpu.VMEM((2 * half_k, 2, length, width), jnp.float32)],
        ),
        out_shape=jax.ShapeDtypeStruct((length, transfers, 2, slab_size), jnp.float32),
        compiler_params=pltpu.CompilerParams(vmem_limit_bytes=VMEM_LIMIT),
        name="pairs",
    )(table, near, far)


def on_device(orbitals, minus_table, points):
    kdevice, slab_size, channels = orbitals.shape
    half = lax.axis_index("half")
    groups = lax.axis_size("inner")
    slabs = lax.axis_size("hi") * lax.axis_size("lo")
    lo = lax.axis_index("lo")
    here = lax.axis_index("hi") * SPLIT + lo
    total_k = 2 * groups * kdevice

    mine = lax.dynamic_index_in_dim(orbitals, lo, 0, keepdims=False)
    other = lax.dynamic_index_in_dim(orbitals, 1 - lo, 0, keepdims=False)
    near = [mine] + [swap(other if x & 1 else mine, 0, x) for x in range(1, slabs)]
    far = [swap(other if x & 1 else mine, 1, x) for x in range(slabs)]

    half_points = points.shape[0] // 2
    wanted = lax.dynamic_slice_in_dim(points, half * half_points, half_points)
    starts = jnp.stack([(here ^ x) * slab_size for x in range(slabs)])
    rows = wanted[:, None] - starts[None, :]

    def share(fields):
        fields = fields.reshape((groups * SPLIT,) + fields.shape[2:])
        return lax.all_to_all(fields, ("inner", "lo"), split_axis=0, concat_axis=0, tiled=True)

    near_fields = make_fields(near, rows, groups, lo.reshape(1))
    near_fields, rows = lax.optimization_barrier((near_fields, rows))
    near_fields = share(near_fields)
    far_fields = share(make_fields(far, rows, groups, lo.reshape(1)))

    turn = half * (total_k // 2)
    table = (jnp.roll(minus_table, -turn, axis=1) - turn) % total_k
    return make_pairs(near_fields, far_fields, table)


def solution(mesh):
    kplaces, slabs = mesh.shape["ka"], mesh.shape["ga"]
    devices = mesh.devices.reshape(2, kplaces // 2, slabs // SPLIT, SPLIT)
    finer = Mesh(devices, ALL)
    return jax.shard_map(
        on_device,
        mesh=finer,
        in_specs=(P(("half", "inner"), ("hi", "lo"), None), P(), P()),
        out_specs=P(("half", "inner"), None, None, ("hi", "lo")),
        check_vma=False,
    )
```

```python
import functools
import math

import jax
import jax.numpy as jnp
from jax import lax
from jax.experimental import pallas as pl
from jax.experimental.pallas import tpu as pltpu
from jax.sharding import Mesh
from jax.sharding import PartitionSpec as P

VMEM_LIMIT = 40 * 1024 * 1024
SPLIT = 2
ALL = ("half", "inner", "hi", "lo")


def swap(block, cut, other):
    half, inner, hi, lo = (lax.axis_size(name) for name in ALL)
    slabs = hi * lo
    size = half * inner * slabs
    route = []
    for place in range(size):
        kplace, slab = divmod(place, slabs)
        kplace = (kplace + cut * inner) % (half * inner)
        route.append((place, kplace * slabs + (slab ^ other)))
    return lax.ppermute(block, ALL, route)


def field_kernel(count, lo_ref, rows_ref, *refs):
    slab_refs, (out_ref, picked_ref) = refs[:count], refs[count:]
    slab_size, channels = slab_refs[0].shape
    npoints = rows_ref.shape[0]
    half = channels // 2
    groups, _, _, length, _ = out_ref.shape
    place = pl.program_id(0)

    @pl.when(place == 0)
    def _():
        spot = lax.broadcasted_iota(jnp.int32, (npoints, slab_size), 1)
        picked = jnp.zeros((npoints, channels), jnp.float32)
        for number, slab_ref in enumerate(slab_refs):
            chosen = (rows_ref[:, number : number + 1] == spot).astype(jnp.float32)
            picked += jnp.dot(
                chosen.astype(jnp.bfloat16), slab_ref[...], preferred_element_type=jnp.float32
            )
        rotated = jnp.concatenate([-picked[:, half:], picked[:, :half]], axis=1)
        picked_ref[0] = picked.astype(jnp.bfloat16)
        picked_ref[1] = rotated.astype(jnp.bfloat16)

    for number in range(SPLIT):

        @pl.when(place == number)
        def _(number=number):
            for part in range(2):
                product = lax.dot_general(
                    picked_ref[part],
                    slab_refs[number][...],
                    (((1,), (1,)), ((), ())),
                    preferred_element_type=jnp.float32,
                )
                pieces = product.reshape(groups, length, slab_size)
                out_ref[:, 0, part] = pieces.astype(jnp.bfloat16)


def make_fields(slabs, rows, groups, lo):
    slab_size, channels = slabs[0].shape
    npoints = rows.shape[0]
    length = npoints // groups
    whole = lambda place, lo: (0, 0)
    return pl.pallas_call(
        functools.partial(field_kernel, len(slabs)),
        grid_spec=pltpu.PrefetchScalarGridSpec(
            num_scalar_prefetch=1,
            grid=(SPLIT,),
            in_specs=[pl.BlockSpec(rows.shape, whole)]
            + [pl.BlockSpec((slab_size, channels), whole) for _ in slabs],
            out_specs=pl.BlockSpec(
                (groups, 1, 2, length, slab_size), lambda place, lo: (0, lo[0] ^ place, 0, 0, 0)
            ),
            scratch_shapes=[pltpu.VMEM((2, npoints, channels), jnp.bfloat16)],
        ),
        out_shape=jax.ShapeDtypeStruct((groups, SPLIT, 2, length, slab_size), jnp.bfloat16),
        compiler_params=pltpu.CompilerParams(vmem_limit_bytes=VMEM_LIMIT),
        name="fields",
    )(lo, rows, *slabs)


def pair_kernel(scale, table_ref, near_ref, far_ref, out_ref, held_ref):
    total_k, _, length, width = held_ref.shape
    transfers = table_ref.shape[0]
    held_ref[: total_k // 2] = near_ref[...].astype(jnp.float32)
    held_ref[total_k // 2 :] = far_ref[...].astype(jnp.float32)

    def load(k, part, start, count):
        return held_ref[k, part, pl.ds(start, count), :]

    count = min(16, length)
    for start in range(0, length, count):

        def step(k, sums):
            real, imag = load(k, 0, start, count), load(k, 1, start, count)
            after = []
            for transfer in range(transfers):
                other = table_ref[transfer, k]
                other_real = load(other, 0, start, count)
                other_imag = load(other, 1, start, count)
                after.append(sums[2 * transfer] + (real * other_real + imag * other_imag))
                after.append(sums[2 * transfer + 1] + (imag * other_real - real * other_imag))
            return tuple(after)

        zero = jnp.zeros((count, width), jnp.float32)
        sums = lax.fori_loop(0, total_k, step, (zero,) * (2 * transfers), unroll=4)
        for place, value in enumerate(sums):
            out_ref[pl.ds(start, count), place // 2, place % 2, :] = value * scale


def make_pairs(near, far, table):
    half_k, _, length, slab_size = near.shape
    transfers = table.shape[0]
    width = 256
    fields = pl.BlockSpec((half_k, 2, length, width), lambda r, table: (0, 0, 0, r))
    return pl.pallas_call(
        functools.partial(pair_kernel, 1.0 / math.sqrt(2 * half_k)),
        grid_spec=pltpu.PrefetchScalarGridSpec(
            num_scalar_prefetch=1,
            grid=(slab_size // width,),
            in_specs=[fields, fields],
            out_specs=pl.BlockSpec((length, transfers, 2, width), lambda r, table: (0, 0, 0, r)),
            scratch_shapes=[pltpu.VMEM((2 * half_k, 2, length, width), jnp.float32)],
        ),
        out_shape=jax.ShapeDtypeStruct((length, transfers, 2, slab_size), jnp.float32),
        compiler_params=pltpu.CompilerParams(vmem_limit_bytes=VMEM_LIMIT),
        name="pairs",
    )(table, near, far)


def on_device(orbitals, minus_table, points):
    kdevice, slab_size, channels = orbitals.shape
    half = lax.axis_index("half")
    groups = lax.axis_size("inner")
    slabs = lax.axis_size("hi") * lax.axis_size("lo")
    lo = lax.axis_index("lo")
    here = lax.axis_index("hi") * SPLIT + lo
    total_k = 2 * groups * kdevice

    mine = lax.dynamic_index_in_dim(orbitals, lo, 0, keepdims=False)
    other = lax.dynamic_index_in_dim(orbitals, 1 - lo, 0, keepdims=False)
    near = [mine] + [swap(other if x & 1 else mine, 0, x) for x in range(1, slabs)]
    far = [swap(other if x & 1 else mine, 1, x) for x in range(slabs)]

    half_points = points.shape[0] // 2
    wanted = lax.dynamic_slice_in_dim(points, half * half_points, half_points)
    starts = jnp.stack([(here ^ x) * slab_size for x in range(slabs)])
    rows = wanted[:, None] - starts[None, :]

    def share(fields):
        fields = fields.reshape((groups * SPLIT,) + fields.shape[2:])
        return lax.all_to_all(fields, ("inner", "lo"), split_axis=0, concat_axis=0, tiled=True)

    near_fields = share(make_fields(near, rows, groups, lo.reshape(1)))
    near_fields, rows = lax.optimization_barrier((near_fields, rows))
    far_fields = share(make_fields(far, rows, groups, lo.reshape(1)))

    turn = half * (total_k // 2)
    table = (jnp.roll(minus_table, -turn, axis=1) - turn) % total_k
    return make_pairs(near_fields, far_fields, table)


def solution(mesh):
    kplaces, slabs = mesh.shape["ka"], mesh.shape["ga"]
    devices = mesh.devices.reshape(2, kplaces // 2, slabs // SPLIT, SPLIT)
    finer = Mesh(devices, ALL)
    return jax.shard_map(
        on_device,
        mesh=finer,
        in_specs=(P(("half", "inner"), ("hi", "lo"), None), P(), P()),
        out_specs=P(("half", "inner"), None, None, ("hi", "lo")),
        check_vma=False,
    )
```

```python
import functools
import math

import jax
import jax.numpy as jnp
from jax import lax
from jax.experimental import pallas as pl
from jax.experimental.pallas import tpu as pltpu
from jax.sharding import Mesh
from jax.sharding import PartitionSpec as P

VMEM_LIMIT = 40 * 1024 * 1024
SPLIT = 2
ALL = ("half", "inner", "hi", "lo")


def swap(block, cut, other):
    half, inner, hi, lo = (lax.axis_size(name) for name in ALL)
    slabs = hi * lo
    size = half * inner * slabs
    route = []
    for place in range(size):
        kplace, slab = divmod(place, slabs)
        kplace = (kplace + cut * inner) % (half * inner)
        route.append((place, kplace * slabs + (slab ^ other)))
    return lax.ppermute(block, ALL, route)


def field_kernel(count, lo_ref, rows_ref, *refs):
    slab_refs, (out_ref, picked_ref) = refs[:count], refs[count:]
    slab_size, channels = slab_refs[0].shape
    npoints = rows_ref.shape[0]
    half = channels // 2
    groups, _, _, length, _ = out_ref.shape
    place = pl.program_id(0)

    @pl.when(place == 0)
    def _():
        spot = lax.broadcasted_iota(jnp.int32, (npoints, slab_size), 1)
        picked = jnp.zeros((npoints, channels), jnp.float32)
        for number, slab_ref in enumerate(slab_refs):
            chosen = (rows_ref[:, number : number + 1] == spot).astype(jnp.float32)
            picked += jnp.dot(
                chosen.astype(jnp.bfloat16), slab_ref[...], preferred_element_type=jnp.float32
            )
        rotated = jnp.concatenate([-picked[:, half:], picked[:, :half]], axis=1)
        picked_ref[0] = picked.astype(jnp.bfloat16)
        picked_ref[1] = rotated.astype(jnp.bfloat16)

    for number in range(SPLIT):

        @pl.when(place == number)
        def _(number=number):
            for part in range(2):
                product = lax.dot_general(
                    picked_ref[part],
                    slab_refs[number][...],
                    (((1,), (1,)), ((), ())),
                    preferred_element_type=jnp.float32,
                )
                pieces = product.reshape(groups, length, slab_size)
                out_ref[:, 0, part] = pieces.astype(jnp.bfloat16)


def make_fields(slabs, rows, groups, lo):
    slab_size, channels = slabs[0].shape
    npoints = rows.shape[0]
    length = npoints // groups
    whole = lambda place, lo: (0, 0)
    return pl.pallas_call(
        functools.partial(field_kernel, len(slabs)),
        grid_spec=pltpu.PrefetchScalarGridSpec(
            num_scalar_prefetch=1,
            grid=(SPLIT,),
            in_specs=[pl.BlockSpec(rows.shape, whole)]
            + [pl.BlockSpec((slab_size, channels), whole) for _ in slabs],
            out_specs=pl.BlockSpec(
                (groups, 1, 2, length, slab_size), lambda place, lo: (0, lo[0] ^ place, 0, 0, 0)
            ),
            scratch_shapes=[pltpu.VMEM((2, npoints, channels), jnp.bfloat16)],
        ),
        out_shape=jax.ShapeDtypeStruct((groups, SPLIT, 2, length, slab_size), jnp.bfloat16),
        compiler_params=pltpu.CompilerParams(vmem_limit_bytes=VMEM_LIMIT),
        name="fields",
    )(lo, rows, *slabs)


def pair_kernel(scale, table_ref, near_ref, far_ref, out_ref, held_ref):
    total_k, _, length, width = held_ref.shape
    transfers = table_ref.shape[0]
    held_ref[: total_k // 2] = near_ref[...].astype(jnp.float32)
    held_ref[total_k // 2 :] = far_ref[...].astype(jnp.float32)

    def load(k, part, start, count):
        return held_ref[k, part, pl.ds(start, count), :]

    count = min(16, length)
    for start in range(0, length, count):

        def step(k, sums):
            real, imag = load(k, 0, start, count), load(k, 1, start, count)
            after = []
            for transfer in range(transfers):
                other = table_ref[transfer, k]
                other_real = load(other, 0, start, count)
                other_imag = load(other, 1, start, count)
                after.append(sums[2 * transfer] + (real * other_real + imag * other_imag))
                after.append(sums[2 * transfer + 1] + (imag * other_real - real * other_imag))
            return tuple(after)

        zero = jnp.zeros((count, width), jnp.float32)
        sums = lax.fori_loop(0, total_k, step, (zero,) * (2 * transfers), unroll=4)
        for place, value in enumerate(sums):
            out_ref[pl.ds(start, count), place // 2, place % 2, :] = value * scale


def make_pairs(near, far, table):
    half_k, _, length, slab_size = near.shape
    transfers = table.shape[0]
    width = 256
    fields = pl.BlockSpec((half_k, 2, length, width), lambda r, table: (0, 0, 0, r))
    return pl.pallas_call(
        functools.partial(pair_kernel, 1.0 / math.sqrt(2 * half_k)),
        grid_spec=pltpu.PrefetchScalarGridSpec(
            num_scalar_prefetch=1,
            grid=(slab_size // width,),
            in_specs=[fields, fields],
            out_specs=pl.BlockSpec((length, transfers, 2, width), lambda r, table: (0, 0, 0, r)),
            scratch_shapes=[pltpu.VMEM((2 * half_k, 2, length, width), jnp.float32)],
        ),
        out_shape=jax.ShapeDtypeStruct((length, transfers, 2, slab_size), jnp.float32),
        compiler_params=pltpu.CompilerParams(vmem_limit_bytes=VMEM_LIMIT),
        name="pairs",
    )(table, near, far)


def on_device(orbitals, minus_table, points):
    kdevice, slab_size, channels = orbitals.shape
    half = lax.axis_index("half")
    groups = lax.axis_size("inner")
    slabs = lax.axis_size("hi") * lax.axis_size("lo")
    lo = lax.axis_index("lo")
    here = lax.axis_index("hi") * SPLIT + lo
    total_k = 2 * groups * kdevice

    mine = lax.dynamic_index_in_dim(orbitals, lo, 0, keepdims=False)
    other = lax.dynamic_index_in_dim(orbitals, 1 - lo, 0, keepdims=False)
    near = [mine] + [swap(other if x & 1 else mine, 0, x) for x in range(1, slabs)]
    far = [swap(slab, 1, 0) for slab in near]

    half_points = points.shape[0] // 2
    wanted = lax.dynamic_slice_in_dim(points, half * half_points, half_points)
    starts = jnp.stack([(here ^ x) * slab_size for x in range(slabs)])
    rows = wanted[:, None] - starts[None, :]

    def share(fields):
        fields = fields.reshape((groups * SPLIT,) + fields.shape[2:])
        return lax.all_to_all(fields, ("inner", "lo"), split_axis=0, concat_axis=0, tiled=True)

    near_fields = make_fields(near, rows, groups, lo.reshape(1))
    near_fields, rows = lax.optimization_barrier((near_fields, rows))
    far_fields = make_fields(far, rows, groups, lo.reshape(1))
    near_fields, far_fields = lax.optimization_barrier((share(near_fields), far_fields))
    far_fields = share(far_fields)

    turn = half * (total_k // 2)
    table = (jnp.roll(minus_table, -turn, axis=1) - turn) % total_k
    return make_pairs(near_fields, far_fields, table)


def solution(mesh):
    kplaces, slabs = mesh.shape["ka"], mesh.shape["ga"]
    devices = mesh.devices.reshape(2, kplaces // 2, slabs // SPLIT, SPLIT)
    finer = Mesh(devices, ALL)
    return jax.shard_map(
        on_device,
        mesh=finer,
        in_specs=(P(("half", "inner"), ("hi", "lo"), None), P(), P()),
        out_specs=P(("half", "inner"), None, None, ("hi", "lo")),
        check_vma=False,
    )
```

```python
import functools
import math

import jax
import jax.numpy as jnp
from jax import lax
from jax.experimental import pallas as pl
from jax.experimental.pallas import tpu as pltpu
from jax.sharding import Mesh
from jax.sharding import PartitionSpec as P

VMEM_LIMIT = 40 * 1024 * 1024
SPLIT = 2
ALL = ("half", "inner", "hi", "lo")


def swap(block, cut, other):
    half, inner, hi, lo = (lax.axis_size(name) for name in ALL)
    slabs = hi * lo
    size = half * inner * slabs
    route = []
    for place in range(size):
        kplace, slab = divmod(place, slabs)
        kplace = (kplace + cut * inner) % (half * inner)
        route.append((place, kplace * slabs + (slab ^ other)))
    return lax.ppermute(block, ALL, route)


def field_kernel(count, lo_ref, rows_ref, *refs):
    slab_refs, (out_ref, picked_ref) = refs[:count], refs[count:]
    slab_size, channels = slab_refs[0].shape
    npoints = rows_ref.shape[0]
    half = channels // 2
    groups, _, _, length, _ = out_ref.shape
    place = pl.program_id(0)

    @pl.when(place == 0)
    def _():
        spot = lax.broadcasted_iota(jnp.int32, (npoints, slab_size), 1)
        picked = jnp.zeros((npoints, channels), jnp.float32)
        for number, slab_ref in enumerate(slab_refs):
            chosen = (rows_ref[:, number : number + 1] == spot).astype(jnp.float32)
            picked += jnp.dot(
                chosen.astype(jnp.bfloat16), slab_ref[...], preferred_element_type=jnp.float32
            )
        rotated = jnp.concatenate([-picked[:, half:], picked[:, :half]], axis=1)
        picked_ref[0] = picked.astype(jnp.bfloat16)
        picked_ref[1] = rotated.astype(jnp.bfloat16)

    for number in range(SPLIT):

        @pl.when(place == number)
        def _(number=number):
            for part in range(2):
                product = lax.dot_general(
                    picked_ref[part],
                    slab_refs[number][...],
                    (((1,), (1,)), ((), ())),
                    preferred_element_type=jnp.float32,
                )
                pieces = product.reshape(groups, length, slab_size)
                out_ref[:, 0, part] = pieces.astype(jnp.bfloat16)


def make_fields(slabs, rows, groups, lo):
    slab_size, channels = slabs[0].shape
    npoints = rows.shape[0]
    length = npoints // groups
    whole = lambda place, lo: (0, 0)
    return pl.pallas_call(
        functools.partial(field_kernel, len(slabs)),
        grid_spec=pltpu.PrefetchScalarGridSpec(
            num_scalar_prefetch=1,
            grid=(SPLIT,),
            in_specs=[pl.BlockSpec(rows.shape, whole)]
            + [pl.BlockSpec((slab_size, channels), whole) for _ in slabs],
            out_specs=pl.BlockSpec(
                (groups, 1, 2, length, slab_size), lambda place, lo: (0, lo[0] ^ place, 0, 0, 0)
            ),
            scratch_shapes=[pltpu.VMEM((2, npoints, channels), jnp.bfloat16)],
        ),
        out_shape=jax.ShapeDtypeStruct((groups, SPLIT, 2, length, slab_size), jnp.bfloat16),
        cost_estimate=pl.CostEstimate(
            flops=7_000_000_000, bytes_accessed=22_000_000, transcendentals=0
        ),
        compiler_params=pltpu.CompilerParams(vmem_limit_bytes=VMEM_LIMIT),
        name="fields",
    )(lo, rows, *slabs)


def pair_kernel(scale, table_ref, near_ref, far_ref, out_ref, held_ref):
    total_k, _, length, width = held_ref.shape
    transfers = table_ref.shape[0]
    held_ref[: total_k // 2] = near_ref[...].astype(jnp.float32)
    held_ref[total_k // 2 :] = far_ref[...].astype(jnp.float32)

    def load(k, part, start, count):
        return held_ref[k, part, pl.ds(start, count), :]

    count = min(16, length)
    for start in range(0, length, count):

        def step(k, sums):
            real, imag = load(k, 0, start, count), load(k, 1, start, count)
            after = []
            for transfer in range(transfers):
                other = table_ref[transfer, k]
                other_real = load(other, 0, start, count)
                other_imag = load(other, 1, start, count)
                after.append(sums[2 * transfer] + (real * other_real + imag * other_imag))
                after.append(sums[2 * transfer + 1] + (imag * other_real - real * other_imag))
            return tuple(after)

        zero = jnp.zeros((count, width), jnp.float32)
        sums = lax.fori_loop(0, total_k, step, (zero,) * (2 * transfers), unroll=4)
        for place, value in enumerate(sums):
            out_ref[pl.ds(start, count), place // 2, place % 2, :] = value * scale


def make_pairs(near, far, table):
    half_k, _, length, slab_size = near.shape
    transfers = table.shape[0]
    width = 256
    fields = pl.BlockSpec((half_k, 2, length, width), lambda r, table: (0, 0, 0, r))
    return pl.pallas_call(
        functools.partial(pair_kernel, 1.0 / math.sqrt(2 * half_k)),
        grid_spec=pltpu.PrefetchScalarGridSpec(
            num_scalar_prefetch=1,
            grid=(slab_size // width,),
            in_specs=[fields, fields],
            out_specs=pl.BlockSpec((length, transfers, 2, width), lambda r, table: (0, 0, 0, r)),
            scratch_shapes=[pltpu.VMEM((2 * half_k, 2, length, width), jnp.float32)],
        ),
        out_shape=jax.ShapeDtypeStruct((length, transfers, 2, slab_size), jnp.float32),
        compiler_params=pltpu.CompilerParams(vmem_limit_bytes=VMEM_LIMIT),
        name="pairs",
    )(table, near, far)


def on_device(orbitals, minus_table, points):
    kdevice, slab_size, channels = orbitals.shape
    half = lax.axis_index("half")
    groups = lax.axis_size("inner")
    slabs = lax.axis_size("hi") * lax.axis_size("lo")
    lo = lax.axis_index("lo")
    here = lax.axis_index("hi") * SPLIT + lo
    total_k = 2 * groups * kdevice

    mine = lax.dynamic_index_in_dim(orbitals, lo, 0, keepdims=False)
    other = lax.dynamic_index_in_dim(orbitals, 1 - lo, 0, keepdims=False)
    near = [mine] + [swap(other if x & 1 else mine, 0, x) for x in range(1, slabs)]
    far = [swap(slab, 1, 0) for slab in near]

    half_points = points.shape[0] // 2
    wanted = lax.dynamic_slice_in_dim(points, half * half_points, half_points)
    starts = jnp.stack([(here ^ x) * slab_size for x in range(slabs)])
    rows = wanted[:, None] - starts[None, :]

    def share(fields):
        fields = fields.reshape((groups * SPLIT,) + fields.shape[2:])
        return lax.all_to_all(fields, ("inner", "lo"), split_axis=0, concat_axis=0, tiled=True)

    near_fields = make_fields(near, rows, groups, lo.reshape(1))
    near_fields, rows = lax.optimization_barrier((near_fields, rows))
    far_fields = make_fields(far, rows, groups, lo.reshape(1))
    near_fields, far_fields = lax.optimization_barrier((share(near_fields), far_fields))
    far_fields = share(far_fields)

    turn = half * (total_k // 2)
    table = (jnp.roll(minus_table, -turn, axis=1) - turn) % total_k
    return make_pairs(near_fields, far_fields, table)


def solution(mesh):
    kplaces, slabs = mesh.shape["ka"], mesh.shape["ga"]
    devices = mesh.devices.reshape(2, kplaces // 2, slabs // SPLIT, SPLIT)
    finer = Mesh(devices, ALL)
    return jax.shard_map(
        on_device,
        mesh=finer,
        in_specs=(P(("half", "inner"), ("hi", "lo"), None), P(), P()),
        out_specs=P(("half", "inner"), None, None, ("hi", "lo")),
        check_vma=False,
    )
```

```python
import functools
import math

import jax
import jax.numpy as jnp
from jax import lax
from jax.experimental import pallas as pl
from jax.experimental.pallas import tpu as pltpu
from jax.sharding import Mesh
from jax.sharding import PartitionSpec as P

VMEM_LIMIT = 40 * 1024 * 1024
SPLIT = 2
ALL = ("half", "inner", "hi", "lo")


def swap(block, cut, other):
    half, inner, hi, lo = (lax.axis_size(name) for name in ALL)
    slabs = hi * lo
    size = half * inner * slabs
    route = []
    for place in range(size):
        kplace, slab = divmod(place, slabs)
        kplace = (kplace + cut * inner) % (half * inner)
        route.append((place, kplace * slabs + (slab ^ other)))
    return lax.ppermute(block, ALL, route)


def field_kernel(count, lo_ref, rows_ref, *refs):
    slab_refs, (out_ref, picked_ref) = refs[:count], refs[count:]
    slab_size, channels = slab_refs[0].shape
    npoints = rows_ref.shape[0]
    half = channels // 2
    groups, _, _, length, _ = out_ref.shape
    place = pl.program_id(0)

    @pl.when(place == 0)
    def _():
        spot = lax.broadcasted_iota(jnp.int32, (npoints, slab_size), 1)
        picked = jnp.zeros((npoints, channels), jnp.float32)
        for number, slab_ref in enumerate(slab_refs):
            chosen = (rows_ref[:, number : number + 1] == spot).astype(jnp.float32)
            picked += jnp.dot(
                chosen.astype(jnp.bfloat16), slab_ref[...], preferred_element_type=jnp.float32
            )
        rotated = jnp.concatenate([-picked[:, half:], picked[:, :half]], axis=1)
        picked_ref[0] = picked.astype(jnp.bfloat16)
        picked_ref[1] = rotated.astype(jnp.bfloat16)

    for number in range(SPLIT):

        @pl.when(place == number)
        def _(number=number):
            for part in range(2):
                product = lax.dot_general(
                    picked_ref[part],
                    slab_refs[number][...],
                    (((1,), (1,)), ((), ())),
                    preferred_element_type=jnp.float32,
                )
                pieces = product.reshape(groups, length, slab_size)
                out_ref[:, 0, part] = pieces.astype(jnp.bfloat16)


def make_fields(slabs, rows, groups, lo):
    slab_size, channels = slabs[0].shape
    npoints = rows.shape[0]
    length = npoints // groups
    whole = lambda place, lo: (0, 0)
    return pl.pallas_call(
        functools.partial(field_kernel, len(slabs)),
        grid_spec=pltpu.PrefetchScalarGridSpec(
            num_scalar_prefetch=1,
            grid=(SPLIT,),
            in_specs=[pl.BlockSpec(rows.shape, whole)]
            + [pl.BlockSpec((slab_size, channels), whole) for _ in slabs],
            out_specs=pl.BlockSpec(
                (groups, 1, 2, length, slab_size), lambda place, lo: (0, lo[0] ^ place, 0, 0, 0)
            ),
            scratch_shapes=[pltpu.VMEM((2, npoints, channels), jnp.bfloat16)],
        ),
        out_shape=jax.ShapeDtypeStruct((groups, SPLIT, 2, length, slab_size), jnp.bfloat16),
        compiler_params=pltpu.CompilerParams(vmem_limit_bytes=VMEM_LIMIT),
        name="fields",
    )(lo, rows, *slabs)


def pair_kernel(scale, table_ref, near_ref, far_ref, out_ref, held_ref):
    total_k, _, length, width = held_ref.shape
    transfers = table_ref.shape[0]
    held_ref[: total_k // 2] = near_ref[...].astype(jnp.float32)
    held_ref[total_k // 2 :] = far_ref[...].astype(jnp.float32)

    def load(k, part, start, count):
        return held_ref[k, part, pl.ds(start, count), :]

    count = min(16, length)
    for start in range(0, length, count):

        def step(k, sums):
            real, imag = load(k, 0, start, count), load(k, 1, start, count)
            after = []
            for transfer in range(transfers):
                other = table_ref[transfer, k]
                other_real = load(other, 0, start, count)
                other_imag = load(other, 1, start, count)
                after.append(sums[2 * transfer] + (real * other_real + imag * other_imag))
                after.append(sums[2 * transfer + 1] + (imag * other_real - real * other_imag))
            return tuple(after)

        zero = jnp.zeros((count, width), jnp.float32)
        sums = lax.fori_loop(0, total_k, step, (zero,) * (2 * transfers), unroll=4)
        for place, value in enumerate(sums):
            out_ref[pl.ds(start, count), place // 2, place % 2, :] = value * scale


def make_pairs(near, far, table):
    half_k, _, length, slab_size = near.shape
    transfers = table.shape[0]
    width = 256
    fields = pl.BlockSpec((half_k, 2, length, width), lambda r, table: (0, 0, 0, r))
    return pl.pallas_call(
        functools.partial(pair_kernel, 1.0 / math.sqrt(2 * half_k)),
        grid_spec=pltpu.PrefetchScalarGridSpec(
            num_scalar_prefetch=1,
            grid=(slab_size // width,),
            in_specs=[fields, fields],
            out_specs=pl.BlockSpec((length, transfers, 2, width), lambda r, table: (0, 0, 0, r)),
            scratch_shapes=[pltpu.VMEM((2 * half_k, 2, length, width), jnp.float32)],
        ),
        out_shape=jax.ShapeDtypeStruct((length, transfers, 2, slab_size), jnp.float32),
        compiler_params=pltpu.CompilerParams(vmem_limit_bytes=VMEM_LIMIT),
        name="pairs",
    )(table, near, far)


def on_device(orbitals, minus_table, points):
    kdevice, slab_size, channels = orbitals.shape
    half = lax.axis_index("half")
    groups = lax.axis_size("inner")
    slabs = lax.axis_size("hi") * lax.axis_size("lo")
    lo = lax.axis_index("lo")
    here = lax.axis_index("hi") * SPLIT + lo
    total_k = 2 * groups * kdevice

    mine = lax.dynamic_index_in_dim(orbitals, lo, 0, keepdims=False)
    other = lax.dynamic_index_in_dim(orbitals, 1 - lo, 0, keepdims=False)
    near = [mine] + [swap(other if x & 1 else mine, 0, x) for x in range(1, slabs)]
    far = [swap(slab, 1, 0) for slab in near]

    half_points = points.shape[0] // 2
    wanted = lax.dynamic_slice_in_dim(points, half * half_points, half_points)
    starts = jnp.stack([(here ^ x) * slab_size for x in range(slabs)])
    rows = wanted[:, None] - starts[None, :]

    def flat(fields):
        return fields.reshape((groups * SPLIT,) + fields.shape[2:])

    def share(fields):
        return lax.all_to_all(fields, ("inner", "lo"), split_axis=0, concat_axis=0, tiled=True)

    near_fields = flat(make_fields(near, rows, groups, lo.reshape(1)))
    near_fields, rows = lax.optimization_barrier((near_fields, rows))
    far_fields = flat(make_fields(far, rows, groups, lo.reshape(1)))
    near_fields = lax.cond(minus_table[0, 0] >= 0, share, lambda fields: fields, near_fields)
    near_fields, far_fields = lax.optimization_barrier((near_fields, far_fields))
    far_fields = share(far_fields)

    turn = half * (total_k // 2)
    table = (jnp.roll(minus_table, -turn, axis=1) - turn) % total_k
    return make_pairs(near_fields, far_fields, table)


def solution(mesh):
    kplaces, slabs = mesh.shape["ka"], mesh.shape["ga"]
    devices = mesh.devices.reshape(2, kplaces // 2, slabs // SPLIT, SPLIT)
    finer = Mesh(devices, ALL)
    return jax.shard_map(
        on_device,
        mesh=finer,
        in_specs=(P(("half", "inner"), ("hi", "lo"), None), P(), P()),
        out_specs=P(("half", "inner"), None, None, ("hi", "lo")),
        check_vma=False,
    )
```

```python
import functools
import math

import jax
import jax.numpy as jnp
from jax import lax
from jax.experimental import pallas as pl
from jax.experimental.pallas import tpu as pltpu
from jax.sharding import Mesh
from jax.sharding import PartitionSpec as P

VMEM_LIMIT = 40 * 1024 * 1024
SPLIT = 2
KA, GA = ("half", "inner"), ("hi", "lo")


def field_kernel(place_ref, points_ref, held_ref, out_ref, picked_ref):
    slabs, slab_size, channels = held_ref.shape
    npoints = points_ref.shape[1] // 2
    middle = channels // 2
    groups, _, _, length, _ = out_ref.shape
    step = pl.program_id(0)

    @pl.when(step == 0)
    def _():
        first = pl.multiple_of(place_ref[0] * npoints, npoints)
        wanted = points_ref[:, pl.ds(first, npoints)]
        spot = lax.broadcasted_iota(jnp.int32, (slab_size, npoints), 0)
        picked = jnp.zeros((npoints, channels), jnp.float32)
        for slab in range(slabs):
            chosen = (spot == wanted - slab * slab_size).astype(jnp.float32)
            picked += lax.dot_general(
                chosen.astype(jnp.bfloat16),
                held_ref[slab],
                (((0,), (0,)), ((), ())),
                preferred_element_type=jnp.float32,
            )
        rotated = jnp.concatenate([-picked[:, middle:], picked[:, :middle]], axis=1)
        picked_ref[0] = picked.astype(jnp.bfloat16)
        picked_ref[1] = rotated.astype(jnp.bfloat16)

    for part in range(2):
        product = lax.dot_general(
            picked_ref[part],
            held_ref[place_ref[1] * SPLIT + step],
            (((1,), (1,)), ((), ())),
            preferred_element_type=jnp.float32,
        )
        pieces = product.reshape(groups, length, slab_size)
        out_ref[:, 0, part] = pieces.astype(jnp.bfloat16)


def make_fields(held, points, groups, place):
    slabs, slab_size, channels = held.shape
    npoints = points.shape[1] // 2
    length = npoints // groups
    return pl.pallas_call(
        field_kernel,
        grid_spec=pltpu.PrefetchScalarGridSpec(
            num_scalar_prefetch=1,
            grid=(SPLIT,),
            in_specs=[
                pl.BlockSpec(points.shape, lambda step, place: (0, 0)),
                pl.BlockSpec(held.shape, lambda step, place: (0, 0, 0)),
            ],
            out_specs=pl.BlockSpec(
                (groups, 1, 2, length, slab_size), lambda step, place: (0, step, 0, 0, 0)
            ),
            scratch_shapes=[pltpu.VMEM((2, npoints, channels), jnp.bfloat16)],
        ),
        out_shape=jax.ShapeDtypeStruct((groups, SPLIT, 2, length, slab_size), jnp.bfloat16),
        compiler_params=pltpu.CompilerParams(vmem_limit_bytes=VMEM_LIMIT),
        name="fields",
    )(place, points, held)


def pair_kernel(scale, table_ref, near_ref, far_ref, out_ref, held_ref):
    total_k, _, length, width = held_ref.shape
    transfers = table_ref.shape[0]
    held_ref[: total_k // 2] = near_ref[...].astype(jnp.float32)
    held_ref[total_k // 2 :] = far_ref[...].astype(jnp.float32)

    def load(k, part, start, count):
        return held_ref[k, part, pl.ds(start, count), :]

    count = min(16, length)
    for start in range(0, length, count):

        def step(k, sums):
            real, imag = load(k, 0, start, count), load(k, 1, start, count)
            after = []
            for transfer in range(transfers):
                other = table_ref[transfer, k]
                other_real = load(other, 0, start, count)
                other_imag = load(other, 1, start, count)
                after.append(sums[2 * transfer] + (real * other_real + imag * other_imag))
                after.append(sums[2 * transfer + 1] + (imag * other_real - real * other_imag))
            return tuple(after)

        zero = jnp.zeros((count, width), jnp.float32)
        sums = lax.fori_loop(0, total_k, step, (zero,) * (2 * transfers), unroll=4)
        for place, value in enumerate(sums):
            out_ref[pl.ds(start, count), place // 2, place % 2, :] = value * scale


def make_pairs(near, far, table):
    half_k, _, length, slab_size = near.shape
    transfers = table.shape[0]
    width = 256
    fields = pl.BlockSpec((half_k, 2, length, width), lambda r, table: (0, 0, 0, r))
    return pl.pallas_call(
        functools.partial(pair_kernel, 1.0 / math.sqrt(2 * half_k)),
        grid_spec=pltpu.PrefetchScalarGridSpec(
            num_scalar_prefetch=1,
            grid=(slab_size // width,),
            in_specs=[fields, fields],
            out_specs=pl.BlockSpec((length, transfers, 2, width), lambda r, table: (0, 0, 0, r)),
            scratch_shapes=[pltpu.VMEM((2 * half_k, 2, length, width), jnp.float32)],
        ),
        out_shape=jax.ShapeDtypeStruct((length, transfers, 2, slab_size), jnp.float32),
        compiler_params=pltpu.CompilerParams(vmem_limit_bytes=VMEM_LIMIT),
        name="pairs",
    )(table, near, far)


def on_device(orbitals, minus_table, points):
    kdevice, slab_size, channels = orbitals.shape
    half = lax.axis_index("half")
    groups = lax.axis_size("inner")
    total_k = 2 * groups * kdevice

    near = lax.all_to_all(orbitals, "lo", split_axis=0, concat_axis=0, tiled=True)
    if lax.axis_size("hi") > 1:
        near = lax.all_gather(near, "hi", axis=0, tiled=True)
    far = lax.ppermute(near, "half", [(0, 1), (1, 0)])

    points = points.reshape(1, -1)
    place = jnp.stack([half, lax.axis_index("hi")])

    def flat(fields):
        return fields.reshape((groups * SPLIT,) + fields.shape[2:])

    def share(fields):
        return lax.all_to_all(fields, ("inner", "lo"), split_axis=0, concat_axis=0, tiled=True)

    near_fields = flat(make_fields(near, points, groups, place))
    near_fields, points = lax.optimization_barrier((near_fields, points))
    far_fields = flat(make_fields(far, points, groups, place))
    near_fields = lax.cond(half >= 0, share, lambda fields: fields, near_fields)
    near_fields, far_fields = lax.optimization_barrier((near_fields, far_fields))
    far_fields = share(far_fields)

    turn = half * (total_k // 2)
    table = (jnp.roll(minus_table, -turn, axis=1) - turn) % total_k
    return make_pairs(near_fields, far_fields, table)


def solution(mesh):
    kplaces, slabs = mesh.shape["ka"], mesh.shape["ga"]
    devices = mesh.devices.reshape(2, kplaces // 2, slabs // SPLIT, SPLIT)
    finer = Mesh(devices, KA + GA)
    return jax.shard_map(
        on_device,
        mesh=finer,
        in_specs=(P(KA, GA, None), P(), P()),
        out_specs=P(KA, None, None, GA),
        check_vma=False,
    )
```

```python
import functools
import math

import jax
import jax.numpy as jnp
from jax import lax
from jax.experimental import pallas as pl
from jax.experimental.pallas import tpu as pltpu
from jax.sharding import Mesh
from jax.sharding import PartitionSpec as P

VMEM_LIMIT = 40 * 1024 * 1024
SPLIT = 2
KA, GA = ("half", "inner"), ("hi", "lo")


def swap(block, cut, other):
    half, inner, hi, lo = (lax.axis_size(name) for name in KA + GA)
    slabs = hi * lo
    route = []
    for place in range(half * inner * slabs):
        kplace, slab = divmod(place, slabs)
        kplace = (kplace + cut * inner) % (half * inner)
        route.append((place, kplace * slabs + (slab ^ other)))
    return lax.ppermute(block, KA + GA, route)


def field_kernel(count, place_ref, points_ref, *refs):
    slab_refs, (out_ref, picked_ref) = refs[:count], refs[count:]
    slab_size, channels = slab_refs[0].shape
    npoints = points_ref.shape[1] // 2
    middle = channels // 2
    groups, _, _, length, _ = out_ref.shape
    step = pl.program_id(0)

    @pl.when(step == 0)
    def _():
        first = pl.multiple_of(place_ref[0] * npoints, npoints)
        wanted = points_ref[:, pl.ds(first, npoints)]
        spot = lax.broadcasted_iota(jnp.int32, (slab_size, npoints), 0)
        picked = jnp.zeros((npoints, channels), jnp.float32)
        for number, slab_ref in enumerate(slab_refs):
            chosen = spot == wanted - (place_ref[1] ^ number) * slab_size
            picked += lax.dot_general(
                chosen.astype(jnp.float32).astype(jnp.bfloat16),
                slab_ref[...],
                (((0,), (0,)), ((), ())),
                preferred_element_type=jnp.float32,
            )
        rotated = jnp.concatenate([-picked[:, middle:], picked[:, :middle]], axis=1)
        picked_ref[0] = picked.astype(jnp.bfloat16)
        picked_ref[1] = rotated.astype(jnp.bfloat16)

    for number in range(SPLIT):

        @pl.when(step == number)
        def _(number=number):
            for part in range(2):
                product = lax.dot_general(
                    picked_ref[part],
                    slab_refs[number][...],
                    (((1,), (1,)), ((), ())),
                    preferred_element_type=jnp.float32,
                )
                pieces = product.reshape(groups, length, slab_size)
                out_ref[:, 0, part] = pieces.astype(jnp.bfloat16)


def make_fields(slabs, points, groups, place):
    slab_size, channels = slabs[0].shape
    npoints = points.shape[1] // 2
    length = npoints // groups
    return pl.pallas_call(
        functools.partial(field_kernel, len(slabs)),
        grid_spec=pltpu.PrefetchScalarGridSpec(
            num_scalar_prefetch=1,
            grid=(SPLIT,),
            in_specs=[pl.BlockSpec(points.shape, lambda step, place: (0, 0))]
            + [pl.BlockSpec((slab_size, channels), lambda step, place: (0, 0)) for _ in slabs],
            out_specs=pl.BlockSpec(
                (groups, 1, 2, length, slab_size),
                lambda step, place: (0, place[1] % SPLIT ^ step, 0, 0, 0),
            ),
            scratch_shapes=[pltpu.VMEM((2, npoints, channels), jnp.bfloat16)],
        ),
        out_shape=jax.ShapeDtypeStruct((groups, SPLIT, 2, length, slab_size), jnp.bfloat16),
        compiler_params=pltpu.CompilerParams(vmem_limit_bytes=VMEM_LIMIT),
        name="fields",
    )(place, points, *slabs)


def pair_kernel(scale, table_ref, near_ref, far_ref, out_ref, held_ref):
    total_k, _, length, width = held_ref.shape
    transfers = table_ref.shape[0]
    held_ref[: total_k // 2] = near_ref[...].astype(jnp.float32)
    held_ref[total_k // 2 :] = far_ref[...].astype(jnp.float32)

    def load(k, part, start, count):
        return held_ref[k, part, pl.ds(start, count), :]

    count = min(16, length)
    for start in range(0, length, count):

        def step(k, sums):
            real, imag = load(k, 0, start, count), load(k, 1, start, count)
            after = []
            for transfer in range(transfers):
                other = table_ref[transfer, k]
                other_real = load(other, 0, start, count)
                other_imag = load(other, 1, start, count)
                after.append(sums[2 * transfer] + (real * other_real + imag * other_imag))
                after.append(sums[2 * transfer + 1] + (imag * other_real - real * other_imag))
            return tuple(after)

        zero = jnp.zeros((count, width), jnp.float32)
        sums = lax.fori_loop(0, total_k, step, (zero,) * (2 * transfers), unroll=4)
        for place, value in enumerate(sums):
            out_ref[pl.ds(start, count), place // 2, place % 2, :] = value * scale


def make_pairs(near, far, table):
    half_k, _, length, slab_size = near.shape
    transfers = table.shape[0]
    width = 256
    fields = pl.BlockSpec((half_k, 2, length, width), lambda r, table: (0, 0, 0, r))
    return pl.pallas_call(
        functools.partial(pair_kernel, 1.0 / math.sqrt(2 * half_k)),
        grid_spec=pltpu.PrefetchScalarGridSpec(
            num_scalar_prefetch=1,
            grid=(slab_size // width,),
            in_specs=[fields, fields],
            out_specs=pl.BlockSpec((length, transfers, 2, width), lambda r, table: (0, 0, 0, r)),
            scratch_shapes=[pltpu.VMEM((2 * half_k, 2, length, width), jnp.float32)],
        ),
        out_shape=jax.ShapeDtypeStruct((length, transfers, 2, slab_size), jnp.float32),
        compiler_params=pltpu.CompilerParams(vmem_limit_bytes=VMEM_LIMIT),
        name="pairs",
    )(table, near, far)


def on_device(orbitals, minus_table, points):
    kdevice, slab_size, channels = orbitals.shape
    half = lax.axis_index("half")
    groups = lax.axis_size("inner")
    total_k = 2 * groups * kdevice

    lo = lax.axis_index("lo")
    slabs = lax.axis_size("hi") * SPLIT
    mine = lax.dynamic_index_in_dim(orbitals, lo, 0, keepdims=False)
    other = lax.dynamic_index_in_dim(orbitals, 1 - lo, 0, keepdims=False)
    near = [mine] + [swap(other if x & 1 else mine, 0, x) for x in range(1, slabs)]
    far = [swap(other if x & 1 else mine, 1, x) for x in range(slabs)]

    points = points.reshape(1, -1)
    place = jnp.stack([half, lax.axis_index("hi") * SPLIT + lo])

    def flat(fields):
        return fields.reshape((groups * SPLIT,) + fields.shape[2:])

    def share(fields):
        return lax.all_to_all(fields, ("inner", "lo"), split_axis=0, concat_axis=0, tiled=True)

    near_fields = flat(make_fields(near, points, groups, place))
    near_fields, points = lax.optimization_barrier((near_fields, points))
    far_fields = flat(make_fields(far, points, groups, place))
    near_fields = lax.cond(half >= 0, share, lambda fields: fields, near_fields)
    near_fields, far_fields = lax.optimization_barrier((near_fields, far_fields))
    far_fields = share(far_fields)

    turn = half * (total_k // 2)
    table = (jnp.roll(minus_table, -turn, axis=1) - turn) % total_k
    return make_pairs(near_fields, far_fields, table)


def solution(mesh):
    kplaces, slabs = mesh.shape["ka"], mesh.shape["ga"]
    devices = mesh.devices.reshape(2, kplaces // 2, slabs // SPLIT, SPLIT)
    finer = Mesh(devices, KA + GA)
    return jax.shard_map(
        on_device,
        mesh=finer,
        in_specs=(P(KA, GA, None), P(), P()),
        out_specs=P(KA, None, None, GA),
        check_vma=False,
    )
```

```python
import functools
import math

import jax
import jax.numpy as jnp
from jax import lax
from jax.experimental import pallas as pl
from jax.experimental.pallas import tpu as pltpu
from jax.sharding import Mesh
from jax.sharding import PartitionSpec as P

VMEM_LIMIT = 40 * 1024 * 1024
SPLIT = 2
KA, GA = ("half", "quarter", "inner"), ("hi", "lo")
OUTER, MIDDLE = (0, 3), (1, 2)


def swap(block, other, quarters=None):
    half, quarter, inner, hi, lo = (lax.axis_size(name) for name in KA + GA)
    slabs = hi * lo
    route = []
    for place in range(half * quarter * inner * slabs):
        kplace, slab = divmod(place, slabs)
        part, within = divmod(kplace, inner)
        if quarters is not None and part not in quarters:
            continue
        part = part if quarters is None else half * quarter - 1 - part
        route.append((place, (part * inner + within) * slabs + (slab ^ other)))
    return lax.ppermute(block, KA + GA, route)


def field_kernel(sets, place_ref, points_ref, *refs):
    *source_refs, out_ref, picked_ref, held_ref = refs
    slabs, slab_size, channels = held_ref.shape
    slab_refs = [held_ref.at[number] for number in range(slabs)]
    if sets == 1:
        slab_refs = source_refs
    npoints = points_ref.shape[1] // 2
    middle = channels // 2
    groups, _, _, length, _ = out_ref.shape
    step = pl.program_id(0)

    @pl.when(step == 0)
    def _():
        for number in range(slabs if sets > 1 else 0):
            for choice in range(sets):

                @pl.when(place_ref[2] == choice)
                def _(number=number, choice=choice):
                    held_ref[number] = source_refs[choice * slabs + number][...]

        first = pl.multiple_of(place_ref[0] * npoints, npoints)
        wanted = points_ref[:, pl.ds(first, npoints)]
        spot = lax.broadcasted_iota(jnp.int32, (slab_size, npoints), 0)
        picked = jnp.zeros((npoints, channels), jnp.float32)
        for number, slab_ref in enumerate(slab_refs):
            chosen = spot == wanted - (place_ref[1] ^ number) * slab_size
            picked += lax.dot_general(
                chosen.astype(jnp.float32).astype(jnp.bfloat16),
                slab_ref[...],
                (((0,), (0,)), ((), ())),
                preferred_element_type=jnp.float32,
            )
        rotated = jnp.concatenate([-picked[:, middle:], picked[:, :middle]], axis=1)
        picked_ref[0] = picked.astype(jnp.bfloat16)
        picked_ref[1] = rotated.astype(jnp.bfloat16)

    for number in range(SPLIT):

        @pl.when(step == number)
        def _(number=number):
            for part in range(2):
                product = lax.dot_general(
                    picked_ref[part],
                    slab_refs[number][...],
                    (((1,), (1,)), ((), ())),
                    preferred_element_type=jnp.float32,
                )
                pieces = product.reshape(groups, length, slab_size)
                out_ref[:, 0, part] = pieces.astype(jnp.bfloat16)


def make_fields(sources, points, groups, place):
    slab_size, channels = sources[0][0].shape
    slabs = [slab for source in sources for slab in source]
    npoints = points.shape[1] // 2
    length = npoints // groups
    return pl.pallas_call(
        functools.partial(field_kernel, len(sources)),
        grid_spec=pltpu.PrefetchScalarGridSpec(
            num_scalar_prefetch=1,
            grid=(SPLIT,),
            in_specs=[pl.BlockSpec(points.shape, lambda step, place: (0, 0))]
            + [pl.BlockSpec((slab_size, channels), lambda step, place: (0, 0)) for _ in slabs],
            out_specs=pl.BlockSpec(
                (groups, 1, 2, length, slab_size),
                lambda step, place: (0, place[1] % SPLIT ^ step, 0, 0, 0),
            ),
            scratch_shapes=[
                pltpu.VMEM((2, npoints, channels), jnp.bfloat16),
                pltpu.VMEM((len(sources[0]), slab_size, channels), jnp.bfloat16),
            ],
        ),
        out_shape=jax.ShapeDtypeStruct((groups, SPLIT, 2, length, slab_size), jnp.bfloat16),
        compiler_params=pltpu.CompilerParams(vmem_limit_bytes=VMEM_LIMIT),
        name="fields",
    )(place, points, *slabs)


def pair_kernel(scale, table_ref, near_ref, far_ref, out_ref, held_ref):
    total_k, _, length, width = held_ref.shape
    transfers = table_ref.shape[0]
    held_ref[: total_k // 2] = near_ref[...].astype(jnp.float32)
    held_ref[total_k // 2 :] = far_ref[...].astype(jnp.float32)

    def load(k, part, start, count):
        return held_ref[k, part, pl.ds(start, count), :]

    count = min(16, length)
    for start in range(0, length, count):

        def step(k, sums):
            real, imag = load(k, 0, start, count), load(k, 1, start, count)
            after = []
            for transfer in range(transfers):
                other = table_ref[transfer, k]
                other_real = load(other, 0, start, count)
                other_imag = load(other, 1, start, count)
                after.append(sums[2 * transfer] + (real * other_real + imag * other_imag))
                after.append(sums[2 * transfer + 1] + (imag * other_real - real * other_imag))
            return tuple(after)

        zero = jnp.zeros((count, width), jnp.float32)
        sums = lax.fori_loop(0, total_k, step, (zero,) * (2 * transfers), unroll=4)
        for place, value in enumerate(sums):
            out_ref[pl.ds(start, count), place // 2, place % 2, :] = value * scale


def make_pairs(near, far, table):
    half_k, _, length, slab_size = near.shape
    transfers = table.shape[0]
    width = 256
    fields = pl.BlockSpec((half_k, 2, length, width), lambda r, table: (0, 0, 0, r))
    return pl.pallas_call(
        functools.partial(pair_kernel, 1.0 / math.sqrt(2 * half_k)),
        grid_spec=pltpu.PrefetchScalarGridSpec(
            num_scalar_prefetch=1,
            grid=(slab_size // width,),
            in_specs=[fields, fields],
            out_specs=pl.BlockSpec((length, transfers, 2, width), lambda r, table: (0, 0, 0, r)),
            scratch_shapes=[pltpu.VMEM((2 * half_k, 2, length, width), jnp.float32)],
        ),
        out_shape=jax.ShapeDtypeStruct((length, transfers, 2, slab_size), jnp.float32),
        compiler_params=pltpu.CompilerParams(vmem_limit_bytes=VMEM_LIMIT),
        name="pairs",
    )(table, near, far)


def on_device(orbitals, minus_table, points):
    kdevice, slab_size, channels = orbitals.shape
    half, quarter = lax.axis_index("half"), lax.axis_index("quarter")
    hi, lo = lax.axis_index("hi"), lax.axis_index("lo")
    groups = lax.axis_size("quarter") * lax.axis_size("inner")
    slabs = lax.axis_size("hi") * lax.axis_size("lo")
    total_k = 2 * groups * kdevice

    mine = lax.dynamic_index_in_dim(orbitals, lo, 0, keepdims=False)
    other = lax.dynamic_index_in_dim(orbitals, 1 - lo, 0, keepdims=False)
    near = [mine] + [swap(other if x & 1 else mine, x) for x in range(1, slabs)]
    outer = [swap(other if x & 1 else mine, x, OUTER) for x in range(slabs)]
    later = lax.optimization_barrier(near)
    middle = [swap(slab, 0, MIDDLE) for slab in later]

    points = points.reshape(1, -1)
    place = jnp.stack([half, hi * SPLIT + lo, (half == quarter).astype(jnp.int32)])

    def flat(fields):
        return fields.reshape((groups * SPLIT,) + fields.shape[2:])

    def share(fields):
        around = ("quarter", "inner", "lo")
        return lax.all_to_all(fields, around, split_axis=0, concat_axis=0, tiled=True)

    near_fields = flat(make_fields([near], points, groups, place))
    near_fields, points = lax.optimization_barrier((near_fields, points))
    far_fields = flat(make_fields([middle, outer], points, groups, place))
    near_fields = lax.cond(half >= 0, share, lambda fields: fields, near_fields)
    near_fields, far_fields = lax.optimization_barrier((near_fields, far_fields))
    far_fields = share(far_fields)

    def mirrored(kpoints):
        return total_k // 2 + (kpoints + total_k // 4) % (total_k // 2)

    turn = half * (total_k // 2)
    table = (jnp.roll(minus_table, -turn, axis=1) - turn) % total_k
    table = jnp.where(table < total_k // 2, table, mirrored(table))
    first, third, fourth = jnp.split(table, (total_k // 2, 3 * total_k // 4), axis=1)
    return make_pairs(near_fields, far_fields, jnp.concatenate([first, fourth, third], axis=1))


def solution(mesh):
    kplaces, slabs = mesh.shape["ka"], mesh.shape["ga"]
    devices = mesh.devices.reshape(2, 2, kplaces // 4, slabs // SPLIT, SPLIT)
    finer = Mesh(devices, KA + GA)
    return jax.shard_map(
        on_device,
        mesh=finer,
        in_specs=(P(KA, GA, None), P(), P()),
        out_specs=P(KA, None, None, GA),
        check_vma=False,
    )
```

```python
import functools
import math

import jax
import jax.numpy as jnp
from jax import lax
from jax.experimental import pallas as pl
from jax.experimental.pallas import tpu as pltpu
from jax.sharding import Mesh
from jax.sharding import PartitionSpec as P

VMEM_LIMIT = 40 * 1024 * 1024
SPLIT = 2
KA, GA = ("half", "inner"), ("hi", "lo")


def swap(block, cut, other):
    half, inner, hi, lo = (lax.axis_size(name) for name in KA + GA)
    slabs = hi * lo
    route = []
    for place in range(half * inner * slabs):
        kplace, slab = divmod(place, slabs)
        kplace = (kplace + cut * inner) % (half * inner)
        route.append((place, kplace * slabs + (slab ^ other)))
    return lax.ppermute(block, KA + GA, route)


def field_kernel(count, place_ref, points_ref, *refs):
    slab_refs, (out_ref, picked_ref) = refs[:count], refs[count:]
    slab_size, channels = slab_refs[0].shape
    npoints = points_ref.shape[1] // 2
    middle = channels // 2
    groups, _, _, length, _ = out_ref.shape
    step = pl.program_id(0)

    @pl.when(step == 0)
    def _():
        first = pl.multiple_of(place_ref[0] * npoints, npoints)
        wanted = points_ref[:, pl.ds(first, npoints)]
        spot = lax.broadcasted_iota(jnp.int32, (slab_size, npoints), 0)
        picked = jnp.zeros((npoints, channels), jnp.float32)
        for number, slab_ref in enumerate(slab_refs):
            chosen = spot == wanted - (place_ref[1] ^ number) * slab_size
            picked += lax.dot_general(
                chosen.astype(jnp.float32).astype(jnp.bfloat16),
                slab_ref[...],
                (((0,), (0,)), ((), ())),
                preferred_element_type=jnp.float32,
            )
        rotated = jnp.concatenate([-picked[:, middle:], picked[:, :middle]], axis=1)
        picked_ref[0] = picked.astype(jnp.bfloat16)
        picked_ref[1] = rotated.astype(jnp.bfloat16)

    for number in range(SPLIT):

        @pl.when(step == number)
        def _(number=number):
            for part in range(2):
                product = lax.dot_general(
                    picked_ref[part],
                    slab_refs[number][...],
                    (((1,), (1,)), ((), ())),
                    preferred_element_type=jnp.float32,
                )
                pieces = product.reshape(groups, length, slab_size)
                out_ref[:, 0, part] = pieces.astype(jnp.bfloat16)


def make_fields(slabs, points, groups, place):
    slab_size, channels = slabs[0].shape
    npoints = points.shape[1] // 2
    length = npoints // groups
    return pl.pallas_call(
        functools.partial(field_kernel, len(slabs)),
        grid_spec=pltpu.PrefetchScalarGridSpec(
            num_scalar_prefetch=1,
            grid=(SPLIT,),
            in_specs=[pl.BlockSpec(points.shape, lambda step, place: (0, 0))]
            + [pl.BlockSpec((slab_size, channels), lambda step, place: (0, 0)) for _ in slabs],
            out_specs=pl.BlockSpec(
                (groups, 1, 2, length, slab_size),
                lambda step, place: (0, place[1] % SPLIT ^ step, 0, 0, 0),
            ),
            scratch_shapes=[pltpu.VMEM((2, npoints, channels), jnp.bfloat16)],
        ),
        out_shape=jax.ShapeDtypeStruct((groups, SPLIT, 2, length, slab_size), jnp.bfloat16),
        compiler_params=pltpu.CompilerParams(vmem_limit_bytes=VMEM_LIMIT),
        name="fields",
    )(place, points, *slabs)


def pair_kernel(scale, table_ref, near_ref, far_ref, out_ref, held_ref):
    total_k, _, length, width = held_ref.shape
    transfers = table_ref.shape[0]
    held_ref[: total_k // 2] = near_ref[...].astype(jnp.float32)
    held_ref[total_k // 2 :] = far_ref[...].astype(jnp.float32)

    def load(k, part, start, count):
        return held_ref[k, part, pl.ds(start, count), :]

    count = min(16, length)
    for start in range(0, length, count):

        def step(k, sums):
            real, imag = load(k, 0, start, count), load(k, 1, start, count)
            after = []
            for transfer in range(transfers):
                other = table_ref[transfer, k]
                other_real = load(other, 0, start, count)
                other_imag = load(other, 1, start, count)
                after.append(sums[2 * transfer] + (real * other_real + imag * other_imag))
                after.append(sums[2 * transfer + 1] + (imag * other_real - real * other_imag))
            return tuple(after)

        zero = jnp.zeros((count, width), jnp.float32)
        sums = lax.fori_loop(0, total_k, step, (zero,) * (2 * transfers), unroll=4)
        for place, value in enumerate(sums):
            out_ref[pl.ds(start, count), place // 2, place % 2, :] = value * scale


def make_pairs(near, far, table):
    half_k, _, length, slab_size = near.shape
    transfers = table.shape[0]
    width = 256
    fields = pl.BlockSpec((half_k, 2, length, width), lambda r, table: (0, 0, 0, r))
    return pl.pallas_call(
        functools.partial(pair_kernel, 1.0 / math.sqrt(2 * half_k)),
        grid_spec=pltpu.PrefetchScalarGridSpec(
            num_scalar_prefetch=1,
            grid=(slab_size // width,),
            in_specs=[fields, fields],
            out_specs=pl.BlockSpec((length, transfers, 2, width), lambda r, table: (0, 0, 0, r)),
            scratch_shapes=[pltpu.VMEM((2 * half_k, 2, length, width), jnp.float32)],
        ),
        out_shape=jax.ShapeDtypeStruct((length, transfers, 2, slab_size), jnp.float32),
        compiler_params=pltpu.CompilerParams(vmem_limit_bytes=VMEM_LIMIT),
        name="pairs",
    )(table, near, far)


def on_device(orbitals, minus_table, points):
    kdevice, slab_size, channels = orbitals.shape
    half = lax.axis_index("half")
    groups = lax.axis_size("inner")
    total_k = 2 * groups * kdevice

    lo = lax.axis_index("lo")
    slabs = lax.axis_size("hi") * SPLIT
    mine = lax.dynamic_index_in_dim(orbitals, lo, 0, keepdims=False)
    other = lax.dynamic_index_in_dim(orbitals, 1 - lo, 0, keepdims=False)
    near = [mine] + [swap(other if x & 1 else mine, 0, x) for x in range(1, slabs)]
    far = [swap(mine, 1, 0)]

    points = points.reshape(1, -1)
    place = jnp.stack([half, lax.axis_index("hi") * SPLIT + lo])

    def flat(fields):
        return fields.reshape((groups * SPLIT,) + fields.shape[2:])

    def share(fields):
        return lax.all_to_all(fields, ("inner", "lo"), split_axis=0, concat_axis=0, tiled=True)

    def cross(fields, slabs):
        return share(fields), [swap(slab, 1, 0) for slab in slabs]

    near_fields = flat(make_fields(near, points, groups, place))
    near_fields, crossed = lax.cond(
        half >= 0, cross, lambda fields, slabs: (fields, slabs), near_fields, near[1:]
    )
    far_fields = share(flat(make_fields(far + crossed, points, groups, place)))

    turn = half * (total_k // 2)
    table = (jnp.roll(minus_table, -turn, axis=1) - turn) % total_k
    return make_pairs(near_fields, far_fields, table)


def solution(mesh):
    kplaces, slabs = mesh.shape["ka"], mesh.shape["ga"]
    devices = mesh.devices.reshape(2, kplaces // 2, slabs // SPLIT, SPLIT)
    finer = Mesh(devices, KA + GA)
    return jax.shard_map(
        on_device,
        mesh=finer,
        in_specs=(P(KA, GA, None), P(), P()),
        out_specs=P(KA, None, None, GA),
        check_vma=False,
    )
```

```python
import functools
import math

import jax
import jax.numpy as jnp
from jax import lax
from jax.experimental import pallas as pl
from jax.experimental.pallas import tpu as pltpu
from jax.sharding import Mesh
from jax.sharding import PartitionSpec as P

VMEM_LIMIT = 40 * 1024 * 1024
SPLIT = 2
KA, GA = ("half", "inner"), ("hi", "lo")


def swap(block, cut, other):
    half, inner, hi, lo = (lax.axis_size(name) for name in KA + GA)
    slabs = hi * lo
    route = []
    for place in range(half * inner * slabs):
        kplace, slab = divmod(place, slabs)
        kplace = (kplace + cut * inner) % (half * inner)
        route.append((place, kplace * slabs + (slab ^ other)))
    return lax.ppermute(block, KA + GA, route)


def field_kernel(plan, place_ref, points_ref, *refs):
    *slab_refs, out_ref, picked_ref = refs
    slabs = len(slab_refs) // len(plan)
    slab_size, channels = slab_refs[0].shape
    npoints = points_ref.shape[1] // 2
    middle = channels // 2
    groups, _, _, length, _ = out_ref.shape
    step = pl.program_id(0)

    @pl.when(step == 0)
    def _():
        first = pl.multiple_of(place_ref[0] * npoints, npoints)
        wanted = points_ref[:, pl.ds(first, npoints)]
        spot = lax.broadcasted_iota(jnp.int32, (slab_size, npoints), 0)
        for source in range(len(plan)):
            picked = jnp.zeros((npoints, channels), jnp.float32)
            for number in range(slabs):
                chosen = spot == wanted - (place_ref[1] ^ number) * slab_size
                picked += lax.dot_general(
                    chosen.astype(jnp.float32).astype(jnp.bfloat16),
                    slab_refs[source * slabs + number][...],
                    (((0,), (0,)), ((), ())),
                    preferred_element_type=jnp.float32,
                )
            rotated = jnp.concatenate([-picked[:, middle:], picked[:, :middle]], axis=1)
            picked_ref[source, 0] = picked.astype(jnp.bfloat16)
            picked_ref[source, 1] = rotated.astype(jnp.bfloat16)

    for number in range(SPLIT):

        @pl.when(step == number)
        def _(number=number):
            wanted = [(source, part) for source, parts in enumerate(plan) for part in parts]
            for place, (source, part) in enumerate(wanted):
                product = lax.dot_general(
                    picked_ref[source, part],
                    slab_refs[source * slabs + number][...],
                    (((1,), (1,)), ((), ())),
                    preferred_element_type=jnp.float32,
                )
                pieces = product.reshape(groups, length, slab_size)
                out_ref[:, 0, place] = pieces.astype(jnp.bfloat16)


def make_fields(sources, plan, points, groups, place):
    slab_size, channels = sources[0][0].shape
    slabs = [slab for source in sources for slab in source]
    npoints = points.shape[1] // 2
    length = npoints // groups
    parts = sum(len(parts) for parts in plan)
    out = pl.pallas_call(
        functools.partial(field_kernel, plan),
        grid_spec=pltpu.PrefetchScalarGridSpec(
            num_scalar_prefetch=1,
            grid=(SPLIT,),
            in_specs=[pl.BlockSpec(points.shape, lambda step, place: (0, 0))]
            + [pl.BlockSpec((slab_size, channels), lambda step, place: (0, 0)) for _ in slabs],
            out_specs=pl.BlockSpec(
                (groups, 1, parts, length, slab_size),
                lambda step, place: (0, place[1] % SPLIT ^ step, 0, 0, 0),
            ),
            scratch_shapes=[pltpu.VMEM((len(sources), 2, npoints, channels), jnp.bfloat16)],
        ),
        out_shape=jax.ShapeDtypeStruct((groups, SPLIT, parts, length, slab_size), jnp.bfloat16),
        compiler_params=pltpu.CompilerParams(vmem_limit_bytes=VMEM_LIMIT),
        name="fields",
    )(place, points, *slabs)
    return out.reshape((groups * SPLIT,) + out.shape[2:])


def pair_kernel(scale, table_ref, first_ref, second_ref, out_ref, held_ref):
    total_k, _, length, width = held_ref.shape
    transfers = table_ref.shape[0]
    near, far = pl.ds(0, total_k // 2), pl.ds(total_k // 2, total_k // 2)
    held_ref[near, 0] = first_ref[:, 0].astype(jnp.float32)
    held_ref[near, 1] = second_ref[:, 0].astype(jnp.float32)
    held_ref[far] = second_ref[:, 1:].astype(jnp.float32)

    def load(k, part, start, count):
        return held_ref[k, part, pl.ds(start, count), :]

    count = min(16, length)
    for start in range(0, length, count):

        def step(k, sums):
            real, imag = load(k, 0, start, count), load(k, 1, start, count)
            after = []
            for transfer in range(transfers):
                other = table_ref[transfer, k]
                other_real = load(other, 0, start, count)
                other_imag = load(other, 1, start, count)
                after.append(sums[2 * transfer] + (real * other_real + imag * other_imag))
                after.append(sums[2 * transfer + 1] + (imag * other_real - real * other_imag))
            return tuple(after)

        zero = jnp.zeros((count, width), jnp.float32)
        sums = lax.fori_loop(0, total_k, step, (zero,) * (2 * transfers), unroll=4)
        for place, value in enumerate(sums):
            out_ref[pl.ds(start, count), place // 2, place % 2, :] = value * scale


def make_pairs(first, second, table):
    half_k, _, length, slab_size = first.shape
    transfers = table.shape[0]
    width = 256
    fields = [
        pl.BlockSpec((half_k, array.shape[1], length, width), lambda r, table: (0, 0, 0, r))
        for array in (first, second)
    ]
    return pl.pallas_call(
        functools.partial(pair_kernel, 1.0 / math.sqrt(2 * half_k)),
        grid_spec=pltpu.PrefetchScalarGridSpec(
            num_scalar_prefetch=1,
            grid=(slab_size // width,),
            in_specs=fields,
            out_specs=pl.BlockSpec((length, transfers, 2, width), lambda r, table: (0, 0, 0, r)),
            scratch_shapes=[pltpu.VMEM((2 * half_k, 2, length, width), jnp.float32)],
        ),
        out_shape=jax.ShapeDtypeStruct((length, transfers, 2, slab_size), jnp.float32),
        compiler_params=pltpu.CompilerParams(vmem_limit_bytes=VMEM_LIMIT),
        name="pairs",
    )(table, first, second)


def on_device(orbitals, minus_table, points):
    kdevice, slab_size, channels = orbitals.shape
    half = lax.axis_index("half")
    groups = lax.axis_size("inner")
    total_k = 2 * groups * kdevice

    lo = lax.axis_index("lo")
    slabs = lax.axis_size("hi") * SPLIT
    mine = lax.dynamic_index_in_dim(orbitals, lo, 0, keepdims=False)
    other = lax.dynamic_index_in_dim(orbitals, 1 - lo, 0, keepdims=False)
    near = [mine] + [swap(other if x & 1 else mine, 0, x) for x in range(1, slabs)]
    far = [swap(other if x & 1 else mine, 1, x) for x in range(slabs)]

    points = points.reshape(1, -1)
    place = jnp.stack([half, lax.axis_index("hi") * SPLIT + lo])

    def share(fields):
        return lax.all_to_all(fields, ("inner", "lo"), split_axis=0, concat_axis=0, tiled=True)

    first = make_fields([near], ((0,),), points, groups, place)
    first, points = lax.optimization_barrier((first, points))
    second = make_fields([near, far], ((1,), (0, 1)), points, groups, place)
    first = lax.cond(half >= 0, share, lambda fields: fields, first)
    first, second = lax.optimization_barrier((first, second))
    second = share(second)

    turn = half * (total_k // 2)
    table = (jnp.roll(minus_table, -turn, axis=1) - turn) % total_k
    return make_pairs(first, second, table)


def solution(mesh):
    kplaces, slabs = mesh.shape["ka"], mesh.shape["ga"]
    devices = mesh.devices.reshape(2, kplaces // 2, slabs // SPLIT, SPLIT)
    finer = Mesh(devices, KA + GA)
    return jax.shard_map(
        on_device,
        mesh=finer,
        in_specs=(P(KA, GA, None), P(), P()),
        out_specs=P(KA, None, None, GA),
        check_vma=False,
    )
```

```python
import functools
import math

import jax
import jax.numpy as jnp
from jax import lax
from jax.experimental import pallas as pl
from jax.experimental.pallas import tpu as pltpu
from jax.sharding import Mesh
from jax.sharding import PartitionSpec as P

VMEM_LIMIT = 40 * 1024 * 1024
SPLIT = 2
KA, GA = ("half", "quarter", "inner"), ("hi", "lo")
OUTER, MIDDLE = (0, 3), (1, 2)


def swap(block, other, quarters=None):
    half, quarter, inner, hi, lo = (lax.axis_size(name) for name in KA + GA)
    slabs = hi * lo
    route = []
    for place in range(half * quarter * inner * slabs):
        kplace, slab = divmod(place, slabs)
        part, within = divmod(kplace, inner)
        if quarters is not None and part not in quarters:
            continue
        part = part if quarters is None else half * quarter - 1 - part
        route.append((place, (part * inner + within) * slabs + (slab ^ other)))
    return lax.ppermute(block, KA + GA, route)


def field_kernel(sets, place_ref, points_ref, *refs):
    *source_refs, out_ref, picked_ref, held_ref = refs
    slabs, slab_size, channels = held_ref.shape
    slab_refs = [held_ref.at[number] for number in range(slabs)]
    if sets == 1:
        slab_refs = source_refs
    npoints = points_ref.shape[1] // 2
    middle = channels // 2
    groups, _, _, length, _ = out_ref.shape
    step = pl.program_id(0)

    @pl.when(step == 0)
    def _():
        for number in range(slabs if sets > 1 else 0):
            for choice in range(sets):

                @pl.when(place_ref[2] == choice)
                def _(number=number, choice=choice):
                    held_ref[number] = source_refs[choice * slabs + number][...]

        first = pl.multiple_of(place_ref[0] * npoints, npoints)
        wanted = points_ref[:, pl.ds(first, npoints)]
        spot = lax.broadcasted_iota(jnp.int32, (slab_size, npoints), 0)
        picked = jnp.zeros((npoints, channels), jnp.float32)
        for number, slab_ref in enumerate(slab_refs):
            chosen = spot == wanted - (place_ref[1] ^ number) * slab_size
            picked += lax.dot_general(
                chosen.astype(jnp.float32).astype(jnp.bfloat16),
                slab_ref[...],
                (((0,), (0,)), ((), ())),
                preferred_element_type=jnp.float32,
            )
        rotated = jnp.concatenate([-picked[:, middle:], picked[:, :middle]], axis=1)
        picked_ref[0] = picked.astype(jnp.bfloat16)
        picked_ref[1] = rotated.astype(jnp.bfloat16)

    for number in range(SPLIT):

        @pl.when(step == number)
        def _(number=number):
            for part in range(2):
                product = lax.dot_general(
                    picked_ref[part],
                    slab_refs[number][...],
                    (((1,), (1,)), ((), ())),
                    preferred_element_type=jnp.float32,
                )
                pieces = product.reshape(groups, length, slab_size)
                out_ref[:, 0, part] = pieces.astype(jnp.bfloat16)


def make_fields(sources, points, groups, place):
    slab_size, channels = sources[0][0].shape
    slabs = [slab for source in sources for slab in source]
    npoints = points.shape[1] // 2
    length = npoints // groups
    return pl.pallas_call(
        functools.partial(field_kernel, len(sources)),
        grid_spec=pltpu.PrefetchScalarGridSpec(
            num_scalar_prefetch=1,
            grid=(SPLIT,),
            in_specs=[pl.BlockSpec(points.shape, lambda step, place: (0, 0))]
            + [pl.BlockSpec((slab_size, channels), lambda step, place: (0, 0)) for _ in slabs],
            out_specs=pl.BlockSpec(
                (groups, 1, 2, length, slab_size),
                lambda step, place: (0, place[1] % SPLIT ^ step, 0, 0, 0),
            ),
            scratch_shapes=[
                pltpu.VMEM((2, npoints, channels), jnp.bfloat16),
                pltpu.VMEM((len(sources[0]), slab_size, channels), jnp.bfloat16),
            ],
        ),
        out_shape=jax.ShapeDtypeStruct((groups, SPLIT, 2, length, slab_size), jnp.bfloat16),
        compiler_params=pltpu.CompilerParams(vmem_limit_bytes=VMEM_LIMIT),
        name="fields",
    )(place, points, *slabs)


def pair_kernel(scale, table_ref, near_ref, far_ref, out_ref, held_ref):
    total_k, _, length, width = held_ref.shape
    transfers = table_ref.shape[0]
    held_ref[: total_k // 2] = near_ref[...].astype(jnp.float32)
    held_ref[total_k // 2 :] = far_ref[...].astype(jnp.float32)

    def load(k, part, start, count):
        return held_ref[k, part, pl.ds(start, count), :]

    count = min(16, length)
    for start in range(0, length, count):

        def step(k, sums):
            real, imag = load(k, 0, start, count), load(k, 1, start, count)
            after = []
            for transfer in range(transfers):
                other = table_ref[transfer, k]
                other_real = load(other, 0, start, count)
                other_imag = load(other, 1, start, count)
                after.append(sums[2 * transfer] + (real * other_real + imag * other_imag))
                after.append(sums[2 * transfer + 1] + (imag * other_real - real * other_imag))
            return tuple(after)

        zero = jnp.zeros((count, width), jnp.float32)
        sums = lax.fori_loop(0, total_k, step, (zero,) * (2 * transfers), unroll=4)
        for place, value in enumerate(sums):
            out_ref[pl.ds(start, count), place // 2, place % 2, :] = value * scale


def make_pairs(near, far, table):
    half_k, _, length, slab_size = near.shape
    transfers = table.shape[0]
    width = 256
    fields = pl.BlockSpec((half_k, 2, length, width), lambda r, table: (0, 0, 0, r))
    return pl.pallas_call(
        functools.partial(pair_kernel, 1.0 / math.sqrt(2 * half_k)),
        grid_spec=pltpu.PrefetchScalarGridSpec(
            num_scalar_prefetch=1,
            grid=(slab_size // width,),
            in_specs=[fields, fields],
            out_specs=pl.BlockSpec((length, transfers, 2, width), lambda r, table: (0, 0, 0, r)),
            scratch_shapes=[pltpu.VMEM((2 * half_k, 2, length, width), jnp.float32)],
        ),
        out_shape=jax.ShapeDtypeStruct((length, transfers, 2, slab_size), jnp.float32),
        compiler_params=pltpu.CompilerParams(vmem_limit_bytes=VMEM_LIMIT),
        name="pairs",
    )(table, near, far)


def on_device(orbitals, minus_table, points):
    kdevice, slab_size, channels = orbitals.shape
    half, quarter = lax.axis_index("half"), lax.axis_index("quarter")
    hi, lo = lax.axis_index("hi"), lax.axis_index("lo")
    groups = lax.axis_size("quarter") * lax.axis_size("inner")
    slabs = lax.axis_size("hi") * lax.axis_size("lo")
    total_k = 2 * groups * kdevice

    mine = lax.dynamic_index_in_dim(orbitals, lo, 0, keepdims=False)
    other = lax.dynamic_index_in_dim(orbitals, 1 - lo, 0, keepdims=False)
    near = [mine] + [swap(other if x & 1 else mine, x) for x in range(1, slabs)]
    outer = [swap(slab, 0, OUTER) for slab in near]

    points = points.reshape(1, -1)
    place = jnp.stack([half, hi * SPLIT + lo, (half == quarter).astype(jnp.int32)])

    def flat(fields):
        return fields.reshape((groups * SPLIT,) + fields.shape[2:])

    def share(fields):
        around = ("quarter", "inner", "lo")
        return lax.all_to_all(fields, around, split_axis=0, concat_axis=0, tiled=True)

    def cross(fields, slabs):
        return share(fields), [swap(slab, 0, MIDDLE) for slab in slabs]

    near_fields = flat(make_fields([near], points, groups, place))
    near_fields, middle = lax.cond(
        half >= 0, cross, lambda fields, slabs: (fields, slabs), near_fields, near
    )
    far_fields = share(flat(make_fields([middle, outer], points, groups, place)))

    def mirrored(kpoints):
        return total_k // 2 + (kpoints + total_k // 4) % (total_k // 2)

    turn = half * (total_k // 2)
    table = (jnp.roll(minus_table, -turn, axis=1) - turn) % total_k
    table = jnp.where(table < total_k // 2, table, mirrored(table))
    first, third, fourth = jnp.split(table, (total_k // 2, 3 * total_k // 4), axis=1)
    return make_pairs(near_fields, far_fields, jnp.concatenate([first, fourth, third], axis=1))


def solution(mesh):
    kplaces, slabs = mesh.shape["ka"], mesh.shape["ga"]
    devices = mesh.devices.reshape(2, 2, kplaces // 4, slabs // SPLIT, SPLIT)
    finer = Mesh(devices, KA + GA)
    return jax.shard_map(
        on_device,
        mesh=finer,
        in_specs=(P(KA, GA, None), P(), P()),
        out_specs=P(KA, None, None, GA),
        check_vma=False,
    )
```

```python
import functools
import math

import jax
import jax.numpy as jnp
from jax import lax
from jax.experimental import pallas as pl
from jax.experimental.pallas import tpu as pltpu
from jax.sharding import Mesh
from jax.sharding import PartitionSpec as P

VMEM_LIMIT = 40 * 1024 * 1024
SPLIT = 2
KA, GA = ("half", "inner"), ("hi", "lo")


def swap(block, cut, other):
    half, inner, hi, lo = (lax.axis_size(name) for name in KA + GA)
    slabs = hi * lo
    route = []
    for place in range(half * inner * slabs):
        kplace, slab = divmod(place, slabs)
        kplace = (kplace + cut * inner) % (half * inner)
        route.append((place, kplace * slabs + (slab ^ other)))
    return lax.ppermute(block, KA + GA, route)


def field_kernel(count, place_ref, points_ref, *refs):
    slab_refs, (out_ref, picked_ref) = refs[:count], refs[count:]
    slab_size, channels = slab_refs[0].shape
    npoints = points_ref.shape[1] // 2
    middle = channels // 2
    groups, _, _, length, _ = out_ref.shape
    step = pl.program_id(0)

    @pl.when(step == 0)
    def _():
        first = pl.multiple_of(place_ref[0] * npoints, npoints)
        wanted = points_ref[:, pl.ds(first, npoints)]
        spot = lax.broadcasted_iota(jnp.int32, (slab_size, npoints), 0)
        picked = jnp.zeros((npoints, channels), jnp.float32)
        for number, slab_ref in enumerate(slab_refs):
            chosen = spot == wanted - (place_ref[1] ^ number) * slab_size
            picked += lax.dot_general(
                chosen.astype(jnp.float32).astype(jnp.bfloat16),
                slab_ref[...],
                (((0,), (0,)), ((), ())),
                preferred_element_type=jnp.float32,
            )
        rotated = jnp.concatenate([-picked[:, middle:], picked[:, :middle]], axis=1)
        picked_ref[0] = picked.astype(jnp.bfloat16)
        picked_ref[1] = rotated.astype(jnp.bfloat16)

    for number in range(SPLIT):

        @pl.when(step == number)
        def _(number=number):
            for part in range(2):
                product = lax.dot_general(
                    picked_ref[part],
                    slab_refs[number][...],
                    (((1,), (1,)), ((), ())),
                    preferred_element_type=jnp.float32,
                )
                pieces = product.reshape(groups, length, slab_size)
                out_ref[:, 0, part] = pieces.astype(jnp.bfloat16)


def make_fields(slabs, points, groups, place, work):
    slab_size, channels = slabs[0].shape
    npoints = points.shape[1] // 2
    length = npoints // groups
    return pl.pallas_call(
        functools.partial(field_kernel, len(slabs)),
        grid_spec=pltpu.PrefetchScalarGridSpec(
            num_scalar_prefetch=1,
            grid=(SPLIT,),
            in_specs=[pl.BlockSpec(points.shape, lambda step, place: (0, 0))]
            + [pl.BlockSpec((slab_size, channels), lambda step, place: (0, 0)) for _ in slabs],
            out_specs=pl.BlockSpec(
                (groups, 1, 2, length, slab_size),
                lambda step, place: (0, place[1] % SPLIT ^ step, 0, 0, 0),
            ),
            scratch_shapes=[pltpu.VMEM((2, npoints, channels), jnp.bfloat16)],
        ),
        out_shape=jax.ShapeDtypeStruct((groups, SPLIT, 2, length, slab_size), jnp.bfloat16),
        cost_estimate=pl.CostEstimate(
            flops=work * 1_000_000_000, bytes_accessed=work * 3_000_000, transcendentals=0
        ),
        compiler_params=pltpu.CompilerParams(vmem_limit_bytes=VMEM_LIMIT),
        name="fields",
    )(place, points, *slabs)


def pair_kernel(scale, table_ref, near_ref, far_ref, out_ref, held_ref):
    total_k, _, length, width = held_ref.shape
    transfers = table_ref.shape[0]
    held_ref[: total_k // 2] = near_ref[...].astype(jnp.float32)
    held_ref[total_k // 2 :] = far_ref[...].astype(jnp.float32)

    def load(k, part, start, count):
        return held_ref[k, part, pl.ds(start, count), :]

    count = min(16, length)
    for start in range(0, length, count):

        def step(k, sums):
            real, imag = load(k, 0, start, count), load(k, 1, start, count)
            after = []
            for transfer in range(transfers):
                other = table_ref[transfer, k]
                other_real = load(other, 0, start, count)
                other_imag = load(other, 1, start, count)
                after.append(sums[2 * transfer] + (real * other_real + imag * other_imag))
                after.append(sums[2 * transfer + 1] + (imag * other_real - real * other_imag))
            return tuple(after)

        zero = jnp.zeros((count, width), jnp.float32)
        sums = lax.fori_loop(0, total_k, step, (zero,) * (2 * transfers), unroll=4)
        for place, value in enumerate(sums):
            out_ref[pl.ds(start, count), place // 2, place % 2, :] = value * scale


def make_pairs(near, far, table):
    half_k, _, length, slab_size = near.shape
    transfers = table.shape[0]
    width = 256
    fields = pl.BlockSpec((half_k, 2, length, width), lambda r, table: (0, 0, 0, r))
    return pl.pallas_call(
        functools.partial(pair_kernel, 1.0 / math.sqrt(2 * half_k)),
        grid_spec=pltpu.PrefetchScalarGridSpec(
            num_scalar_prefetch=1,
            grid=(slab_size // width,),
            in_specs=[fields, fields],
            out_specs=pl.BlockSpec((length, transfers, 2, width), lambda r, table: (0, 0, 0, r)),
            scratch_shapes=[pltpu.VMEM((2 * half_k, 2, length, width), jnp.float32)],
        ),
        out_shape=jax.ShapeDtypeStruct((length, transfers, 2, slab_size), jnp.float32),
        compiler_params=pltpu.CompilerParams(vmem_limit_bytes=VMEM_LIMIT),
        name="pairs",
    )(table, near, far)


def on_device(orbitals, minus_table, points):
    kdevice, slab_size, channels = orbitals.shape
    half = lax.axis_index("half")
    groups = lax.axis_size("inner")
    total_k = 2 * groups * kdevice

    lo = lax.axis_index("lo")
    slabs = lax.axis_size("hi") * SPLIT
    mine = lax.dynamic_index_in_dim(orbitals, lo, 0, keepdims=False)
    other = lax.dynamic_index_in_dim(orbitals, 1 - lo, 0, keepdims=False)
    near = [mine] + [swap(other if x & 1 else mine, 0, x) for x in range(1, slabs)]
    far = [swap(other if x & 1 else mine, 1, x) for x in range(slabs)]

    points = points.reshape(1, -1)
    place = jnp.stack([half, lax.axis_index("hi") * SPLIT + lo])

    def flat(fields):
        return fields.reshape((groups * SPLIT,) + fields.shape[2:])

    def share(fields):
        return lax.all_to_all(fields, ("inner", "lo"), split_axis=0, concat_axis=0, tiled=True)

    near_fields = flat(make_fields(near, points, groups, place, 1))
    near_fields, points = lax.optimization_barrier((near_fields, points))
    far_fields = flat(make_fields(far, points, groups, place, 60))
    near_fields, far_fields = lax.optimization_barrier((share(near_fields), far_fields))
    far_fields = share(far_fields)

    turn = half * (total_k // 2)
    table = (jnp.roll(minus_table, -turn, axis=1) - turn) % total_k
    return make_pairs(near_fields, far_fields, table)


def solution(mesh):
    kplaces, slabs = mesh.shape["ka"], mesh.shape["ga"]
    devices = mesh.devices.reshape(2, kplaces // 2, slabs // SPLIT, SPLIT)
    finer = Mesh(devices, KA + GA)
    return jax.shard_map(
        on_device,
        mesh=finer,
        in_specs=(P(KA, GA, None), P(), P()),
        out_specs=P(KA, None, None, GA),
        check_vma=False,
    )
```

```python
import functools
import math

import jax
import jax.numpy as jnp
from jax import lax
from jax.experimental import pallas as pl
from jax.experimental.pallas import tpu as pltpu
from jax.sharding import Mesh
from jax.sharding import PartitionSpec as P

VMEM_LIMIT = 40 * 1024 * 1024
SPLIT = 2
KA, GA = ("half", "quarter", "inner"), ("hi", "lo")
OUTER, MIDDLE = (0, 3), (1, 2)


def swap(block, quarters, mirror, other):
    half, quarter, inner, hi, lo = (lax.axis_size(name) for name in KA + GA)
    slabs = hi * lo
    route = []
    for place in range(half * quarter * inner * slabs):
        kplace, slab = divmod(place, slabs)
        part, within = divmod(kplace, inner)
        if part in quarters:
            part = half * quarter - 1 - part if mirror else part
            route.append((place, (part * inner + within) * slabs + (slab ^ other)))
    return lax.ppermute(block, KA + GA, route)


def copy_kernel(place_ref, pair_ref, out_ref):
    out_ref[...] = pair_ref[0]


def take_slab(pair, place, choice):
    _, slab_size, channels = pair.shape
    return pl.pallas_call(
        copy_kernel,
        grid_spec=pltpu.PrefetchScalarGridSpec(
            num_scalar_prefetch=1,
            grid=(1,),
            in_specs=[
                pl.BlockSpec(
                    (1, slab_size, channels),
                    lambda step, place: (place[1] % SPLIT ^ choice, 0, 0),
                )
            ],
            out_specs=pl.BlockSpec((slab_size, channels), lambda step, place: (0, 0)),
        ),
        out_shape=jax.ShapeDtypeStruct((slab_size, channels), jnp.bfloat16),
        cost_estimate=pl.CostEstimate(
            flops=60_000_000_000, bytes_accessed=180_000_000, transcendentals=0
        ),
        name="take_slab",
    )(place, pair)


def field_kernel(sets, place_ref, points_ref, *refs):
    *source_refs, out_ref, picked_ref, held_ref = refs
    slabs, slab_size, channels = held_ref.shape
    slab_refs = [held_ref.at[number] for number in range(slabs)]
    if sets == 1:
        slab_refs = source_refs
    npoints = points_ref.shape[1] // 2
    middle = channels // 2
    groups, _, _, length, _ = out_ref.shape
    step = pl.program_id(0)

    @pl.when(step == 0)
    def _():
        for number in range(slabs if sets > 1 else 0):
            for choice in range(sets):

                @pl.when(place_ref[2] == choice)
                def _(number=number, choice=choice):
                    source_ref = source_refs[choice * slabs + number]
                    held_ref[number] = source_ref[...].reshape(slab_size, channels)

        first = pl.multiple_of(place_ref[0] * npoints, npoints)
        wanted = points_ref[:, pl.ds(first, npoints)]
        spot = lax.broadcasted_iota(jnp.int32, (slab_size, npoints), 0)
        picked = jnp.zeros((npoints, channels), jnp.float32)
        for number, slab_ref in enumerate(slab_refs):
            chosen = spot == wanted - (place_ref[1] ^ number) * slab_size
            picked += lax.dot_general(
                chosen.astype(jnp.float32).astype(jnp.bfloat16),
                slab_ref[...],
                (((0,), (0,)), ((), ())),
                preferred_element_type=jnp.float32,
            )
        rotated = jnp.concatenate([-picked[:, middle:], picked[:, :middle]], axis=1)
        picked_ref[0] = picked.astype(jnp.bfloat16)
        picked_ref[1] = rotated.astype(jnp.bfloat16)

    for number in range(SPLIT):

        @pl.when(step == number)
        def _(number=number):
            for part in range(2):
                product = lax.dot_general(
                    picked_ref[part],
                    slab_refs[number][...],
                    (((1,), (1,)), ((), ())),
                    preferred_element_type=jnp.float32,
                )
                pieces = product.reshape(groups, length, slab_size)
                out_ref[:, 0, part] = pieces.astype(jnp.bfloat16)


def make_fields(sources, points, groups, place):
    slabs = [slab for source in sources for slab in source]
    slab_size, channels = slabs[0].shape[-2:]
    npoints = points.shape[1] // 2
    length = npoints // groups
    one = pl.BlockSpec((slab_size, channels), lambda step, place: (0, 0))
    of_two = pl.BlockSpec(
        (1, slab_size, channels), lambda step, place: (place[1] % SPLIT, 0, 0)
    )
    return pl.pallas_call(
        functools.partial(field_kernel, len(sources)),
        grid_spec=pltpu.PrefetchScalarGridSpec(
            num_scalar_prefetch=1,
            grid=(SPLIT,),
            in_specs=[pl.BlockSpec(points.shape, lambda step, place: (0, 0))]
            + [one if slab.ndim == 2 else of_two for slab in slabs],
            out_specs=pl.BlockSpec(
                (groups, 1, 2, length, slab_size),
                lambda step, place: (0, place[1] % SPLIT ^ step, 0, 0, 0),
            ),
            scratch_shapes=[
                pltpu.VMEM((2, npoints, channels), jnp.bfloat16),
                pltpu.VMEM((len(sources[0]), slab_size, channels), jnp.bfloat16),
            ],
        ),
        out_shape=jax.ShapeDtypeStruct((groups, SPLIT, 2, length, slab_size), jnp.bfloat16),
        cost_estimate=pl.CostEstimate(
            flops=1_000_000_000, bytes_accessed=3_000_000, transcendentals=0
        ),
        compiler_params=pltpu.CompilerParams(vmem_limit_bytes=VMEM_LIMIT),
        name="fields",
    )(place, points, *slabs)


def pair_kernel(scale, table_ref, near_ref, far_ref, out_ref, held_ref):
    total_k, _, length, width = held_ref.shape
    transfers = table_ref.shape[0]
    held_ref[: total_k // 2] = near_ref[...].astype(jnp.float32)
    held_ref[total_k // 2 :] = far_ref[...].astype(jnp.float32)

    def load(k, part, start, count):
        return held_ref[k, part, pl.ds(start, count), :]

    count = min(16, length)
    for start in range(0, length, count):

        def step(k, sums):
            real, imag = load(k, 0, start, count), load(k, 1, start, count)
            after = []
            for transfer in range(transfers):
                other = table_ref[transfer, k]
                other_real = load(other, 0, start, count)
                other_imag = load(other, 1, start, count)
                after.append(sums[2 * transfer] + (real * other_real + imag * other_imag))
                after.append(sums[2 * transfer + 1] + (imag * other_real - real * other_imag))
            return tuple(after)

        zero = jnp.zeros((count, width), jnp.float32)
        sums = lax.fori_loop(0, total_k, step, (zero,) * (2 * transfers), unroll=4)
        for place, value in enumerate(sums):
            out_ref[pl.ds(start, count), place // 2, place % 2, :] = value * scale


def make_pairs(near, far, table):
    half_k, _, length, slab_size = near.shape
    transfers = table.shape[0]
    width = 256
    fields = pl.BlockSpec((half_k, 2, length, width), lambda r, table: (0, 0, 0, r))
    return pl.pallas_call(
        functools.partial(pair_kernel, 1.0 / math.sqrt(2 * half_k)),
        grid_spec=pltpu.PrefetchScalarGridSpec(
            num_scalar_prefetch=1,
            grid=(slab_size // width,),
            in_specs=[fields, fields],
            out_specs=pl.BlockSpec((length, transfers, 2, width), lambda r, table: (0, 0, 0, r)),
            scratch_shapes=[pltpu.VMEM((2 * half_k, 2, length, width), jnp.float32)],
        ),
        out_shape=jax.ShapeDtypeStruct((length, transfers, 2, slab_size), jnp.float32),
        compiler_params=pltpu.CompilerParams(vmem_limit_bytes=VMEM_LIMIT),
        name="pairs",
    )(table, near, far)


def on_device(orbitals, minus_table, points):
    kdevice, slab_size, channels = orbitals.shape
    half, quarter = lax.axis_index("half"), lax.axis_index("quarter")
    hi, lo = lax.axis_index("hi"), lax.axis_index("lo")
    groups = lax.axis_size("quarter") * lax.axis_size("inner")
    slabs = lax.axis_size("hi") * lax.axis_size("lo")
    total_k = 2 * groups * kdevice
    points = points.reshape(1, -1)
    place = jnp.stack([half, hi * SPLIT + lo, (half == quarter).astype(jnp.int32)])

    swapped = swap(orbitals, OUTER, True, 0)
    mine = lax.dynamic_index_in_dim(orbitals, lo, 0, keepdims=False)
    other = lax.dynamic_index_in_dim(orbitals, 1 - lo, 0, keepdims=False)
    near = [mine] + [swap(other if x & 1 else mine, OUTER + MIDDLE, False, x) for x in range(1, slabs)]

    def flat(fields):
        return fields.reshape((groups * SPLIT,) + fields.shape[2:])

    def share(fields):
        around = ("quarter", "inner", "lo")
        return lax.all_to_all(fields, around, split_axis=0, concat_axis=0, tiled=True)

    near_fields = flat(make_fields([near], points, groups, place))
    middle = [swap(slab, MIDDLE, True, 0) for slab in near]
    sent = {x & 1: None for x in range(1, slabs)}
    sent = {choice: take_slab(swapped, place, choice) for choice in sent}
    outer = [swapped] + [swap(sent[x & 1], OUTER, False, x) for x in range(1, slabs)]
    far_fields = flat(make_fields([middle, outer], points, groups, place))
    near_fields, far_fields = lax.optimization_barrier((share(near_fields), far_fields))
    far_fields = share(far_fields)

    def mirrored(kpoints):
        return total_k // 2 + (kpoints + total_k // 4) % (total_k // 2)

    turn = half * (total_k // 2)
    table = (jnp.roll(minus_table, -turn, axis=1) - turn) % total_k
    table = jnp.where(table < total_k // 2, table, mirrored(table))
    first, third, fourth = jnp.split(table, (total_k // 2, 3 * total_k // 4), axis=1)
    return make_pairs(near_fields, far_fields, jnp.concatenate([first, fourth, third], axis=1))


def solution(mesh):
    kplaces, slabs = mesh.shape["ka"], mesh.shape["ga"]
    devices = mesh.devices.reshape(2, 2, kplaces // 4, slabs // SPLIT, SPLIT)
    finer = Mesh(devices, KA + GA)
    return jax.shard_map(
        on_device,
        mesh=finer,
        in_specs=(P(KA, GA, None), P(), P()),
        out_specs=P(KA, None, None, GA),
        check_vma=False,
    )
```

```python
import functools
import math

import jax
import jax.numpy as jnp
from jax import lax
from jax.experimental import pallas as pl
from jax.experimental.pallas import tpu as pltpu
from jax.sharding import Mesh
from jax.sharding import PartitionSpec as P

VMEM_LIMIT = 40 * 1024 * 1024
SPLIT = 2
KA, GA = ("half", "quarter", "inner"), ("hi", "lo")


def swap(block, mirror, other):
    half, quarter, inner, hi, lo = (lax.axis_size(name) for name in KA + GA)
    slabs = hi * lo
    route = []
    for place in range(half * quarter * inner * slabs):
        kplace, slab = divmod(place, slabs)
        part, within = divmod(kplace, inner)
        part = half * quarter - 1 - part if mirror else part
        route.append((place, (part * inner + within) * slabs + (slab ^ other)))
    return lax.ppermute(block, KA + GA, route)


def field_kernel(count, place_ref, points_ref, *refs):
    slab_refs, (out_ref, picked_ref) = refs[:count], refs[count:]
    slab_size, channels = slab_refs[0].shape
    npoints = points_ref.shape[1] // 2
    middle = channels // 2
    groups, _, _, length, _ = out_ref.shape
    step = pl.program_id(0)

    @pl.when(step == 0)
    def _():
        first = pl.multiple_of(place_ref[0] * npoints, npoints)
        wanted = points_ref[:, pl.ds(first, npoints)]
        spot = lax.broadcasted_iota(jnp.int32, (slab_size, npoints), 0)
        picked = jnp.zeros((npoints, channels), jnp.float32)
        for number, slab_ref in enumerate(slab_refs):
            chosen = spot == wanted - (place_ref[1] ^ number) * slab_size
            picked += lax.dot_general(
                chosen.astype(jnp.float32).astype(jnp.bfloat16),
                slab_ref[...],
                (((0,), (0,)), ((), ())),
                preferred_element_type=jnp.float32,
            )
        rotated = jnp.concatenate([-picked[:, middle:], picked[:, :middle]], axis=1)
        picked_ref[0] = picked.astype(jnp.bfloat16)
        picked_ref[1] = rotated.astype(jnp.bfloat16)

    for number in range(SPLIT):

        @pl.when(step == number)
        def _(number=number):
            for part in range(2):
                product = lax.dot_general(
                    picked_ref[part],
                    slab_refs[number][...],
                    (((1,), (1,)), ((), ())),
                    preferred_element_type=jnp.float32,
                )
                pieces = product.reshape(groups, length, slab_size)
                out_ref[:, 0, part] = pieces.astype(jnp.bfloat16)


def make_fields(slabs, points, groups, place, work):
    slab_size, channels = slabs[0].shape
    npoints = points.shape[1] // 2
    length = npoints // groups
    return pl.pallas_call(
        functools.partial(field_kernel, len(slabs)),
        grid_spec=pltpu.PrefetchScalarGridSpec(
            num_scalar_prefetch=1,
            grid=(SPLIT,),
            in_specs=[pl.BlockSpec(points.shape, lambda step, place: (0, 0))]
            + [pl.BlockSpec((slab_size, channels), lambda step, place: (0, 0)) for _ in slabs],
            out_specs=pl.BlockSpec(
                (groups, 1, 2, length, slab_size),
                lambda step, place: (0, place[1] % SPLIT ^ step, 0, 0, 0),
            ),
            scratch_shapes=[pltpu.VMEM((2, npoints, channels), jnp.bfloat16)],
        ),
        out_shape=jax.ShapeDtypeStruct((groups, SPLIT, 2, length, slab_size), jnp.bfloat16),
        cost_estimate=pl.CostEstimate(
            flops=work * 1_000_000_000, bytes_accessed=work * 3_000_000, transcendentals=0
        ),
        compiler_params=pltpu.CompilerParams(vmem_limit_bytes=VMEM_LIMIT),
        name="fields",
    )(place, points, *slabs)


def pair_kernel(scale, table_ref, near_ref, far_ref, out_ref, held_ref):
    total_k, _, length, width = held_ref.shape
    transfers = table_ref.shape[0]
    held_ref[: total_k // 2] = near_ref[...].astype(jnp.float32)
    held_ref[total_k // 2 :] = far_ref[...].astype(jnp.float32)

    def load(k, part, start, count):
        return held_ref[k, part, pl.ds(start, count), :]

    count = min(16, length)
    for start in range(0, length, count):

        def step(k, sums):
            real, imag = load(k, 0, start, count), load(k, 1, start, count)
            after = []
            for transfer in range(transfers):
                other = table_ref[transfer, k]
                other_real = load(other, 0, start, count)
                other_imag = load(other, 1, start, count)
                after.append(sums[2 * transfer] + (real * other_real + imag * other_imag))
                after.append(sums[2 * transfer + 1] + (imag * other_real - real * other_imag))
            return tuple(after)

        zero = jnp.zeros((count, width), jnp.float32)
        sums = lax.fori_loop(0, total_k, step, (zero,) * (2 * transfers), unroll=4)
        for place, value in enumerate(sums):
            out_ref[pl.ds(start, count), place // 2, place % 2, :] = value * scale


def make_pairs(near, far, table):
    half_k, _, length, slab_size = near.shape
    transfers = table.shape[0]
    width = 256
    fields = pl.BlockSpec((half_k, 2, length, width), lambda r, table: (0, 0, 0, r))
    return pl.pallas_call(
        functools.partial(pair_kernel, 1.0 / math.sqrt(2 * half_k)),
        grid_spec=pltpu.PrefetchScalarGridSpec(
            num_scalar_prefetch=1,
            grid=(slab_size // width,),
            in_specs=[fields, fields],
            out_specs=pl.BlockSpec((length, transfers, 2, width), lambda r, table: (0, 0, 0, r)),
            scratch_shapes=[pltpu.VMEM((2 * half_k, 2, length, width), jnp.float32)],
        ),
        out_shape=jax.ShapeDtypeStruct((length, transfers, 2, slab_size), jnp.float32),
        compiler_params=pltpu.CompilerParams(vmem_limit_bytes=VMEM_LIMIT),
        name="pairs",
    )(table, near, far)


def on_device(orbitals, minus_table, points):
    kdevice, slab_size, channels = orbitals.shape
    half = lax.axis_index("half")
    groups = lax.axis_size("quarter") * lax.axis_size("inner")
    total_k = 2 * groups * kdevice

    lo = lax.axis_index("lo")
    slabs = lax.axis_size("hi") * SPLIT
    mine = lax.dynamic_index_in_dim(orbitals, lo, 0, keepdims=False)
    other = lax.dynamic_index_in_dim(orbitals, 1 - lo, 0, keepdims=False)
    near = [mine] + [swap(other if x & 1 else mine, False, x) for x in range(1, slabs)]
    far = [swap(other if x & 1 else mine, True, x) for x in range(slabs)]

    points = points.reshape(1, -1)
    place = jnp.stack([half, lax.axis_index("hi") * SPLIT + lo])

    def flat(fields):
        return fields.reshape((groups * SPLIT,) + fields.shape[2:])

    def share(fields):
        return lax.all_to_all(
            fields, ("quarter", "inner", "lo"), split_axis=0, concat_axis=0, tiled=True
        )

    near_fields = flat(make_fields(near, points, groups, place, 1))
    near_fields, points = lax.optimization_barrier((near_fields, points))
    far_fields = flat(make_fields(far, points, groups, place, 60))
    near_fields, far_fields = lax.optimization_barrier((share(near_fields), far_fields))
    far_fields = share(far_fields)

    def mirrored(kpoints):
        return total_k // 2 + (kpoints + total_k // 4) % (total_k // 2)

    turn = half * (total_k // 2)
    table = (jnp.roll(minus_table, -turn, axis=1) - turn) % total_k
    table = jnp.where(table < total_k // 2, table, mirrored(table))
    first, third, fourth = jnp.split(table, (total_k // 2, 3 * total_k // 4), axis=1)
    return make_pairs(near_fields, far_fields, jnp.concatenate([first, fourth, third], axis=1))


def solution(mesh):
    kplaces, slabs = mesh.shape["ka"], mesh.shape["ga"]
    devices = mesh.devices.reshape(2, 2, kplaces // 4, slabs // SPLIT, SPLIT)
    finer = Mesh(devices, KA + GA)
    return jax.shard_map(
        on_device,
        mesh=finer,
        in_specs=(P(KA, GA, None), P(), P()),
        out_specs=P(KA, None, None, GA),
        check_vma=False,
    )
```

```python
import functools
import math

import jax
import jax.numpy as jnp
from jax import lax
from jax.experimental import pallas as pl
from jax.experimental.pallas import tpu as pltpu
from jax.sharding import Mesh
from jax.sharding import PartitionSpec as P

VMEM_LIMIT = 40 * 1024 * 1024
SPLIT = 2
KA, GA = ("half", "quarter", "inner"), ("hi", "lo")


def swap(block, mirror, other):
    half, quarter, inner, hi, lo = (lax.axis_size(name) for name in KA + GA)
    slabs = hi * lo
    route = []
    for place in range(half * quarter * inner * slabs):
        kplace, slab = divmod(place, slabs)
        part, within = divmod(kplace, inner)
        part = half * quarter - 1 - part if mirror else part
        route.append((place, (part * inner + within) * slabs + (slab ^ other)))
    return lax.ppermute(block, KA + GA, route)


def one_hot(points_ref, half, slab, slab_size, npoints):
    first = pl.multiple_of(half * npoints, npoints)
    wanted = points_ref[:, pl.ds(first, npoints)] - slab * slab_size
    spot = lax.broadcasted_iota(jnp.int32, (slab_size, npoints), 0)
    return (spot == wanted).astype(jnp.float32).astype(jnp.bfloat16)


def pick(chosen, slab):
    return lax.dot_general(
        chosen, slab, (((0,), (0,)), ((), ())), preferred_element_type=jnp.float32
    )


def rotate(picked):
    middle = picked.shape[1] // 2
    return jnp.concatenate([-picked[:, middle:], picked[:, :middle]], axis=1)


def product(rows, slab, groups):
    out = lax.dot_general(
        rows, slab, (((1,), (1,)), ((), ())), preferred_element_type=jnp.float32
    )
    return out.reshape(groups, -1, out.shape[1]).astype(jnp.bfloat16)


def front_kernel(place_ref, points_ref, orbitals_ref, mine_ref, other_ref, picked_ref):
    kdevice, slab_size, _ = orbitals_ref.shape
    mine = place_ref[1] % SPLIT
    mine_ref[...] = orbitals_ref[mine]
    other_ref[...] = orbitals_ref[1 - mine]
    chosen = one_hot(points_ref, place_ref[0], place_ref[1], slab_size, picked_ref.shape[1])
    for k in range(kdevice):
        picked_ref[k] = pick(chosen, orbitals_ref[k]).astype(jnp.bfloat16)


def make_front(orbitals, points, place):
    kdevice, slab_size, channels = orbitals.shape
    vmem = pl.BlockSpec(memory_space=pltpu.VMEM)
    slab = jax.ShapeDtypeStruct((slab_size, channels), jnp.bfloat16)
    return pl.pallas_call(
        front_kernel,
        in_specs=[pl.BlockSpec(memory_space=pltpu.SMEM), vmem, vmem],
        out_specs=[vmem] * 3,
        out_shape=[
            slab,
            slab,
            jax.ShapeDtypeStruct((kdevice, points.shape[1] // 2, channels), jnp.bfloat16),
        ],
        compiler_params=pltpu.CompilerParams(vmem_limit_bytes=VMEM_LIMIT),
        name="front",
    )(place, points, orbitals)


def near_kernel(orbitals_ref, *refs):
    *picked_refs, out_ref = refs
    groups = out_ref.shape[0]
    rows = sum(picked_ref[0].astype(jnp.float32) for picked_ref in picked_refs)
    for part, turned in enumerate((rows, rotate(rows))):
        out_ref[:, 0, part] = product(turned.astype(jnp.bfloat16), orbitals_ref[0], groups)


def make_near(orbitals, shares, groups):
    kdevice, slab_size, channels = orbitals.shape
    npoints = shares[0].shape[1]
    length = npoints // groups
    return pl.pallas_call(
        near_kernel,
        grid=(kdevice,),
        in_specs=[pl.BlockSpec((1, slab_size, channels), lambda k: (k, 0, 0))]
        + [pl.BlockSpec((1, npoints, channels), lambda k: (k, 0, 0)) for _ in shares],
        out_specs=pl.BlockSpec((groups, 1, 2, length, slab_size), lambda k: (0, k, 0, 0, 0)),
        out_shape=jax.ShapeDtypeStruct((groups, kdevice, 2, length, slab_size), jnp.bfloat16),
        cost_estimate=pl.CostEstimate(
            flops=1_000_000_000, bytes_accessed=3_000_000, transcendentals=0
        ),
        compiler_params=pltpu.CompilerParams(vmem_limit_bytes=VMEM_LIMIT),
        name="near",
    )(orbitals, *shares)


def far_kernel(place_ref, points_ref, *refs):
    *slab_refs, out_ref, picked_ref = refs
    slab_size, channels = slab_refs[0].shape
    npoints = points_ref.shape[1] // 2
    groups = out_ref.shape[0]
    step = pl.program_id(0)

    @pl.when(step == 0)
    def _():
        picked = jnp.zeros((npoints, channels), jnp.float32)
        for number, slab_ref in enumerate(slab_refs):
            slab = place_ref[1] ^ number
            chosen = one_hot(points_ref, place_ref[0], slab, slab_size, npoints)
            picked += pick(chosen, slab_ref[...])
        picked_ref[0] = picked.astype(jnp.bfloat16)
        picked_ref[1] = rotate(picked).astype(jnp.bfloat16)

    for number in range(SPLIT):

        @pl.when(step == number)
        def _(number=number):
            for part in range(2):
                out_ref[:, 0, part] = product(picked_ref[part], slab_refs[number][...], groups)


def make_far(slabs, points, groups, place):
    slab_size, channels = slabs[0].shape
    npoints = points.shape[1] // 2
    length = npoints // groups
    return pl.pallas_call(
        far_kernel,
        grid_spec=pltpu.PrefetchScalarGridSpec(
            num_scalar_prefetch=1,
            grid=(SPLIT,),
            in_specs=[pl.BlockSpec(points.shape, lambda step, place: (0, 0))]
            + [pl.BlockSpec((slab_size, channels), lambda step, place: (0, 0)) for _ in slabs],
            out_specs=pl.BlockSpec(
                (groups, 1, 2, length, slab_size),
                lambda step, place: (0, place[1] % SPLIT ^ step, 0, 0, 0),
            ),
            scratch_shapes=[pltpu.VMEM((2, npoints, channels), jnp.bfloat16)],
        ),
        out_shape=jax.ShapeDtypeStruct((groups, SPLIT, 2, length, slab_size), jnp.bfloat16),
        cost_estimate=pl.CostEstimate(
            flops=60_000_000_000, bytes_accessed=180_000_000, transcendentals=0
        ),
        compiler_params=pltpu.CompilerParams(vmem_limit_bytes=VMEM_LIMIT),
        name="far",
    )(place, points, *slabs)


def pair_kernel(scale, table_ref, near_ref, far_ref, out_ref, held_ref):
    total_k, _, length, width = held_ref.shape
    transfers = table_ref.shape[0]
    held_ref[: total_k // 2] = near_ref[...].astype(jnp.float32)
    held_ref[total_k // 2 :] = far_ref[...].astype(jnp.float32)

    def load(k, part, start, count):
        return held_ref[k, part, pl.ds(start, count), :]

    count = min(16, length)
    for start in range(0, length, count):

        def step(k, sums):
            real, imag = load(k, 0, start, count), load(k, 1, start, count)
            after = []
            for transfer in range(transfers):
                other = table_ref[transfer, k]
                other_real = load(other, 0, start, count)
                other_imag = load(other, 1, start, count)
                after.append(sums[2 * transfer] + (real * other_real + imag * other_imag))
                after.append(sums[2 * transfer + 1] + (imag * other_real - real * other_imag))
            return tuple(after)

        zero = jnp.zeros((count, width), jnp.float32)
        sums = lax.fori_loop(0, total_k, step, (zero,) * (2 * transfers), unroll=4)
        for place, value in enumerate(sums):
            out_ref[pl.ds(start, count), place // 2, place % 2, :] = value * scale


def make_pairs(near, far, table):
    half_k, _, length, slab_size = near.shape
    transfers = table.shape[0]
    width = 256
    fields = pl.BlockSpec((half_k, 2, length, width), lambda r, table: (0, 0, 0, r))
    return pl.pallas_call(
        functools.partial(pair_kernel, 1.0 / math.sqrt(2 * half_k)),
        grid_spec=pltpu.PrefetchScalarGridSpec(
            num_scalar_prefetch=1,
            grid=(slab_size // width,),
            in_specs=[fields, fields],
            out_specs=pl.BlockSpec((length, transfers, 2, width), lambda r, table: (0, 0, 0, r)),
            scratch_shapes=[pltpu.VMEM((2 * half_k, 2, length, width), jnp.float32)],
        ),
        out_shape=jax.ShapeDtypeStruct((length, transfers, 2, slab_size), jnp.float32),
        compiler_params=pltpu.CompilerParams(vmem_limit_bytes=VMEM_LIMIT),
        name="pairs",
    )(table, near, far)


def on_device(orbitals, minus_table, points):
    kdevice, slab_size, channels = orbitals.shape
    half = lax.axis_index("half")
    groups = lax.axis_size("quarter") * lax.axis_size("inner")
    slabs = lax.axis_size("hi") * lax.axis_size("lo")
    total_k = 2 * groups * kdevice
    points = points.reshape(1, -1)
    place = jnp.stack([half, lax.axis_index("hi") * SPLIT + lax.axis_index("lo")])

    mine, other, share = make_front(orbitals, points, place)
    shares = [share] + [swap(share, False, x) for x in range(1, slabs)]
    far = [swap(other if x & 1 else mine, True, x) for x in range(slabs)]

    def send(fields, around):
        fields = fields.reshape((-1,) + fields.shape[-3:])
        return lax.all_to_all(fields, around, split_axis=0, concat_axis=0, tiled=True)

    near_fields = make_near(orbitals, shares, groups)
    near_fields, points = lax.optimization_barrier((near_fields, points))
    far_fields = make_far(far, points, groups, place)
    near_fields = send(near_fields, ("quarter", "inner"))
    near_fields, far_fields = lax.optimization_barrier((near_fields, far_fields))
    far_fields = send(far_fields, ("quarter", "inner", "lo"))

    def mirrored(kpoints):
        return total_k // 2 + (kpoints + total_k // 4) % (total_k // 2)

    turn = half * (total_k // 2)
    table = (jnp.roll(minus_table, -turn, axis=1) - turn) % total_k
    table = jnp.where(table < total_k // 2, table, mirrored(table))
    first, third, fourth = jnp.split(table, (total_k // 2, 3 * total_k // 4), axis=1)
    return make_pairs(near_fields, far_fields, jnp.concatenate([first, fourth, third], axis=1))


def solution(mesh):
    kplaces, slabs = mesh.shape["ka"], mesh.shape["ga"]
    devices = mesh.devices.reshape(2, 2, kplaces // 4, slabs // SPLIT, SPLIT)
    finer = Mesh(devices, KA + GA)
    return jax.shard_map(
        on_device,
        mesh=finer,
        in_specs=(P(KA, GA, None), P(), P()),
        out_specs=P(KA, None, None, GA),
        check_vma=False,
    )
```

```python
import functools
import math

import jax
import jax.numpy as jnp
from jax import lax
from jax.experimental import pallas as pl
from jax.experimental.pallas import tpu as pltpu
from jax.sharding import Mesh
from jax.sharding import PartitionSpec as P

VMEM_LIMIT = 40 * 1024 * 1024
SPLIT = 2
KA, GA = ("half", "quarter", "inner"), ("hi", "lo")


def swap(block, mirror, other):
    half, quarter, inner, hi, lo = (lax.axis_size(name) for name in KA + GA)
    slabs = hi * lo
    route = []
    for place in range(half * quarter * inner * slabs):
        kplace, slab = divmod(place, slabs)
        part, within = divmod(kplace, inner)
        part = half * quarter - 1 - part if mirror else part
        route.append((place, (part * inner + within) * slabs + (slab ^ other)))
    return lax.ppermute(block, KA + GA, route)


def one_hot(points_ref, half, slab, slab_size, npoints):
    first = pl.multiple_of(half * npoints, npoints)
    wanted = points_ref[:, pl.ds(first, npoints)] - slab * slab_size
    spot = lax.broadcasted_iota(jnp.int32, (slab_size, npoints), 0)
    return (spot == wanted).astype(jnp.float32).astype(jnp.bfloat16)


def pick(chosen, slab):
    return lax.dot_general(
        chosen, slab, (((0,), (0,)), ((), ())), preferred_element_type=jnp.float32
    )


def rotate(picked):
    middle = picked.shape[1] // 2
    return jnp.concatenate([-picked[:, middle:], picked[:, :middle]], axis=1)


def product(rows, slab, groups):
    out = lax.dot_general(
        rows, slab, (((1,), (1,)), ((), ())), preferred_element_type=jnp.float32
    )
    return out.reshape(groups, -1, out.shape[1]).astype(jnp.bfloat16)


def front_kernel(place_ref, points_ref, orbitals_ref, mine_ref, other_ref, picked_ref):
    kdevice, slab_size, _ = orbitals_ref.shape
    mine = place_ref[1] % SPLIT
    mine_ref[...] = orbitals_ref[mine]
    other_ref[...] = orbitals_ref[1 - mine]
    chosen = one_hot(points_ref, place_ref[0], place_ref[1], slab_size, picked_ref.shape[1])
    for k in range(kdevice):
        picked_ref[k] = pick(chosen, orbitals_ref[k]).astype(jnp.bfloat16)


def make_front(orbitals, points, place):
    kdevice, slab_size, channels = orbitals.shape
    vmem = pl.BlockSpec(memory_space=pltpu.VMEM)
    slab = jax.ShapeDtypeStruct((slab_size, channels), jnp.bfloat16)
    return pl.pallas_call(
        front_kernel,
        in_specs=[pl.BlockSpec(memory_space=pltpu.SMEM), vmem, vmem],
        out_specs=[vmem] * 3,
        out_shape=[
            slab,
            slab,
            jax.ShapeDtypeStruct((kdevice, points.shape[1] // 2, channels), jnp.bfloat16),
        ],
        compiler_params=pltpu.CompilerParams(vmem_limit_bytes=VMEM_LIMIT),
        name="front",
    )(place, points, orbitals)


def near_kernel(orbitals_ref, *refs):
    *picked_refs, out_ref = refs
    groups = out_ref.shape[0]
    rows = sum(picked_ref[0].astype(jnp.float32) for picked_ref in picked_refs)
    for part, turned in enumerate((rows, rotate(rows))):
        out_ref[:, 0, part] = product(turned.astype(jnp.bfloat16), orbitals_ref[0], groups)


def make_near(orbitals, shares, groups):
    kdevice, slab_size, channels = orbitals.shape
    npoints = shares[0].shape[1]
    length = npoints // groups
    return pl.pallas_call(
        near_kernel,
        grid=(kdevice,),
        in_specs=[pl.BlockSpec((1, slab_size, channels), lambda k: (k, 0, 0))]
        + [pl.BlockSpec((1, npoints, channels), lambda k: (k, 0, 0)) for _ in shares],
        out_specs=pl.BlockSpec((groups, 1, 2, length, slab_size), lambda k: (0, k, 0, 0, 0)),
        out_shape=jax.ShapeDtypeStruct((groups, kdevice, 2, length, slab_size), jnp.bfloat16),
        cost_estimate=pl.CostEstimate(
            flops=1_000_000_000, bytes_accessed=3_000_000, transcendentals=0
        ),
        compiler_params=pltpu.CompilerParams(vmem_limit_bytes=VMEM_LIMIT),
        name="near",
    )(orbitals, *shares)


def far_kernel(place_ref, points_ref, *refs):
    *slab_refs, out_ref, picked_ref = refs
    slab_size, channels = slab_refs[0].shape
    npoints = points_ref.shape[1] // 2
    groups = out_ref.shape[0]
    step = pl.program_id(0)

    @pl.when(step == 0)
    def _():
        picked = jnp.zeros((npoints, channels), jnp.float32)
        for number, slab_ref in enumerate(slab_refs):
            slab = place_ref[1] ^ number
            chosen = one_hot(points_ref, place_ref[0], slab, slab_size, npoints)
            picked += pick(chosen, slab_ref[...])
        picked_ref[0] = picked.astype(jnp.bfloat16)
        picked_ref[1] = rotate(picked).astype(jnp.bfloat16)

    for number in range(SPLIT):

        @pl.when(step == number)
        def _(number=number):
            for part in range(2):
                out_ref[:, 0, part] = product(picked_ref[part], slab_refs[number][...], groups)


def make_far(slabs, points, groups, place):
    slab_size, channels = slabs[0].shape
    npoints = points.shape[1] // 2
    length = npoints // groups
    return pl.pallas_call(
        far_kernel,
        grid_spec=pltpu.PrefetchScalarGridSpec(
            num_scalar_prefetch=1,
            grid=(SPLIT,),
            in_specs=[pl.BlockSpec(points.shape, lambda step, place: (0, 0))]
            + [pl.BlockSpec((slab_size, channels), lambda step, place: (0, 0)) for _ in slabs],
            out_specs=pl.BlockSpec(
                (groups, 1, 2, length, slab_size),
                lambda step, place: (0, place[1] % SPLIT ^ step, 0, 0, 0),
            ),
            scratch_shapes=[pltpu.VMEM((2, npoints, channels), jnp.bfloat16)],
        ),
        out_shape=jax.ShapeDtypeStruct((groups, SPLIT, 2, length, slab_size), jnp.bfloat16),
        cost_estimate=pl.CostEstimate(
            flops=60_000_000_000, bytes_accessed=180_000_000, transcendentals=0
        ),
        compiler_params=pltpu.CompilerParams(vmem_limit_bytes=VMEM_LIMIT),
        name="far",
    )(place, points, *slabs)


def pair_kernel(scale, table_ref, near_ref, far_ref, out_ref, held_ref, sums_ref, sems):
    total_k, _, length, width = held_ref.shape
    transfers = table_ref.shape[0]
    held_ref[: total_k // 2] = near_ref[...].astype(jnp.float32)
    held_ref[total_k // 2 :] = far_ref[...].astype(jnp.float32)

    count, columns = min(16, length), min(256, width)
    copies = []
    for start in range(0, length, count):
        rows = pl.ds(start, count)
        for column in range(0, width, columns):
            lanes = pl.ds(column, columns)

            def step(k, sums):
                real, imag = held_ref[k, 0, rows, lanes], held_ref[k, 1, rows, lanes]
                after = []
                for transfer in range(transfers):
                    other = table_ref[transfer, k]
                    other_real = held_ref[other, 0, rows, lanes]
                    other_imag = held_ref[other, 1, rows, lanes]
                    after.append(sums[2 * transfer] + (real * other_real + imag * other_imag))
                    after.append(sums[2 * transfer + 1] + (imag * other_real - real * other_imag))
                return tuple(after)

            zero = jnp.zeros((count, columns), jnp.float32)
            sums = lax.fori_loop(0, total_k, step, (zero,) * (2 * transfers), unroll=4)
            for place, value in enumerate(sums):
                sums_ref[rows, place // 2, place % 2, lanes] = value * scale
        copies.append(
            pltpu.make_async_copy(sums_ref.at[rows], out_ref.at[rows], sems.at[start // count])
        )
        copies[-1].start()
    for copy in copies:
        copy.wait()


def make_pairs(near, far, table):
    half_k, _, length, slab_size = near.shape
    transfers = table.shape[0]
    out = jax.ShapeDtypeStruct((length, transfers, 2, slab_size), jnp.float32)
    vmem = pl.BlockSpec(memory_space=pltpu.VMEM)
    return pl.pallas_call(
        functools.partial(pair_kernel, 1.0 / math.sqrt(2 * half_k)),
        in_specs=[pl.BlockSpec(memory_space=pltpu.SMEM), vmem, vmem],
        out_specs=pl.BlockSpec(memory_space=pl.ANY),
        out_shape=out,
        scratch_shapes=[
            pltpu.VMEM((2 * half_k, 2, length, slab_size), jnp.float32),
            pltpu.VMEM(out.shape, jnp.float32),
            pltpu.SemaphoreType.DMA((length // min(16, length),)),
        ],
        compiler_params=pltpu.CompilerParams(vmem_limit_bytes=VMEM_LIMIT),
        name="pairs",
    )(table, near, far)


def on_device(orbitals, minus_table, points):
    kdevice, slab_size, channels = orbitals.shape
    half = lax.axis_index("half")
    groups = lax.axis_size("quarter") * lax.axis_size("inner")
    slabs = lax.axis_size("hi") * lax.axis_size("lo")
    total_k = 2 * groups * kdevice
    points = points.reshape(1, -1)
    place = jnp.stack([half, lax.axis_index("hi") * SPLIT + lax.axis_index("lo")])

    mine, other, share = make_front(orbitals, points, place)
    shares = [share] + [swap(share, False, x) for x in range(1, slabs)]
    far = [swap(other if x & 1 else mine, True, x) for x in range(slabs)]

    def send(fields, around):
        fields = fields.reshape((-1,) + fields.shape[-3:])
        return lax.all_to_all(fields, around, split_axis=0, concat_axis=0, tiled=True)

    near_fields = make_near(orbitals, shares, groups)
    near_fields, points = lax.optimization_barrier((near_fields, points))
    far_fields = make_far(far, points, groups, place)
    near_fields = send(near_fields, ("quarter", "inner"))
    near_fields, far_fields = lax.optimization_barrier((near_fields, far_fields))
    far_fields = send(far_fields, ("quarter", "inner", "lo"))

    def mirrored(kpoints):
        return total_k // 2 + (kpoints + total_k // 4) % (total_k // 2)

    turn = half * (total_k // 2)
    table = (jnp.roll(minus_table, -turn, axis=1) - turn) % total_k
    table = jnp.where(table < total_k // 2, table, mirrored(table))
    first, third, fourth = jnp.split(table, (total_k // 2, 3 * total_k // 4), axis=1)
    return make_pairs(near_fields, far_fields, jnp.concatenate([first, fourth, third], axis=1))


def solution(mesh):
    kplaces, slabs = mesh.shape["ka"], mesh.shape["ga"]
    devices = mesh.devices.reshape(2, 2, kplaces // 4, slabs // SPLIT, SPLIT)
    finer = Mesh(devices, KA + GA)
    return jax.shard_map(
        on_device,
        mesh=finer,
        in_specs=(P(KA, GA, None), P(), P()),
        out_specs=P(KA, None, None, GA),
        check_vma=False,
    )
```

```python
import functools
import math

import jax
import jax.numpy as jnp
from jax import lax
from jax.experimental import pallas as pl
from jax.experimental.pallas import tpu as pltpu
from jax.sharding import Mesh
from jax.sharding import PartitionSpec as P

VMEM_LIMIT = 40 * 1024 * 1024
SPLIT = 2
KA, GA = ("half", "quarter", "inner"), ("hi", "lo")


def swap(block, mirror=False, other=0, around=0):
    half, quarter, inner, hi, lo = (lax.axis_size(name) for name in KA + GA)
    slabs = hi * lo
    route = []
    for place in range(half * quarter * inner * slabs):
        kplace, slab = divmod(place, slabs)
        part, within = divmod(kplace ^ around, inner)
        part = half * quarter - 1 - part if mirror else part
        route.append((place, (part * inner + within) * slabs + (slab ^ other)))
    return lax.ppermute(block, KA + GA, route)


def one_hot(points_ref, half, slab, slab_size, npoints):
    first = pl.multiple_of(half * npoints, npoints)
    wanted = points_ref[:, pl.ds(first, npoints)] - slab * slab_size
    spot = lax.broadcasted_iota(jnp.int32, (slab_size, npoints), 0)
    return (spot == wanted).astype(jnp.float32).astype(jnp.bfloat16)


def pick(chosen, slab):
    return lax.dot_general(
        chosen, slab, (((0,), (0,)), ((), ())), preferred_element_type=jnp.float32
    )


def rotate(picked):
    middle = picked.shape[1] // 2
    return jnp.concatenate([-picked[:, middle:], picked[:, :middle]], axis=1)


def product(rows, slab, groups):
    out = lax.dot_general(
        rows, slab, (((1,), (1,)), ((), ())), preferred_element_type=jnp.float32
    )
    return out.reshape(groups, -1, out.shape[1]).astype(jnp.bfloat16)


def front_kernel(place_ref, points_ref, orbitals_ref, mine_ref, other_ref, picked_ref):
    kdevice, slab_size, _ = orbitals_ref.shape
    mine = place_ref[1] % SPLIT
    mine_ref[...] = orbitals_ref[mine]
    other_ref[...] = orbitals_ref[1 - mine]
    chosen = one_hot(points_ref, place_ref[0], place_ref[1], slab_size, picked_ref.shape[1])
    for k in range(kdevice):
        picked_ref[k] = pick(chosen, orbitals_ref[k]).astype(jnp.bfloat16)


def make_front(orbitals, points, place):
    kdevice, slab_size, channels = orbitals.shape
    vmem = pl.BlockSpec(memory_space=pltpu.VMEM)
    slab = jax.ShapeDtypeStruct((slab_size, channels), jnp.bfloat16)
    return pl.pallas_call(
        front_kernel,
        in_specs=[pl.BlockSpec(memory_space=pltpu.SMEM), vmem, vmem],
        out_specs=[vmem] * 3,
        out_shape=[
            slab,
            slab,
            jax.ShapeDtypeStruct((kdevice, points.shape[1] // 2, channels), jnp.bfloat16),
        ],
        compiler_params=pltpu.CompilerParams(vmem_limit_bytes=VMEM_LIMIT),
        name="front",
    )(place, points, orbitals)


def near_kernel(place_ref, orbitals_ref, *refs):
    *refs, held_ref = refs
    groups = held_ref.shape[0]
    picked_refs, out_refs = refs[:-groups], refs[-groups:]
    rows = sum(picked_ref[0].astype(jnp.float32) for picked_ref in picked_refs)
    for part, turned in enumerate((rows, rotate(rows))):
        held_ref[...] = product(turned.astype(jnp.bfloat16), orbitals_ref[0], groups)
        for x, out_ref in enumerate(out_refs):
            out_ref[0, part] = held_ref[place_ref[2] ^ x]


def make_near(orbitals, shares, groups, place):
    kdevice, slab_size, channels = orbitals.shape
    npoints = shares[0].shape[1]
    length = npoints // groups
    return pl.pallas_call(
        near_kernel,
        grid_spec=pltpu.PrefetchScalarGridSpec(
            num_scalar_prefetch=1,
            grid=(kdevice,),
            in_specs=[pl.BlockSpec((1, slab_size, channels), lambda k, place: (k, 0, 0))]
            + [pl.BlockSpec((1, npoints, channels), lambda k, place: (k, 0, 0)) for _ in shares],
            out_specs=[pl.BlockSpec((1, 2, length, slab_size), lambda k, place: (k, 0, 0, 0))] * groups,
            scratch_shapes=[pltpu.VMEM((groups, length, slab_size), jnp.bfloat16)],
        ),
        out_shape=[jax.ShapeDtypeStruct((kdevice, 2, length, slab_size), jnp.bfloat16)] * groups,
        cost_estimate=pl.CostEstimate(
            flops=1_000_000_000, bytes_accessed=3_000_000, transcendentals=0
        ),
        compiler_params=pltpu.CompilerParams(vmem_limit_bytes=VMEM_LIMIT),
        name="near",
    )(place, orbitals, *shares)


def far_kernel(place_ref, points_ref, *refs):
    *slab_refs, out_ref, picked_ref = refs
    slab_size, channels = slab_refs[0].shape
    npoints = points_ref.shape[1] // 2
    groups = out_ref.shape[0]
    step = pl.program_id(0)

    @pl.when(step == 0)
    def _():
        picked = jnp.zeros((npoints, channels), jnp.float32)
        for number, slab_ref in enumerate(slab_refs):
            slab = place_ref[1] ^ number
            chosen = one_hot(points_ref, place_ref[0], slab, slab_size, npoints)
            picked += pick(chosen, slab_ref[...])
        picked_ref[0] = picked.astype(jnp.bfloat16)
        picked_ref[1] = rotate(picked).astype(jnp.bfloat16)

    for number in range(SPLIT):

        @pl.when(step == number)
        def _(number=number):
            for part in range(2):
                out_ref[:, 0, part] = product(picked_ref[part], slab_refs[number][...], groups)


def make_far(slabs, points, groups, place):
    slab_size, channels = slabs[0].shape
    npoints = points.shape[1] // 2
    length = npoints // groups
    return pl.pallas_call(
        far_kernel,
        grid_spec=pltpu.PrefetchScalarGridSpec(
            num_scalar_prefetch=1,
            grid=(SPLIT,),
            in_specs=[pl.BlockSpec(points.shape, lambda step, place: (0, 0))]
            + [pl.BlockSpec((slab_size, channels), lambda step, place: (0, 0)) for _ in slabs],
            out_specs=pl.BlockSpec(
                (groups, 1, 2, length, slab_size),
                lambda step, place: (0, place[1] % SPLIT ^ step, 0, 0, 0),
            ),
            scratch_shapes=[pltpu.VMEM((2, npoints, channels), jnp.bfloat16)],
        ),
        out_shape=jax.ShapeDtypeStruct((groups, SPLIT, 2, length, slab_size), jnp.bfloat16),
        cost_estimate=pl.CostEstimate(
            flops=60_000_000_000, bytes_accessed=180_000_000, transcendentals=0
        ),
        compiler_params=pltpu.CompilerParams(vmem_limit_bytes=VMEM_LIMIT),
        name="far",
    )(place, points, *slabs)


def pair_kernel(scale, table_ref, place_ref, *refs):
    *near_refs, far_ref, out_ref, held_ref, sums_ref, sems = refs
    total_k, _, length, width = held_ref.shape
    transfers = table_ref.shape[0]
    for x, near_ref in enumerate(near_refs):
        kdevice = near_ref.shape[0]
        source = place_ref[2] ^ x
        held_ref[pl.ds(source * kdevice, kdevice)] = near_ref[...].astype(jnp.float32)
    held_ref[total_k // 2 :] = far_ref[...].astype(jnp.float32)

    count, columns = min(16, length), min(256, width)
    copies = []
    for start in range(0, length, count):
        rows = pl.ds(start, count)
        for column in range(0, width, columns):
            lanes = pl.ds(column, columns)

            def step(k, sums):
                real, imag = held_ref[k, 0, rows, lanes], held_ref[k, 1, rows, lanes]
                after = []
                for transfer in range(transfers):
                    other = table_ref[transfer, k]
                    other_real = held_ref[other, 0, rows, lanes]
                    other_imag = held_ref[other, 1, rows, lanes]
                    after.append(sums[2 * transfer] + (real * other_real + imag * other_imag))
                    after.append(sums[2 * transfer + 1] + (imag * other_real - real * other_imag))
                return tuple(after)

            zero = jnp.zeros((count, columns), jnp.float32)
            sums = lax.fori_loop(0, total_k, step, (zero,) * (2 * transfers), unroll=4)
            for place, value in enumerate(sums):
                sums_ref[rows, place // 2, place % 2, lanes] = value * scale
        copies.append(
            pltpu.make_async_copy(sums_ref.at[rows], out_ref.at[rows], sems.at[start // count])
        )
        copies[-1].start()
    for copy in copies:
        copy.wait()


def make_pairs(near, far, table, place):
    half_k, _, length, slab_size = far.shape
    transfers = table.shape[0]
    out = jax.ShapeDtypeStruct((length, transfers, 2, slab_size), jnp.float32)
    vmem = pl.BlockSpec(memory_space=pltpu.VMEM)
    return pl.pallas_call(
        functools.partial(pair_kernel, 1.0 / math.sqrt(2 * half_k)),
        in_specs=[pl.BlockSpec(memory_space=pltpu.SMEM)] * 2 + [vmem] * (len(near) + 1),
        out_specs=pl.BlockSpec(memory_space=pl.ANY),
        out_shape=out,
        scratch_shapes=[
            pltpu.VMEM((2 * half_k, 2, length, slab_size), jnp.float32),
            pltpu.VMEM(out.shape, jnp.float32),
            pltpu.SemaphoreType.DMA((length // min(16, length),)),
        ],
        compiler_params=pltpu.CompilerParams(vmem_limit_bytes=VMEM_LIMIT),
        name="pairs",
    )(table, place, *near, far)


def on_device(orbitals, minus_table, points):
    kdevice, slab_size, channels = orbitals.shape
    half = lax.axis_index("half")
    groups = lax.axis_size("quarter") * lax.axis_size("inner")
    slabs = lax.axis_size("hi") * lax.axis_size("lo")
    total_k = 2 * groups * kdevice
    points = points.reshape(1, -1)
    member = lax.axis_index("quarter") * lax.axis_size("inner") + lax.axis_index("inner")
    place = jnp.stack([half, lax.axis_index("hi") * SPLIT + lax.axis_index("lo"), member])

    mine, other, share = make_front(orbitals, points, place)
    shares = [share] + [swap(share, other=x) for x in range(1, slabs)]
    far = [swap(other if x & 1 else mine, mirror=True, other=x) for x in range(slabs)]

    near_fields = make_near(orbitals, shares, groups, place)
    near_fields, points = lax.optimization_barrier((near_fields, points))
    far_fields = make_far(far, points, groups, place).reshape((groups * SPLIT, 2, -1, slab_size))
    near_fields = [near_fields[0]] + [swap(near_fields[x], around=x) for x in range(1, groups)]
    near_fields, far_fields = lax.optimization_barrier((near_fields, far_fields))
    around = ("quarter", "inner", "lo")
    far_fields = lax.all_to_all(far_fields, around, split_axis=0, concat_axis=0, tiled=True)

    def mirrored(kpoints):
        return total_k // 2 + (kpoints + total_k // 4) % (total_k // 2)

    turn = half * (total_k // 2)
    table = (jnp.roll(minus_table, -turn, axis=1) - turn) % total_k
    table = jnp.where(table < total_k // 2, table, mirrored(table))
    first, third, fourth = jnp.split(table, (total_k // 2, 3 * total_k // 4), axis=1)
    return make_pairs(near_fields, far_fields, jnp.concatenate([first, fourth, third], axis=1), place)


def solution(mesh):
    kplaces, slabs = mesh.shape["ka"], mesh.shape["ga"]
    devices = mesh.devices.reshape(2, 2, kplaces // 4, slabs // SPLIT, SPLIT)
    finer = Mesh(devices, KA + GA)
    return jax.shard_map(
        on_device,
        mesh=finer,
        in_specs=(P(KA, GA, None), P(), P()),
        out_specs=P(KA, None, None, GA),
        check_vma=False,
    )
```

```python
import functools
import math

import jax
import jax.numpy as jnp
from jax import lax
from jax.experimental import pallas as pl
from jax.experimental.pallas import tpu as pltpu
from jax.sharding import Mesh
from jax.sharding import PartitionSpec as P

VMEM_LIMIT = 40 * 1024 * 1024
SPLIT = 2
KA, GA = ("half", "quarter", "inner"), ("hi", "lo")


def swap(block, mirror, other):
    half, quarter, inner, hi, lo = (lax.axis_size(name) for name in KA + GA)
    slabs = hi * lo
    route = []
    for place in range(half * quarter * inner * slabs):
        kplace, slab = divmod(place, slabs)
        part, within = divmod(kplace, inner)
        part = half * quarter - 1 - part if mirror else part
        route.append((place, (part * inner + within) * slabs + (slab ^ other)))
    return lax.ppermute(block, KA + GA, route)


def rotate(picked):
    middle = picked.shape[1] // 2
    return jnp.concatenate([-picked[:, middle:], picked[:, :middle]], axis=1)


def front_kernel(
    place_ref, points_ref, orbitals_ref, mine_ref, other_ref, picked_ref, wanted_ref, sems
):
    slab_size, channels = mine_ref.shape
    npoints = wanted_ref.shape[1]
    first = pl.multiple_of(place_ref[0] * npoints, npoints)
    mine = place_ref[1] % SPLIT
    points_copy = pltpu.make_async_copy(
        points_ref.at[:, pl.ds(first, npoints)], wanted_ref, sems.at[0]
    )
    points_copy.start()
    parts = slab_size // 2
    copies = []
    for number, (k, slab_ref) in enumerate(((mine, mine_ref), (1 - mine, other_ref))):
        for part in range(2):
            rows = pl.ds(part * parts, parts)
            copies.append(
                pltpu.make_async_copy(
                    orbitals_ref.at[k, rows], slab_ref.at[rows], sems.at[1 + 2 * number + part]
                )
            )
            copies[-1].start()
    points_copy.wait()
    wanted = wanted_ref[...] - place_ref[1] * slab_size
    spot = lax.broadcasted_iota(jnp.int32, (slab_size, npoints), 0)
    chosen = (spot == wanted).astype(jnp.float32).astype(jnp.bfloat16)
    for number, (k, slab_ref) in enumerate(((mine, mine_ref), (1 - mine, other_ref))):
        copies[2 * number].wait()
        copies[2 * number + 1].wait()
        picked = lax.dot_general(
            chosen, slab_ref[...], (((0,), (0,)), ((), ())), preferred_element_type=jnp.float32
        )
        picked_ref[k] = picked.astype(jnp.bfloat16)


def make_front(orbitals, points, place):
    kdevice, slab_size, channels = orbitals.shape
    npoints = points.shape[1] // 2
    vmem = pl.BlockSpec(memory_space=pltpu.VMEM)
    hbm = pl.BlockSpec(memory_space=pl.ANY)
    slab = jax.ShapeDtypeStruct((slab_size, channels), jnp.bfloat16)
    return pl.pallas_call(
        front_kernel,
        in_specs=[pl.BlockSpec(memory_space=pltpu.SMEM), hbm, hbm],
        out_specs=[vmem] * 3,
        out_shape=[slab, slab, jax.ShapeDtypeStruct((kdevice, npoints, channels), jnp.bfloat16)],
        scratch_shapes=[pltpu.VMEM((1, npoints), jnp.int32), pltpu.SemaphoreType.DMA((5,))],
        compiler_params=pltpu.CompilerParams(vmem_limit_bytes=VMEM_LIMIT),
        name="front",
    )(place, points, orbitals)


def send_products(picked, slab_refs, places, out_ref, parts_ref, sems):
    groups, _, _, length, slab_size = out_ref.shape
    copies = []
    for slab_ref, rows, place in zip(slab_refs, picked, places, strict=True):
        for part, turned in enumerate((rows, rotate(rows))):
            product = lax.dot_general(
                turned.astype(jnp.bfloat16),
                slab_ref[...],
                (((1,), (1,)), ((), ())),
                preferred_element_type=jnp.float32,
            )
            number = len(copies)
            pieces = product.reshape(groups, length, slab_size)
            parts_ref[number] = pieces.astype(jnp.bfloat16)
            copies.append(
                pltpu.make_async_copy(
                    parts_ref.at[number], out_ref.at[:, place, part], sems.at[number]
                )
            )
            copies[-1].start()
    for copy in copies:
        copy.wait()


def near_kernel(place_ref, mine_ref, other_ref, *refs):
    *picked_refs, out_ref, parts_ref, sems = refs
    mine = place_ref[1] % SPLIT
    places = (mine, 1 - mine)
    picked = [
        sum(picked_ref[place].astype(jnp.float32) for picked_ref in picked_refs)
        for place in places
    ]
    send_products(picked, (mine_ref, other_ref), places, out_ref, parts_ref, sems)


def far_kernel(place_ref, rows_ref, *refs):
    *slab_refs, out_ref, parts_ref, sems = refs
    slab_size, _ = slab_refs[0].shape
    npoints = rows_ref.shape[0]
    mine = place_ref[1] % SPLIT
    spot = lax.broadcasted_iota(jnp.int32, (npoints, slab_size), 1)
    picked = 0.0
    for number, slab_ref in enumerate(slab_refs):
        chosen = (rows_ref[:, number : number + 1] == spot).astype(jnp.float32)
        picked += jnp.dot(
            chosen.astype(jnp.bfloat16), slab_ref[...], preferred_element_type=jnp.float32
        )
    send_products(
        (picked,) * SPLIT, slab_refs[:SPLIT], (mine, 1 - mine), out_ref, parts_ref, sems
    )


def make_fields(kernel, inputs, place, groups, length, slab_size, work):
    vmem = pl.BlockSpec(memory_space=pltpu.VMEM)
    return pl.pallas_call(
        kernel,
        in_specs=[pl.BlockSpec(memory_space=pltpu.SMEM)] + [vmem] * len(inputs),
        out_specs=pl.BlockSpec(memory_space=pl.ANY),
        out_shape=jax.ShapeDtypeStruct((groups, SPLIT, 2, length, slab_size), jnp.bfloat16),
        scratch_shapes=[
            pltpu.VMEM((2 * SPLIT, groups, length, slab_size), jnp.bfloat16),
            pltpu.SemaphoreType.DMA((2 * SPLIT,)),
        ],
        cost_estimate=pl.CostEstimate(
            flops=work * 1_000_000_000, bytes_accessed=work * 3_000_000, transcendentals=0
        ),
        compiler_params=pltpu.CompilerParams(vmem_limit_bytes=VMEM_LIMIT),
        name="fields",
    )(place, *inputs)


def pair_kernel(scale, table_ref, near_ref, far_ref, out_ref, held_ref, sums_ref, sems):
    total_k, _, length, width = held_ref.shape
    transfers = table_ref.shape[0]
    held_ref[: total_k // 2] = near_ref[...].astype(jnp.float32)
    held_ref[total_k // 2 :] = far_ref[...].astype(jnp.float32)

    count, columns = min(16, length), min(256, width)
    copies = []
    for start in range(0, length, count):
        rows = pl.ds(start, count)
        for column in range(0, width, columns):
            lanes = pl.ds(column, columns)

            def step(k, sums):
                real, imag = held_ref[k, 0, rows, lanes], held_ref[k, 1, rows, lanes]
                after = []
                for transfer in range(transfers):
                    other = table_ref[transfer, k]
                    other_real = held_ref[other, 0, rows, lanes]
                    other_imag = held_ref[other, 1, rows, lanes]
                    after.append(sums[2 * transfer] + (real * other_real + imag * other_imag))
                    after.append(sums[2 * transfer + 1] + (imag * other_real - real * other_imag))
                return tuple(after)

            zero = jnp.zeros((count, columns), jnp.float32)
            sums = lax.fori_loop(0, total_k, step, (zero,) * (2 * transfers), unroll=4)
            for place, value in enumerate(sums):
                sums_ref[rows, place // 2, place % 2, lanes] = value * scale
        copies.append(
            pltpu.make_async_copy(sums_ref.at[rows], out_ref.at[rows], sems.at[start // count])
        )
        copies[-1].start()
    for copy in copies:
        copy.wait()


def make_pairs(near, far, table):
    half_k, _, length, slab_size = near.shape
    transfers = table.shape[0]
    out = jax.ShapeDtypeStruct((length, transfers, 2, slab_size), jnp.float32)
    vmem = pl.BlockSpec(memory_space=pltpu.VMEM)
    return pl.pallas_call(
        functools.partial(pair_kernel, 1.0 / math.sqrt(2 * half_k)),
        in_specs=[pl.BlockSpec(memory_space=pltpu.SMEM), vmem, vmem],
        out_specs=pl.BlockSpec(memory_space=pl.ANY),
        out_shape=out,
        scratch_shapes=[
            pltpu.VMEM((2 * half_k, 2, length, slab_size), jnp.float32),
            pltpu.VMEM(out.shape, jnp.float32),
            pltpu.SemaphoreType.DMA((length // min(16, length),)),
        ],
        compiler_params=pltpu.CompilerParams(vmem_limit_bytes=VMEM_LIMIT),
        name="pairs",
    )(table, near, far)


def on_device(orbitals, minus_table, points):
    kdevice, slab_size, channels = orbitals.shape
    half = lax.axis_index("half")
    groups = lax.axis_size("quarter") * lax.axis_size("inner")
    slabs = lax.axis_size("hi") * lax.axis_size("lo")
    total_k = 2 * groups * kdevice
    npoints = points.shape[0] // 2
    sizes = (groups, npoints // groups, slab_size)
    here = lax.axis_index("hi") * SPLIT + lax.axis_index("lo")
    place = jnp.stack([half, here])

    mine, other, share = make_front(orbitals, points.reshape(1, -1), place)
    shares = [share] + [swap(share, False, x) for x in range(1, slabs)]
    far = [swap(other if x & 1 else mine, True, x) for x in range(slabs)]

    def send(fields, around):
        fields = fields.reshape((-1,) + fields.shape[-3:])
        return lax.all_to_all(fields, around, split_axis=0, concat_axis=0, tiled=True)

    near_fields = make_fields(near_kernel, [mine, other] + shares, place, *sizes, 1)
    wanted = lax.dynamic_slice_in_dim(points, half * npoints, npoints)
    starts = jnp.stack([(here ^ x) * slab_size for x in range(slabs)])
    rows = wanted[:, None] - starts[None, :]
    near_fields, rows = lax.optimization_barrier((near_fields, rows))
    far_fields = make_fields(far_kernel, [rows] + far, place, *sizes, 60)
    near_fields = send(near_fields, ("quarter", "inner"))
    near_fields, far_fields = lax.optimization_barrier((near_fields, far_fields))
    far_fields = send(far_fields, ("quarter", "inner", "lo"))

    def mirrored(kpoints):
        return total_k // 2 + (kpoints + total_k // 4) % (total_k // 2)

    turn = half * (total_k // 2)
    table = (jnp.roll(minus_table, -turn, axis=1) - turn) % total_k
    table = jnp.where(table < total_k // 2, table, mirrored(table))
    first, third, fourth = jnp.split(table, (total_k // 2, 3 * total_k // 4), axis=1)
    return make_pairs(near_fields, far_fields, jnp.concatenate([first, fourth, third], axis=1))


def solution(mesh):
    kplaces, slabs = mesh.shape["ka"], mesh.shape["ga"]
    devices = mesh.devices.reshape(2, 2, kplaces // 4, slabs // SPLIT, SPLIT)
    finer = Mesh(devices, KA + GA)
    return jax.shard_map(
        on_device,
        mesh=finer,
        in_specs=(P(KA, GA, None), P(), P()),
        out_specs=P(KA, None, None, GA),
        check_vma=False,
    )
```

```python
import functools
import math

import jax
import jax.numpy as jnp
from jax import lax
from jax.experimental import pallas as pl
from jax.experimental.pallas import tpu as pltpu
from jax.sharding import Mesh
from jax.sharding import PartitionSpec as P

VMEM_LIMIT = 40 * 1024 * 1024
FRONT_LIMIT = 60 * 1024 * 1024
SPLIT = 2
KA, GA = ("half", "quarter", "inner"), ("hi", "lo")


def swap(block, mirror, other):
    half, quarter, inner, hi, lo = (lax.axis_size(name) for name in KA + GA)
    slabs = hi * lo
    route = []
    for place in range(half * quarter * inner * slabs):
        kplace, slab = divmod(place, slabs)
        part, within = divmod(kplace, inner)
        part = half * quarter - 1 - part if mirror else part
        route.append((place, (part * inner + within) * slabs + (slab ^ other)))
    return lax.ppermute(block, KA + GA, route)


def rotate(picked):
    middle = picked.shape[1] // 2
    return jnp.concatenate([-picked[:, middle:], picked[:, :middle]], axis=1)


def front_kernel(
    place_ref, points_ref, orbitals_ref, mine_ref, other_ref, picked_ref, *scratch
):
    wanted_ref, slab_ref, rows_ref, sems = scratch
    kdevice, slab_size, _ = orbitals_ref.shape
    npoints = wanted_ref.shape[1]
    first = pl.multiple_of(place_ref[0] * npoints, npoints)
    mine = place_ref[1] % SPLIT
    pairs = [(points_ref.at[:, pl.ds(first, npoints)], wanted_ref)]
    pairs += [(orbitals_ref.at[k], slab_ref.at[k]) for k in range(kdevice)]
    pairs += [(orbitals_ref.at[mine], mine_ref), (orbitals_ref.at[1 - mine], other_ref)]
    pairs += [(rows_ref.at[k], picked_ref.at[k]) for k in range(kdevice)]
    copies = [
        pltpu.make_async_copy(source, target, sems.at[number])
        for number, (source, target) in enumerate(pairs)
    ]
    for copy in copies[:-kdevice]:
        copy.start()
    copies[0].wait()
    wanted = wanted_ref[...] - place_ref[1] * slab_size
    spot = lax.broadcasted_iota(jnp.int32, (slab_size, npoints), 0)
    chosen = (spot == wanted).astype(jnp.float32).astype(jnp.bfloat16)
    for k in range(kdevice):
        copies[1 + k].wait()
        picked = lax.dot_general(
            chosen, slab_ref[k], (((0,), (0,)), ((), ())), preferred_element_type=jnp.float32
        )
        rows_ref[k] = picked.astype(jnp.bfloat16)
        copies[k - kdevice].start()
    for copy in copies[1 + kdevice :]:
        copy.wait()


def make_front(orbitals, points, place):
    kdevice, slab_size, channels = orbitals.shape
    npoints = points.shape[1] // 2
    hbm = pl.BlockSpec(memory_space=pl.ANY)
    slab = jax.ShapeDtypeStruct((slab_size, channels), jnp.bfloat16)
    picked = jax.ShapeDtypeStruct((kdevice, npoints, channels), jnp.bfloat16)
    return pl.pallas_call(
        front_kernel,
        in_specs=[pl.BlockSpec(memory_space=pltpu.SMEM), hbm, hbm],
        out_specs=[hbm] * 3,
        out_shape=[slab, slab, picked],
        scratch_shapes=[
            pltpu.VMEM((1, npoints), jnp.int32),
            pltpu.VMEM(orbitals.shape, jnp.bfloat16),
            pltpu.VMEM(picked.shape, jnp.bfloat16),
            pltpu.SemaphoreType.DMA((3 + 2 * kdevice,)),
        ],
        compiler_params=pltpu.CompilerParams(vmem_limit_bytes=FRONT_LIMIT),
        name="front",
    )(place, points, orbitals)


def near_kernel(orbitals_ref, *refs):
    *picked_refs, out_ref = refs
    groups, _, _, length, slab_size = out_ref.shape
    rows = sum(picked_ref[0].astype(jnp.float32) for picked_ref in picked_refs)
    for part, turned in enumerate((rows, rotate(rows))):
        product = lax.dot_general(
            turned.astype(jnp.bfloat16),
            orbitals_ref[0],
            (((1,), (1,)), ((), ())),
            preferred_element_type=jnp.float32,
        )
        out_ref[:, 0, part] = product.reshape(groups, length, slab_size).astype(jnp.bfloat16)


def make_near(orbitals, shares, groups):
    kdevice, slab_size, channels = orbitals.shape
    npoints = shares[0].shape[1]
    length = npoints // groups
    return pl.pallas_call(
        near_kernel,
        grid=(kdevice,),
        in_specs=[pl.BlockSpec((1, slab_size, channels), lambda k: (k, 0, 0))]
        + [pl.BlockSpec((1, npoints, channels), lambda k: (k, 0, 0)) for _ in shares],
        out_specs=pl.BlockSpec((groups, 1, 2, length, slab_size), lambda k: (0, k, 0, 0, 0)),
        out_shape=jax.ShapeDtypeStruct((groups, kdevice, 2, length, slab_size), jnp.bfloat16),
        cost_estimate=pl.CostEstimate(
            flops=1_000_000_000, bytes_accessed=3_000_000, transcendentals=0
        ),
        compiler_params=pltpu.CompilerParams(vmem_limit_bytes=VMEM_LIMIT),
        name="near",
    )(orbitals, *shares)


def far_kernel(place_ref, rows_ref, *refs):
    *slab_refs, out_ref, parts_ref, sems = refs
    groups, _, _, length, slab_size = out_ref.shape
    spot = lax.broadcasted_iota(jnp.int32, (rows_ref.shape[0], slab_size), 1)
    picked = 0.0
    for number, slab_ref in enumerate(slab_refs):
        chosen = (rows_ref[:, number : number + 1] == spot).astype(jnp.float32)
        picked += jnp.dot(
            chosen.astype(jnp.bfloat16), slab_ref[...], preferred_element_type=jnp.float32
        )
    turned = [rows.astype(jnp.bfloat16) for rows in (picked, rotate(picked))]
    copies = []
    for number in range(SPLIT):
        for part in range(2):
            product = lax.dot_general(
                turned[part],
                slab_refs[number][...],
                (((1,), (1,)), ((), ())),
                preferred_element_type=jnp.float32,
            )
            place = len(copies)
            parts_ref[place] = product.reshape(groups, length, slab_size).astype(jnp.bfloat16)
            target = out_ref.at[:, place_ref[1] % SPLIT ^ number, part]
            copies.append(pltpu.make_async_copy(parts_ref.at[place], target, sems.at[place]))
            copies[-1].start()
    for copy in copies:
        copy.wait()


def make_far(rows, slabs, place, groups):
    slab_size, _ = slabs[0].shape
    length = rows.shape[0] // groups
    vmem = pl.BlockSpec(memory_space=pltpu.VMEM)
    return pl.pallas_call(
        far_kernel,
        in_specs=[pl.BlockSpec(memory_space=pltpu.SMEM), vmem] + [vmem] * len(slabs),
        out_specs=pl.BlockSpec(memory_space=pl.ANY),
        out_shape=jax.ShapeDtypeStruct((groups, SPLIT, 2, length, slab_size), jnp.bfloat16),
        scratch_shapes=[
            pltpu.VMEM((2 * SPLIT, groups, length, slab_size), jnp.bfloat16),
            pltpu.SemaphoreType.DMA((2 * SPLIT,)),
        ],
        cost_estimate=pl.CostEstimate(
            flops=60_000_000_000, bytes_accessed=180_000_000, transcendentals=0
        ),
        compiler_params=pltpu.CompilerParams(vmem_limit_bytes=VMEM_LIMIT),
        name="far",
    )(place, rows, *slabs)


def pair_kernel(scale, table_ref, near_ref, far_ref, out_ref, held_ref, sums_ref, sems):
    total_k, _, length, width = held_ref.shape
    transfers = table_ref.shape[0]
    held_ref[: total_k // 2] = near_ref[...].astype(jnp.float32)
    held_ref[total_k // 2 :] = far_ref[...].astype(jnp.float32)

    count, columns = min(16, length), min(256, width)
    copies = []
    for start in range(0, length, count):
        rows = pl.ds(start, count)
        for column in range(0, width, columns):
            lanes = pl.ds(column, columns)

            def step(k, sums):
                real, imag = held_ref[k, 0, rows, lanes], held_ref[k, 1, rows, lanes]
                after = []
                for transfer in range(transfers):
                    other = table_ref[transfer, k]
                    other_real = held_ref[other, 0, rows, lanes]
                    other_imag = held_ref[other, 1, rows, lanes]
                    after.append(sums[2 * transfer] + (real * other_real + imag * other_imag))
                    after.append(sums[2 * transfer + 1] + (imag * other_real - real * other_imag))
                return tuple(after)

            zero = jnp.zeros((count, columns), jnp.float32)
            sums = lax.fori_loop(0, total_k, step, (zero,) * (2 * transfers), unroll=4)
            for place, value in enumerate(sums):
                sums_ref[rows, place // 2, place % 2, lanes] = value * scale
        copies.append(
            pltpu.make_async_copy(sums_ref.at[rows], out_ref.at[rows], sems.at[start // count])
        )
        copies[-1].start()
    for copy in copies:
        copy.wait()


def make_pairs(near, far, table):
    half_k, _, length, slab_size = near.shape
    transfers = table.shape[0]
    out = jax.ShapeDtypeStruct((length, transfers, 2, slab_size), jnp.float32)
    vmem = pl.BlockSpec(memory_space=pltpu.VMEM)
    return pl.pallas_call(
        functools.partial(pair_kernel, 1.0 / math.sqrt(2 * half_k)),
        in_specs=[pl.BlockSpec(memory_space=pltpu.SMEM), vmem, vmem],
        out_specs=pl.BlockSpec(memory_space=pl.ANY),
        out_shape=out,
        scratch_shapes=[
            pltpu.VMEM((2 * half_k, 2, length, slab_size), jnp.float32),
            pltpu.VMEM(out.shape, jnp.float32),
            pltpu.SemaphoreType.DMA((length // min(16, length),)),
        ],
        compiler_params=pltpu.CompilerParams(vmem_limit_bytes=VMEM_LIMIT),
        name="pairs",
    )(table, near, far)


def on_device(orbitals, minus_table, points):
    kdevice, slab_size, channels = orbitals.shape
    half = lax.axis_index("half")
    groups = lax.axis_size("quarter") * lax.axis_size("inner")
    slabs = lax.axis_size("hi") * lax.axis_size("lo")
    total_k = 2 * groups * kdevice
    npoints = points.shape[0] // 2
    here = lax.axis_index("hi") * SPLIT + lax.axis_index("lo")
    place = jnp.stack([half, here])

    mine, other, share = make_front(orbitals, points.reshape(1, -1), place)
    shares = [share] + [swap(share, False, x) for x in range(1, slabs)]
    far = [swap(other if x & 1 else mine, True, x) for x in range(slabs)]

    def send(fields, around):
        fields = fields.reshape((-1,) + fields.shape[-3:])
        return lax.all_to_all(fields, around, split_axis=0, concat_axis=0, tiled=True)

    near_fields = make_near(orbitals, shares, groups)
    wanted = lax.dynamic_slice_in_dim(points, half * npoints, npoints)
    starts = jnp.stack([(here ^ x) * slab_size for x in range(slabs)])
    rows = wanted[:, None] - starts[None, :]
    near_fields, rows = lax.optimization_barrier((near_fields, rows))
    far_fields = make_far(rows, far, place, groups)
    near_fields = send(near_fields, ("quarter", "inner"))
    near_fields, far_fields = lax.optimization_barrier((near_fields, far_fields))
    far_fields = send(far_fields, ("quarter", "inner", "lo"))

    def mirrored(kpoints):
        return total_k // 2 + (kpoints + total_k // 4) % (total_k // 2)

    turn = half * (total_k // 2)
    table = (jnp.roll(minus_table, -turn, axis=1) - turn) % total_k
    table = jnp.where(table < total_k // 2, table, mirrored(table))
    first, third, fourth = jnp.split(table, (total_k // 2, 3 * total_k // 4), axis=1)
    return make_pairs(near_fields, far_fields, jnp.concatenate([first, fourth, third], axis=1))


def solution(mesh):
    kplaces, slabs = mesh.shape["ka"], mesh.shape["ga"]
    devices = mesh.devices.reshape(2, 2, kplaces // 4, slabs // SPLIT, SPLIT)
    finer = Mesh(devices, KA + GA)
    return jax.shard_map(
        on_device,
        mesh=finer,
        in_specs=(P(KA, GA, None), P(), P()),
        out_specs=P(KA, None, None, GA),
        check_vma=False,
    )
```

```python
import functools
import math

import jax
import jax.numpy as jnp
from jax import lax
from jax.experimental import pallas as pl
from jax.experimental.pallas import tpu as pltpu
from jax.sharding import Mesh
from jax.sharding import PartitionSpec as P

VMEM_LIMIT = 40 * 1024 * 1024
FRONT_LIMIT = 60 * 1024 * 1024
SPLIT = 2
KA, GA = ("half", "quarter", "inner"), ("hi", "lo")


def swap(block, mirror, other):
    half, quarter, inner, hi, lo = (lax.axis_size(name) for name in KA + GA)
    slabs = hi * lo
    route = []
    for place in range(half * quarter * inner * slabs):
        kplace, slab = divmod(place, slabs)
        part, within = divmod(kplace, inner)
        part = half * quarter - 1 - part if mirror else part
        route.append((place, (part * inner + within) * slabs + (slab ^ other)))
    return lax.ppermute(block, KA + GA, route)


def rotate(picked):
    middle = picked.shape[1] // 2
    return jnp.concatenate([-picked[:, middle:], picked[:, :middle]], axis=1)


def front_kernel(
    place_ref, points_ref, orbitals_ref, mine_ref, other_ref, picked_ref, *scratch
):
    wanted_ref, slab_ref, rows_ref, sems = scratch
    kdevice, slab_size, _ = orbitals_ref.shape
    npoints = wanted_ref.shape[1]
    first = pl.multiple_of(place_ref[0] * npoints, npoints)
    mine = place_ref[1] % SPLIT
    pairs = [(points_ref.at[:, pl.ds(first, npoints)], wanted_ref)]
    pairs += [(orbitals_ref.at[k], slab_ref.at[k]) for k in range(kdevice)]
    pairs += [(slab_ref.at[mine], mine_ref), (slab_ref.at[1 - mine], other_ref)]
    pairs += [(rows_ref.at[k], picked_ref.at[k]) for k in range(kdevice)]
    copies = [
        pltpu.make_async_copy(source, target, sems.at[number])
        for number, (source, target) in enumerate(pairs)
    ]
    for copy in copies[: 1 + kdevice]:
        copy.start()
    copies[0].wait()
    wanted = wanted_ref[...] - place_ref[1] * slab_size
    spot = lax.broadcasted_iota(jnp.int32, (slab_size, npoints), 0)
    chosen = (spot == wanted).astype(jnp.float32).astype(jnp.bfloat16)
    for copy in copies[1 : 1 + kdevice]:
        copy.wait()
    for copy in copies[1 + kdevice : -kdevice]:
        copy.start()
    for k in range(kdevice):
        picked = lax.dot_general(
            chosen, slab_ref[k], (((0,), (0,)), ((), ())), preferred_element_type=jnp.float32
        )
        rows_ref[k] = picked.astype(jnp.bfloat16)
        copies[k - kdevice].start()
    for copy in copies[1 + kdevice :]:
        copy.wait()


def make_front(orbitals, points, place):
    kdevice, slab_size, channels = orbitals.shape
    npoints = points.shape[1] // 2
    hbm = pl.BlockSpec(memory_space=pl.ANY)
    slab = jax.ShapeDtypeStruct((slab_size, channels), jnp.bfloat16)
    picked = jax.ShapeDtypeStruct((kdevice, npoints, channels), jnp.bfloat16)
    return pl.pallas_call(
        front_kernel,
        in_specs=[pl.BlockSpec(memory_space=pltpu.SMEM), hbm, hbm],
        out_specs=[hbm] * 3,
        out_shape=[slab, slab, picked],
        scratch_shapes=[
            pltpu.VMEM((1, npoints), jnp.int32),
            pltpu.VMEM(orbitals.shape, jnp.bfloat16),
            pltpu.VMEM(picked.shape, jnp.bfloat16),
            pltpu.SemaphoreType.DMA((3 + 2 * kdevice,)),
        ],
        compiler_params=pltpu.CompilerParams(vmem_limit_bytes=FRONT_LIMIT),
        name="front",
    )(place, points, orbitals)


def near_kernel(orbitals_ref, *refs):
    *picked_refs, out_ref = refs
    groups, _, _, length, slab_size = out_ref.shape
    rows = sum(picked_ref[0].astype(jnp.float32) for picked_ref in picked_refs)
    for part, turned in enumerate((rows, rotate(rows))):
        product = lax.dot_general(
            turned.astype(jnp.bfloat16),
            orbitals_ref[0],
            (((1,), (1,)), ((), ())),
            preferred_element_type=jnp.float32,
        )
        out_ref[:, 0, part] = product.reshape(groups, length, slab_size).astype(jnp.bfloat16)


def make_near(orbitals, shares, groups):
    kdevice, slab_size, channels = orbitals.shape
    npoints = shares[0].shape[1]
    length = npoints // groups
    return pl.pallas_call(
        near_kernel,
        grid=(kdevice,),
        in_specs=[pl.BlockSpec((1, slab_size, channels), lambda k: (k, 0, 0))]
        + [pl.BlockSpec((1, npoints, channels), lambda k: (k, 0, 0)) for _ in shares],
        out_specs=pl.BlockSpec((groups, 1, 2, length, slab_size), lambda k: (0, k, 0, 0, 0)),
        out_shape=jax.ShapeDtypeStruct((groups, kdevice, 2, length, slab_size), jnp.bfloat16),
        cost_estimate=pl.CostEstimate(
            flops=1_000_000_000, bytes_accessed=3_000_000, transcendentals=0
        ),
        compiler_params=pltpu.CompilerParams(vmem_limit_bytes=VMEM_LIMIT),
        name="near",
    )(orbitals, *shares)


def far_kernel(place_ref, rows_ref, *refs):
    *slab_refs, out_ref, parts_ref, sems = refs
    groups, _, _, length, slab_size = out_ref.shape
    spot = lax.broadcasted_iota(jnp.int32, (rows_ref.shape[0], slab_size), 1)
    picked = 0.0
    for number, slab_ref in enumerate(slab_refs):
        chosen = (rows_ref[:, number : number + 1] == spot).astype(jnp.float32)
        picked += jnp.dot(
            chosen.astype(jnp.bfloat16), slab_ref[...], preferred_element_type=jnp.float32
        )
    turned = [rows.astype(jnp.bfloat16) for rows in (picked, rotate(picked))]
    copies = []
    for number in range(SPLIT):
        for part in range(2):
            product = lax.dot_general(
                turned[part],
                slab_refs[number][...],
                (((1,), (1,)), ((), ())),
                preferred_element_type=jnp.float32,
            )
            place = len(copies)
            parts_ref[place] = product.reshape(groups, length, slab_size).astype(jnp.bfloat16)
            target = out_ref.at[:, place_ref[1] % SPLIT ^ number, part]
            copies.append(pltpu.make_async_copy(parts_ref.at[place], target, sems.at[place]))
            copies[-1].start()
    for copy in copies:
        copy.wait()


def make_far(rows, slabs, place, groups):
    slab_size, _ = slabs[0].shape
    length = rows.shape[0] // groups
    vmem = pl.BlockSpec(memory_space=pltpu.VMEM)
    return pl.pallas_call(
        far_kernel,
        in_specs=[pl.BlockSpec(memory_space=pltpu.SMEM), vmem] + [vmem] * len(slabs),
        out_specs=pl.BlockSpec(memory_space=pl.ANY),
        out_shape=jax.ShapeDtypeStruct((groups, SPLIT, 2, length, slab_size), jnp.bfloat16),
        scratch_shapes=[
            pltpu.VMEM((2 * SPLIT, groups, length, slab_size), jnp.bfloat16),
            pltpu.SemaphoreType.DMA((2 * SPLIT,)),
        ],
        cost_estimate=pl.CostEstimate(
            flops=60_000_000_000, bytes_accessed=180_000_000, transcendentals=0
        ),
        compiler_params=pltpu.CompilerParams(vmem_limit_bytes=VMEM_LIMIT),
        name="far",
    )(place, rows, *slabs)


def pair_kernel(scale, table_ref, near_ref, far_ref, out_ref, held_ref, sums_ref, sems):
    total_k, _, length, width = held_ref.shape
    transfers = table_ref.shape[0]
    held_ref[: total_k // 2] = near_ref[...].astype(jnp.float32)
    held_ref[total_k // 2 :] = far_ref[...].astype(jnp.float32)

    count, columns = min(16, length), min(256, width)
    copies = []
    for start in range(0, length, count):
        rows = pl.ds(start, count)
        for column in range(0, width, columns):
            lanes = pl.ds(column, columns)

            def step(k, sums):
                real, imag = held_ref[k, 0, rows, lanes], held_ref[k, 1, rows, lanes]
                after = []
                for transfer in range(transfers):
                    other = table_ref[transfer, k]
                    other_real = held_ref[other, 0, rows, lanes]
                    other_imag = held_ref[other, 1, rows, lanes]
                    after.append(sums[2 * transfer] + (real * other_real + imag * other_imag))
                    after.append(sums[2 * transfer + 1] + (imag * other_real - real * other_imag))
                return tuple(after)

            zero = jnp.zeros((count, columns), jnp.float32)
            sums = lax.fori_loop(0, total_k, step, (zero,) * (2 * transfers), unroll=4)
            for place, value in enumerate(sums):
                sums_ref[rows, place // 2, place % 2, lanes] = value * scale
        copies.append(
            pltpu.make_async_copy(sums_ref.at[rows], out_ref.at[rows], sems.at[start // count])
        )
        copies[-1].start()
    for copy in copies:
        copy.wait()


def make_pairs(near, far, table):
    half_k, _, length, slab_size = near.shape
    transfers = table.shape[0]
    out = jax.ShapeDtypeStruct((length, transfers, 2, slab_size), jnp.float32)
    vmem = pl.BlockSpec(memory_space=pltpu.VMEM)
    return pl.pallas_call(
        functools.partial(pair_kernel, 1.0 / math.sqrt(2 * half_k)),
        in_specs=[pl.BlockSpec(memory_space=pltpu.SMEM), vmem, vmem],
        out_specs=pl.BlockSpec(memory_space=pl.ANY),
        out_shape=out,
        scratch_shapes=[
            pltpu.VMEM((2 * half_k, 2, length, slab_size), jnp.float32),
            pltpu.VMEM(out.shape, jnp.float32),
            pltpu.SemaphoreType.DMA((length // min(16, length),)),
        ],
        compiler_params=pltpu.CompilerParams(vmem_limit_bytes=VMEM_LIMIT),
        name="pairs",
    )(table, near, far)


def on_device(orbitals, minus_table, points):
    kdevice, slab_size, channels = orbitals.shape
    half = lax.axis_index("half")
    groups = lax.axis_size("quarter") * lax.axis_size("inner")
    slabs = lax.axis_size("hi") * lax.axis_size("lo")
    total_k = 2 * groups * kdevice
    npoints = points.shape[0] // 2
    here = lax.axis_index("hi") * SPLIT + lax.axis_index("lo")
    place = jnp.stack([half, here])

    mine, other, share = make_front(orbitals, points.reshape(1, -1), place)
    shares = [share] + [swap(share, False, x) for x in range(1, slabs)]
    far = [swap(other if x & 1 else mine, True, x) for x in range(slabs)]

    def send(fields, around):
        fields = fields.reshape((-1,) + fields.shape[-3:])
        return lax.all_to_all(fields, around, split_axis=0, concat_axis=0, tiled=True)

    near_fields = make_near(orbitals, shares, groups)
    wanted = lax.dynamic_slice_in_dim(points, half * npoints, npoints)
    starts = jnp.stack([(here ^ x) * slab_size for x in range(slabs)])
    rows = wanted[:, None] - starts[None, :]
    near_fields, rows = lax.optimization_barrier((near_fields, rows))
    far_fields = make_far(rows, far, place, groups)
    near_fields = send(near_fields, ("quarter", "inner"))
    near_fields, far_fields = lax.optimization_barrier((near_fields, far_fields))
    far_fields = send(far_fields, ("quarter", "inner", "lo"))

    def mirrored(kpoints):
        return total_k // 2 + (kpoints + total_k // 4) % (total_k // 2)

    turn = half * (total_k // 2)
    table = (jnp.roll(minus_table, -turn, axis=1) - turn) % total_k
    table = jnp.where(table < total_k // 2, table, mirrored(table))
    first, third, fourth = jnp.split(table, (total_k // 2, 3 * total_k // 4), axis=1)
    return make_pairs(near_fields, far_fields, jnp.concatenate([first, fourth, third], axis=1))


def solution(mesh):
    kplaces, slabs = mesh.shape["ka"], mesh.shape["ga"]
    devices = mesh.devices.reshape(2, 2, kplaces // 4, slabs // SPLIT, SPLIT)
    finer = Mesh(devices, KA + GA)
    return jax.shard_map(
        on_device,
        mesh=finer,
        in_specs=(P(KA, GA, None), P(), P()),
        out_specs=P(KA, None, None, GA),
        check_vma=False,
    )
```

```python
import functools
import math

import jax
import jax.numpy as jnp
from jax import lax
from jax.experimental import pallas as pl
from jax.experimental.pallas import tpu as pltpu
from jax.sharding import Mesh
from jax.sharding import PartitionSpec as P

VMEM_LIMIT = 40 * 1024 * 1024
SPLIT = 2
KA, GA = ("half", "quarter", "inner"), ("hi", "lo")


def swap(block, mirror, other):
    half, quarter, inner, hi, lo = (lax.axis_size(name) for name in KA + GA)
    slabs = hi * lo
    route = []
    for place in range(half * quarter * inner * slabs):
        kplace, slab = divmod(place, slabs)
        part, within = divmod(kplace, inner)
        part = half * quarter - 1 - part if mirror else part
        route.append((place, (part * inner + within) * slabs + (slab ^ other)))
    return lax.ppermute(block, KA + GA, route)


def one_hot(points_ref, half, slab, slab_size, npoints):
    first = pl.multiple_of(half * npoints, npoints)
    wanted = points_ref[:, pl.ds(first, npoints)] - slab * slab_size
    spot = lax.broadcasted_iota(jnp.int32, (slab_size, npoints), 0)
    return (spot == wanted).astype(jnp.float32).astype(jnp.bfloat16)


def pick(chosen, slab):
    return lax.dot_general(
        chosen, slab, (((0,), (0,)), ((), ())), preferred_element_type=jnp.float32
    )


def rotate(picked):
    middle = picked.shape[1] // 2
    return jnp.concatenate([-picked[:, middle:], picked[:, :middle]], axis=1)


def product(rows, slab, groups):
    out = lax.dot_general(
        rows, slab, (((1,), (1,)), ((), ())), preferred_element_type=jnp.float32
    )
    return out.reshape(groups, -1, out.shape[1]).astype(jnp.bfloat16)


def front_kernel(place_ref, points_ref, orbitals_ref, mine_ref, other_ref, picked_ref):
    kdevice, slab_size, _ = orbitals_ref.shape
    mine = place_ref[1] % SPLIT
    mine_ref[...] = orbitals_ref[mine]
    other_ref[...] = orbitals_ref[1 - mine]
    chosen = one_hot(points_ref, place_ref[0], place_ref[1], slab_size, picked_ref.shape[1])
    for k in range(kdevice):
        picked_ref[k] = pick(chosen, orbitals_ref[k]).astype(jnp.bfloat16)


def make_front(orbitals, points, place):
    kdevice, slab_size, channels = orbitals.shape
    vmem = pl.BlockSpec(memory_space=pltpu.VMEM)
    slab = jax.ShapeDtypeStruct((slab_size, channels), jnp.bfloat16)
    return pl.pallas_call(
        front_kernel,
        in_specs=[pl.BlockSpec(memory_space=pltpu.SMEM), vmem, vmem],
        out_specs=[vmem] * 3,
        out_shape=[
            slab,
            slab,
            jax.ShapeDtypeStruct((kdevice, points.shape[1] // 2, channels), jnp.bfloat16),
        ],
        compiler_params=pltpu.CompilerParams(vmem_limit_bytes=VMEM_LIMIT),
        name="front",
    )(place, points, orbitals)


def near_kernel(orbitals_ref, *refs):
    *picked_refs, out_ref = refs
    groups = out_ref.shape[0]
    rows = sum(picked_ref[0].astype(jnp.float32) for picked_ref in picked_refs)
    for part, turned in enumerate((rows, rotate(rows))):
        out_ref[:, 0, part] = product(turned.astype(jnp.bfloat16), orbitals_ref[0], groups)


def make_near(orbitals, shares, groups):
    kdevice, slab_size, channels = orbitals.shape
    npoints = shares[0].shape[1]
    length = npoints // groups
    return pl.pallas_call(
        near_kernel,
        grid=(kdevice,),
        in_specs=[pl.BlockSpec((1, slab_size, channels), lambda k: (k, 0, 0))]
        + [pl.BlockSpec((1, npoints, channels), lambda k: (k, 0, 0)) for _ in shares],
        out_specs=pl.BlockSpec((groups, 1, 2, length, slab_size), lambda k: (0, k, 0, 0, 0)),
        out_shape=jax.ShapeDtypeStruct((groups, kdevice, 2, length, slab_size), jnp.bfloat16),
        cost_estimate=pl.CostEstimate(
            flops=1_000_000_000, bytes_accessed=3_000_000, transcendentals=0
        ),
        compiler_params=pltpu.CompilerParams(vmem_limit_bytes=VMEM_LIMIT),
        name="near",
    )(orbitals, *shares)


def far_kernel(place_ref, rows_ref, *refs):
    *slab_refs, out_ref, parts_ref, sems = refs
    groups, _, _, length, slab_size = out_ref.shape
    spot = lax.broadcasted_iota(jnp.int32, (rows_ref.shape[0], slab_size), 1)
    picked = 0.0
    for number, slab_ref in enumerate(slab_refs):
        chosen = (rows_ref[:, number : number + 1] == spot).astype(jnp.float32)
        picked += jnp.dot(
            chosen.astype(jnp.bfloat16), slab_ref[...], preferred_element_type=jnp.float32
        )
    turned = [rows.astype(jnp.bfloat16) for rows in (picked, rotate(picked))]
    copies = []
    for number in range(SPLIT):
        for part in range(2):
            product = lax.dot_general(
                turned[part],
                slab_refs[number][...],
                (((1,), (1,)), ((), ())),
                preferred_element_type=jnp.float32,
            )
            place = len(copies)
            parts_ref[place] = product.reshape(groups, length, slab_size).astype(jnp.bfloat16)
            target = out_ref.at[:, place_ref[1] % SPLIT ^ number, part]
            copies.append(pltpu.make_async_copy(parts_ref.at[place], target, sems.at[place]))
            copies[-1].start()
    for copy in copies:
        copy.wait()


def make_far(rows, slabs, place, groups):
    slab_size, _ = slabs[0].shape
    length = rows.shape[0] // groups
    vmem = pl.BlockSpec(memory_space=pltpu.VMEM)
    return pl.pallas_call(
        far_kernel,
        in_specs=[pl.BlockSpec(memory_space=pltpu.SMEM), vmem] + [vmem] * len(slabs),
        out_specs=pl.BlockSpec(memory_space=pl.ANY),
        out_shape=jax.ShapeDtypeStruct((groups, SPLIT, 2, length, slab_size), jnp.bfloat16),
        scratch_shapes=[
            pltpu.VMEM((2 * SPLIT, groups, length, slab_size), jnp.bfloat16),
            pltpu.SemaphoreType.DMA((2 * SPLIT,)),
        ],
        cost_estimate=pl.CostEstimate(
            flops=60_000_000_000, bytes_accessed=180_000_000, transcendentals=0
        ),
        compiler_params=pltpu.CompilerParams(vmem_limit_bytes=VMEM_LIMIT),
        name="far",
    )(place, rows, *slabs)


def add_products(table_ref, held_ref, sums_ref, own_half, write):
    total_k = table_ref.shape[1]
    half_k = total_k // 2
    _, _, length, _ = held_ref.shape
    transfers = table_ref.shape[0]
    count = min(16, length)
    for start in range(0, length, count):
        rows = pl.ds(start, count)
        for transfer in range(transfers):
            shift = lax.rem(total_k - table_ref[transfer, 0], total_k)
            past = jnp.where(shift < half_k, half_k, shift - half_k)
            if own_half:
                begin = jnp.where(shift < half_k, shift, 0)
                steps = past - begin
            else:
                begin = past
                steps = jnp.where(shift < half_k, half_k + shift, total_k + half_k - shift)

            def step(i, sums, begin=begin, shift=shift, rows=rows):
                real_sum, imag_sum = sums
                for place in range(2):
                    k = lax.rem(begin + 2 * i + place, total_k)
                    other = lax.rem(k + total_k - shift, total_k)
                    real, imag = held_ref[k, 0, rows], held_ref[k, 1, rows]
                    other_real, other_imag = held_ref[other, 0, rows], held_ref[other, 1, rows]
                    real_sum += real * other_real + imag * other_imag
                    imag_sum += imag * other_real - real * other_imag
                return real_sum, imag_sum

            if own_half:
                sums = (jnp.zeros((count, held_ref.shape[3]), jnp.float32),) * 2
            else:
                sums = sums_ref[rows, transfer, 0], sums_ref[rows, transfer, 1]
            sums = lax.fori_loop(0, lax.div(steps, 2), step, sums)
            for part, value in enumerate(sums):
                sums_ref[rows, transfer, part] = value
        if write is not None:
            write(start // count, rows)


def early_kernel(table_ref, near_ref, sums_ref, held_ref):
    held_ref[...] = near_ref[...].astype(jnp.float32)
    add_products(table_ref, held_ref, sums_ref, True, None)


def pair_kernel(scale, table_ref, near_ref, far_ref, early_ref, out_ref, *scratch):
    held_ref, sums_ref, sems = scratch
    half_k = near_ref.shape[0]
    quarter_k = half_k // 2
    held_ref[:half_k] = near_ref[...].astype(jnp.float32)
    held_ref[half_k : half_k + quarter_k] = far_ref[quarter_k:].astype(jnp.float32)
    held_ref[half_k + quarter_k :] = far_ref[:quarter_k].astype(jnp.float32)
    sums_ref[...] = early_ref[...]
    copies = []

    def write(number, rows):
        sums_ref[rows] = sums_ref[rows] * scale
        copies.append(
            pltpu.make_async_copy(sums_ref.at[rows], out_ref.at[rows], sems.at[number])
        )
        copies[-1].start()

    add_products(table_ref, held_ref, sums_ref, False, write)
    for copy in copies:
        copy.wait()


def make_pairs(near, far, table):
    half_k, _, length, slab_size = near.shape
    out = jax.ShapeDtypeStruct((length, table.shape[0], 2, slab_size), jnp.float32)
    smem, vmem = pl.BlockSpec(memory_space=pltpu.SMEM), pl.BlockSpec(memory_space=pltpu.VMEM)
    early = pl.pallas_call(
        early_kernel,
        in_specs=[smem, vmem],
        out_specs=vmem,
        out_shape=out,
        scratch_shapes=[pltpu.VMEM(near.shape, jnp.float32)],
        cost_estimate=pl.CostEstimate(
            flops=60_000_000_000, bytes_accessed=180_000_000, transcendentals=0
        ),
        compiler_params=pltpu.CompilerParams(vmem_limit_bytes=VMEM_LIMIT),
        name="early",
    )(table, near)
    return pl.pallas_call(
        functools.partial(pair_kernel, 1.0 / math.sqrt(2 * half_k)),
        in_specs=[smem, vmem, vmem, vmem],
        out_specs=pl.BlockSpec(memory_space=pl.ANY),
        out_shape=out,
        scratch_shapes=[
            pltpu.VMEM((2 * half_k,) + near.shape[1:], jnp.float32),
            pltpu.VMEM(out.shape, jnp.float32),
            pltpu.SemaphoreType.DMA((length // min(16, length),)),
        ],
        compiler_params=pltpu.CompilerParams(vmem_limit_bytes=VMEM_LIMIT),
        name="pairs",
    )(table, near, far, early)


def on_device(orbitals, minus_table, points):
    kdevice, slab_size, channels = orbitals.shape
    half = lax.axis_index("half")
    groups = lax.axis_size("quarter") * lax.axis_size("inner")
    slabs = lax.axis_size("hi") * lax.axis_size("lo")
    points = points.reshape(1, -1)
    place = jnp.stack([half, lax.axis_index("hi") * SPLIT + lax.axis_index("lo")])

    mine, other, share = make_front(orbitals, points, place)
    shares = [share] + [swap(share, False, x) for x in range(1, slabs)]
    far = [swap(other if x & 1 else mine, True, x) for x in range(slabs)]

    def send(fields, around):
        fields = fields.reshape((-1,) + fields.shape[-3:])
        return lax.all_to_all(fields, around, split_axis=0, concat_axis=0, tiled=True)

    near_fields = make_near(orbitals, shares, groups)
    npoints = points.shape[1] // 2
    wanted = lax.dynamic_slice_in_dim(points[0], half * npoints, npoints)
    starts = jnp.stack([(place[1] ^ x) * slab_size for x in range(slabs)])
    rows = wanted[:, None] - starts[None, :]
    near_fields, rows = lax.optimization_barrier((near_fields, rows))
    far_fields = make_far(rows, far, place, groups)
    near_fields = send(near_fields, ("quarter", "inner"))
    far_fields = send(far_fields, ("quarter", "inner", "lo"))
    return make_pairs(near_fields, far_fields, minus_table)


def solution(mesh):
    kplaces, slabs = mesh.shape["ka"], mesh.shape["ga"]
    devices = mesh.devices.reshape(2, 2, kplaces // 4, slabs // SPLIT, SPLIT)
    finer = Mesh(devices, KA + GA)
    return jax.shard_map(
        on_device,
        mesh=finer,
        in_specs=(P(KA, GA, None), P(), P()),
        out_specs=P(KA, None, None, GA),
        check_vma=False,
    )
```

```python
import functools
import math

import jax
import jax.numpy as jnp
from jax import lax
from jax.experimental import pallas as pl
from jax.experimental.pallas import tpu as pltpu
from jax.sharding import Mesh
from jax.sharding import PartitionSpec as P

VMEM_LIMIT = 40 * 1024 * 1024
SPLIT = 2
KA, GA = ("half", "quarter", "inner"), ("hi", "lo")


def swap(block, mirror, other):
    half, quarter, inner, hi, lo = (lax.axis_size(name) for name in KA + GA)
    slabs = hi * lo
    route = []
    for place in range(half * quarter * inner * slabs):
        kplace, slab = divmod(place, slabs)
        part, within = divmod(kplace, inner)
        part = half * quarter - 1 - part if mirror else part
        route.append((place, (part * inner + within) * slabs + (slab ^ other)))
    return lax.ppermute(block, KA + GA, route)


def one_hot(points_ref, half, slab, slab_size, npoints):
    first = pl.multiple_of(half * npoints, npoints)
    wanted = points_ref[:, pl.ds(first, npoints)] - slab * slab_size
    spot = lax.broadcasted_iota(jnp.int32, (slab_size, npoints), 0)
    return (spot == wanted).astype(jnp.float32).astype(jnp.bfloat16)


def pick(chosen, slab):
    return lax.dot_general(
        chosen, slab, (((0,), (0,)), ((), ())), preferred_element_type=jnp.float32
    )


def rotate(picked):
    middle = picked.shape[1] // 2
    return jnp.concatenate([-picked[:, middle:], picked[:, :middle]], axis=1)


def product(rows, slab, groups):
    out = lax.dot_general(
        rows, slab, (((1,), (1,)), ((), ())), preferred_element_type=jnp.float32
    )
    return out.reshape(groups, -1, out.shape[1]).astype(jnp.bfloat16)


def front_kernel(place_ref, points_ref, mine_ref, other_ref, picked_ref):
    slab_size, _ = mine_ref.shape
    _, npoints, _ = picked_ref.shape
    mine = place_ref[1] % SPLIT
    chosen = one_hot(points_ref, place_ref[0], place_ref[1], slab_size, npoints)
    for k, slab_ref in ((mine, mine_ref), (1 - mine, other_ref)):
        picked_ref[k] = pick(chosen, slab_ref[...]).astype(jnp.bfloat16)


def make_front(mine, other, points, place):
    vmem = pl.BlockSpec(memory_space=pltpu.VMEM)
    return pl.pallas_call(
        front_kernel,
        in_specs=[pl.BlockSpec(memory_space=pltpu.SMEM)] + [vmem] * 3,
        out_specs=vmem,
        out_shape=jax.ShapeDtypeStruct(
            (SPLIT, points.shape[1] // 2, mine.shape[1]), jnp.bfloat16
        ),
        compiler_params=pltpu.CompilerParams(vmem_limit_bytes=VMEM_LIMIT),
        name="front",
    )(place, points, mine, other)


def near_kernel(orbitals_ref, *refs):
    *picked_refs, out_ref = refs
    groups = out_ref.shape[0]
    rows = sum(picked_ref[0].astype(jnp.float32) for picked_ref in picked_refs)
    for part, turned in enumerate((rows, rotate(rows))):
        out_ref[:, 0, part] = product(turned.astype(jnp.bfloat16), orbitals_ref[0], groups)


def make_near(orbitals, shares, groups):
    kdevice, slab_size, channels = orbitals.shape
    npoints = shares[0].shape[1]
    length = npoints // groups
    return pl.pallas_call(
        near_kernel,
        grid=(kdevice,),
        in_specs=[pl.BlockSpec((1, slab_size, channels), lambda k: (k, 0, 0))]
        + [pl.BlockSpec((1, npoints, channels), lambda k: (k, 0, 0)) for _ in shares],
        out_specs=pl.BlockSpec((groups, 1, 2, length, slab_size), lambda k: (0, k, 0, 0, 0)),
        out_shape=jax.ShapeDtypeStruct((groups, kdevice, 2, length, slab_size), jnp.bfloat16),
        cost_estimate=pl.CostEstimate(
            flops=1_000_000_000, bytes_accessed=3_000_000, transcendentals=0
        ),
        compiler_params=pltpu.CompilerParams(vmem_limit_bytes=VMEM_LIMIT),
        name="near",
    )(orbitals, *shares)


def far_kernel(place_ref, rows_ref, *refs):
    *slab_refs, out_ref, parts_ref, sems = refs
    groups, _, _, length, slab_size = out_ref.shape
    spot = lax.broadcasted_iota(jnp.int32, (rows_ref.shape[0], slab_size), 1)
    picked = 0.0
    for number, slab_ref in enumerate(slab_refs):
        chosen = (rows_ref[:, number : number + 1] == spot).astype(jnp.float32)
        picked += jnp.dot(
            chosen.astype(jnp.bfloat16), slab_ref[...], preferred_element_type=jnp.float32
        )
    turned = [rows.astype(jnp.bfloat16) for rows in (picked, rotate(picked))]
    copies = []
    for number in range(SPLIT):
        for part in range(2):
            product = lax.dot_general(
                turned[part],
                slab_refs[number][...],
                (((1,), (1,)), ((), ())),
                preferred_element_type=jnp.float32,
            )
            place = len(copies)
            parts_ref[place] = product.reshape(groups, length, slab_size).astype(jnp.bfloat16)
            target = out_ref.at[:, place_ref[1] % SPLIT ^ number, part]
            copies.append(pltpu.make_async_copy(parts_ref.at[place], target, sems.at[place]))
            copies[-1].start()
    for copy in copies:
        copy.wait()


def make_far(rows, slabs, place, groups):
    slab_size, _ = slabs[0].shape
    length = rows.shape[0] // groups
    vmem = pl.BlockSpec(memory_space=pltpu.VMEM)
    return pl.pallas_call(
        far_kernel,
        in_specs=[pl.BlockSpec(memory_space=pltpu.SMEM), vmem] + [vmem] * len(slabs),
        out_specs=pl.BlockSpec(memory_space=pl.ANY),
        out_shape=jax.ShapeDtypeStruct((groups, SPLIT, 2, length, slab_size), jnp.bfloat16),
        scratch_shapes=[
            pltpu.VMEM((2 * SPLIT, groups, length, slab_size), jnp.bfloat16),
            pltpu.SemaphoreType.DMA((2 * SPLIT,)),
        ],
        cost_estimate=pl.CostEstimate(
            flops=60_000_000_000, bytes_accessed=180_000_000, transcendentals=0
        ),
        compiler_params=pltpu.CompilerParams(vmem_limit_bytes=VMEM_LIMIT),
        name="far",
    )(place, rows, *slabs)


def pair_kernel(scale, table_ref, near_ref, far_ref, out_ref, held_ref, sums_ref, sems):
    total_k, _, length, width = held_ref.shape
    transfers = table_ref.shape[0]
    held_ref[: total_k // 2] = near_ref[...].astype(jnp.float32)
    held_ref[total_k // 2 :] = far_ref[...].astype(jnp.float32)

    count, columns = min(16, length), min(256, width)
    copies = []
    for start in range(0, length, count):
        rows = pl.ds(start, count)
        for column in range(0, width, columns):
            lanes = pl.ds(column, columns)

            def step(k, sums):
                real, imag = held_ref[k, 0, rows, lanes], held_ref[k, 1, rows, lanes]
                after = []
                for transfer in range(transfers):
                    other = table_ref[transfer, k]
                    other_real = held_ref[other, 0, rows, lanes]
                    other_imag = held_ref[other, 1, rows, lanes]
                    after.append(sums[2 * transfer] + (real * other_real + imag * other_imag))
                    after.append(sums[2 * transfer + 1] + (imag * other_real - real * other_imag))
                return tuple(after)

            zero = jnp.zeros((count, columns), jnp.float32)
            sums = lax.fori_loop(0, total_k, step, (zero,) * (2 * transfers), unroll=4)
            for place, value in enumerate(sums):
                sums_ref[rows, place // 2, place % 2, lanes] = value * scale
        copies.append(
            pltpu.make_async_copy(sums_ref.at[rows], out_ref.at[rows], sems.at[start // count])
        )
        copies[-1].start()
    for copy in copies:
        copy.wait()


def make_pairs(near, far, table):
    half_k, _, length, slab_size = near.shape
    transfers = table.shape[0]
    out = jax.ShapeDtypeStruct((length, transfers, 2, slab_size), jnp.float32)
    vmem = pl.BlockSpec(memory_space=pltpu.VMEM)
    return pl.pallas_call(
        functools.partial(pair_kernel, 1.0 / math.sqrt(2 * half_k)),
        in_specs=[pl.BlockSpec(memory_space=pltpu.SMEM), vmem, vmem],
        out_specs=pl.BlockSpec(memory_space=pl.ANY),
        out_shape=out,
        scratch_shapes=[
            pltpu.VMEM((2 * half_k, 2, length, slab_size), jnp.float32),
            pltpu.VMEM(out.shape, jnp.float32),
            pltpu.SemaphoreType.DMA((length // min(16, length),)),
        ],
        compiler_params=pltpu.CompilerParams(vmem_limit_bytes=VMEM_LIMIT),
        name="pairs",
    )(table, near, far)


def on_device(orbitals, minus_table, points):
    kdevice, slab_size, channels = orbitals.shape
    half = lax.axis_index("half")
    groups = lax.axis_size("quarter") * lax.axis_size("inner")
    slabs = lax.axis_size("hi") * lax.axis_size("lo")
    total_k = 2 * groups * kdevice
    points = points.reshape(1, -1)
    place = jnp.stack([half, lax.axis_index("hi") * SPLIT + lax.axis_index("lo")])

    lo = lax.axis_index("lo")
    mine = lax.dynamic_index_in_dim(orbitals, lo, 0, keepdims=False)
    other = lax.dynamic_index_in_dim(orbitals, 1 - lo, 0, keepdims=False)
    share = make_front(mine, other, points, place)
    shares = [share] + [swap(share, False, x) for x in range(1, slabs)]
    far = [swap(other if x & 1 else mine, True, x) for x in range(slabs)]

    def send(fields, around):
        fields = fields.reshape((-1,) + fields.shape[-3:])
        return lax.all_to_all(fields, around, split_axis=0, concat_axis=0, tiled=True)

    near_fields = make_near(orbitals, shares, groups)
    npoints = points.shape[1] // 2
    wanted = lax.dynamic_slice_in_dim(points[0], half * npoints, npoints)
    starts = jnp.stack([(place[1] ^ x) * slab_size for x in range(slabs)])
    rows = wanted[:, None] - starts[None, :]
    near_fields, rows = lax.optimization_barrier((near_fields, rows))
    far_fields = make_far(rows, far, place, groups)
    near_fields = send(near_fields, ("quarter", "inner"))
    near_fields, far_fields = lax.optimization_barrier((near_fields, far_fields))
    far_fields = send(far_fields, ("quarter", "inner", "lo"))

    def mirrored(kpoints):
        return total_k // 2 + (kpoints + total_k // 4) % (total_k // 2)

    turn = half * (total_k // 2)
    table = (jnp.roll(minus_table, -turn, axis=1) - turn) % total_k
    table = jnp.where(table < total_k // 2, table, mirrored(table))
    first, third, fourth = jnp.split(table, (total_k // 2, 3 * total_k // 4), axis=1)
    return make_pairs(near_fields, far_fields, jnp.concatenate([first, fourth, third], axis=1))


def solution(mesh):
    kplaces, slabs = mesh.shape["ka"], mesh.shape["ga"]
    devices = mesh.devices.reshape(2, 2, kplaces // 4, slabs // SPLIT, SPLIT)
    finer = Mesh(devices, KA + GA)
    return jax.shard_map(
        on_device,
        mesh=finer,
        in_specs=(P(KA, GA, None), P(), P()),
        out_specs=P(KA, None, None, GA),
        check_vma=False,
    )
```

```python
import functools
import math

import jax
import jax.numpy as jnp
from jax import lax
from jax.experimental import pallas as pl
from jax.experimental.pallas import tpu as pltpu
from jax.sharding import Mesh
from jax.sharding import PartitionSpec as P

VMEM_LIMIT = 40 * 1024 * 1024
SPLIT = 2
KA, GA = ("half", "quarter", "inner"), ("hi", "lo")


def swap(block, mirror, other):
    half, quarter, inner, hi, lo = (lax.axis_size(name) for name in KA + GA)
    slabs = hi * lo
    route = []
    for place in range(half * quarter * inner * slabs):
        kplace, slab = divmod(place, slabs)
        part, within = divmod(kplace, inner)
        part = half * quarter - 1 - part if mirror else part
        route.append((place, (part * inner + within) * slabs + (slab ^ other)))
    return lax.ppermute(block, KA + GA, route)


def one_hot(points_ref, half, slab, slab_size, npoints):
    first = pl.multiple_of(half * npoints, npoints)
    wanted = points_ref[:, pl.ds(first, npoints)] - slab * slab_size
    spot = lax.broadcasted_iota(jnp.int32, (slab_size, npoints), 0)
    return (spot == wanted).astype(jnp.float32).astype(jnp.bfloat16)


def pick(chosen, slab):
    return lax.dot_general(
        chosen, slab, (((0,), (0,)), ((), ())), preferred_element_type=jnp.float32
    )


def rotate(picked):
    middle = picked.shape[1] // 2
    return jnp.concatenate([-picked[:, middle:], picked[:, :middle]], axis=1)


def product(rows, slab, groups):
    out = lax.dot_general(
        rows, slab, (((1,), (1,)), ((), ())), preferred_element_type=jnp.float32
    )
    return out.reshape(groups, -1, out.shape[1]).astype(jnp.bfloat16)


def front_kernel(place_ref, points_ref, mine_ref, other_ref, picked_ref):
    slab_size, _ = mine_ref.shape
    _, npoints, _ = picked_ref.shape
    mine = place_ref[1] % SPLIT
    chosen = one_hot(points_ref, place_ref[0], place_ref[1], slab_size, npoints)
    for k, slab_ref in ((mine, mine_ref), (1 - mine, other_ref)):
        picked_ref[k] = pick(chosen, slab_ref[...]).astype(jnp.bfloat16)


def make_front(mine, other, points, place):
    vmem = pl.BlockSpec(memory_space=pltpu.VMEM)
    return pl.pallas_call(
        front_kernel,
        in_specs=[pl.BlockSpec(memory_space=pltpu.SMEM)] + [vmem] * 3,
        out_specs=vmem,
        out_shape=jax.ShapeDtypeStruct(
            (SPLIT, points.shape[1] // 2, mine.shape[1]), jnp.bfloat16
        ),
        compiler_params=pltpu.CompilerParams(vmem_limit_bytes=VMEM_LIMIT),
        name="front",
    )(place, points, mine, other)


def near_kernel(orbitals_ref, *refs):
    *picked_refs, out_ref = refs
    groups = out_ref.shape[0]
    rows = sum(picked_ref[0].astype(jnp.float32) for picked_ref in picked_refs)
    for part, turned in enumerate((rows, rotate(rows))):
        out_ref[:, 0, part] = product(turned.astype(jnp.bfloat16), orbitals_ref[0], groups)


def make_near(orbitals, shares, groups):
    kdevice, slab_size, channels = orbitals.shape
    npoints = shares[0].shape[1]
    length = npoints // groups
    return pl.pallas_call(
        near_kernel,
        grid=(kdevice,),
        in_specs=[pl.BlockSpec((1, slab_size, channels), lambda k: (k, 0, 0))]
        + [pl.BlockSpec((1, npoints, channels), lambda k: (k, 0, 0)) for _ in shares],
        out_specs=pl.BlockSpec((groups, 1, 2, length, slab_size), lambda k: (0, k, 0, 0, 0)),
        out_shape=jax.ShapeDtypeStruct((groups, kdevice, 2, length, slab_size), jnp.bfloat16),
        cost_estimate=pl.CostEstimate(
            flops=1_000_000_000, bytes_accessed=3_000_000, transcendentals=0
        ),
        compiler_params=pltpu.CompilerParams(vmem_limit_bytes=VMEM_LIMIT),
        name="near",
    )(orbitals, *shares)


def far_kernel(place_ref, rows_ref, *refs):
    *slab_refs, out_ref, parts_ref, sems = refs
    groups, _, _, length, slab_size = out_ref.shape
    spot = lax.broadcasted_iota(jnp.int32, (rows_ref.shape[0], slab_size), 1)
    picked = 0.0
    for number, slab_ref in enumerate(slab_refs):
        chosen = (rows_ref[:, number : number + 1] == spot).astype(jnp.float32)
        picked += jnp.dot(
            chosen.astype(jnp.bfloat16), slab_ref[...], preferred_element_type=jnp.float32
        )
    turned = [rows.astype(jnp.bfloat16) for rows in (picked, rotate(picked))]
    copies = []
    for number in range(SPLIT):
        for part in range(2):
            product = lax.dot_general(
                turned[part],
                slab_refs[number][...],
                (((1,), (1,)), ((), ())),
                preferred_element_type=jnp.float32,
            )
            place = len(copies)
            parts_ref[place] = product.reshape(groups, length, slab_size).astype(jnp.bfloat16)
            target = out_ref.at[:, place_ref[1] % SPLIT ^ number, part]
            copies.append(pltpu.make_async_copy(parts_ref.at[place], target, sems.at[place]))
            copies[-1].start()
    for copy in copies:
        copy.wait()


def make_far(rows, slabs, place, groups):
    slab_size, _ = slabs[0].shape
    length = rows.shape[0] // groups
    vmem = pl.BlockSpec(memory_space=pltpu.VMEM)
    return pl.pallas_call(
        far_kernel,
        in_specs=[pl.BlockSpec(memory_space=pltpu.SMEM), vmem] + [vmem] * len(slabs),
        out_specs=pl.BlockSpec(memory_space=pl.ANY),
        out_shape=jax.ShapeDtypeStruct((groups, SPLIT, 2, length, slab_size), jnp.bfloat16),
        scratch_shapes=[
            pltpu.VMEM((2 * SPLIT, groups, length, slab_size), jnp.bfloat16),
            pltpu.SemaphoreType.DMA((2 * SPLIT,)),
        ],
        cost_estimate=pl.CostEstimate(
            flops=60_000_000_000, bytes_accessed=180_000_000, transcendentals=0
        ),
        compiler_params=pltpu.CompilerParams(vmem_limit_bytes=VMEM_LIMIT),
        name="far",
    )(place, rows, *slabs)


def pair_kernel(scale, table_ref, near_ref, far_ref, out_ref, held_ref, sums_ref, sems):
    total_k, _, length, width = held_ref.shape
    transfers = table_ref.shape[0]
    held_ref[: total_k // 2] = near_ref[...].astype(jnp.float32)
    held_ref[total_k // 2 :] = far_ref[...].astype(jnp.float32)

    count, columns = min(16, length), min(256, width)
    copies = []
    for start in range(0, length, count):
        rows = pl.ds(start, count)
        for column in range(0, width, columns):
            lanes = pl.ds(column, columns)

            def step(k, sums):
                real, imag = held_ref[k, 0, rows, lanes], held_ref[k, 1, rows, lanes]
                after = []
                for transfer in range(transfers):
                    other = table_ref[transfer, k]
                    other_real = held_ref[other, 0, rows, lanes]
                    other_imag = held_ref[other, 1, rows, lanes]
                    after.append(sums[2 * transfer] + (real * other_real + imag * other_imag))
                    after.append(sums[2 * transfer + 1] + (imag * other_real - real * other_imag))
                return tuple(after)

            zero = jnp.zeros((count, columns), jnp.float32)
            sums = lax.fori_loop(0, total_k, step, (zero,) * (2 * transfers), unroll=4)
            for place, value in enumerate(sums):
                sums_ref[rows, place // 2, place % 2, lanes] = value * scale
        copies.append(
            pltpu.make_async_copy(sums_ref.at[rows], out_ref.at[rows], sems.at[start // count])
        )
        copies[-1].start()
    for copy in copies:
        copy.wait()


def make_pairs(near, far, table):
    half_k, _, length, slab_size = near.shape
    transfers = table.shape[0]
    out = jax.ShapeDtypeStruct((length, transfers, 2, slab_size), jnp.float32)
    vmem = pl.BlockSpec(memory_space=pltpu.VMEM)
    return pl.pallas_call(
        functools.partial(pair_kernel, 1.0 / math.sqrt(2 * half_k)),
        in_specs=[pl.BlockSpec(memory_space=pltpu.SMEM), vmem, vmem],
        out_specs=pl.BlockSpec(memory_space=pl.ANY),
        out_shape=out,
        scratch_shapes=[
            pltpu.VMEM((2 * half_k, 2, length, slab_size), jnp.float32),
            pltpu.VMEM(out.shape, jnp.float32),
            pltpu.SemaphoreType.DMA((length // min(16, length),)),
        ],
        compiler_params=pltpu.CompilerParams(vmem_limit_bytes=VMEM_LIMIT),
        name="pairs",
    )(table, near, far)


def on_device(orbitals, minus_table, points):
    kdevice, slab_size, channels = orbitals.shape
    half = lax.axis_index("half")
    groups = lax.axis_size("quarter") * lax.axis_size("inner")
    slabs = lax.axis_size("hi") * lax.axis_size("lo")
    total_k = 2 * groups * kdevice
    points = points.reshape(1, -1)
    place = jnp.stack([half, lax.axis_index("hi") * SPLIT + lax.axis_index("lo")])

    lo = lax.axis_index("lo")
    mine = lax.dynamic_index_in_dim(orbitals, lo, 0, keepdims=False)
    other = lax.dynamic_index_in_dim(orbitals, 1 - lo, 0, keepdims=False)
    share = make_front(mine, other, points, place)
    share, other = lax.optimization_barrier((share, other))
    shares = [share] + [swap(share, False, x) for x in range(1, slabs)]
    far = [swap(other if x & 1 else mine, True, x) for x in range(slabs)]

    def send(fields, around):
        fields = fields.reshape((-1,) + fields.shape[-3:])
        return lax.all_to_all(fields, around, split_axis=0, concat_axis=0, tiled=True)

    near_fields = make_near(orbitals, shares, groups)
    npoints = points.shape[1] // 2
    wanted = lax.dynamic_slice_in_dim(points[0], half * npoints, npoints)
    starts = jnp.stack([(place[1] ^ x) * slab_size for x in range(slabs)])
    rows = wanted[:, None] - starts[None, :]
    near_fields, rows = lax.optimization_barrier((near_fields, rows))
    far_fields = make_far(rows, far, place, groups)
    near_fields = send(near_fields, ("quarter", "inner"))
    near_fields, far_fields = lax.optimization_barrier((near_fields, far_fields))
    far_fields = send(far_fields, ("quarter", "inner", "lo"))

    def mirrored(kpoints):
        return total_k // 2 + (kpoints + total_k // 4) % (total_k // 2)

    turn = half * (total_k // 2)
    table = (jnp.roll(minus_table, -turn, axis=1) - turn) % total_k
    table = jnp.where(table < total_k // 2, table, mirrored(table))
    first, third, fourth = jnp.split(table, (total_k // 2, 3 * total_k // 4), axis=1)
    return make_pairs(near_fields, far_fields, jnp.concatenate([first, fourth, third], axis=1))


def solution(mesh):
    kplaces, slabs = mesh.shape["ka"], mesh.shape["ga"]
    devices = mesh.devices.reshape(2, 2, kplaces // 4, slabs // SPLIT, SPLIT)
    finer = Mesh(devices, KA + GA)
    return jax.shard_map(
        on_device,
        mesh=finer,
        in_specs=(P(KA, GA, None), P(), P()),
        out_specs=P(KA, None, None, GA),
        check_vma=False,
    )
```

```python
import functools
import math

import jax
import jax.numpy as jnp
from jax import lax
from jax.experimental import pallas as pl
from jax.experimental.pallas import tpu as pltpu
from jax.sharding import Mesh
from jax.sharding import PartitionSpec as P

VMEM_LIMIT = 40 * 1024 * 1024
SPLIT = 2
KA, GA = ("half", "quarter", "inner"), ("hi", "lo")


def swap(block, mirror, other):
    half, quarter, inner, hi, lo = (lax.axis_size(name) for name in KA + GA)
    slabs = hi * lo
    route = []
    for place in range(half * quarter * inner * slabs):
        kplace, slab = divmod(place, slabs)
        part, within = divmod(kplace, inner)
        part = half * quarter - 1 - part if mirror else part
        route.append((place, (part * inner + within) * slabs + (slab ^ other)))
    return lax.ppermute(block, KA + GA, route)


def one_hot(points_ref, half, slab, slab_size, npoints):
    first = pl.multiple_of(half * npoints, npoints)
    wanted = points_ref[:, pl.ds(first, npoints)] - slab * slab_size
    spot = lax.broadcasted_iota(jnp.int32, (slab_size, npoints), 0)
    return (spot == wanted).astype(jnp.float32).astype(jnp.bfloat16)


def pick(chosen, slab):
    return lax.dot_general(
        chosen, slab, (((0,), (0,)), ((), ())), preferred_element_type=jnp.float32
    )


def rotate(picked):
    middle = picked.shape[1] // 2
    return jnp.concatenate([-picked[:, middle:], picked[:, :middle]], axis=1)


def product(rows, slab, groups):
    out = lax.dot_general(
        rows, slab, (((1,), (1,)), ((), ())), preferred_element_type=jnp.float32
    )
    return out.reshape(groups, -1, out.shape[1]).astype(jnp.bfloat16)


def front_kernel(place_ref, points_ref, mine_ref, other_ref, picked_ref):
    slab_size, _ = mine_ref.shape
    _, npoints, _ = picked_ref.shape
    mine = place_ref[1] % SPLIT
    chosen = one_hot(points_ref, place_ref[0], place_ref[1], slab_size, npoints)
    for k, slab_ref in ((mine, mine_ref), (1 - mine, other_ref)):
        picked_ref[k] = pick(chosen, slab_ref[...]).astype(jnp.bfloat16)


def make_front(mine, other, points, place):
    vmem = pl.BlockSpec(memory_space=pltpu.VMEM)
    return pl.pallas_call(
        front_kernel,
        in_specs=[pl.BlockSpec(memory_space=pltpu.SMEM)] + [vmem] * 3,
        out_specs=vmem,
        out_shape=jax.ShapeDtypeStruct(
            (SPLIT, points.shape[1] // 2, mine.shape[1]), jnp.bfloat16
        ),
        compiler_params=pltpu.CompilerParams(vmem_limit_bytes=VMEM_LIMIT),
        name="front",
    )(place, points, mine, other)


def near_kernel(orbitals_ref, *refs):
    *picked_refs, out_ref = refs
    groups = out_ref.shape[0]
    rows = sum(picked_ref[0].astype(jnp.float32) for picked_ref in picked_refs)
    for part, turned in enumerate((rows, rotate(rows))):
        out_ref[:, 0, part] = product(turned.astype(jnp.bfloat16), orbitals_ref[0], groups)


def make_near(orbitals, shares, groups):
    kdevice, slab_size, channels = orbitals.shape
    npoints = shares[0].shape[1]
    length = npoints // groups
    return pl.pallas_call(
        near_kernel,
        grid=(kdevice,),
        in_specs=[pl.BlockSpec((1, slab_size, channels), lambda k: (k, 0, 0))]
        + [pl.BlockSpec((1, npoints, channels), lambda k: (k, 0, 0)) for _ in shares],
        out_specs=pl.BlockSpec((groups, 1, 2, length, slab_size), lambda k: (0, k, 0, 0, 0)),
        out_shape=jax.ShapeDtypeStruct((groups, kdevice, 2, length, slab_size), jnp.bfloat16),
        cost_estimate=pl.CostEstimate(
            flops=1_000_000_000, bytes_accessed=3_000_000, transcendentals=0
        ),
        compiler_params=pltpu.CompilerParams(vmem_limit_bytes=VMEM_LIMIT),
        name="near",
    )(orbitals, *shares)


def far_kernel(place_ref, rows_ref, *refs):
    *slab_refs, out_ref, parts_ref, sems = refs
    groups, _, _, length, slab_size = out_ref.shape
    spot = lax.broadcasted_iota(jnp.int32, (rows_ref.shape[0], slab_size), 1)
    picked = 0.0
    for number, slab_ref in enumerate(slab_refs):
        chosen = (rows_ref[:, number : number + 1] == spot).astype(jnp.float32)
        picked += jnp.dot(
            chosen.astype(jnp.bfloat16), slab_ref[...], preferred_element_type=jnp.float32
        )
    turned = [rows.astype(jnp.bfloat16) for rows in (picked, rotate(picked))]
    copies = []
    for number in range(SPLIT):
        for part in range(2):
            product = lax.dot_general(
                turned[part],
                slab_refs[number][...],
                (((1,), (1,)), ((), ())),
                preferred_element_type=jnp.float32,
            )
            place = len(copies)
            parts_ref[place] = product.reshape(groups, length, slab_size).astype(jnp.bfloat16)
            target = out_ref.at[:, place_ref[1] % SPLIT ^ number, part]
            copies.append(pltpu.make_async_copy(parts_ref.at[place], target, sems.at[place]))
            copies[-1].start()
    for copy in copies:
        copy.wait()


def make_far(rows, slabs, place, groups):
    slab_size, _ = slabs[0].shape
    length = rows.shape[0] // groups
    vmem = pl.BlockSpec(memory_space=pltpu.VMEM)
    return pl.pallas_call(
        far_kernel,
        in_specs=[pl.BlockSpec(memory_space=pltpu.SMEM), vmem] + [vmem] * len(slabs),
        out_specs=pl.BlockSpec(memory_space=pl.ANY),
        out_shape=jax.ShapeDtypeStruct((groups, SPLIT, 2, length, slab_size), jnp.bfloat16),
        scratch_shapes=[
            pltpu.VMEM((2 * SPLIT, groups, length, slab_size), jnp.bfloat16),
            pltpu.SemaphoreType.DMA((2 * SPLIT,)),
        ],
        cost_estimate=pl.CostEstimate(
            flops=60_000_000_000, bytes_accessed=180_000_000, transcendentals=0
        ),
        compiler_params=pltpu.CompilerParams(vmem_limit_bytes=VMEM_LIMIT),
        name="far",
    )(place, rows, *slabs)


def pair_kernel(scale, table_ref, near_ref, far_ref, out_ref, held_ref, sums_ref, sems):
    total_k, _, length, width = held_ref.shape
    transfers = table_ref.shape[0]
    held_ref[: total_k // 2] = near_ref[...].astype(jnp.float32)
    held_ref[total_k // 2 :] = far_ref[...].astype(jnp.float32)

    count, columns = min(16, length), min(256, width)
    copies = []
    for start in range(0, length, count):
        rows = pl.ds(start, count)
        for column in range(0, width, columns):
            lanes = pl.ds(column, columns)

            def step(k, sums):
                real, imag = held_ref[k, 0, rows, lanes], held_ref[k, 1, rows, lanes]
                after = []
                for transfer in range(transfers):
                    other = table_ref[transfer, k]
                    other_real = held_ref[other, 0, rows, lanes]
                    other_imag = held_ref[other, 1, rows, lanes]
                    after.append(sums[2 * transfer] + (real * other_real + imag * other_imag))
                    after.append(sums[2 * transfer + 1] + (imag * other_real - real * other_imag))
                return tuple(after)

            zero = jnp.zeros((count, columns), jnp.float32)
            sums = lax.fori_loop(0, total_k, step, (zero,) * (2 * transfers), unroll=4)
            for place, value in enumerate(sums):
                sums_ref[rows, place // 2, place % 2, lanes] = value * scale
        copies.append(
            pltpu.make_async_copy(sums_ref.at[rows], out_ref.at[rows], sems.at[start // count])
        )
        copies[-1].start()
    for copy in copies:
        copy.wait()


def make_pairs(near, far, table):
    half_k, _, length, slab_size = near.shape
    transfers = table.shape[0]
    out = jax.ShapeDtypeStruct((length, transfers, 2, slab_size), jnp.float32)
    vmem = pl.BlockSpec(memory_space=pltpu.VMEM)
    return pl.pallas_call(
        functools.partial(pair_kernel, 1.0 / math.sqrt(2 * half_k)),
        in_specs=[pl.BlockSpec(memory_space=pltpu.SMEM), vmem, vmem],
        out_specs=pl.BlockSpec(memory_space=pl.ANY),
        out_shape=out,
        scratch_shapes=[
            pltpu.VMEM((2 * half_k, 2, length, slab_size), jnp.float32),
            pltpu.VMEM(out.shape, jnp.float32),
            pltpu.SemaphoreType.DMA((length // min(16, length),)),
        ],
        compiler_params=pltpu.CompilerParams(vmem_limit_bytes=VMEM_LIMIT),
        name="pairs",
    )(table, near, far)


def on_device(orbitals, minus_table, points):
    kdevice, slab_size, channels = orbitals.shape
    half = lax.axis_index("half")
    groups = lax.axis_size("quarter") * lax.axis_size("inner")
    slabs = lax.axis_size("hi") * lax.axis_size("lo")
    total_k = 2 * groups * kdevice
    points = points.reshape(1, -1)
    place = jnp.stack([half, lax.axis_index("hi") * SPLIT + lax.axis_index("lo")])

    lo = lax.axis_index("lo")
    mine = lax.dynamic_index_in_dim(orbitals, lo, 0, keepdims=False)
    other = lax.dynamic_index_in_dim(orbitals, 1 - lo, 0, keepdims=False)
    share = make_front(mine, other, points, place)
    share, mine, other = lax.optimization_barrier((share, mine, other))
    shares = [share] + [swap(share, False, x) for x in range(1, slabs)]
    far = [swap(other if x & 1 else mine, True, x) for x in range(slabs)]

    def send(fields, around):
        fields = fields.reshape((-1,) + fields.shape[-3:])
        return lax.all_to_all(fields, around, split_axis=0, concat_axis=0, tiled=True)

    near_fields = make_near(orbitals, shares, groups)
    npoints = points.shape[1] // 2
    wanted = lax.dynamic_slice_in_dim(points[0], half * npoints, npoints)
    starts = jnp.stack([(place[1] ^ x) * slab_size for x in range(slabs)])
    rows = wanted[:, None] - starts[None, :]
    near_fields, rows = lax.optimization_barrier((near_fields, rows))
    far_fields = make_far(rows, far, place, groups)
    near_fields = send(near_fields, ("quarter", "inner"))
    near_fields, far_fields = lax.optimization_barrier((near_fields, far_fields))
    far_fields = send(far_fields, ("quarter", "inner", "lo"))

    def mirrored(kpoints):
        return total_k // 2 + (kpoints + total_k // 4) % (total_k // 2)

    turn = half * (total_k // 2)
    table = (jnp.roll(minus_table, -turn, axis=1) - turn) % total_k
    table = jnp.where(table < total_k // 2, table, mirrored(table))
    first, third, fourth = jnp.split(table, (total_k // 2, 3 * total_k // 4), axis=1)
    return make_pairs(near_fields, far_fields, jnp.concatenate([first, fourth, third], axis=1))


def solution(mesh):
    kplaces, slabs = mesh.shape["ka"], mesh.shape["ga"]
    devices = mesh.devices.reshape(2, 2, kplaces // 4, slabs // SPLIT, SPLIT)
    finer = Mesh(devices, KA + GA)
    return jax.shard_map(
        on_device,
        mesh=finer,
        in_specs=(P(KA, GA, None), P(), P()),
        out_specs=P(KA, None, None, GA),
        check_vma=False,
    )
```

```python
import functools
import math

import jax
import jax.numpy as jnp
from jax import lax
from jax.experimental import pallas as pl
from jax.experimental.pallas import tpu as pltpu
from jax.sharding import Mesh
from jax.sharding import PartitionSpec as P

VMEM_LIMIT = 40 * 1024 * 1024
SPLIT = 2
KA, GA = ("half", "quarter", "inner"), ("hi", "lo")


def swap(block, mirror, other):
    half, quarter, inner, hi, lo = (lax.axis_size(name) for name in KA + GA)
    slabs = hi * lo
    route = []
    for place in range(half * quarter * inner * slabs):
        kplace, slab = divmod(place, slabs)
        part, within = divmod(kplace, inner)
        part = half * quarter - 1 - part if mirror else part
        route.append((place, (part * inner + within) * slabs + (slab ^ other)))
    return lax.ppermute(block, KA + GA, route)


def one_hot(points_ref, half, slab, slab_size, npoints):
    first = pl.multiple_of(half * npoints, npoints)
    wanted = points_ref[:, pl.ds(first, npoints)] - slab * slab_size
    spot = lax.broadcasted_iota(jnp.int32, (slab_size, npoints), 0)
    return (spot == wanted).astype(jnp.float32).astype(jnp.bfloat16)


def pick(chosen, slab):
    return lax.dot_general(
        chosen, slab, (((0,), (0,)), ((), ())), preferred_element_type=jnp.float32
    )


def rotate(picked):
    middle = picked.shape[1] // 2
    return jnp.concatenate([-picked[:, middle:], picked[:, :middle]], axis=1)


def product(rows, slab, groups):
    out = lax.dot_general(
        rows, slab, (((1,), (1,)), ((), ())), preferred_element_type=jnp.float32
    )
    return out.reshape(groups, -1, out.shape[1]).astype(jnp.bfloat16)


def front_kernel(place_ref, points_ref, mine_ref, other_ref, picked_ref):
    slab_size, _ = mine_ref.shape
    _, npoints, _ = picked_ref.shape
    mine = place_ref[1] % SPLIT
    chosen = one_hot(points_ref, place_ref[0], place_ref[1], slab_size, npoints)
    for k, slab_ref in ((mine, mine_ref), (1 - mine, other_ref)):
        picked_ref[k] = pick(chosen, slab_ref[...]).astype(jnp.bfloat16)


def make_front(mine, other, points, place):
    vmem = pl.BlockSpec(memory_space=pltpu.VMEM)
    return pl.pallas_call(
        front_kernel,
        in_specs=[pl.BlockSpec(memory_space=pltpu.SMEM)] + [vmem] * 3,
        out_specs=vmem,
        out_shape=jax.ShapeDtypeStruct(
            (SPLIT, points.shape[1] // 2, mine.shape[1]), jnp.bfloat16
        ),
        compiler_params=pltpu.CompilerParams(vmem_limit_bytes=VMEM_LIMIT),
        name="front",
    )(place, points, mine, other)


def near_kernel(orbitals_ref, *refs):
    *picked_refs, out_ref = refs
    groups = out_ref.shape[0]
    rows = sum(picked_ref[0].astype(jnp.float32) for picked_ref in picked_refs)
    for part, turned in enumerate((rows, rotate(rows))):
        out_ref[:, 0, part] = product(turned.astype(jnp.bfloat16), orbitals_ref[0], groups)


def make_near(orbitals, shares, groups):
    kdevice, slab_size, channels = orbitals.shape
    npoints = shares[0].shape[1]
    length = npoints // groups
    return pl.pallas_call(
        near_kernel,
        grid=(kdevice,),
        in_specs=[pl.BlockSpec((1, slab_size, channels), lambda k: (k, 0, 0))]
        + [pl.BlockSpec((1, npoints, channels), lambda k: (k, 0, 0)) for _ in shares],
        out_specs=pl.BlockSpec((groups, 1, 2, length, slab_size), lambda k: (0, k, 0, 0, 0)),
        out_shape=jax.ShapeDtypeStruct((groups, kdevice, 2, length, slab_size), jnp.bfloat16),
        cost_estimate=pl.CostEstimate(
            flops=1_000_000_000, bytes_accessed=3_000_000, transcendentals=0
        ),
        compiler_params=pltpu.CompilerParams(vmem_limit_bytes=VMEM_LIMIT),
        name="near",
    )(orbitals, *shares)


def ahead_kernel(rows_ref, slab_ref, picked_ref, chosen_ref):
    npoints, slabs = rows_ref.shape
    spot = lax.broadcasted_iota(jnp.int32, (npoints, slab_ref.shape[0]), 1)
    for number in range(slabs):
        chosen = (rows_ref[:, number : number + 1] == spot).astype(jnp.float32)
        chosen = chosen.astype(jnp.bfloat16)
        if number:
            chosen_ref[number - 1] = chosen
        else:
            picked = jnp.dot(chosen, slab_ref[...], preferred_element_type=jnp.float32)
            picked_ref[...] = picked.astype(jnp.bfloat16)


def far_kernel(place_ref, picked_ref, chosen_ref, *refs):
    *slab_refs, out_ref, parts_ref, sems = refs
    groups, _, _, length, slab_size = out_ref.shape
    picked = picked_ref[...].astype(jnp.float32)
    for number, slab_ref in enumerate(slab_refs[1:]):
        picked += jnp.dot(chosen_ref[number], slab_ref[...], preferred_element_type=jnp.float32)
    turned = [rows.astype(jnp.bfloat16) for rows in (picked, rotate(picked))]
    copies = []
    for number in range(SPLIT):
        for part in range(2):
            place = len(copies)
            parts_ref[place] = product(turned[part], slab_refs[number][...], groups)
            target = out_ref.at[:, place_ref[1] % SPLIT ^ number, part]
            copies.append(pltpu.make_async_copy(parts_ref.at[place], target, sems.at[place]))
            copies[-1].start()
    for copy in copies:
        copy.wait()


def make_far(rows, slabs, place, groups):
    slab_size, channels = slabs[0].shape
    npoints, _ = rows.shape
    length = npoints // groups
    vmem = pl.BlockSpec(memory_space=pltpu.VMEM)
    picked, chosen = pl.pallas_call(
        ahead_kernel,
        in_specs=[vmem] * 2,
        out_specs=[vmem] * 2,
        out_shape=[
            jax.ShapeDtypeStruct((npoints, channels), jnp.bfloat16),
            jax.ShapeDtypeStruct((len(slabs) - 1, npoints, slab_size), jnp.bfloat16),
        ],
        cost_estimate=pl.CostEstimate(flops=1_000_000, bytes_accessed=3_000, transcendentals=0),
        compiler_params=pltpu.CompilerParams(vmem_limit_bytes=VMEM_LIMIT),
        name="ahead",
    )(rows, slabs[0])
    return pl.pallas_call(
        far_kernel,
        in_specs=[pl.BlockSpec(memory_space=pltpu.SMEM)] + [vmem] * (2 + len(slabs)),
        out_specs=pl.BlockSpec(memory_space=pl.ANY),
        out_shape=jax.ShapeDtypeStruct((groups, SPLIT, 2, length, slab_size), jnp.bfloat16),
        scratch_shapes=[
            pltpu.VMEM((2 * SPLIT, groups, length, slab_size), jnp.bfloat16),
            pltpu.SemaphoreType.DMA((2 * SPLIT,)),
        ],
        cost_estimate=pl.CostEstimate(
            flops=60_000_000_000, bytes_accessed=180_000_000, transcendentals=0
        ),
        compiler_params=pltpu.CompilerParams(vmem_limit_bytes=VMEM_LIMIT),
        name="far",
    )(place, picked, chosen, *slabs)


def pair_kernel(scale, table_ref, near_ref, far_ref, out_ref, held_ref, sums_ref, sems):
    total_k, _, length, width = held_ref.shape
    transfers = table_ref.shape[0]
    held_ref[: total_k // 2] = near_ref[...].astype(jnp.float32)
    held_ref[total_k // 2 :] = far_ref[...].astype(jnp.float32)

    columns = min(256, width)
    copies = []
    for column in range(0, width, columns):
        lanes = pl.ds(column, columns)

        def step(k, sums, lanes=lanes):
            real, imag = held_ref[k, 0, :, lanes], held_ref[k, 1, :, lanes]
            after = []
            for transfer in range(transfers):
                other = table_ref[transfer, k]
                other_real = held_ref[other, 0, :, lanes]
                other_imag = held_ref[other, 1, :, lanes]
                after.append(sums[2 * transfer] + (real * other_real + imag * other_imag))
                after.append(sums[2 * transfer + 1] + (imag * other_real - real * other_imag))
            return tuple(after)

        zero = jnp.zeros((length, columns), jnp.float32)
        sums = lax.fori_loop(0, total_k, step, (zero,) * (2 * transfers), unroll=4)
        for place, value in enumerate(sums):
            sums_ref[:, place // 2, place % 2, lanes] = value * scale
        source, target = sums_ref.at[:, :, :, lanes], out_ref.at[:, :, :, lanes]
        copies.append(pltpu.make_async_copy(source, target, sems.at[column // columns]))
        copies[-1].start()
    for copy in copies:
        copy.wait()


def make_pairs(near, far, table):
    half_k, _, length, slab_size = near.shape
    transfers = table.shape[0]
    out = jax.ShapeDtypeStruct((length, transfers, 2, slab_size), jnp.float32)
    vmem = pl.BlockSpec(memory_space=pltpu.VMEM)
    return pl.pallas_call(
        functools.partial(pair_kernel, 1.0 / math.sqrt(2 * half_k)),
        in_specs=[pl.BlockSpec(memory_space=pltpu.SMEM), vmem, vmem],
        out_specs=pl.BlockSpec(memory_space=pl.ANY),
        out_shape=out,
        scratch_shapes=[
            pltpu.VMEM((2 * half_k, 2, length, slab_size), jnp.float32),
            pltpu.VMEM(out.shape, jnp.float32),
            pltpu.SemaphoreType.DMA((slab_size // min(256, slab_size),)),
        ],
        compiler_params=pltpu.CompilerParams(vmem_limit_bytes=VMEM_LIMIT),
        name="pairs",
    )(table, near, far)


def on_device(orbitals, minus_table, points):
    kdevice, slab_size, channels = orbitals.shape
    half = lax.axis_index("half")
    groups = lax.axis_size("quarter") * lax.axis_size("inner")
    slabs = lax.axis_size("hi") * lax.axis_size("lo")
    total_k = 2 * groups * kdevice
    points = points.reshape(1, -1)
    place = jnp.stack([half, lax.axis_index("hi") * SPLIT + lax.axis_index("lo")])

    lo = lax.axis_index("lo")
    mine = lax.dynamic_index_in_dim(orbitals, lo, 0, keepdims=False)
    other = lax.dynamic_index_in_dim(orbitals, 1 - lo, 0, keepdims=False)
    share = make_front(mine, other, points, place)
    share, mine, other = lax.optimization_barrier((share, mine, other))
    shares = [share] + [swap(share, False, x) for x in range(1, slabs)]
    far = [swap(other if x & 1 else mine, True, x) for x in range(slabs)]

    def send(fields, around):
        fields = fields.reshape((-1,) + fields.shape[-3:])
        return lax.all_to_all(fields, around, split_axis=0, concat_axis=0, tiled=True)

    near_fields = make_near(orbitals, shares, groups)
    npoints = points.shape[1] // 2
    wanted = lax.dynamic_slice_in_dim(points[0], half * npoints, npoints)
    starts = jnp.stack([(place[1] ^ x) * slab_size for x in range(slabs)])
    rows = wanted[:, None] - starts[None, :]
    near_fields, rows = lax.optimization_barrier((near_fields, rows))
    far_fields = make_far(rows, far, place, groups)
    near_fields = send(near_fields, ("quarter", "inner"))
    near_fields, far_fields = lax.optimization_barrier((near_fields, far_fields))
    far_fields = send(far_fields, ("quarter", "inner", "lo"))

    def mirrored(kpoints):
        return total_k // 2 + (kpoints + total_k // 4) % (total_k // 2)

    turn = half * (total_k // 2)
    table = (jnp.roll(minus_table, -turn, axis=1) - turn) % total_k
    table = jnp.where(table < total_k // 2, table, mirrored(table))
    first, third, fourth = jnp.split(table, (total_k // 2, 3 * total_k // 4), axis=1)
    return make_pairs(near_fields, far_fields, jnp.concatenate([first, fourth, third], axis=1))


def solution(mesh):
    kplaces, slabs = mesh.shape["ka"], mesh.shape["ga"]
    devices = mesh.devices.reshape(2, 2, kplaces // 4, slabs // SPLIT, SPLIT)
    finer = Mesh(devices, KA + GA)
    return jax.shard_map(
        on_device,
        mesh=finer,
        in_specs=(P(KA, GA, None), P(), P()),
        out_specs=P(KA, None, None, GA),
        check_vma=False,
    )
```

```python
import functools
import math

import jax
import jax.numpy as jnp
from jax import lax
from jax.experimental import pallas as pl
from jax.experimental.pallas import tpu as pltpu
from jax.sharding import Mesh
from jax.sharding import PartitionSpec as P

VMEM_LIMIT = 40 * 1024 * 1024
SPLIT = 2
KA, GA = ("half", "quarter", "inner"), ("hi", "lo")


def swap(block, mirror, other):
    half, quarter, inner, hi, lo = (lax.axis_size(name) for name in KA + GA)
    slabs = hi * lo
    route = []
    for place in range(half * quarter * inner * slabs):
        kplace, slab = divmod(place, slabs)
        part, within = divmod(kplace, inner)
        part = half * quarter - 1 - part if mirror else part
        route.append((place, (part * inner + within) * slabs + (slab ^ other)))
    return lax.ppermute(block, KA + GA, route)


def one_hot(points_ref, half, slab, slab_size, npoints):
    first = pl.multiple_of(half * npoints, npoints)
    wanted = points_ref[:, pl.ds(first, npoints)] - slab * slab_size
    spot = lax.broadcasted_iota(jnp.int32, (slab_size, npoints), 0)
    return (spot == wanted).astype(jnp.float32).astype(jnp.bfloat16)


def pick(chosen, slab):
    return lax.dot_general(
        chosen, slab, (((0,), (0,)), ((), ())), preferred_element_type=jnp.float32
    )


def rotate(picked):
    middle = picked.shape[1] // 2
    return jnp.concatenate([-picked[:, middle:], picked[:, :middle]], axis=1)


def product(rows, slab, groups):
    out = lax.dot_general(
        rows, slab, (((1,), (1,)), ((), ())), preferred_element_type=jnp.float32
    )
    return out.reshape(groups, -1, out.shape[1]).astype(jnp.bfloat16)


def front_kernel(place_ref, points_ref, mine_ref, other_ref, picked_ref):
    slab_size, _ = mine_ref.shape
    _, npoints, _ = picked_ref.shape
    mine = place_ref[1] % SPLIT
    chosen = one_hot(points_ref, place_ref[0], place_ref[1], slab_size, npoints)
    for k, slab_ref in ((mine, mine_ref), (1 - mine, other_ref)):
        picked_ref[k] = pick(chosen, slab_ref[...]).astype(jnp.bfloat16)


def make_front(mine, other, points, place):
    vmem = pl.BlockSpec(memory_space=pltpu.VMEM)
    return pl.pallas_call(
        front_kernel,
        in_specs=[pl.BlockSpec(memory_space=pltpu.SMEM)] + [vmem] * 3,
        out_specs=vmem,
        out_shape=jax.ShapeDtypeStruct(
            (SPLIT, points.shape[1] // 2, mine.shape[1]), jnp.bfloat16
        ),
        compiler_params=pltpu.CompilerParams(vmem_limit_bytes=VMEM_LIMIT),
        name="front",
    )(place, points, mine, other)


def near_kernel(orbitals_ref, *refs):
    *picked_refs, out_ref = refs
    groups = out_ref.shape[0]
    rows = sum(picked_ref[0].astype(jnp.float32) for picked_ref in picked_refs)
    for part, turned in enumerate((rows, rotate(rows))):
        out_ref[:, 0, part] = product(turned.astype(jnp.bfloat16), orbitals_ref[0], groups)


def make_near(orbitals, shares, groups):
    kdevice, slab_size, channels = orbitals.shape
    npoints = shares[0].shape[1]
    length = npoints // groups
    return pl.pallas_call(
        near_kernel,
        grid=(kdevice,),
        in_specs=[pl.BlockSpec((1, slab_size, channels), lambda k: (k, 0, 0))]
        + [pl.BlockSpec((1, npoints, channels), lambda k: (k, 0, 0)) for _ in shares],
        out_specs=pl.BlockSpec((groups, 1, 2, length, slab_size), lambda k: (0, k, 0, 0, 0)),
        out_shape=jax.ShapeDtypeStruct((groups, kdevice, 2, length, slab_size), jnp.bfloat16),
        cost_estimate=pl.CostEstimate(
            flops=1_000_000_000, bytes_accessed=3_000_000, transcendentals=0
        ),
        compiler_params=pltpu.CompilerParams(vmem_limit_bytes=VMEM_LIMIT),
        name="near",
    )(orbitals, *shares)


def far_kernel(place_ref, rows_ref, *refs):
    *slab_refs, out_ref, parts_ref, sems = refs
    groups, _, _, length, slab_size = out_ref.shape
    spot = lax.broadcasted_iota(jnp.int32, (rows_ref.shape[0], slab_size), 1)
    picked = 0.0
    for number, slab_ref in enumerate(slab_refs):
        chosen = (rows_ref[:, number : number + 1] == spot).astype(jnp.float32)
        picked += jnp.dot(
            chosen.astype(jnp.bfloat16), slab_ref[...], preferred_element_type=jnp.float32
        )
    turned = [rows.astype(jnp.bfloat16) for rows in (picked, rotate(picked))]
    copies = []
    for number in range(SPLIT):
        for part in range(2):
            product = lax.dot_general(
                turned[part],
                slab_refs[number][...],
                (((1,), (1,)), ((), ())),
                preferred_element_type=jnp.float32,
            )
            place = len(copies)
            parts_ref[place] = product.reshape(groups, length, slab_size).astype(jnp.bfloat16)
            target = out_ref.at[:, place_ref[1] % SPLIT ^ number, part]
            copies.append(pltpu.make_async_copy(parts_ref.at[place], target, sems.at[place]))
            copies[-1].start()
    for copy in copies:
        copy.wait()


def make_far(rows, slabs, place, groups):
    slab_size, _ = slabs[0].shape
    length = rows.shape[0] // groups
    vmem = pl.BlockSpec(memory_space=pltpu.VMEM)
    return pl.pallas_call(
        far_kernel,
        in_specs=[pl.BlockSpec(memory_space=pltpu.SMEM), vmem] + [vmem] * len(slabs),
        out_specs=pl.BlockSpec(memory_space=pl.ANY),
        out_shape=jax.ShapeDtypeStruct((groups, SPLIT, 2, length, slab_size), jnp.bfloat16),
        scratch_shapes=[
            pltpu.VMEM((2 * SPLIT, groups, length, slab_size), jnp.bfloat16),
            pltpu.SemaphoreType.DMA((2 * SPLIT,)),
        ],
        cost_estimate=pl.CostEstimate(
            flops=60_000_000_000, bytes_accessed=180_000_000, transcendentals=0
        ),
        compiler_params=pltpu.CompilerParams(vmem_limit_bytes=VMEM_LIMIT),
        name="far",
    )(place, rows, *slabs)


def pair_kernel(scale, table_ref, near_ref, far_ref, out_ref, held_ref, sums_ref, sems):
    total_k, _, length, width = held_ref.shape
    transfers = table_ref.shape[0]
    held_ref[: total_k // 2] = near_ref[...].astype(jnp.float32)
    held_ref[total_k // 2 :] = far_ref[...].astype(jnp.float32)

    count, columns = min(16, length), min(256, width)
    copies = []
    for start in range(0, length, count):
        rows = pl.ds(start, count)
        for column in range(0, width, columns):
            lanes = pl.ds(column, columns)

            def step(k, sums):
                real, imag = held_ref[k, 0, rows, lanes], held_ref[k, 1, rows, lanes]
                after = []
                for transfer in range(transfers):
                    other = table_ref[transfer, k]
                    other_real = held_ref[other, 0, rows, lanes]
                    other_imag = held_ref[other, 1, rows, lanes]
                    after.append(sums[2 * transfer] + (real * other_real + imag * other_imag))
                    after.append(sums[2 * transfer + 1] + (imag * other_real - real * other_imag))
                return tuple(after)

            zero = jnp.zeros((count, columns), jnp.float32)
            sums = lax.fori_loop(0, total_k, step, (zero,) * (2 * transfers), unroll=4)
            for place, value in enumerate(sums):
                sums_ref[rows, place // 2, place % 2, lanes] = value * scale
        copies.append(
            pltpu.make_async_copy(sums_ref.at[rows], out_ref.at[rows], sems.at[start // count])
        )
        copies[-1].start()
    for copy in copies:
        copy.wait()


def make_pairs(near, far, table):
    half_k, _, length, slab_size = near.shape
    transfers = table.shape[0]
    out = jax.ShapeDtypeStruct((length, transfers, 2, slab_size), jnp.float32)
    vmem = pl.BlockSpec(memory_space=pltpu.VMEM)
    return pl.pallas_call(
        functools.partial(pair_kernel, 1.0 / math.sqrt(2 * half_k)),
        in_specs=[pl.BlockSpec(memory_space=pltpu.SMEM), vmem, vmem],
        out_specs=pl.BlockSpec(memory_space=pl.ANY),
        out_shape=out,
        scratch_shapes=[
            pltpu.VMEM((2 * half_k, 2, length, slab_size), jnp.float32),
            pltpu.VMEM(out.shape, jnp.float32),
            pltpu.SemaphoreType.DMA((length // min(16, length),)),
        ],
        compiler_params=pltpu.CompilerParams(vmem_limit_bytes=VMEM_LIMIT),
        name="pairs",
    )(table, near, far)


def on_device(orbitals, minus_table, points):
    kdevice, slab_size, channels = orbitals.shape
    half = lax.axis_index("half")
    groups = lax.axis_size("quarter") * lax.axis_size("inner")
    slabs = lax.axis_size("hi") * lax.axis_size("lo")
    total_k = 2 * groups * kdevice
    points = points.reshape(1, -1)
    place = jnp.stack([half, lax.axis_index("hi") * SPLIT + lax.axis_index("lo")])

    lo = lax.axis_index("lo")
    mine = lax.dynamic_index_in_dim(orbitals, lo, 0, keepdims=False)
    other = lax.dynamic_index_in_dim(orbitals, 1 - lo, 0, keepdims=False)
    share = make_front(mine, other, points, place)
    shares = [share] + [swap(share, False, x) for x in range(1, slabs)]
    shares, other = lax.optimization_barrier((shares, other))
    far = [swap(other if x & 1 else mine, True, x) for x in range(slabs)]

    def send(fields, around):
        fields = fields.reshape((-1,) + fields.shape[-3:])
        return lax.all_to_all(fields, around, split_axis=0, concat_axis=0, tiled=True)

    near_fields = make_near(orbitals, shares, groups)
    npoints = points.shape[1] // 2
    wanted = lax.dynamic_slice_in_dim(points[0], half * npoints, npoints)
    starts = jnp.stack([(place[1] ^ x) * slab_size for x in range(slabs)])
    rows = wanted[:, None] - starts[None, :]
    near_fields, rows = lax.optimization_barrier((near_fields, rows))
    far_fields = make_far(rows, far, place, groups)
    near_fields = send(near_fields, ("quarter", "inner"))
    near_fields, far_fields = lax.optimization_barrier((near_fields, far_fields))
    far_fields = send(far_fields, ("quarter", "inner", "lo"))

    def mirrored(kpoints):
        return total_k // 2 + (kpoints + total_k // 4) % (total_k // 2)

    turn = half * (total_k // 2)
    table = (jnp.roll(minus_table, -turn, axis=1) - turn) % total_k
    table = jnp.where(table < total_k // 2, table, mirrored(table))
    first, third, fourth = jnp.split(table, (total_k // 2, 3 * total_k // 4), axis=1)
    return make_pairs(near_fields, far_fields, jnp.concatenate([first, fourth, third], axis=1))


def solution(mesh):
    kplaces, slabs = mesh.shape["ka"], mesh.shape["ga"]
    devices = mesh.devices.reshape(2, 2, kplaces // 4, slabs // SPLIT, SPLIT)
    finer = Mesh(devices, KA + GA)
    return jax.shard_map(
        on_device,
        mesh=finer,
        in_specs=(P(KA, GA, None), P(), P()),
        out_specs=P(KA, None, None, GA),
        check_vma=False,
    )
```

```python
import functools
import math

import jax
import jax.numpy as jnp
from jax import lax
from jax.experimental import pallas as pl
from jax.experimental.pallas import tpu as pltpu
from jax.sharding import Mesh
from jax.sharding import PartitionSpec as P

VMEM_LIMIT = 40 * 1024 * 1024
SPLIT = 2
KA, GA = ("half", "quarter", "inner"), ("hi", "lo")


def swap(block, mirror, other):
    half, quarter, inner, hi, lo = (lax.axis_size(name) for name in KA + GA)
    slabs = hi * lo
    route = []
    for place in range(half * quarter * inner * slabs):
        kplace, slab = divmod(place, slabs)
        part, within = divmod(kplace, inner)
        part = half * quarter - 1 - part if mirror else part
        route.append((place, (part * inner + within) * slabs + (slab ^ other)))
    return lax.ppermute(block, KA + GA, route)


def one_hot(points_ref, half, slab, slab_size, npoints):
    first = pl.multiple_of(half * npoints, npoints)
    wanted = points_ref[:, pl.ds(first, npoints)] - slab * slab_size
    spot = lax.broadcasted_iota(jnp.int32, (slab_size, npoints), 0)
    return (spot == wanted).astype(jnp.float32).astype(jnp.bfloat16)


def pick(chosen, slab):
    return lax.dot_general(
        chosen, slab, (((0,), (0,)), ((), ())), preferred_element_type=jnp.float32
    )


def rotate(picked):
    middle = picked.shape[1] // 2
    return jnp.concatenate([-picked[:, middle:], picked[:, :middle]], axis=1)


def product(rows, slab, groups):
    out = lax.dot_general(
        rows, slab, (((1,), (1,)), ((), ())), preferred_element_type=jnp.float32
    )
    return out.reshape(groups, -1, out.shape[1]).astype(jnp.bfloat16)


def front_kernel(place_ref, points_ref, mine_ref, other_ref, picked_ref):
    slab_size, _ = mine_ref.shape
    _, npoints, _ = picked_ref.shape
    mine = place_ref[1] % SPLIT
    chosen = one_hot(points_ref, place_ref[0], place_ref[1], slab_size, npoints)
    for k, slab_ref in ((mine, mine_ref), (1 - mine, other_ref)):
        picked_ref[k] = pick(chosen, slab_ref[...]).astype(jnp.bfloat16)


def make_front(mine, other, points, place):
    vmem = pl.BlockSpec(memory_space=pltpu.VMEM)
    return pl.pallas_call(
        front_kernel,
        in_specs=[pl.BlockSpec(memory_space=pltpu.SMEM)] + [vmem] * 3,
        out_specs=vmem,
        out_shape=jax.ShapeDtypeStruct(
            (SPLIT, points.shape[1] // 2, mine.shape[1]), jnp.bfloat16
        ),
        compiler_params=pltpu.CompilerParams(vmem_limit_bytes=VMEM_LIMIT),
        name="front",
    )(place, points, mine, other)


def near_kernel(orbitals_ref, *refs):
    *picked_refs, out_ref = refs
    groups = out_ref.shape[0]
    rows = sum(picked_ref[0].astype(jnp.float32) for picked_ref in picked_refs)
    for part, turned in enumerate((rows, rotate(rows))):
        out_ref[:, 0, part] = product(turned.astype(jnp.bfloat16), orbitals_ref[0], groups)


def make_near(orbitals, shares, groups):
    kdevice, slab_size, channels = orbitals.shape
    npoints = shares[0].shape[1]
    length = npoints // groups
    return pl.pallas_call(
        near_kernel,
        grid=(kdevice,),
        in_specs=[pl.BlockSpec((1, slab_size, channels), lambda k: (k, 0, 0))]
        + [pl.BlockSpec((1, npoints, channels), lambda k: (k, 0, 0)) for _ in shares],
        out_specs=pl.BlockSpec((groups, 1, 2, length, slab_size), lambda k: (0, k, 0, 0, 0)),
        out_shape=jax.ShapeDtypeStruct((groups, kdevice, 2, length, slab_size), jnp.bfloat16),
        cost_estimate=pl.CostEstimate(
            flops=1_000_000_000, bytes_accessed=3_000_000, transcendentals=0
        ),
        compiler_params=pltpu.CompilerParams(vmem_limit_bytes=VMEM_LIMIT),
        name="near",
    )(orbitals, *shares)


def ahead_kernel(rows_ref, slab_ref, picked_ref, chosen_ref):
    npoints, slabs = rows_ref.shape
    spot = lax.broadcasted_iota(jnp.int32, (npoints, slab_ref.shape[0]), 1)
    for number in range(slabs):
        chosen = (rows_ref[:, number : number + 1] == spot).astype(jnp.float32)
        chosen = chosen.astype(jnp.bfloat16)
        if number:
            chosen_ref[number - 1] = chosen
        else:
            picked = jnp.dot(chosen, slab_ref[...], preferred_element_type=jnp.float32)
            picked_ref[...] = picked.astype(jnp.bfloat16)


def far_kernel(place_ref, picked_ref, chosen_ref, *refs):
    *slab_refs, out_ref, parts_ref, sems = refs
    groups, _, _, length, slab_size = out_ref.shape
    picked = picked_ref[...].astype(jnp.float32)
    for number, slab_ref in enumerate(slab_refs[1:]):
        picked += jnp.dot(chosen_ref[number], slab_ref[...], preferred_element_type=jnp.float32)
    turned = [rows.astype(jnp.bfloat16) for rows in (picked, rotate(picked))]
    copies = []
    for number in range(SPLIT):
        for part in range(2):
            place = len(copies)
            parts_ref[place] = product(turned[part], slab_refs[number][...], groups)
            target = out_ref.at[:, place_ref[1] % SPLIT ^ number, part]
            copies.append(pltpu.make_async_copy(parts_ref.at[place], target, sems.at[place]))
            copies[-1].start()
    for copy in copies:
        copy.wait()


def make_far(rows, slabs, place, groups):
    slab_size, channels = slabs[0].shape
    npoints, _ = rows.shape
    length = npoints // groups
    vmem = pl.BlockSpec(memory_space=pltpu.VMEM)
    picked, chosen = pl.pallas_call(
        ahead_kernel,
        in_specs=[vmem] * 2,
        out_specs=[vmem] * 2,
        out_shape=[
            jax.ShapeDtypeStruct((npoints, channels), jnp.bfloat16),
            jax.ShapeDtypeStruct((len(slabs) - 1, npoints, slab_size), jnp.bfloat16),
        ],
        cost_estimate=pl.CostEstimate(flops=1_000_000, bytes_accessed=3_000, transcendentals=0),
        compiler_params=pltpu.CompilerParams(vmem_limit_bytes=VMEM_LIMIT),
        name="ahead",
    )(rows, slabs[0])
    return pl.pallas_call(
        far_kernel,
        in_specs=[pl.BlockSpec(memory_space=pltpu.SMEM)] + [vmem] * (2 + len(slabs)),
        out_specs=pl.BlockSpec(memory_space=pl.ANY),
        out_shape=jax.ShapeDtypeStruct((groups, SPLIT, 2, length, slab_size), jnp.bfloat16),
        scratch_shapes=[
            pltpu.VMEM((2 * SPLIT, groups, length, slab_size), jnp.bfloat16),
            pltpu.SemaphoreType.DMA((2 * SPLIT,)),
        ],
        cost_estimate=pl.CostEstimate(
            flops=60_000_000_000, bytes_accessed=180_000_000, transcendentals=0
        ),
        compiler_params=pltpu.CompilerParams(vmem_limit_bytes=VMEM_LIMIT),
        name="far",
    )(place, picked, chosen, *slabs)


def pair_kernel(scale, table_ref, near_ref, far_ref, out_ref, held_ref, sums_ref, sems):
    total_k, _, length, width = held_ref.shape
    transfers = table_ref.shape[0]
    held_ref[: total_k // 2] = near_ref[...].astype(jnp.float32)
    held_ref[total_k // 2 :] = far_ref[...].astype(jnp.float32)

    count, columns = min(16, length), min(256, width)
    copies = []
    for start in range(0, length, count):
        rows = pl.ds(start, count)
        for column in range(0, width, columns):
            lanes = pl.ds(column, columns)

            def step(k, sums):
                real, imag = held_ref[k, 0, rows, lanes], held_ref[k, 1, rows, lanes]
                after = []
                for transfer in range(transfers):
                    other = table_ref[transfer, k]
                    other_real = held_ref[other, 0, rows, lanes]
                    other_imag = held_ref[other, 1, rows, lanes]
                    after.append(sums[2 * transfer] + (real * other_real + imag * other_imag))
                    after.append(sums[2 * transfer + 1] + (imag * other_real - real * other_imag))
                return tuple(after)

            zero = jnp.zeros((count, columns), jnp.float32)
            sums = lax.fori_loop(0, total_k, step, (zero,) * (2 * transfers), unroll=8)
            for place, value in enumerate(sums):
                sums_ref[rows, place // 2, place % 2, lanes] = value * scale
        copies.append(
            pltpu.make_async_copy(sums_ref.at[rows], out_ref.at[rows], sems.at[start // count])
        )
        copies[-1].start()
    for copy in copies:
        copy.wait()


def make_pairs(near, far, table):
    half_k, _, length, slab_size = near.shape
    transfers = table.shape[0]
    out = jax.ShapeDtypeStruct((length, transfers, 2, slab_size), jnp.float32)
    vmem = pl.BlockSpec(memory_space=pltpu.VMEM)
    return pl.pallas_call(
        functools.partial(pair_kernel, 1.0 / math.sqrt(2 * half_k)),
        in_specs=[pl.BlockSpec(memory_space=pltpu.SMEM), vmem, vmem],
        out_specs=pl.BlockSpec(memory_space=pl.ANY),
        out_shape=out,
        scratch_shapes=[
            pltpu.VMEM((2 * half_k, 2, length, slab_size), jnp.float32),
            pltpu.VMEM(out.shape, jnp.float32),
            pltpu.SemaphoreType.DMA((length // min(16, length),)),
        ],
        compiler_params=pltpu.CompilerParams(vmem_limit_bytes=VMEM_LIMIT),
        name="pairs",
    )(table, near, far)


def on_device(orbitals, minus_table, points):
    kdevice, slab_size, channels = orbitals.shape
    half = lax.axis_index("half")
    groups = lax.axis_size("quarter") * lax.axis_size("inner")
    slabs = lax.axis_size("hi") * lax.axis_size("lo")
    total_k = 2 * groups * kdevice
    points = points.reshape(1, -1)
    place = jnp.stack([half, lax.axis_index("hi") * SPLIT + lax.axis_index("lo")])

    lo = lax.axis_index("lo")
    mine = lax.dynamic_index_in_dim(orbitals, lo, 0, keepdims=False)
    other = lax.dynamic_index_in_dim(orbitals, 1 - lo, 0, keepdims=False)
    share = make_front(mine, other, points, place)
    share, mine, other = lax.optimization_barrier((share, mine, other))
    shares = [share] + [swap(share, False, x) for x in range(1, slabs)]
    far = [swap(other if x & 1 else mine, True, x) for x in range(slabs)]

    def send(fields, around):
        fields = fields.reshape((-1,) + fields.shape[-3:])
        return lax.all_to_all(fields, around, split_axis=0, concat_axis=0, tiled=True)

    near_fields = make_near(orbitals, shares, groups)
    npoints = points.shape[1] // 2
    wanted = lax.dynamic_slice_in_dim(points[0], half * npoints, npoints)
    starts = jnp.stack([(place[1] ^ x) * slab_size for x in range(slabs)])
    rows = wanted[:, None] - starts[None, :]
    near_fields, rows = lax.optimization_barrier((near_fields, rows))
    far_fields = make_far(rows, far, place, groups)
    near_fields = send(near_fields, ("quarter", "inner"))
    near_fields, far_fields = lax.optimization_barrier((near_fields, far_fields))
    far_fields = send(far_fields, ("quarter", "inner", "lo"))

    def mirrored(kpoints):
        return total_k // 2 + (kpoints + total_k // 4) % (total_k // 2)

    turn = half * (total_k // 2)
    table = (jnp.roll(minus_table, -turn, axis=1) - turn) % total_k
    table = jnp.where(table < total_k // 2, table, mirrored(table))
    first, third, fourth = jnp.split(table, (total_k // 2, 3 * total_k // 4), axis=1)
    return make_pairs(near_fields, far_fields, jnp.concatenate([first, fourth, third], axis=1))


def solution(mesh):
    kplaces, slabs = mesh.shape["ka"], mesh.shape["ga"]
    devices = mesh.devices.reshape(2, 2, kplaces // 4, slabs // SPLIT, SPLIT)
    finer = Mesh(devices, KA + GA)
    return jax.shard_map(
        on_device,
        mesh=finer,
        in_specs=(P(KA, GA, None), P(), P()),
        out_specs=P(KA, None, None, GA),
        check_vma=False,
    )
```

```python
import functools
import math

import jax
import jax.numpy as jnp
from jax import lax
from jax.experimental import pallas as pl
from jax.experimental.pallas import tpu as pltpu
from jax.sharding import Mesh
from jax.sharding import PartitionSpec as P

VMEM_LIMIT = 40 * 1024 * 1024
SPLIT = 2
KA, GA = ("half", "quarter", "inner"), ("hi", "lo")


def swap(block, mirror, other, senders=(0, 1)):
    half, quarter, inner, hi, lo = (lax.axis_size(name) for name in KA + GA)
    slabs = hi * lo
    route = []
    for place in range(half * quarter * inner * slabs):
        kplace, slab = divmod(place, slabs)
        part, within = divmod(kplace, inner)
        if part // quarter not in senders:
            continue
        part = half * quarter - 1 - part if mirror else part
        route.append((place, (part * inner + within) * slabs + (slab ^ other)))
    return lax.ppermute(block, KA + GA, route)


def one_hot(points_ref, half, slab, slab_size, npoints):
    first = pl.multiple_of(half * npoints, npoints)
    wanted = points_ref[:, pl.ds(first, npoints)] - slab * slab_size
    spot = lax.broadcasted_iota(jnp.int32, (slab_size, npoints), 0)
    return (spot == wanted).astype(jnp.float32).astype(jnp.bfloat16)


def pick(chosen, slab):
    return lax.dot_general(
        chosen, slab, (((0,), (0,)), ((), ())), preferred_element_type=jnp.float32
    )


def rotate(picked):
    middle = picked.shape[1] // 2
    return jnp.concatenate([-picked[:, middle:], picked[:, :middle]], axis=1)


def product(rows, slab, groups):
    out = lax.dot_general(
        rows, slab, (((1,), (1,)), ((), ())), preferred_element_type=jnp.float32
    )
    return out.reshape(groups, -1, out.shape[1]).astype(jnp.bfloat16)


def front_kernel(place_ref, points_ref, mine_ref, other_ref, picked_ref):
    slab_size, _ = mine_ref.shape
    _, npoints, _ = picked_ref.shape
    mine = place_ref[1] % SPLIT
    chosen = one_hot(points_ref, place_ref[0], place_ref[1], slab_size, npoints)
    for k, slab_ref in ((mine, mine_ref), (1 - mine, other_ref)):
        picked_ref[k] = pick(chosen, slab_ref[...]).astype(jnp.bfloat16)


def make_front(mine, other, points, place):
    vmem = pl.BlockSpec(memory_space=pltpu.VMEM)
    return pl.pallas_call(
        front_kernel,
        in_specs=[pl.BlockSpec(memory_space=pltpu.SMEM)] + [vmem] * 3,
        out_specs=vmem,
        out_shape=jax.ShapeDtypeStruct(
            (SPLIT, points.shape[1] // 2, mine.shape[1]), jnp.bfloat16
        ),
        compiler_params=pltpu.CompilerParams(vmem_limit_bytes=VMEM_LIMIT),
        name="front",
    )(place, points, mine, other)


def near_kernel(orbitals_ref, *refs):
    *picked_refs, out_ref = refs
    groups = out_ref.shape[0]
    rows = sum(picked_ref[0].astype(jnp.float32) for picked_ref in picked_refs)
    for part, turned in enumerate((rows, rotate(rows))):
        out_ref[:, 0, part] = product(turned.astype(jnp.bfloat16), orbitals_ref[0], groups)


def make_near(orbitals, shares, groups):
    kdevice, slab_size, channels = orbitals.shape
    npoints = shares[0].shape[1]
    length = npoints // groups
    return pl.pallas_call(
        near_kernel,
        grid=(kdevice,),
        in_specs=[pl.BlockSpec((1, slab_size, channels), lambda k: (k, 0, 0))]
        + [pl.BlockSpec((1, npoints, channels), lambda k: (k, 0, 0)) for _ in shares],
        out_specs=pl.BlockSpec((groups, 1, 2, length, slab_size), lambda k: (0, k, 0, 0, 0)),
        out_shape=jax.ShapeDtypeStruct((groups, kdevice, 2, length, slab_size), jnp.bfloat16),
        cost_estimate=pl.CostEstimate(
            flops=1_000_000_000, bytes_accessed=3_000_000, transcendentals=0
        ),
        compiler_params=pltpu.CompilerParams(vmem_limit_bytes=VMEM_LIMIT),
        name="near",
    )(orbitals, *shares)


def ahead_kernel(place_ref, rows_ref, *refs):
    *source_refs, slab_ref, picked_ref, chosen_ref = refs
    npoints, slabs = rows_ref.shape
    for half, source_ref in enumerate(source_refs):

        @pl.when(place_ref[0] == half)
        def _(source_ref=source_ref):
            slab_ref[...] = source_ref[...]

    spot = lax.broadcasted_iota(jnp.int32, (npoints, slab_ref.shape[0]), 1)
    for number in range(slabs):
        chosen = (rows_ref[:, number : number + 1] == spot).astype(jnp.float32)
        chosen = chosen.astype(jnp.bfloat16)
        if number:
            chosen_ref[number - 1] = chosen
        else:
            picked = jnp.dot(chosen, slab_ref[...], preferred_element_type=jnp.float32)
            picked_ref[...] = picked.astype(jnp.bfloat16)


def far_kernel(place_ref, picked_ref, chosen_ref, *refs):
    *slab_refs, out_ref, parts_ref, sems = refs
    groups, _, _, length, slab_size = out_ref.shape
    picked = picked_ref[...].astype(jnp.float32)
    for number, slab_ref in enumerate(slab_refs[1:]):
        picked += jnp.dot(chosen_ref[number], slab_ref[...], preferred_element_type=jnp.float32)
    turned = [rows.astype(jnp.bfloat16) for rows in (picked, rotate(picked))]
    copies = []
    for number in range(SPLIT):
        for part in range(2):
            place = len(copies)
            parts_ref[place] = product(turned[part], slab_refs[number][...], groups)
            target = out_ref.at[:, place_ref[1] % SPLIT ^ number, part]
            copies.append(pltpu.make_async_copy(parts_ref.at[place], target, sems.at[place]))
            copies[-1].start()
    for copy in copies:
        copy.wait()


def make_far(rows, firsts, slabs, place, groups):
    slab_size, channels = slabs[0].shape
    npoints, _ = rows.shape
    length = npoints // groups
    vmem = pl.BlockSpec(memory_space=pltpu.VMEM)
    first, picked, chosen = pl.pallas_call(
        ahead_kernel,
        in_specs=[pl.BlockSpec(memory_space=pltpu.SMEM)] + [vmem] * 3,
        out_specs=[vmem] * 3,
        out_shape=[
            jax.ShapeDtypeStruct((slab_size, channels), jnp.bfloat16),
            jax.ShapeDtypeStruct((npoints, channels), jnp.bfloat16),
            jax.ShapeDtypeStruct((len(slabs), npoints, slab_size), jnp.bfloat16),
        ],
        cost_estimate=pl.CostEstimate(flops=1_000_000, bytes_accessed=3_000, transcendentals=0),
        compiler_params=pltpu.CompilerParams(vmem_limit_bytes=VMEM_LIMIT),
        name="ahead",
    )(place, rows, *firsts)
    return pl.pallas_call(
        far_kernel,
        in_specs=[pl.BlockSpec(memory_space=pltpu.SMEM)] + [vmem] * (3 + len(slabs)),
        out_specs=pl.BlockSpec(memory_space=pl.ANY),
        out_shape=jax.ShapeDtypeStruct((groups, SPLIT, 2, length, slab_size), jnp.bfloat16),
        scratch_shapes=[
            pltpu.VMEM((2 * SPLIT, groups, length, slab_size), jnp.bfloat16),
            pltpu.SemaphoreType.DMA((2 * SPLIT,)),
        ],
        cost_estimate=pl.CostEstimate(
            flops=60_000_000_000, bytes_accessed=180_000_000, transcendentals=0
        ),
        compiler_params=pltpu.CompilerParams(vmem_limit_bytes=VMEM_LIMIT),
        name="far",
    )(place, picked, chosen, first, *slabs)


def pair_kernel(scale, table_ref, near_ref, far_ref, out_ref, held_ref, sums_ref, sems):
    total_k, _, length, width = held_ref.shape
    transfers = table_ref.shape[0]
    held_ref[: total_k // 2] = near_ref[...].astype(jnp.float32)
    held_ref[total_k // 2 :] = far_ref[...].astype(jnp.float32)

    count, columns = min(16, length), min(256, width)
    copies = []
    for start in range(0, length, count):
        rows = pl.ds(start, count)
        for column in range(0, width, columns):
            lanes = pl.ds(column, columns)

            def step(k, sums):
                real, imag = held_ref[k, 0, rows, lanes], held_ref[k, 1, rows, lanes]
                after = []
                for transfer in range(transfers):
                    other = table_ref[transfer, k]
                    other_real = held_ref[other, 0, rows, lanes]
                    other_imag = held_ref[other, 1, rows, lanes]
                    after.append(sums[2 * transfer] + (real * other_real + imag * other_imag))
                    after.append(sums[2 * transfer + 1] + (imag * other_real - real * other_imag))
                return tuple(after)

            zero = jnp.zeros((count, columns), jnp.float32)
            sums = lax.fori_loop(0, total_k, step, (zero,) * (2 * transfers), unroll=8)
            for place, value in enumerate(sums):
                sums_ref[rows, place // 2, place % 2, lanes] = value * scale
        copies.append(
            pltpu.make_async_copy(sums_ref.at[rows], out_ref.at[rows], sems.at[start // count])
        )
        copies[-1].start()
    for copy in copies:
        copy.wait()


def make_pairs(near, far, table):
    half_k, _, length, slab_size = near.shape
    transfers = table.shape[0]
    out = jax.ShapeDtypeStruct((length, transfers, 2, slab_size), jnp.float32)
    vmem = pl.BlockSpec(memory_space=pltpu.VMEM)
    return pl.pallas_call(
        functools.partial(pair_kernel, 1.0 / math.sqrt(2 * half_k)),
        in_specs=[pl.BlockSpec(memory_space=pltpu.SMEM), vmem, vmem],
        out_specs=pl.BlockSpec(memory_space=pl.ANY),
        out_shape=out,
        scratch_shapes=[
            pltpu.VMEM((2 * half_k, 2, length, slab_size), jnp.float32),
            pltpu.VMEM(out.shape, jnp.float32),
            pltpu.SemaphoreType.DMA((length // min(16, length),)),
        ],
        compiler_params=pltpu.CompilerParams(vmem_limit_bytes=VMEM_LIMIT),
        name="pairs",
    )(table, near, far)


def on_device(orbitals, minus_table, points):
    kdevice, slab_size, channels = orbitals.shape
    half = lax.axis_index("half")
    groups = lax.axis_size("quarter") * lax.axis_size("inner")
    slabs = lax.axis_size("hi") * lax.axis_size("lo")
    total_k = 2 * groups * kdevice
    points = points.reshape(1, -1)
    place = jnp.stack([half, lax.axis_index("hi") * SPLIT + lax.axis_index("lo")])

    lo = lax.axis_index("lo")
    mine = lax.dynamic_index_in_dim(orbitals, lo, 0, keepdims=False)
    other = lax.dynamic_index_in_dim(orbitals, 1 - lo, 0, keepdims=False)
    firsts = [swap(mine, True, 0, (1,))]
    share = make_front(mine, other, points, place)
    share, mine, other = lax.optimization_barrier((share, mine, other))
    shares = [share] + [swap(share, False, x) for x in range(1, slabs)]
    firsts.append(swap(mine, True, 0, (0,)))
    far = [swap(other if x & 1 else mine, True, x) for x in range(1, slabs)]

    def send(fields, around):
        fields = fields.reshape((-1,) + fields.shape[-3:])
        return lax.all_to_all(fields, around, split_axis=0, concat_axis=0, tiled=True)

    near_fields = make_near(orbitals, shares, groups)
    npoints = points.shape[1] // 2
    wanted = lax.dynamic_slice_in_dim(points[0], half * npoints, npoints)
    starts = jnp.stack([(place[1] ^ x) * slab_size for x in range(slabs)])
    rows = wanted[:, None] - starts[None, :]
    near_fields, rows = lax.optimization_barrier((near_fields, rows))
    far_fields = make_far(rows, firsts, far, place, groups)
    near_fields = send(near_fields, ("quarter", "inner"))
    near_fields, far_fields = lax.optimization_barrier((near_fields, far_fields))
    far_fields = send(far_fields, ("quarter", "inner", "lo"))

    def mirrored(kpoints):
        return total_k // 2 + (kpoints + total_k // 4) % (total_k // 2)

    turn = half * (total_k // 2)
    table = (jnp.roll(minus_table, -turn, axis=1) - turn) % total_k
    table = jnp.where(table < total_k // 2, table, mirrored(table))
    first, third, fourth = jnp.split(table, (total_k // 2, 3 * total_k // 4), axis=1)
    return make_pairs(near_fields, far_fields, jnp.concatenate([first, fourth, third], axis=1))


def solution(mesh):
    kplaces, slabs = mesh.shape["ka"], mesh.shape["ga"]
    devices = mesh.devices.reshape(2, 2, kplaces // 4, slabs // SPLIT, SPLIT)
    finer = Mesh(devices, KA + GA)
    return jax.shard_map(
        on_device,
        mesh=finer,
        in_specs=(P(KA, GA, None), P(), P()),
        out_specs=P(KA, None, None, GA),
        check_vma=False,
    )
```

```python
import functools
import math

import jax
import jax.numpy as jnp
from jax import lax
from jax.experimental import pallas as pl
from jax.experimental.pallas import tpu as pltpu
from jax.sharding import Mesh
from jax.sharding import PartitionSpec as P

VMEM_LIMIT = 40 * 1024 * 1024
SPLIT = 2
KA, GA = ("half", "quarter", "inner"), ("hi", "lo")


def swap(block, mirror, other):
    half, quarter, inner, hi, lo = (lax.axis_size(name) for name in KA + GA)
    slabs = hi * lo
    route = []
    for place in range(half * quarter * inner * slabs):
        kplace, slab = divmod(place, slabs)
        part, within = divmod(kplace, inner)
        part = half * quarter - 1 - part if mirror else part
        route.append((place, (part * inner + within) * slabs + (slab ^ other)))
    return lax.ppermute(block, KA + GA, route)


def one_hot(points_ref, half, slab, slab_size, npoints):
    first = pl.multiple_of(half * npoints, npoints)
    wanted = points_ref[:, pl.ds(first, npoints)] - slab * slab_size
    spot = lax.broadcasted_iota(jnp.int32, (slab_size, npoints), 0)
    return (spot == wanted).astype(jnp.float32).astype(jnp.bfloat16)


def pick(chosen, slab):
    return lax.dot_general(
        chosen, slab, (((0,), (0,)), ((), ())), preferred_element_type=jnp.float32
    )


def crossed(member, groups):
    quarter, inner = divmod(member, groups // 2)
    return inner * 2 + quarter


def rotate(picked):
    middle = picked.shape[1] // 2
    return jnp.concatenate([-picked[:, middle:], picked[:, :middle]], axis=1)


def product(rows, slab, groups):
    out = lax.dot_general(
        rows, slab, (((1,), (1,)), ((), ())), preferred_element_type=jnp.float32
    )
    return out.reshape(groups, -1, out.shape[1]).astype(jnp.bfloat16)


def front_kernel(place_ref, points_ref, mine_ref, other_ref, picked_ref):
    slab_size, _ = mine_ref.shape
    _, npoints, _ = picked_ref.shape
    mine = place_ref[1] % SPLIT
    chosen = one_hot(points_ref, place_ref[0], place_ref[1], slab_size, npoints)
    for k, slab_ref in ((mine, mine_ref), (1 - mine, other_ref)):
        picked_ref[k] = pick(chosen, slab_ref[...]).astype(jnp.bfloat16)


def make_front(mine, other, points, place):
    vmem = pl.BlockSpec(memory_space=pltpu.VMEM)
    return pl.pallas_call(
        front_kernel,
        in_specs=[pl.BlockSpec(memory_space=pltpu.SMEM)] + [vmem] * 3,
        out_specs=vmem,
        out_shape=jax.ShapeDtypeStruct(
            (SPLIT, points.shape[1] // 2, mine.shape[1]), jnp.bfloat16
        ),
        compiler_params=pltpu.CompilerParams(vmem_limit_bytes=VMEM_LIMIT),
        name="front",
    )(place, points, mine, other)


def near_kernel(orbitals_ref, *refs):
    *picked_refs, out_ref = refs
    groups = out_ref.shape[0]
    rows = sum(picked_ref[0].astype(jnp.float32) for picked_ref in picked_refs)
    for part, turned in enumerate((rows, rotate(rows))):
        pieces = product(turned.astype(jnp.bfloat16), orbitals_ref[0], groups)
        for member in range(groups):
            out_ref[crossed(member, groups), 0, part] = pieces[member]


def make_near(orbitals, shares, groups):
    kdevice, slab_size, channels = orbitals.shape
    npoints = shares[0].shape[1]
    length = npoints // groups
    return pl.pallas_call(
        near_kernel,
        grid=(kdevice,),
        in_specs=[pl.BlockSpec((1, slab_size, channels), lambda k: (k, 0, 0))]
        + [pl.BlockSpec((1, npoints, channels), lambda k: (k, 0, 0)) for _ in shares],
        out_specs=pl.BlockSpec((groups, 1, 2, length, slab_size), lambda k: (0, k, 0, 0, 0)),
        out_shape=jax.ShapeDtypeStruct((groups, kdevice, 2, length, slab_size), jnp.bfloat16),
        cost_estimate=pl.CostEstimate(
            flops=1_000_000_000, bytes_accessed=3_000_000, transcendentals=0
        ),
        compiler_params=pltpu.CompilerParams(vmem_limit_bytes=VMEM_LIMIT),
        name="near",
    )(orbitals, *shares)


def ahead_kernel(rows_ref, slab_ref, picked_ref, chosen_ref):
    npoints, slabs = rows_ref.shape
    spot = lax.broadcasted_iota(jnp.int32, (npoints, slab_ref.shape[0]), 1)
    for number in range(slabs):
        chosen = (rows_ref[:, number : number + 1] == spot).astype(jnp.float32)
        chosen = chosen.astype(jnp.bfloat16)
        if number:
            chosen_ref[number - 1] = chosen
        else:
            picked = jnp.dot(chosen, slab_ref[...], preferred_element_type=jnp.float32)
            picked_ref[...] = picked.astype(jnp.bfloat16)


def far_kernel(place_ref, picked_ref, chosen_ref, *refs):
    *slab_refs, out_ref, parts_ref, sems = refs
    _, groups, _, length, slab_size = out_ref.shape
    picked = picked_ref[...].astype(jnp.float32)
    for number, slab_ref in enumerate(slab_refs[1:]):
        picked += jnp.dot(chosen_ref[number], slab_ref[...], preferred_element_type=jnp.float32)
    turned = [rows.astype(jnp.bfloat16) for rows in (picked, rotate(picked))]
    copies = []
    for number in range(SPLIT):
        for part in range(2):
            place = len(copies)
            parts_ref[place] = product(turned[part], slab_refs[number][...], groups)
            target = out_ref.at[place_ref[1] % SPLIT ^ number, :, part]
            copies.append(pltpu.make_async_copy(parts_ref.at[place], target, sems.at[place]))
            copies[-1].start()
    for copy in copies:
        copy.wait()


def make_far(rows, slabs, place, groups):
    slab_size, channels = slabs[0].shape
    npoints, _ = rows.shape
    length = npoints // groups
    vmem = pl.BlockSpec(memory_space=pltpu.VMEM)
    picked, chosen = pl.pallas_call(
        ahead_kernel,
        in_specs=[vmem] * 2,
        out_specs=[vmem] * 2,
        out_shape=[
            jax.ShapeDtypeStruct((npoints, channels), jnp.bfloat16),
            jax.ShapeDtypeStruct((len(slabs) - 1, npoints, slab_size), jnp.bfloat16),
        ],
        cost_estimate=pl.CostEstimate(flops=1_000_000, bytes_accessed=3_000, transcendentals=0),
        compiler_params=pltpu.CompilerParams(vmem_limit_bytes=VMEM_LIMIT),
        name="ahead",
    )(rows, slabs[0])
    return pl.pallas_call(
        far_kernel,
        in_specs=[pl.BlockSpec(memory_space=pltpu.SMEM)] + [vmem] * (2 + len(slabs)),
        out_specs=pl.BlockSpec(memory_space=pl.ANY),
        out_shape=jax.ShapeDtypeStruct((SPLIT, groups, 2, length, slab_size), jnp.bfloat16),
        scratch_shapes=[
            pltpu.VMEM((2 * SPLIT, groups, length, slab_size), jnp.bfloat16),
            pltpu.SemaphoreType.DMA((2 * SPLIT,)),
        ],
        cost_estimate=pl.CostEstimate(
            flops=60_000_000_000, bytes_accessed=180_000_000, transcendentals=0
        ),
        compiler_params=pltpu.CompilerParams(vmem_limit_bytes=VMEM_LIMIT),
        name="far",
    )(place, picked, chosen, *slabs)


def pair_kernel(scale, table_ref, near_ref, far_ref, out_ref, held_ref, sums_ref, sems):
    total_k, _, length, width = held_ref.shape
    transfers = table_ref.shape[0]
    groups = near_ref.shape[0] // SPLIT
    for member in range(groups):
        place = crossed(member, groups) * SPLIT
        for k in range(SPLIT):
            held_ref[member * SPLIT + k] = near_ref[place + k].astype(jnp.float32)
            far = far_ref[k * groups + member]
            held_ref[total_k // 2 + member * SPLIT + k] = far.astype(jnp.float32)

    count, columns = min(16, length), min(256, width)
    copies = []
    for start in range(0, length, count):
        rows = pl.ds(start, count)
        for column in range(0, width, columns):
            lanes = pl.ds(column, columns)

            def step(k, sums):
                real, imag = held_ref[k, 0, rows, lanes], held_ref[k, 1, rows, lanes]
                after = []
                for transfer in range(transfers):
                    other = table_ref[transfer, k]
                    other_real = held_ref[other, 0, rows, lanes]
                    other_imag = held_ref[other, 1, rows, lanes]
                    after.append(sums[2 * transfer] + (real * other_real + imag * other_imag))
                    after.append(sums[2 * transfer + 1] + (imag * other_real - real * other_imag))
                return tuple(after)

            zero = jnp.zeros((count, columns), jnp.float32)
            sums = lax.fori_loop(0, total_k, step, (zero,) * (2 * transfers), unroll=8)
            for place, value in enumerate(sums):
                sums_ref[rows, place // 2, place % 2, lanes] = value * scale
        copies.append(
            pltpu.make_async_copy(sums_ref.at[rows], out_ref.at[rows], sems.at[start // count])
        )
        copies[-1].start()
    for copy in copies:
        copy.wait()


def make_pairs(near, far, table):
    half_k, _, length, slab_size = near.shape
    transfers = table.shape[0]
    out = jax.ShapeDtypeStruct((length, transfers, 2, slab_size), jnp.float32)
    vmem = pl.BlockSpec(memory_space=pltpu.VMEM)
    return pl.pallas_call(
        functools.partial(pair_kernel, 1.0 / math.sqrt(2 * half_k)),
        in_specs=[pl.BlockSpec(memory_space=pltpu.SMEM), vmem, vmem],
        out_specs=pl.BlockSpec(memory_space=pl.ANY),
        out_shape=out,
        scratch_shapes=[
            pltpu.VMEM((2 * half_k, 2, length, slab_size), jnp.float32),
            pltpu.VMEM(out.shape, jnp.float32),
            pltpu.SemaphoreType.DMA((length // min(16, length),)),
        ],
        compiler_params=pltpu.CompilerParams(vmem_limit_bytes=VMEM_LIMIT),
        name="pairs",
    )(table, near, far)


def on_device(orbitals, minus_table, points):
    kdevice, slab_size, channels = orbitals.shape
    half = lax.axis_index("half")
    groups = lax.axis_size("quarter") * lax.axis_size("inner")
    slabs = lax.axis_size("hi") * lax.axis_size("lo")
    total_k = 2 * groups * kdevice
    points = points.reshape(1, -1)
    place = jnp.stack([half, lax.axis_index("hi") * SPLIT + lax.axis_index("lo")])

    lo = lax.axis_index("lo")
    mine = lax.dynamic_index_in_dim(orbitals, lo, 0, keepdims=False)
    other = lax.dynamic_index_in_dim(orbitals, 1 - lo, 0, keepdims=False)
    share = make_front(mine, other, points, place)
    share, mine, other = lax.optimization_barrier((share, mine, other))
    shares = [share] + [swap(share, False, x) for x in range(1, slabs)]
    far = [swap(other if x & 1 else mine, True, x) for x in range(slabs)]

    def send(fields, around):
        fields = fields.reshape((-1,) + fields.shape[-3:])
        return lax.all_to_all(fields, around, split_axis=0, concat_axis=0, tiled=True)

    near_fields = make_near(orbitals, shares, groups)
    npoints = points.shape[1] // 2
    wanted = lax.dynamic_slice_in_dim(points[0], half * npoints, npoints)
    starts = jnp.stack([(place[1] ^ x) * slab_size for x in range(slabs)])
    rows = wanted[:, None] - starts[None, :]
    near_fields, rows = lax.optimization_barrier((near_fields, rows))
    far_fields = make_far(rows, far, place, groups)
    near_fields = send(near_fields, ("inner", "quarter"))
    near_fields, far_fields = lax.optimization_barrier((near_fields, far_fields))
    far_fields = send(far_fields, ("lo", "quarter", "inner"))

    def mirrored(kpoints):
        return total_k // 2 + (kpoints + total_k // 4) % (total_k // 2)

    turn = half * (total_k // 2)
    table = (jnp.roll(minus_table, -turn, axis=1) - turn) % total_k
    table = jnp.where(table < total_k // 2, table, mirrored(table))
    first, third, fourth = jnp.split(table, (total_k // 2, 3 * total_k // 4), axis=1)
    return make_pairs(near_fields, far_fields, jnp.concatenate([first, fourth, third], axis=1))


def solution(mesh):
    kplaces, slabs = mesh.shape["ka"], mesh.shape["ga"]
    devices = mesh.devices.reshape(2, 2, kplaces // 4, slabs // SPLIT, SPLIT)
    finer = Mesh(devices, KA + GA)
    return jax.shard_map(
        on_device,
        mesh=finer,
        in_specs=(P(KA, GA, None), P(), P()),
        out_specs=P(KA, None, None, GA),
        check_vma=False,
    )
```

```python
import functools
import math

import jax
import jax.numpy as jnp
from jax import lax
from jax.experimental import pallas as pl
from jax.experimental.pallas import tpu as pltpu
from jax.sharding import Mesh
from jax.sharding import PartitionSpec as P

VMEM_LIMIT = 40 * 1024 * 1024
SPLIT = 2
KA, GA = ("half", "quarter", "inner"), ("hi", "lo")


def swap(block, mirror, other):
    half, quarter, inner, hi, lo = (lax.axis_size(name) for name in KA + GA)
    slabs = hi * lo
    route = []
    for place in range(half * quarter * inner * slabs):
        kplace, slab = divmod(place, slabs)
        part, within = divmod(kplace, inner)
        part = half * quarter - 1 - part if mirror else part
        route.append((place, (part * inner + within) * slabs + (slab ^ other)))
    return lax.ppermute(block, KA + GA, route)


def one_hot(points_ref, half, slab, slab_size, npoints):
    first = pl.multiple_of(half * npoints, npoints)
    wanted = points_ref[:, pl.ds(first, npoints)] - slab * slab_size
    spot = lax.broadcasted_iota(jnp.int32, (slab_size, npoints), 0)
    return (spot == wanted).astype(jnp.float32).astype(jnp.bfloat16)


def pick(chosen, slab):
    return lax.dot_general(
        chosen, slab, (((0,), (0,)), ((), ())), preferred_element_type=jnp.float32
    )


def crossed(member, groups):
    quarter, inner = divmod(member, groups // 2)
    return inner * 2 + quarter


def far_place(member, lo, groups):
    return lo * groups + crossed(member, groups)


def rotate(picked):
    middle = picked.shape[1] // 2
    return jnp.concatenate([-picked[:, middle:], picked[:, :middle]], axis=1)


def product(rows, slab, groups):
    out = lax.dot_general(
        rows, slab, (((1,), (1,)), ((), ())), preferred_element_type=jnp.float32
    )
    return out.reshape(groups, -1, out.shape[1]).astype(jnp.bfloat16)


def front_kernel(place_ref, points_ref, mine_ref, other_ref, picked_ref):
    slab_size, _ = mine_ref.shape
    _, npoints, _ = picked_ref.shape
    mine = place_ref[1] % SPLIT
    chosen = one_hot(points_ref, place_ref[0], place_ref[1], slab_size, npoints)
    for k, slab_ref in ((mine, mine_ref), (1 - mine, other_ref)):
        picked_ref[k] = pick(chosen, slab_ref[...]).astype(jnp.bfloat16)


def make_front(mine, other, points, place):
    vmem = pl.BlockSpec(memory_space=pltpu.VMEM)
    return pl.pallas_call(
        front_kernel,
        in_specs=[pl.BlockSpec(memory_space=pltpu.SMEM)] + [vmem] * 3,
        out_specs=vmem,
        out_shape=jax.ShapeDtypeStruct(
            (SPLIT, points.shape[1] // 2, mine.shape[1]), jnp.bfloat16
        ),
        compiler_params=pltpu.CompilerParams(vmem_limit_bytes=VMEM_LIMIT),
        name="front",
    )(place, points, mine, other)


def near_kernel(orbitals_ref, *refs):
    *picked_refs, out_ref = refs
    groups = out_ref.shape[0]
    rows = sum(picked_ref[0].astype(jnp.float32) for picked_ref in picked_refs)
    for part, turned in enumerate((rows, rotate(rows))):
        out_ref[:, 0, part] = product(turned.astype(jnp.bfloat16), orbitals_ref[0], groups)


def make_near(orbitals, shares, groups):
    kdevice, slab_size, channels = orbitals.shape
    npoints = shares[0].shape[1]
    length = npoints // groups
    return pl.pallas_call(
        near_kernel,
        grid=(kdevice,),
        in_specs=[pl.BlockSpec((1, slab_size, channels), lambda k: (k, 0, 0))]
        + [pl.BlockSpec((1, npoints, channels), lambda k: (k, 0, 0)) for _ in shares],
        out_specs=pl.BlockSpec((groups, 1, 2, length, slab_size), lambda k: (0, k, 0, 0, 0)),
        out_shape=jax.ShapeDtypeStruct((groups, kdevice, 2, length, slab_size), jnp.bfloat16),
        cost_estimate=pl.CostEstimate(
            flops=1_000_000_000, bytes_accessed=3_000_000, transcendentals=0
        ),
        compiler_params=pltpu.CompilerParams(vmem_limit_bytes=VMEM_LIMIT),
        name="near",
    )(orbitals, *shares)


def ahead_kernel(rows_ref, slab_ref, picked_ref, chosen_ref):
    npoints, slabs = rows_ref.shape
    spot = lax.broadcasted_iota(jnp.int32, (npoints, slab_ref.shape[0]), 1)
    for number in range(slabs):
        chosen = (rows_ref[:, number : number + 1] == spot).astype(jnp.float32)
        chosen = chosen.astype(jnp.bfloat16)
        if number:
            chosen_ref[number - 1] = chosen
        else:
            picked = jnp.dot(chosen, slab_ref[...], preferred_element_type=jnp.float32)
            picked_ref[...] = picked.astype(jnp.bfloat16)


def far_kernel(place_ref, picked_ref, chosen_ref, *refs):
    *slab_refs, out_ref, parts_ref, sems = refs
    _, groups, _, length, slab_size = out_ref.shape
    picked = picked_ref[...].astype(jnp.float32)
    for number, slab_ref in enumerate(slab_refs[1:]):
        picked += jnp.dot(chosen_ref[number], slab_ref[...], preferred_element_type=jnp.float32)
    turned = [rows.astype(jnp.bfloat16) for rows in (picked, rotate(picked))]
    copies = []
    for number in range(SPLIT):
        for part in range(2):
            place = len(copies)
            pieces = product(turned[part], slab_refs[number][...], groups)
            for member in range(groups):
                parts_ref[place, crossed(member, groups)] = pieces[member]
            target = out_ref.at[place_ref[1] % SPLIT ^ number, :, part]
            copies.append(pltpu.make_async_copy(parts_ref.at[place], target, sems.at[place]))
            copies[-1].start()
    for copy in copies:
        copy.wait()


def make_far(rows, slabs, place, groups):
    slab_size, channels = slabs[0].shape
    npoints, _ = rows.shape
    length = npoints // groups
    vmem = pl.BlockSpec(memory_space=pltpu.VMEM)
    picked, chosen = pl.pallas_call(
        ahead_kernel,
        in_specs=[vmem] * 2,
        out_specs=[vmem] * 2,
        out_shape=[
            jax.ShapeDtypeStruct((npoints, channels), jnp.bfloat16),
            jax.ShapeDtypeStruct((len(slabs) - 1, npoints, slab_size), jnp.bfloat16),
        ],
        cost_estimate=pl.CostEstimate(flops=1_000_000, bytes_accessed=3_000, transcendentals=0),
        compiler_params=pltpu.CompilerParams(vmem_limit_bytes=VMEM_LIMIT),
        name="ahead",
    )(rows, slabs[0])
    return pl.pallas_call(
        far_kernel,
        in_specs=[pl.BlockSpec(memory_space=pltpu.SMEM)] + [vmem] * (2 + len(slabs)),
        out_specs=pl.BlockSpec(memory_space=pl.ANY),
        out_shape=jax.ShapeDtypeStruct((SPLIT, groups, 2, length, slab_size), jnp.bfloat16),
        scratch_shapes=[
            pltpu.VMEM((2 * SPLIT, groups, length, slab_size), jnp.bfloat16),
            pltpu.SemaphoreType.DMA((2 * SPLIT,)),
        ],
        cost_estimate=pl.CostEstimate(
            flops=60_000_000_000, bytes_accessed=180_000_000, transcendentals=0
        ),
        compiler_params=pltpu.CompilerParams(vmem_limit_bytes=VMEM_LIMIT),
        name="far",
    )(place, picked, chosen, *slabs)


def pair_kernel(scale, table_ref, near_ref, far_ref, out_ref, held_ref, sums_ref, sems):
    total_k, _, length, width = held_ref.shape
    transfers = table_ref.shape[0]
    groups = near_ref.shape[0] // SPLIT
    held_ref[: total_k // 2] = near_ref[...].astype(jnp.float32)
    for member in range(groups):
        for k in range(SPLIT):
            far = far_ref[far_place(member, k, groups)]
            held_ref[total_k // 2 + member * SPLIT + k] = far.astype(jnp.float32)

    count, columns = min(16, length), min(256, width)
    copies = []
    for start in range(0, length, count):
        rows = pl.ds(start, count)
        for column in range(0, width, columns):
            lanes = pl.ds(column, columns)

            def step(k, sums):
                real, imag = held_ref[k, 0, rows, lanes], held_ref[k, 1, rows, lanes]
                after = []
                for transfer in range(transfers):
                    other = table_ref[transfer, k]
                    other_real = held_ref[other, 0, rows, lanes]
                    other_imag = held_ref[other, 1, rows, lanes]
                    after.append(sums[2 * transfer] + (real * other_real + imag * other_imag))
                    after.append(sums[2 * transfer + 1] + (imag * other_real - real * other_imag))
                return tuple(after)

            zero = jnp.zeros((count, columns), jnp.float32)
            sums = lax.fori_loop(0, total_k, step, (zero,) * (2 * transfers), unroll=8)
            for place, value in enumerate(sums):
                sums_ref[rows, place // 2, place % 2, lanes] = value * scale
        copies.append(
            pltpu.make_async_copy(sums_ref.at[rows], out_ref.at[rows], sems.at[start // count])
        )
        copies[-1].start()
    for copy in copies:
        copy.wait()


def make_pairs(near, far, table):
    half_k, _, length, slab_size = near.shape
    transfers = table.shape[0]
    out = jax.ShapeDtypeStruct((length, transfers, 2, slab_size), jnp.float32)
    vmem = pl.BlockSpec(memory_space=pltpu.VMEM)
    return pl.pallas_call(
        functools.partial(pair_kernel, 1.0 / math.sqrt(2 * half_k)),
        in_specs=[pl.BlockSpec(memory_space=pltpu.SMEM), vmem, vmem],
        out_specs=pl.BlockSpec(memory_space=pl.ANY),
        out_shape=out,
        scratch_shapes=[
            pltpu.VMEM((2 * half_k, 2, length, slab_size), jnp.float32),
            pltpu.VMEM(out.shape, jnp.float32),
            pltpu.SemaphoreType.DMA((length // min(16, length),)),
        ],
        compiler_params=pltpu.CompilerParams(vmem_limit_bytes=VMEM_LIMIT),
        name="pairs",
    )(table, near, far)


def on_device(orbitals, minus_table, points):
    kdevice, slab_size, channels = orbitals.shape
    half = lax.axis_index("half")
    groups = lax.axis_size("quarter") * lax.axis_size("inner")
    slabs = lax.axis_size("hi") * lax.axis_size("lo")
    total_k = 2 * groups * kdevice
    points = points.reshape(1, -1)
    place = jnp.stack([half, lax.axis_index("hi") * SPLIT + lax.axis_index("lo")])

    lo = lax.axis_index("lo")
    mine = lax.dynamic_index_in_dim(orbitals, lo, 0, keepdims=False)
    other = lax.dynamic_index_in_dim(orbitals, 1 - lo, 0, keepdims=False)
    share = make_front(mine, other, points, place)
    share, mine, other = lax.optimization_barrier((share, mine, other))
    shares = [share] + [swap(share, False, x) for x in range(1, slabs)]
    far = [swap(other if x & 1 else mine, True, x) for x in range(slabs)]

    def send(fields, around):
        fields = fields.reshape((-1,) + fields.shape[-3:])
        return lax.all_to_all(fields, around, split_axis=0, concat_axis=0, tiled=True)

    near_fields = make_near(orbitals, shares, groups)
    npoints = points.shape[1] // 2
    wanted = lax.dynamic_slice_in_dim(points[0], half * npoints, npoints)
    starts = jnp.stack([(place[1] ^ x) * slab_size for x in range(slabs)])
    rows = wanted[:, None] - starts[None, :]
    near_fields, rows = lax.optimization_barrier((near_fields, rows))
    far_fields = make_far(rows, far, place, groups)
    near_fields = send(near_fields, ("quarter", "inner"))
    near_fields, far_fields = lax.optimization_barrier((near_fields, far_fields))
    far_fields = send(far_fields, ("lo", "inner", "quarter"))

    def mirrored(kpoints):
        return total_k // 2 + (kpoints + total_k // 4) % (total_k // 2)

    turn = half * (total_k // 2)
    table = (jnp.roll(minus_table, -turn, axis=1) - turn) % total_k
    table = jnp.where(table < total_k // 2, table, mirrored(table))
    first, third, fourth = jnp.split(table, (total_k // 2, 3 * total_k // 4), axis=1)
    return make_pairs(near_fields, far_fields, jnp.concatenate([first, fourth, third], axis=1))


def solution(mesh):
    kplaces, slabs = mesh.shape["ka"], mesh.shape["ga"]
    devices = mesh.devices.reshape(2, 2, kplaces // 4, slabs // SPLIT, SPLIT)
    finer = Mesh(devices, KA + GA)
    return jax.shard_map(
        on_device,
        mesh=finer,
        in_specs=(P(KA, GA, None), P(), P()),
        out_specs=P(KA, None, None, GA),
        check_vma=False,
    )
```

```python
import functools
import math

import jax
import jax.numpy as jnp
from jax import lax
from jax.experimental import pallas as pl
from jax.experimental.pallas import tpu as pltpu
from jax.sharding import Mesh
from jax.sharding import PartitionSpec as P

VMEM_LIMIT = 40 * 1024 * 1024
SPLIT = 2
KA, GA = ("half", "quarter", "ring", "core"), ("hi", "lo")
NEAR_ORDER = ("core", "quarter", "ring")
FAR_ORDER = ("core", "lo", "ring", "quarter")


def swap(block, mirror, other):
    half, quarter, ring, core, hi, lo = (lax.axis_size(name) for name in KA + GA)
    inner = ring * core
    slabs = hi * lo
    route = []
    for place in range(half * quarter * inner * slabs):
        kplace, slab = divmod(place, slabs)
        part, within = divmod(kplace, inner)
        part = half * quarter - 1 - part if mirror else part
        route.append((place, (part * inner + within) * slabs + (slab ^ other)))
    return lax.ppermute(block, KA + GA, route)


def one_hot(points_ref, half, slab, slab_size, npoints):
    first = pl.multiple_of(half * npoints, npoints)
    wanted = points_ref[:, pl.ds(first, npoints)] - slab * slab_size
    spot = lax.broadcasted_iota(jnp.int32, (slab_size, npoints), 0)
    return (spot == wanted).astype(jnp.float32).astype(jnp.bfloat16)


def pick(chosen, slab):
    return lax.dot_general(
        chosen, slab, (((0,), (0,)), ((), ())), preferred_element_type=jnp.float32
    )


def sizes(groups):
    return {"quarter": 2, "ring": groups // 4, "core": 2, "lo": SPLIT}


def place_of(member, groups, order, lo=0):
    ring, core = divmod(member % (groups // 2), 2)
    at = {"quarter": member // (groups // 2), "ring": ring, "core": core, "lo": lo}
    place = 0
    for name in order:
        place = place * sizes(groups)[name] + at[name]
    return place


def rotate(picked):
    middle = picked.shape[1] // 2
    return jnp.concatenate([-picked[:, middle:], picked[:, :middle]], axis=1)


def product(rows, slab, groups):
    out = lax.dot_general(
        rows, slab, (((1,), (1,)), ((), ())), preferred_element_type=jnp.float32
    )
    return out.reshape(groups, -1, out.shape[1]).astype(jnp.bfloat16)


def front_kernel(place_ref, points_ref, mine_ref, other_ref, picked_ref):
    slab_size, _ = mine_ref.shape
    _, npoints, _ = picked_ref.shape
    mine = place_ref[1] % SPLIT
    chosen = one_hot(points_ref, place_ref[0], place_ref[1], slab_size, npoints)
    for k, slab_ref in ((mine, mine_ref), (1 - mine, other_ref)):
        picked_ref[k] = pick(chosen, slab_ref[...]).astype(jnp.bfloat16)


def make_front(mine, other, points, place):
    vmem = pl.BlockSpec(memory_space=pltpu.VMEM)
    return pl.pallas_call(
        front_kernel,
        in_specs=[pl.BlockSpec(memory_space=pltpu.SMEM)] + [vmem] * 3,
        out_specs=vmem,
        out_shape=jax.ShapeDtypeStruct(
            (SPLIT, points.shape[1] // 2, mine.shape[1]), jnp.bfloat16
        ),
        compiler_params=pltpu.CompilerParams(vmem_limit_bytes=VMEM_LIMIT),
        name="front",
    )(place, points, mine, other)


def near_kernel(orbitals_ref, *refs):
    *picked_refs, out_ref = refs
    groups = out_ref.shape[0]
    rows = sum(picked_ref[0].astype(jnp.float32) for picked_ref in picked_refs)
    for part, turned in enumerate((rows, rotate(rows))):
        pieces = product(turned.astype(jnp.bfloat16), orbitals_ref[0], groups)
        for member in range(groups):
            out_ref[place_of(member, groups, NEAR_ORDER), 0, part] = pieces[member]


def make_near(orbitals, shares, groups):
    kdevice, slab_size, channels = orbitals.shape
    npoints = shares[0].shape[1]
    length = npoints // groups
    return pl.pallas_call(
        near_kernel,
        grid=(kdevice,),
        in_specs=[pl.BlockSpec((1, slab_size, channels), lambda k: (k, 0, 0))]
        + [pl.BlockSpec((1, npoints, channels), lambda k: (k, 0, 0)) for _ in shares],
        out_specs=pl.BlockSpec((groups, 1, 2, length, slab_size), lambda k: (0, k, 0, 0, 0)),
        out_shape=jax.ShapeDtypeStruct((groups, kdevice, 2, length, slab_size), jnp.bfloat16),
        cost_estimate=pl.CostEstimate(
            flops=1_000_000_000, bytes_accessed=3_000_000, transcendentals=0
        ),
        compiler_params=pltpu.CompilerParams(vmem_limit_bytes=VMEM_LIMIT),
        name="near",
    )(orbitals, *shares)


def ahead_kernel(rows_ref, slab_ref, picked_ref, chosen_ref):
    npoints, slabs = rows_ref.shape
    spot = lax.broadcasted_iota(jnp.int32, (npoints, slab_ref.shape[0]), 1)
    for number in range(slabs):
        chosen = (rows_ref[:, number : number + 1] == spot).astype(jnp.float32)
        chosen = chosen.astype(jnp.bfloat16)
        if number:
            chosen_ref[number - 1] = chosen
        else:
            picked = jnp.dot(chosen, slab_ref[...], preferred_element_type=jnp.float32)
            picked_ref[...] = picked.astype(jnp.bfloat16)


def far_kernel(place_ref, picked_ref, chosen_ref, *refs):
    *slab_refs, out_ref, parts_ref, sems = refs
    slower, _, faster, _, length, slab_size = out_ref.shape
    groups = slower * faster
    order = [name for name in FAR_ORDER if name != "lo"]
    picked = picked_ref[...].astype(jnp.float32)
    for number, slab_ref in enumerate(slab_refs[1:]):
        picked += jnp.dot(chosen_ref[number], slab_ref[...], preferred_element_type=jnp.float32)
    turned = [rows.astype(jnp.bfloat16) for rows in (picked, rotate(picked))]
    copies = []
    for number in range(SPLIT):
        for part in range(2):
            place = len(copies)
            pieces = product(turned[part], slab_refs[number][...], groups)
            for member in range(groups):
                at = divmod(place_of(member, groups, order), faster)
                parts_ref[place, at[0], at[1]] = pieces[member]
            target = out_ref.at[:, place_ref[1] % SPLIT ^ number, :, part]
            copies.append(pltpu.make_async_copy(parts_ref.at[place], target, sems.at[place]))
            copies[-1].start()
    for copy in copies:
        copy.wait()


def make_far(rows, slabs, place, groups):
    slab_size, channels = slabs[0].shape
    npoints, _ = rows.shape
    length = npoints // groups
    faster = math.prod(sizes(groups)[name] for name in FAR_ORDER[FAR_ORDER.index("lo") + 1 :])
    around = (groups // faster, faster)
    vmem = pl.BlockSpec(memory_space=pltpu.VMEM)
    picked, chosen = pl.pallas_call(
        ahead_kernel,
        in_specs=[vmem] * 2,
        out_specs=[vmem] * 2,
        out_shape=[
            jax.ShapeDtypeStruct((npoints, channels), jnp.bfloat16),
            jax.ShapeDtypeStruct((len(slabs) - 1, npoints, slab_size), jnp.bfloat16),
        ],
        cost_estimate=pl.CostEstimate(flops=1_000_000, bytes_accessed=3_000, transcendentals=0),
        compiler_params=pltpu.CompilerParams(vmem_limit_bytes=VMEM_LIMIT),
        name="ahead",
    )(rows, slabs[0])
    return pl.pallas_call(
        far_kernel,
        in_specs=[pl.BlockSpec(memory_space=pltpu.SMEM)] + [vmem] * (2 + len(slabs)),
        out_specs=pl.BlockSpec(memory_space=pl.ANY),
        out_shape=jax.ShapeDtypeStruct(
            (around[0], SPLIT, around[1], 2, length, slab_size), jnp.bfloat16
        ),
        scratch_shapes=[
            pltpu.VMEM((2 * SPLIT,) + around + (length, slab_size), jnp.bfloat16),
            pltpu.SemaphoreType.DMA((2 * SPLIT,)),
        ],
        cost_estimate=pl.CostEstimate(
            flops=60_000_000_000, bytes_accessed=180_000_000, transcendentals=0
        ),
        compiler_params=pltpu.CompilerParams(vmem_limit_bytes=VMEM_LIMIT),
        name="far",
    )(place, picked, chosen, *slabs)


def pair_kernel(scale, table_ref, near_ref, far_ref, out_ref, held_ref, sums_ref, sems):
    total_k, _, length, width = held_ref.shape
    transfers = table_ref.shape[0]
    groups = near_ref.shape[0] // SPLIT
    for member in range(groups):
        place = place_of(member, groups, NEAR_ORDER) * SPLIT
        for k in range(SPLIT):
            held_ref[member * SPLIT + k] = near_ref[place + k].astype(jnp.float32)
            far = far_ref[place_of(member, groups, FAR_ORDER, k)]
            held_ref[total_k // 2 + member * SPLIT + k] = far.astype(jnp.float32)

    count, columns = min(16, length), min(256, width)
    copies = []
    for start in range(0, length, count):
        rows = pl.ds(start, count)
        for column in range(0, width, columns):
            lanes = pl.ds(column, columns)

            def step(k, sums):
                real, imag = held_ref[k, 0, rows, lanes], held_ref[k, 1, rows, lanes]
                after = []
                for transfer in range(transfers):
                    other = table_ref[transfer, k]
                    other_real = held_ref[other, 0, rows, lanes]
                    other_imag = held_ref[other, 1, rows, lanes]
                    after.append(sums[2 * transfer] + (real * other_real + imag * other_imag))
                    after.append(sums[2 * transfer + 1] + (imag * other_real - real * other_imag))
                return tuple(after)

            zero = jnp.zeros((count, columns), jnp.float32)
            sums = lax.fori_loop(0, total_k, step, (zero,) * (2 * transfers), unroll=8)
            for place, value in enumerate(sums):
                sums_ref[rows, place // 2, place % 2, lanes] = value * scale
        copies.append(
            pltpu.make_async_copy(sums_ref.at[rows], out_ref.at[rows], sems.at[start // count])
        )
        copies[-1].start()
    for copy in copies:
        copy.wait()


def make_pairs(near, far, table):
    half_k, _, length, slab_size = near.shape
    transfers = table.shape[0]
    out = jax.ShapeDtypeStruct((length, transfers, 2, slab_size), jnp.float32)
    vmem = pl.BlockSpec(memory_space=pltpu.VMEM)
    return pl.pallas_call(
        functools.partial(pair_kernel, 1.0 / math.sqrt(2 * half_k)),
        in_specs=[pl.BlockSpec(memory_space=pltpu.SMEM), vmem, vmem],
        out_specs=pl.BlockSpec(memory_space=pl.ANY),
        out_shape=out,
        scratch_shapes=[
            pltpu.VMEM((2 * half_k, 2, length, slab_size), jnp.float32),
            pltpu.VMEM(out.shape, jnp.float32),
            pltpu.SemaphoreType.DMA((length // min(16, length),)),
        ],
        compiler_params=pltpu.CompilerParams(vmem_limit_bytes=VMEM_LIMIT),
        name="pairs",
    )(table, near, far)


def on_device(orbitals, minus_table, points):
    kdevice, slab_size, channels = orbitals.shape
    half = lax.axis_index("half")
    groups = lax.axis_size("quarter") * lax.axis_size("ring") * lax.axis_size("core")
    slabs = lax.axis_size("hi") * lax.axis_size("lo")
    total_k = 2 * groups * kdevice
    points = points.reshape(1, -1)
    place = jnp.stack([half, lax.axis_index("hi") * SPLIT + lax.axis_index("lo")])

    lo = lax.axis_index("lo")
    mine = lax.dynamic_index_in_dim(orbitals, lo, 0, keepdims=False)
    other = lax.dynamic_index_in_dim(orbitals, 1 - lo, 0, keepdims=False)
    share = make_front(mine, other, points, place)
    share, mine, other = lax.optimization_barrier((share, mine, other))
    shares = [share] + [swap(share, False, x) for x in range(1, slabs)]
    far = [swap(other if x & 1 else mine, True, x) for x in range(slabs)]

    def send(fields, around):
        fields = fields.reshape((-1,) + fields.shape[-3:])
        return lax.all_to_all(fields, around, split_axis=0, concat_axis=0, tiled=True)

    near_fields = make_near(orbitals, shares, groups)
    npoints = points.shape[1] // 2
    wanted = lax.dynamic_slice_in_dim(points[0], half * npoints, npoints)
    starts = jnp.stack([(place[1] ^ x) * slab_size for x in range(slabs)])
    rows = wanted[:, None] - starts[None, :]
    near_fields, rows = lax.optimization_barrier((near_fields, rows))
    far_fields = make_far(rows, far, place, groups)
    near_fields = send(near_fields, NEAR_ORDER)
    near_fields, far_fields = lax.optimization_barrier((near_fields, far_fields))
    far_fields = send(far_fields, FAR_ORDER)

    def mirrored(kpoints):
        return total_k // 2 + (kpoints + total_k // 4) % (total_k // 2)

    turn = half * (total_k // 2)
    table = (jnp.roll(minus_table, -turn, axis=1) - turn) % total_k
    table = jnp.where(table < total_k // 2, table, mirrored(table))
    first, third, fourth = jnp.split(table, (total_k // 2, 3 * total_k // 4), axis=1)
    return make_pairs(near_fields, far_fields, jnp.concatenate([first, fourth, third], axis=1))


def solution(mesh):
    kplaces, slabs = mesh.shape["ka"], mesh.shape["ga"]
    devices = mesh.devices.reshape(2, 2, kplaces // 8, 2, slabs // SPLIT, SPLIT)
    finer = Mesh(devices, KA + GA)
    return jax.shard_map(
        on_device,
        mesh=finer,
        in_specs=(P(KA, GA, None), P(), P()),
        out_specs=P(KA, None, None, GA),
        check_vma=False,
    )
```

```python
import functools
import math

import jax
import jax.numpy as jnp
from jax import lax
from jax.experimental import pallas as pl
from jax.experimental.pallas import tpu as pltpu
from jax.sharding import Mesh
from jax.sharding import PartitionSpec as P

VMEM_LIMIT = 40 * 1024 * 1024
SPLIT = 2
KA, GA = ("half", "quarter", "ring", "core"), ("hi", "lo")
NEAR_ORDER = ("ring", "quarter", "core")
FAR_ORDER = ("ring", "core", "lo", "quarter")


def swap(block, mirror, other):
    half, quarter, ring, core, hi, lo = (lax.axis_size(name) for name in KA + GA)
    inner = ring * core
    slabs = hi * lo
    route = []
    for place in range(half * quarter * inner * slabs):
        kplace, slab = divmod(place, slabs)
        part, within = divmod(kplace, inner)
        part = half * quarter - 1 - part if mirror else part
        route.append((place, (part * inner + within) * slabs + (slab ^ other)))
    return lax.ppermute(block, KA + GA, route)


def one_hot(points_ref, half, slab, slab_size, npoints):
    first = pl.multiple_of(half * npoints, npoints)
    wanted = points_ref[:, pl.ds(first, npoints)] - slab * slab_size
    spot = lax.broadcasted_iota(jnp.int32, (slab_size, npoints), 0)
    return (spot == wanted).astype(jnp.float32).astype(jnp.bfloat16)


def pick(chosen, slab):
    return lax.dot_general(
        chosen, slab, (((0,), (0,)), ((), ())), preferred_element_type=jnp.float32
    )


def sizes(groups):
    return {"quarter": 2, "ring": groups // 4, "core": 2, "lo": SPLIT}


def place_of(member, groups, order, lo=0):
    ring, core = divmod(member % (groups // 2), 2)
    at = {"quarter": member // (groups // 2), "ring": ring, "core": core, "lo": lo}
    place = 0
    for name in order:
        place = place * sizes(groups)[name] + at[name]
    return place


def rotate(picked):
    middle = picked.shape[1] // 2
    return jnp.concatenate([-picked[:, middle:], picked[:, :middle]], axis=1)


def product(rows, slab, groups):
    out = lax.dot_general(
        rows, slab, (((1,), (1,)), ((), ())), preferred_element_type=jnp.float32
    )
    return out.reshape(groups, -1, out.shape[1]).astype(jnp.bfloat16)


def front_kernel(place_ref, points_ref, mine_ref, other_ref, picked_ref):
    slab_size, _ = mine_ref.shape
    _, npoints, _ = picked_ref.shape
    mine = place_ref[1] % SPLIT
    chosen = one_hot(points_ref, place_ref[0], place_ref[1], slab_size, npoints)
    for k, slab_ref in ((mine, mine_ref), (1 - mine, other_ref)):
        picked_ref[k] = pick(chosen, slab_ref[...]).astype(jnp.bfloat16)


def make_front(mine, other, points, place):
    vmem = pl.BlockSpec(memory_space=pltpu.VMEM)
    return pl.pallas_call(
        front_kernel,
        in_specs=[pl.BlockSpec(memory_space=pltpu.SMEM)] + [vmem] * 3,
        out_specs=vmem,
        out_shape=jax.ShapeDtypeStruct(
            (SPLIT, points.shape[1] // 2, mine.shape[1]), jnp.bfloat16
        ),
        compiler_params=pltpu.CompilerParams(vmem_limit_bytes=VMEM_LIMIT),
        name="front",
    )(place, points, mine, other)


def near_kernel(orbitals_ref, *refs):
    *picked_refs, out_ref = refs
    groups = out_ref.shape[0]
    rows = sum(picked_ref[0].astype(jnp.float32) for picked_ref in picked_refs)
    for part, turned in enumerate((rows, rotate(rows))):
        pieces = product(turned.astype(jnp.bfloat16), orbitals_ref[0], groups)
        for member in range(groups):
            out_ref[place_of(member, groups, NEAR_ORDER), 0, part] = pieces[member]


def make_near(orbitals, shares, groups):
    kdevice, slab_size, channels = orbitals.shape
    npoints = shares[0].shape[1]
    length = npoints // groups
    return pl.pallas_call(
        near_kernel,
        grid=(kdevice,),
        in_specs=[pl.BlockSpec((1, slab_size, channels), lambda k: (k, 0, 0))]
        + [pl.BlockSpec((1, npoints, channels), lambda k: (k, 0, 0)) for _ in shares],
        out_specs=pl.BlockSpec((groups, 1, 2, length, slab_size), lambda k: (0, k, 0, 0, 0)),
        out_shape=jax.ShapeDtypeStruct((groups, kdevice, 2, length, slab_size), jnp.bfloat16),
        cost_estimate=pl.CostEstimate(
            flops=1_000_000_000, bytes_accessed=3_000_000, transcendentals=0
        ),
        compiler_params=pltpu.CompilerParams(vmem_limit_bytes=VMEM_LIMIT),
        name="near",
    )(orbitals, *shares)


def ahead_kernel(rows_ref, slab_ref, picked_ref, chosen_ref):
    npoints, slabs = rows_ref.shape
    spot = lax.broadcasted_iota(jnp.int32, (npoints, slab_ref.shape[0]), 1)
    for number in range(slabs):
        chosen = (rows_ref[:, number : number + 1] == spot).astype(jnp.float32)
        chosen = chosen.astype(jnp.bfloat16)
        if number:
            chosen_ref[number - 1] = chosen
        else:
            picked = jnp.dot(chosen, slab_ref[...], preferred_element_type=jnp.float32)
            picked_ref[...] = picked.astype(jnp.bfloat16)


def far_kernel(place_ref, picked_ref, chosen_ref, *refs):
    *slab_refs, out_ref, parts_ref, sems = refs
    slower, _, faster, _, length, slab_size = out_ref.shape
    groups = slower * faster
    order = [name for name in FAR_ORDER if name != "lo"]
    picked = picked_ref[...].astype(jnp.float32)
    for number, slab_ref in enumerate(slab_refs[1:]):
        picked += jnp.dot(chosen_ref[number], slab_ref[...], preferred_element_type=jnp.float32)
    turned = [rows.astype(jnp.bfloat16) for rows in (picked, rotate(picked))]
    copies = []
    for number in range(SPLIT):
        for part in range(2):
            place = len(copies)
            pieces = product(turned[part], slab_refs[number][...], groups)
            for member in range(groups):
                at = divmod(place_of(member, groups, order), faster)
                parts_ref[place, at[0], at[1]] = pieces[member]
            target = out_ref.at[:, place_ref[1] % SPLIT ^ number, :, part]
            copies.append(pltpu.make_async_copy(parts_ref.at[place], target, sems.at[place]))
            copies[-1].start()
    for copy in copies:
        copy.wait()


def make_far(rows, slabs, place, groups):
    slab_size, channels = slabs[0].shape
    npoints, _ = rows.shape
    length = npoints // groups
    faster = math.prod(sizes(groups)[name] for name in FAR_ORDER[FAR_ORDER.index("lo") + 1 :])
    around = (groups // faster, faster)
    vmem = pl.BlockSpec(memory_space=pltpu.VMEM)
    picked, chosen = pl.pallas_call(
        ahead_kernel,
        in_specs=[vmem] * 2,
        out_specs=[vmem] * 2,
        out_shape=[
            jax.ShapeDtypeStruct((npoints, channels), jnp.bfloat16),
            jax.ShapeDtypeStruct((len(slabs) - 1, npoints, slab_size), jnp.bfloat16),
        ],
        cost_estimate=pl.CostEstimate(flops=1_000_000, bytes_accessed=3_000, transcendentals=0),
        compiler_params=pltpu.CompilerParams(vmem_limit_bytes=VMEM_LIMIT),
        name="ahead",
    )(rows, slabs[0])
    return pl.pallas_call(
        far_kernel,
        in_specs=[pl.BlockSpec(memory_space=pltpu.SMEM)] + [vmem] * (2 + len(slabs)),
        out_specs=pl.BlockSpec(memory_space=pl.ANY),
        out_shape=jax.ShapeDtypeStruct(
            (around[0], SPLIT, around[1], 2, length, slab_size), jnp.bfloat16
        ),
        scratch_shapes=[
            pltpu.VMEM((2 * SPLIT,) + around + (length, slab_size), jnp.bfloat16),
            pltpu.SemaphoreType.DMA((2 * SPLIT,)),
        ],
        cost_estimate=pl.CostEstimate(
            flops=60_000_000_000, bytes_accessed=180_000_000, transcendentals=0
        ),
        compiler_params=pltpu.CompilerParams(vmem_limit_bytes=VMEM_LIMIT),
        name="far",
    )(place, picked, chosen, *slabs)


def pair_kernel(scale, table_ref, near_ref, far_ref, out_ref, held_ref, sums_ref, sems):
    total_k, _, length, width = held_ref.shape
    transfers = table_ref.shape[0]
    groups = near_ref.shape[0] // SPLIT
    for member in range(groups):
        place = place_of(member, groups, NEAR_ORDER) * SPLIT
        for k in range(SPLIT):
            held_ref[member * SPLIT + k] = near_ref[place + k].astype(jnp.float32)
            far = far_ref[place_of(member, groups, FAR_ORDER, k)]
            held_ref[total_k // 2 + member * SPLIT + k] = far.astype(jnp.float32)

    count, columns = min(16, length), min(256, width)
    copies = []
    for start in range(0, length, count):
        rows = pl.ds(start, count)
        for column in range(0, width, columns):
            lanes = pl.ds(column, columns)

            def step(k, sums):
                real, imag = held_ref[k, 0, rows, lanes], held_ref[k, 1, rows, lanes]
                after = []
                for transfer in range(transfers):
                    other = table_ref[transfer, k]
                    other_real = held_ref[other, 0, rows, lanes]
                    other_imag = held_ref[other, 1, rows, lanes]
                    after.append(sums[2 * transfer] + (real * other_real + imag * other_imag))
                    after.append(sums[2 * transfer + 1] + (imag * other_real - real * other_imag))
                return tuple(after)

            zero = jnp.zeros((count, columns), jnp.float32)
            sums = lax.fori_loop(0, total_k, step, (zero,) * (2 * transfers), unroll=8)
            for place, value in enumerate(sums):
                sums_ref[rows, place // 2, place % 2, lanes] = value * scale
        copies.append(
            pltpu.make_async_copy(sums_ref.at[rows], out_ref.at[rows], sems.at[start // count])
        )
        copies[-1].start()
    for copy in copies:
        copy.wait()


def make_pairs(near, far, table):
    half_k, _, length, slab_size = near.shape
    transfers = table.shape[0]
    out = jax.ShapeDtypeStruct((length, transfers, 2, slab_size), jnp.float32)
    vmem = pl.BlockSpec(memory_space=pltpu.VMEM)
    return pl.pallas_call(
        functools.partial(pair_kernel, 1.0 / math.sqrt(2 * half_k)),
        in_specs=[pl.BlockSpec(memory_space=pltpu.SMEM), vmem, vmem],
        out_specs=pl.BlockSpec(memory_space=pl.ANY),
        out_shape=out,
        scratch_shapes=[
            pltpu.VMEM((2 * half_k, 2, length, slab_size), jnp.float32),
            pltpu.VMEM(out.shape, jnp.float32),
            pltpu.SemaphoreType.DMA((length // min(16, length),)),
        ],
        compiler_params=pltpu.CompilerParams(vmem_limit_bytes=VMEM_LIMIT),
        name="pairs",
    )(table, near, far)


def on_device(orbitals, minus_table, points):
    kdevice, slab_size, channels = orbitals.shape
    half = lax.axis_index("half")
    groups = lax.axis_size("quarter") * lax.axis_size("ring") * lax.axis_size("core")
    slabs = lax.axis_size("hi") * lax.axis_size("lo")
    total_k = 2 * groups * kdevice
    points = points.reshape(1, -1)
    place = jnp.stack([half, lax.axis_index("hi") * SPLIT + lax.axis_index("lo")])

    lo = lax.axis_index("lo")
    mine = lax.dynamic_index_in_dim(orbitals, lo, 0, keepdims=False)
    other = lax.dynamic_index_in_dim(orbitals, 1 - lo, 0, keepdims=False)
    share = make_front(mine, other, points, place)
    share, mine, other = lax.optimization_barrier((share, mine, other))
    shares = [share] + [swap(share, False, x) for x in range(1, slabs)]
    far = [swap(other if x & 1 else mine, True, x) for x in range(slabs)]

    def send(fields, around):
        fields = fields.reshape((-1,) + fields.shape[-3:])
        return lax.all_to_all(fields, around, split_axis=0, concat_axis=0, tiled=True)

    near_fields = make_near(orbitals, shares, groups)
    npoints = points.shape[1] // 2
    wanted = lax.dynamic_slice_in_dim(points[0], half * npoints, npoints)
    starts = jnp.stack([(place[1] ^ x) * slab_size for x in range(slabs)])
    rows = wanted[:, None] - starts[None, :]
    near_fields, rows = lax.optimization_barrier((near_fields, rows))
    far_fields = make_far(rows, far, place, groups)
    near_fields = send(near_fields, NEAR_ORDER)
    near_fields, far_fields = lax.optimization_barrier((near_fields, far_fields))
    far_fields = send(far_fields, FAR_ORDER)

    def mirrored(kpoints):
        return total_k // 2 + (kpoints + total_k // 4) % (total_k // 2)

    turn = half * (total_k // 2)
    table = (jnp.roll(minus_table, -turn, axis=1) - turn) % total_k
    table = jnp.where(table < total_k // 2, table, mirrored(table))
    first, third, fourth = jnp.split(table, (total_k // 2, 3 * total_k // 4), axis=1)
    return make_pairs(near_fields, far_fields, jnp.concatenate([first, fourth, third], axis=1))


def solution(mesh):
    kplaces, slabs = mesh.shape["ka"], mesh.shape["ga"]
    devices = mesh.devices.reshape(2, 2, kplaces // 8, 2, slabs // SPLIT, SPLIT)
    finer = Mesh(devices, KA + GA)
    return jax.shard_map(
        on_device,
        mesh=finer,
        in_specs=(P(KA, GA, None), P(), P()),
        out_specs=P(KA, None, None, GA),
        check_vma=False,
    )
```

```python
import functools
import math

import jax
import jax.numpy as jnp
from jax import lax
from jax.experimental import pallas as pl
from jax.experimental.pallas import tpu as pltpu
from jax.sharding import Mesh
from jax.sharding import PartitionSpec as P

VMEM_LIMIT = 40 * 1024 * 1024
SPLIT = 2
KA, GA = ("half", "quarter", "inner"), ("hi", "lo")


def swap(block, mirror, other):
    half, quarter, inner, hi, lo = (lax.axis_size(name) for name in KA + GA)
    slabs = hi * lo
    route = []
    for place in range(half * quarter * inner * slabs):
        kplace, slab = divmod(place, slabs)
        part, within = divmod(kplace, inner)
        part = half * quarter - 1 - part if mirror else part
        route.append((place, (part * inner + within) * slabs + (slab ^ other)))
    return lax.ppermute(block, KA + GA, route)


def one_hot(points_ref, half, slab, slab_size, npoints):
    first = pl.multiple_of(half * npoints, npoints)
    wanted = points_ref[:, pl.ds(first, npoints)] - slab * slab_size
    spot = lax.broadcasted_iota(jnp.int32, (slab_size, npoints), 0)
    return (spot == wanted).astype(jnp.float32).astype(jnp.bfloat16)


def pick(chosen, slab):
    return lax.dot_general(
        chosen, slab, (((0,), (0,)), ((), ())), preferred_element_type=jnp.float32
    )


def crossed(member, groups):
    quarter, inner = divmod(member, groups // 2)
    return inner * 2 + quarter


def far_place(member, lo, groups):
    return lo * groups + crossed(member, groups)


def rotate(picked):
    middle = picked.shape[1] // 2
    return jnp.concatenate([-picked[:, middle:], picked[:, :middle]], axis=1)


def product(rows, slab, groups):
    out = lax.dot_general(
        rows, slab, (((1,), (1,)), ((), ())), preferred_element_type=jnp.float32
    )
    return out.reshape(groups, -1, out.shape[1]).astype(jnp.bfloat16)


def front_kernel(place_ref, points_ref, mine_ref, other_ref, picked_ref):
    slab_size, _ = mine_ref.shape
    _, npoints, _ = picked_ref.shape
    mine = place_ref[1] % SPLIT
    chosen = one_hot(points_ref, place_ref[0], place_ref[1], slab_size, npoints)
    for k, slab_ref in ((mine, mine_ref), (1 - mine, other_ref)):
        picked_ref[k] = pick(chosen, slab_ref[...]).astype(jnp.bfloat16)


def make_front(mine, other, points, place):
    vmem = pl.BlockSpec(memory_space=pltpu.VMEM)
    return pl.pallas_call(
        front_kernel,
        in_specs=[pl.BlockSpec(memory_space=pltpu.SMEM)] + [vmem] * 3,
        out_specs=vmem,
        out_shape=jax.ShapeDtypeStruct(
            (SPLIT, points.shape[1] // 2, mine.shape[1]), jnp.bfloat16
        ),
        compiler_params=pltpu.CompilerParams(vmem_limit_bytes=VMEM_LIMIT),
        name="front",
    )(place, points, mine, other)


def near_kernel(orbitals_ref, *refs):
    *picked_refs, out_ref = refs
    groups = out_ref.shape[0]
    rows = sum(picked_ref[0].astype(jnp.float32) for picked_ref in picked_refs)
    for part, turned in enumerate((rows, rotate(rows))):
        out_ref[:, 0, part] = product(turned.astype(jnp.bfloat16), orbitals_ref[0], groups)


def make_near(orbitals, shares, groups):
    kdevice, slab_size, channels = orbitals.shape
    npoints = shares[0].shape[1]
    length = npoints // groups
    return pl.pallas_call(
        near_kernel,
        grid=(kdevice,),
        in_specs=[pl.BlockSpec((1, slab_size, channels), lambda k: (k, 0, 0))]
        + [pl.BlockSpec((1, npoints, channels), lambda k: (k, 0, 0)) for _ in shares],
        out_specs=pl.BlockSpec((groups, 1, 2, length, slab_size), lambda k: (0, k, 0, 0, 0)),
        out_shape=jax.ShapeDtypeStruct((groups, kdevice, 2, length, slab_size), jnp.bfloat16),
        cost_estimate=pl.CostEstimate(
            flops=1_000_000_000, bytes_accessed=3_000_000, transcendentals=0
        ),
        compiler_params=pltpu.CompilerParams(vmem_limit_bytes=VMEM_LIMIT),
        name="near",
    )(orbitals, *shares)


def ahead_kernel(rows_ref, slab_ref, picked_ref, chosen_ref):
    npoints, slabs = rows_ref.shape
    spot = lax.broadcasted_iota(jnp.int32, (npoints, slab_ref.shape[0]), 1)
    for number in range(slabs):
        chosen = (rows_ref[:, number : number + 1] == spot).astype(jnp.float32)
        chosen = chosen.astype(jnp.bfloat16)
        if number:
            chosen_ref[number - 1] = chosen
        else:
            picked = jnp.dot(chosen, slab_ref[...], preferred_element_type=jnp.float32)
            picked_ref[...] = picked.astype(jnp.bfloat16)


def far_kernel(place_ref, picked_ref, chosen_ref, *refs):
    *slab_refs, out_ref, parts_ref, sems = refs
    _, groups, _, length, slab_size = out_ref.shape
    picked = picked_ref[...].astype(jnp.float32)
    for number, slab_ref in enumerate(slab_refs[1:]):
        picked += jnp.dot(chosen_ref[number], slab_ref[...], preferred_element_type=jnp.float32)
    turned = [rows.astype(jnp.bfloat16) for rows in (picked, rotate(picked))]
    copies = []
    for number in range(SPLIT):
        for part in range(2):
            place = len(copies)
            pieces = product(turned[part], slab_refs[number][...], groups)
            for member in range(groups):
                parts_ref[place, crossed(member, groups)] = pieces[member]
            target = out_ref.at[place_ref[1] % SPLIT ^ number, :, part]
            copies.append(pltpu.make_async_copy(parts_ref.at[place], target, sems.at[place]))
            copies[-1].start()
    for copy in copies:
        copy.wait()


def make_far(rows, slabs, place, groups):
    slab_size, channels = slabs[0].shape
    npoints, _ = rows.shape
    length = npoints // groups
    vmem = pl.BlockSpec(memory_space=pltpu.VMEM)
    picked, chosen = pl.pallas_call(
        ahead_kernel,
        in_specs=[vmem] * 2,
        out_specs=[vmem] * 2,
        out_shape=[
            jax.ShapeDtypeStruct((npoints, channels), jnp.bfloat16),
            jax.ShapeDtypeStruct((len(slabs) - 1, npoints, slab_size), jnp.bfloat16),
        ],
        cost_estimate=pl.CostEstimate(flops=1_000_000, bytes_accessed=3_000, transcendentals=0),
        compiler_params=pltpu.CompilerParams(vmem_limit_bytes=VMEM_LIMIT),
        name="ahead",
    )(rows, slabs[0])
    return pl.pallas_call(
        far_kernel,
        in_specs=[pl.BlockSpec(memory_space=pltpu.SMEM)] + [vmem] * (2 + len(slabs)),
        out_specs=pl.BlockSpec(memory_space=pl.ANY),
        out_shape=jax.ShapeDtypeStruct((SPLIT, groups, 2, length, slab_size), jnp.bfloat16),
        scratch_shapes=[
            pltpu.VMEM((2 * SPLIT, groups, length, slab_size), jnp.bfloat16),
            pltpu.SemaphoreType.DMA((2 * SPLIT,)),
        ],
        cost_estimate=pl.CostEstimate(
            flops=60_000_000_000, bytes_accessed=180_000_000, transcendentals=0
        ),
        compiler_params=pltpu.CompilerParams(vmem_limit_bytes=VMEM_LIMIT),
        name="far",
    )(place, picked, chosen, *slabs)


def pair_kernel(scale, table_ref, near_ref, far_ref, out_ref, held_ref, sums_ref, sems):
    total_k, _, length, width = held_ref.shape
    transfers = table_ref.shape[0]
    groups = near_ref.shape[0] // SPLIT
    held_ref[: total_k // 2] = near_ref[...].astype(jnp.float32)
    for member in range(groups):
        for k in range(SPLIT):
            far = far_ref[far_place(member, k, groups)]
            held_ref[total_k // 2 + member * SPLIT + k] = far.astype(jnp.float32)

    count, columns = min(16, length), min(256, width)
    copies = []
    for start in range(0, length, count):
        rows = pl.ds(start, count)
        for column in range(0, width, columns):
            lanes = pl.ds(column, columns)

            def step(k, sums):
                real, imag = held_ref[k, 0, rows, lanes], held_ref[k, 1, rows, lanes]
                after = []
                for transfer in range(transfers):
                    other = table_ref[transfer, k]
                    other_real = held_ref[other, 0, rows, lanes]
                    other_imag = held_ref[other, 1, rows, lanes]
                    after.append(sums[2 * transfer] + (real * other_real + imag * other_imag))
                    after.append(sums[2 * transfer + 1] + (imag * other_real - real * other_imag))
                return tuple(after)

            zero = jnp.zeros((count, columns), jnp.float32)
            sums = lax.fori_loop(0, total_k, step, (zero,) * (2 * transfers), unroll=32)
            for place, value in enumerate(sums):
                sums_ref[rows, place // 2, place % 2, lanes] = value * scale
        copies.append(
            pltpu.make_async_copy(sums_ref.at[rows], out_ref.at[rows], sems.at[start // count])
        )
        copies[-1].start()
    for copy in copies:
        copy.wait()


def make_pairs(near, far, table):
    half_k, _, length, slab_size = near.shape
    transfers = table.shape[0]
    out = jax.ShapeDtypeStruct((length, transfers, 2, slab_size), jnp.float32)
    vmem = pl.BlockSpec(memory_space=pltpu.VMEM)
    return pl.pallas_call(
        functools.partial(pair_kernel, 1.0 / math.sqrt(2 * half_k)),
        in_specs=[pl.BlockSpec(memory_space=pltpu.SMEM), vmem, vmem],
        out_specs=pl.BlockSpec(memory_space=pl.ANY),
        out_shape=out,
        scratch_shapes=[
            pltpu.VMEM((2 * half_k, 2, length, slab_size), jnp.float32),
            pltpu.VMEM(out.shape, jnp.float32),
            pltpu.SemaphoreType.DMA((length // min(16, length),)),
        ],
        compiler_params=pltpu.CompilerParams(vmem_limit_bytes=VMEM_LIMIT),
        name="pairs",
    )(table, near, far)


def on_device(orbitals, minus_table, points):
    kdevice, slab_size, channels = orbitals.shape
    half = lax.axis_index("half")
    groups = lax.axis_size("quarter") * lax.axis_size("inner")
    slabs = lax.axis_size("hi") * lax.axis_size("lo")
    total_k = 2 * groups * kdevice
    points = points.reshape(1, -1)
    place = jnp.stack([half, lax.axis_index("hi") * SPLIT + lax.axis_index("lo")])

    lo = lax.axis_index("lo")
    mine = lax.dynamic_index_in_dim(orbitals, lo, 0, keepdims=False)
    other = lax.dynamic_index_in_dim(orbitals, 1 - lo, 0, keepdims=False)
    share = make_front(mine, other, points, place)
    share, mine, other = lax.optimization_barrier((share, mine, other))
    shares = [share] + [swap(share, False, x) for x in range(1, slabs)]
    far = [swap(other if x & 1 else mine, True, x) for x in range(slabs)]

    def send(fields, around):
        fields = fields.reshape((-1,) + fields.shape[-3:])
        return lax.all_to_all(fields, around, split_axis=0, concat_axis=0, tiled=True)

    near_fields = make_near(orbitals, shares, groups)
    npoints = points.shape[1] // 2
    wanted = lax.dynamic_slice_in_dim(points[0], half * npoints, npoints)
    starts = jnp.stack([(place[1] ^ x) * slab_size for x in range(slabs)])
    rows = wanted[:, None] - starts[None, :]
    near_fields, rows = lax.optimization_barrier((near_fields, rows))
    far_fields = make_far(rows, far, place, groups)
    near_fields = send(near_fields, ("quarter", "inner"))
    near_fields, far_fields = lax.optimization_barrier((near_fields, far_fields))
    far_fields = send(far_fields, ("lo", "inner", "quarter"))

    def mirrored(kpoints):
        return total_k // 2 + (kpoints + total_k // 4) % (total_k // 2)

    turn = half * (total_k // 2)
    table = (jnp.roll(minus_table, -turn, axis=1) - turn) % total_k
    table = jnp.where(table < total_k // 2, table, mirrored(table))
    first, third, fourth = jnp.split(table, (total_k // 2, 3 * total_k // 4), axis=1)
    return make_pairs(near_fields, far_fields, jnp.concatenate([first, fourth, third], axis=1))


def solution(mesh):
    kplaces, slabs = mesh.shape["ka"], mesh.shape["ga"]
    devices = mesh.devices.reshape(2, 2, kplaces // 4, slabs // SPLIT, SPLIT)
    finer = Mesh(devices, KA + GA)
    return jax.shard_map(
        on_device,
        mesh=finer,
        in_specs=(P(KA, GA, None), P(), P()),
        out_specs=P(KA, None, None, GA),
        check_vma=False,
    )
```

```python
import functools
import math

import jax
import jax.numpy as jnp
from jax import lax
from jax.experimental import pallas as pl
from jax.experimental.pallas import tpu as pltpu
from jax.sharding import Mesh
from jax.sharding import PartitionSpec as P

VMEM_LIMIT = 40 * 1024 * 1024
SPLIT = 2
KA, GA = ("half", "quarter", "inner"), ("hi", "lo")


def swap(block, mirror, other):
    half, quarter, inner, hi, lo = (lax.axis_size(name) for name in KA + GA)
    slabs = hi * lo
    route = []
    for place in range(half * quarter * inner * slabs):
        kplace, slab = divmod(place, slabs)
        part, within = divmod(kplace, inner)
        part = half * quarter - 1 - part if mirror else part
        route.append((place, (part * inner + within) * slabs + (slab ^ other)))
    return lax.ppermute(block, KA + GA, route)


def one_hot(points_ref, half, slab, slab_size, npoints):
    first = pl.multiple_of(half * npoints, npoints)
    wanted = points_ref[:, pl.ds(first, npoints)] - slab * slab_size
    spot = lax.broadcasted_iota(jnp.int32, (slab_size, npoints), 0)
    return (spot == wanted).astype(jnp.float32).astype(jnp.bfloat16)


def pick(chosen, slab):
    return lax.dot_general(
        chosen, slab, (((0,), (0,)), ((), ())), preferred_element_type=jnp.float32
    )


def crossed(member, groups):
    quarter, inner = divmod(member, groups // 2)
    return inner * 2 + quarter


def far_place(member, lo, groups):
    return lo * groups + crossed(member, groups)


def rotate(picked):
    middle = picked.shape[1] // 2
    return jnp.concatenate([-picked[:, middle:], picked[:, :middle]], axis=1)


def product(rows, slab, groups):
    out = lax.dot_general(
        rows, slab, (((1,), (1,)), ((), ())), preferred_element_type=jnp.float32
    )
    return out.reshape(groups, -1, out.shape[1]).astype(jnp.bfloat16)


def front_kernel(points_ref, mine_ref, other_ref, picked_ref):
    slab_size, _ = mine_ref.shape
    _, npoints, _ = picked_ref.shape
    mine = lax.axis_index("lo")
    here = lax.axis_index("hi") * SPLIT + mine
    chosen = one_hot(points_ref, lax.axis_index("half"), here, slab_size, npoints)
    for k, slab_ref in ((mine, mine_ref), (1 - mine, other_ref)):
        picked_ref[k] = pick(chosen, slab_ref[...]).astype(jnp.bfloat16)


def make_front(mine, other, points):
    vmem = pl.BlockSpec(memory_space=pltpu.VMEM)
    return pl.pallas_call(
        front_kernel,
        in_specs=[vmem] * 3,
        out_specs=vmem,
        out_shape=jax.ShapeDtypeStruct(
            (SPLIT, points.shape[1] // 2, mine.shape[1]), jnp.bfloat16
        ),
        compiler_params=pltpu.CompilerParams(vmem_limit_bytes=VMEM_LIMIT),
        name="front",
    )(points, mine, other)


def near_kernel(orbitals_ref, *refs):
    *picked_refs, out_ref = refs
    groups = out_ref.shape[0]
    rows = sum(picked_ref[0].astype(jnp.float32) for picked_ref in picked_refs)
    for part, turned in enumerate((rows, rotate(rows))):
        out_ref[:, 0, part] = product(turned.astype(jnp.bfloat16), orbitals_ref[0], groups)


def make_near(orbitals, shares, groups):
    kdevice, slab_size, channels = orbitals.shape
    npoints = shares[0].shape[1]
    length = npoints // groups
    return pl.pallas_call(
        near_kernel,
        grid=(kdevice,),
        in_specs=[pl.BlockSpec((1, slab_size, channels), lambda k: (k, 0, 0))]
        + [pl.BlockSpec((1, npoints, channels), lambda k: (k, 0, 0)) for _ in shares],
        out_specs=pl.BlockSpec((groups, 1, 2, length, slab_size), lambda k: (0, k, 0, 0, 0)),
        out_shape=jax.ShapeDtypeStruct((groups, kdevice, 2, length, slab_size), jnp.bfloat16),
        cost_estimate=pl.CostEstimate(
            flops=1_000_000_000, bytes_accessed=3_000_000, transcendentals=0
        ),
        compiler_params=pltpu.CompilerParams(vmem_limit_bytes=VMEM_LIMIT),
        name="near",
    )(orbitals, *shares)


def ahead_kernel(rows_ref, slab_ref, picked_ref, chosen_ref):
    npoints, slabs = rows_ref.shape
    spot = lax.broadcasted_iota(jnp.int32, (npoints, slab_ref.shape[0]), 1)
    for number in range(slabs):
        chosen = (rows_ref[:, number : number + 1] == spot).astype(jnp.float32)
        chosen = chosen.astype(jnp.bfloat16)
        if number:
            chosen_ref[number - 1] = chosen
        else:
            picked = jnp.dot(chosen, slab_ref[...], preferred_element_type=jnp.float32)
            picked_ref[...] = picked.astype(jnp.bfloat16)


def far_kernel(picked_ref, chosen_ref, *refs):
    *slab_refs, out_ref, parts_ref, sems = refs
    _, groups, _, length, slab_size = out_ref.shape
    picked = picked_ref[...].astype(jnp.float32)
    for number, slab_ref in enumerate(slab_refs[1:]):
        picked += jnp.dot(chosen_ref[number], slab_ref[...], preferred_element_type=jnp.float32)
    turned = [rows.astype(jnp.bfloat16) for rows in (picked, rotate(picked))]
    copies = []
    for number in range(SPLIT):
        for part in range(2):
            place = len(copies)
            pieces = product(turned[part], slab_refs[number][...], groups)
            for member in range(groups):
                parts_ref[place, crossed(member, groups)] = pieces[member]
            target = out_ref.at[lax.axis_index("lo") ^ number, :, part]
            copies.append(pltpu.make_async_copy(parts_ref.at[place], target, sems.at[place]))
            copies[-1].start()
    for copy in copies:
        copy.wait()


def make_far(rows, slabs, groups):
    slab_size, channels = slabs[0].shape
    npoints, _ = rows.shape
    length = npoints // groups
    vmem = pl.BlockSpec(memory_space=pltpu.VMEM)
    picked, chosen = pl.pallas_call(
        ahead_kernel,
        in_specs=[vmem] * 2,
        out_specs=[vmem] * 2,
        out_shape=[
            jax.ShapeDtypeStruct((npoints, channels), jnp.bfloat16),
            jax.ShapeDtypeStruct((len(slabs) - 1, npoints, slab_size), jnp.bfloat16),
        ],
        cost_estimate=pl.CostEstimate(flops=1_000_000, bytes_accessed=3_000, transcendentals=0),
        compiler_params=pltpu.CompilerParams(vmem_limit_bytes=VMEM_LIMIT),
        name="ahead",
    )(rows, slabs[0])
    return pl.pallas_call(
        far_kernel,
        in_specs=[vmem] * (2 + len(slabs)),
        out_specs=pl.BlockSpec(memory_space=pl.ANY),
        out_shape=jax.ShapeDtypeStruct((SPLIT, groups, 2, length, slab_size), jnp.bfloat16),
        scratch_shapes=[
            pltpu.VMEM((2 * SPLIT, groups, length, slab_size), jnp.bfloat16),
            pltpu.SemaphoreType.DMA((2 * SPLIT,)),
        ],
        cost_estimate=pl.CostEstimate(
            flops=60_000_000_000, bytes_accessed=180_000_000, transcendentals=0
        ),
        compiler_params=pltpu.CompilerParams(vmem_limit_bytes=VMEM_LIMIT),
        name="far",
    )(picked, chosen, *slabs)


def pair_kernel(scale, source_ref, near_ref, far_ref, out_ref, table_ref, held_ref, sums_ref, sems):
    total_k, _, length, width = held_ref.shape
    transfers = table_ref.shape[0]
    table_copy = pltpu.make_async_copy(source_ref, table_ref, sems.at[sems.shape[0] - 1])
    table_copy.start()
    groups = near_ref.shape[0] // SPLIT
    held_ref[: total_k // 2] = near_ref[...].astype(jnp.float32)
    for member in range(groups):
        for k in range(SPLIT):
            far = far_ref[far_place(member, k, groups)]
            held_ref[total_k // 2 + member * SPLIT + k] = far.astype(jnp.float32)

    table_copy.wait()
    count, columns = min(16, length), min(256, width)
    copies = []
    for start in range(0, length, count):
        rows = pl.ds(start, count)
        for column in range(0, width, columns):
            lanes = pl.ds(column, columns)

            def step(k, sums):
                real, imag = held_ref[k, 0, rows, lanes], held_ref[k, 1, rows, lanes]
                after = []
                for transfer in range(transfers):
                    other = table_ref[transfer, k]
                    other_real = held_ref[other, 0, rows, lanes]
                    other_imag = held_ref[other, 1, rows, lanes]
                    after.append(sums[2 * transfer] + (real * other_real + imag * other_imag))
                    after.append(sums[2 * transfer + 1] + (imag * other_real - real * other_imag))
                return tuple(after)

            zero = jnp.zeros((count, columns), jnp.float32)
            sums = lax.fori_loop(0, total_k, step, (zero,) * (2 * transfers), unroll=32)
            for place, value in enumerate(sums):
                sums_ref[rows, place // 2, place % 2, lanes] = value * scale
        copies.append(
            pltpu.make_async_copy(sums_ref.at[rows], out_ref.at[rows], sems.at[start // count])
        )
        copies[-1].start()
    for copy in copies:
        copy.wait()


def make_pairs(near, far, table):
    half_k, _, length, slab_size = near.shape
    transfers = table.shape[0]
    out = jax.ShapeDtypeStruct((length, transfers, 2, slab_size), jnp.float32)
    vmem = pl.BlockSpec(memory_space=pltpu.VMEM)
    return pl.pallas_call(
        functools.partial(pair_kernel, 1.0 / math.sqrt(2 * half_k)),
        in_specs=[pl.BlockSpec(memory_space=pl.ANY), vmem, vmem],
        out_specs=pl.BlockSpec(memory_space=pl.ANY),
        out_shape=out,
        scratch_shapes=[
            pltpu.SMEM(table.shape, jnp.int32),
            pltpu.VMEM((2 * half_k, 2, length, slab_size), jnp.float32),
            pltpu.VMEM(out.shape, jnp.float32),
            pltpu.SemaphoreType.DMA((length // min(16, length) + 1,)),
        ],
        compiler_params=pltpu.CompilerParams(vmem_limit_bytes=VMEM_LIMIT),
        name="pairs",
    )(table, near, far)


def on_device(orbitals, minus_table, points):
    kdevice, slab_size, channels = orbitals.shape
    half = lax.axis_index("half")
    groups = lax.axis_size("quarter") * lax.axis_size("inner")
    slabs = lax.axis_size("hi") * lax.axis_size("lo")
    total_k = 2 * groups * kdevice
    points = points.reshape(1, -1)
    here = lax.axis_index("hi") * SPLIT + lax.axis_index("lo")

    lo = lax.axis_index("lo")
    mine = lax.dynamic_index_in_dim(orbitals, lo, 0, keepdims=False)
    other = lax.dynamic_index_in_dim(orbitals, 1 - lo, 0, keepdims=False)
    share = make_front(mine, other, points)
    share, mine, other = lax.optimization_barrier((share, mine, other))
    shares = [share] + [swap(share, False, x) for x in range(1, slabs)]
    far = [swap(other if x & 1 else mine, True, x) for x in range(slabs)]

    def send(fields, around):
        fields = fields.reshape((-1,) + fields.shape[-3:])
        return lax.all_to_all(fields, around, split_axis=0, concat_axis=0, tiled=True)

    near_fields = make_near(orbitals, shares, groups)
    npoints = points.shape[1] // 2
    wanted = lax.dynamic_slice_in_dim(points[0], half * npoints, npoints)
    starts = jnp.stack([(here ^ x) * slab_size for x in range(slabs)])
    rows = wanted[:, None] - starts[None, :]
    near_fields, rows = lax.optimization_barrier((near_fields, rows))
    far_fields = make_far(rows, far, groups)
    near_fields = send(near_fields, ("quarter", "inner"))
    near_fields, far_fields = lax.optimization_barrier((near_fields, far_fields))
    far_fields = send(far_fields, ("lo", "inner", "quarter"))

    def mirrored(kpoints):
        return total_k // 2 + (kpoints + total_k // 4) % (total_k // 2)

    turn = half * (total_k // 2)
    table = (jnp.roll(minus_table, -turn, axis=1) - turn) % total_k
    table = jnp.where(table < total_k // 2, table, mirrored(table))
    first, third, fourth = jnp.split(table, (total_k // 2, 3 * total_k // 4), axis=1)
    return make_pairs(near_fields, far_fields, jnp.concatenate([first, fourth, third], axis=1))


def solution(mesh):
    kplaces, slabs = mesh.shape["ka"], mesh.shape["ga"]
    devices = mesh.devices.reshape(2, 2, kplaces // 4, slabs // SPLIT, SPLIT)
    finer = Mesh(devices, KA + GA)
    return jax.shard_map(
        on_device,
        mesh=finer,
        in_specs=(P(KA, GA, None), P(), P()),
        out_specs=P(KA, None, None, GA),
        check_vma=False,
    )
```

```python
import functools
import math

import jax
import jax.numpy as jnp
from jax import lax
from jax.experimental import pallas as pl
from jax.experimental.pallas import tpu as pltpu
from jax.sharding import Mesh
from jax.sharding import PartitionSpec as P

VMEM_LIMIT = 40 * 1024 * 1024
SPLIT = 2
KA, GA = ("half", "quarter", "inner"), ("hi", "lo")


def swap(block, mirror, other):
    half, quarter, inner, hi, lo = (lax.axis_size(name) for name in KA + GA)
    slabs = hi * lo
    route = []
    for place in range(half * quarter * inner * slabs):
        kplace, slab = divmod(place, slabs)
        part, within = divmod(kplace, inner)
        part = half * quarter - 1 - part if mirror else part
        route.append((place, (part * inner + within) * slabs + (slab ^ other)))
    return lax.ppermute(block, KA + GA, route)


def one_hot(points_ref, half, slab, slab_size, npoints):
    first = pl.multiple_of(half * npoints, npoints)
    wanted = points_ref[:, pl.ds(first, npoints)] - slab * slab_size
    spot = lax.broadcasted_iota(jnp.int32, (slab_size, npoints), 0)
    return (spot == wanted).astype(jnp.float32).astype(jnp.bfloat16)


def pick(chosen, slab):
    return lax.dot_general(
        chosen, slab, (((0,), (0,)), ((), ())), preferred_element_type=jnp.float32
    )


def crossed(member, groups):
    quarter, inner = divmod(member, groups // 2)
    return inner * 2 + quarter


def far_place(member, lo, groups):
    return lo * groups + crossed(member, groups)


def rotate(picked):
    middle = picked.shape[1] // 2
    return jnp.concatenate([-picked[:, middle:], picked[:, :middle]], axis=1)


def product(rows, slab, groups):
    out = lax.dot_general(
        rows, slab, (((1,), (1,)), ((), ())), preferred_element_type=jnp.float32
    )
    return out.reshape(groups, -1, out.shape[1]).astype(jnp.bfloat16)


def front_kernel(points_ref, mine_ref, other_ref, picked_ref):
    slab_size, _ = mine_ref.shape
    _, npoints, _ = picked_ref.shape
    mine = lax.axis_index("lo")
    here = lax.axis_index("hi") * SPLIT + mine
    chosen = one_hot(points_ref, lax.axis_index("half"), here, slab_size, npoints)
    for k, slab_ref in ((mine, mine_ref), (1 - mine, other_ref)):
        picked_ref[k] = pick(chosen, slab_ref[...]).astype(jnp.bfloat16)


def make_front(mine, other, points):
    vmem = pl.BlockSpec(memory_space=pltpu.VMEM)
    return pl.pallas_call(
        front_kernel,
        in_specs=[vmem] * 3,
        out_specs=vmem,
        out_shape=jax.ShapeDtypeStruct(
            (SPLIT, points.shape[1] // 2, mine.shape[1]), jnp.bfloat16
        ),
        compiler_params=pltpu.CompilerParams(vmem_limit_bytes=VMEM_LIMIT),
        name="front",
    )(points, mine, other)


def near_kernel(orbitals_ref, *refs):
    *picked_refs, out_ref = refs
    groups = out_ref.shape[0]
    rows = sum(picked_ref[0].astype(jnp.float32) for picked_ref in picked_refs)
    for part, turned in enumerate((rows, rotate(rows))):
        out_ref[:, 0, part] = product(turned.astype(jnp.bfloat16), orbitals_ref[0], groups)


def make_near(orbitals, shares, groups):
    kdevice, slab_size, channels = orbitals.shape
    npoints = shares[0].shape[1]
    length = npoints // groups
    return pl.pallas_call(
        near_kernel,
        grid=(kdevice,),
        in_specs=[pl.BlockSpec((1, slab_size, channels), lambda k: (k, 0, 0))]
        + [pl.BlockSpec((1, npoints, channels), lambda k: (k, 0, 0)) for _ in shares],
        out_specs=pl.BlockSpec((groups, 1, 2, length, slab_size), lambda k: (0, k, 0, 0, 0)),
        out_shape=jax.ShapeDtypeStruct((groups, kdevice, 2, length, slab_size), jnp.bfloat16),
        cost_estimate=pl.CostEstimate(
            flops=1_000_000_000, bytes_accessed=3_000_000, transcendentals=0
        ),
        compiler_params=pltpu.CompilerParams(vmem_limit_bytes=VMEM_LIMIT),
        name="near",
    )(orbitals, *shares)


def ahead_kernel(rows_ref, slab_ref, picked_ref, chosen_ref):
    npoints, slabs = rows_ref.shape
    spot = lax.broadcasted_iota(jnp.int32, (npoints, slab_ref.shape[0]), 1)
    for number in range(slabs):
        chosen = (rows_ref[:, number : number + 1] == spot).astype(jnp.float32)
        chosen = chosen.astype(jnp.bfloat16)
        if number:
            chosen_ref[number - 1] = chosen
        else:
            picked = jnp.dot(chosen, slab_ref[...], preferred_element_type=jnp.float32)
            picked_ref[...] = picked.astype(jnp.bfloat16)


def far_kernel(picked_ref, chosen_ref, *refs):
    *slab_refs, out_ref, parts_ref, sems = refs
    _, groups, _, length, slab_size = out_ref.shape
    picked = picked_ref[...].astype(jnp.float32)
    for number, slab_ref in enumerate(slab_refs[1:]):
        picked += jnp.dot(chosen_ref[number], slab_ref[...], preferred_element_type=jnp.float32)
    turned = [rows.astype(jnp.bfloat16) for rows in (picked, rotate(picked))]
    copies = []
    for number in range(SPLIT):
        for part in range(2):
            place = len(copies)
            pieces = product(turned[part], slab_refs[number][...], groups)
            for member in range(groups):
                parts_ref[place, crossed(member, groups)] = pieces[member]
            target = out_ref.at[lax.axis_index("lo") ^ number, :, part]
            copies.append(pltpu.make_async_copy(parts_ref.at[place], target, sems.at[place]))
            copies[-1].start()
    for copy in copies:
        copy.wait()


def make_far(rows, slabs, groups):
    slab_size, channels = slabs[0].shape
    npoints, _ = rows.shape
    length = npoints // groups
    vmem = pl.BlockSpec(memory_space=pltpu.VMEM)
    picked, chosen = pl.pallas_call(
        ahead_kernel,
        in_specs=[vmem] * 2,
        out_specs=[vmem] * 2,
        out_shape=[
            jax.ShapeDtypeStruct((npoints, channels), jnp.bfloat16),
            jax.ShapeDtypeStruct((len(slabs) - 1, npoints, slab_size), jnp.bfloat16),
        ],
        cost_estimate=pl.CostEstimate(flops=1_000_000, bytes_accessed=3_000, transcendentals=0),
        compiler_params=pltpu.CompilerParams(vmem_limit_bytes=VMEM_LIMIT),
        name="ahead",
    )(rows, slabs[0])
    return pl.pallas_call(
        far_kernel,
        in_specs=[vmem] * (2 + len(slabs)),
        out_specs=pl.BlockSpec(memory_space=pl.ANY),
        out_shape=jax.ShapeDtypeStruct((SPLIT, groups, 2, length, slab_size), jnp.bfloat16),
        scratch_shapes=[
            pltpu.VMEM((2 * SPLIT, groups, length, slab_size), jnp.bfloat16),
            pltpu.SemaphoreType.DMA((2 * SPLIT,)),
        ],
        cost_estimate=pl.CostEstimate(
            flops=60_000_000_000, bytes_accessed=180_000_000, transcendentals=0
        ),
        compiler_params=pltpu.CompilerParams(vmem_limit_bytes=VMEM_LIMIT),
        name="far",
    )(picked, chosen, *slabs)


def pair_kernel(scale, table_ref, near_ref, far_ref, out_ref, held_ref, sums_ref, sems):
    total_k, _, length, width = held_ref.shape
    transfers = table_ref.shape[0]
    table = table_ref[...]
    shifts = [lax.rem(total_k - table[transfer, 0], total_k) for transfer in range(transfers)]
    groups = near_ref.shape[0] // SPLIT
    held_ref[: total_k // 2] = near_ref[...].astype(jnp.float32)
    for member in range(groups):
        for k in range(SPLIT):
            far = far_ref[far_place(member, k, groups)]
            place = (member * SPLIT + k + total_k // 4) % (total_k // 2)
            held_ref[total_k // 2 + place] = far.astype(jnp.float32)

    count, columns = min(16, length), min(256, width)
    copies = []
    for start in range(0, length, count):
        rows = pl.ds(start, count)
        for column in range(0, width, columns):
            lanes = pl.ds(column, columns)

            def step(k, sums):
                real, imag = held_ref[k, 0, rows, lanes], held_ref[k, 1, rows, lanes]
                after = []
                for transfer in range(transfers):
                    other = lax.rem(k + total_k - shifts[transfer], total_k)
                    other_real = held_ref[other, 0, rows, lanes]
                    other_imag = held_ref[other, 1, rows, lanes]
                    after.append(sums[2 * transfer] + (real * other_real + imag * other_imag))
                    after.append(sums[2 * transfer + 1] + (imag * other_real - real * other_imag))
                return tuple(after)

            zero = jnp.zeros((count, columns), jnp.float32)
            sums = lax.fori_loop(0, total_k, step, (zero,) * (2 * transfers), unroll=32)
            for place, value in enumerate(sums):
                sums_ref[rows, place // 2, place % 2, lanes] = value * scale
        copies.append(
            pltpu.make_async_copy(sums_ref.at[rows], out_ref.at[rows], sems.at[start // count])
        )
        copies[-1].start()
    for copy in copies:
        copy.wait()


def make_pairs(near, far, table):
    half_k, _, length, slab_size = near.shape
    transfers = table.shape[0]
    out = jax.ShapeDtypeStruct((length, transfers, 2, slab_size), jnp.float32)
    vmem = pl.BlockSpec(memory_space=pltpu.VMEM)
    return pl.pallas_call(
        functools.partial(pair_kernel, 1.0 / math.sqrt(2 * half_k)),
        in_specs=[vmem, vmem, vmem],
        out_specs=pl.BlockSpec(memory_space=pl.ANY),
        out_shape=out,
        scratch_shapes=[
            pltpu.VMEM((2 * half_k, 2, length, slab_size), jnp.float32),
            pltpu.VMEM(out.shape, jnp.float32),
            pltpu.SemaphoreType.DMA((length // min(16, length),)),
        ],
        compiler_params=pltpu.CompilerParams(vmem_limit_bytes=VMEM_LIMIT),
        name="pairs",
    )(table, near, far)


def on_device(orbitals, minus_table, points):
    kdevice, slab_size, channels = orbitals.shape
    half = lax.axis_index("half")
    groups = lax.axis_size("quarter") * lax.axis_size("inner")
    slabs = lax.axis_size("hi") * lax.axis_size("lo")
    total_k = 2 * groups * kdevice
    points = points.reshape(1, -1)
    here = lax.axis_index("hi") * SPLIT + lax.axis_index("lo")

    lo = lax.axis_index("lo")
    mine = lax.dynamic_index_in_dim(orbitals, lo, 0, keepdims=False)
    other = lax.dynamic_index_in_dim(orbitals, 1 - lo, 0, keepdims=False)
    share = make_front(mine, other, points)
    share, mine, other = lax.optimization_barrier((share, mine, other))
    shares = [share] + [swap(share, False, x) for x in range(1, slabs)]
    far = [swap(other if x & 1 else mine, True, x) for x in range(slabs)]

    def send(fields, around):
        fields = fields.reshape((-1,) + fields.shape[-3:])
        return lax.all_to_all(fields, around, split_axis=0, concat_axis=0, tiled=True)

    near_fields = make_near(orbitals, shares, groups)
    npoints = points.shape[1] // 2
    wanted = lax.dynamic_slice_in_dim(points[0], half * npoints, npoints)
    starts = jnp.stack([(here ^ x) * slab_size for x in range(slabs)])
    rows = wanted[:, None] - starts[None, :]
    near_fields, rows = lax.optimization_barrier((near_fields, rows))
    far_fields = make_far(rows, far, groups)
    near_fields = send(near_fields, ("quarter", "inner"))
    near_fields, far_fields = lax.optimization_barrier((near_fields, far_fields))
    far_fields = send(far_fields, ("lo", "inner", "quarter"))
    return make_pairs(near_fields, far_fields, minus_table)


def solution(mesh):
    kplaces, slabs = mesh.shape["ka"], mesh.shape["ga"]
    devices = mesh.devices.reshape(2, 2, kplaces // 4, slabs // SPLIT, SPLIT)
    finer = Mesh(devices, KA + GA)
    return jax.shard_map(
        on_device,
        mesh=finer,
        in_specs=(P(KA, GA, None), P(), P()),
        out_specs=P(KA, None, None, GA),
        check_vma=False,
    )
```

```python
import functools
import math

import jax
import jax.numpy as jnp
from jax import lax
from jax.experimental import pallas as pl
from jax.experimental.pallas import tpu as pltpu
from jax.sharding import Mesh
from jax.sharding import PartitionSpec as P

VMEM_LIMIT = 40 * 1024 * 1024
SPLIT = 2
KA, GA = ("half", "quarter", "inner"), ("hi", "lo")


def swap(block, mirror, other):
    half, quarter, inner, hi, lo = (lax.axis_size(name) for name in KA + GA)
    slabs = hi * lo
    route = []
    for place in range(half * quarter * inner * slabs):
        kplace, slab = divmod(place, slabs)
        part, within = divmod(kplace, inner)
        part = half * quarter - 1 - part if mirror else part
        route.append((place, (part * inner + within) * slabs + (slab ^ other)))
    return lax.ppermute(block, KA + GA, route)


def one_hot(points_ref, half, slab, slab_size, npoints):
    first = pl.multiple_of(half * npoints, npoints)
    wanted = points_ref[:, pl.ds(first, npoints)] - slab * slab_size
    spot = lax.broadcasted_iota(jnp.int32, (slab_size, npoints), 0)
    return (spot == wanted).astype(jnp.float32).astype(jnp.bfloat16)


def pick(chosen, slab):
    return lax.dot_general(
        chosen, slab, (((0,), (0,)), ((), ())), preferred_element_type=jnp.float32
    )


def crossed(member, groups):
    quarter, inner = divmod(member, groups // 2)
    return inner * 2 + quarter


def far_place(member, lo, groups):
    return lo * groups + crossed(member, groups)


def rotate(picked):
    middle = picked.shape[1] // 2
    return jnp.concatenate([-picked[:, middle:], picked[:, :middle]], axis=1)


def product(rows, slab, groups):
    out = lax.dot_general(
        rows, slab, (((1,), (1,)), ((), ())), preferred_element_type=jnp.float32
    )
    return out.reshape(groups, -1, out.shape[1]).astype(jnp.bfloat16)


def front_kernel(points_ref, mine_ref, other_ref, picked_ref):
    slab_size, _ = mine_ref.shape
    _, npoints, _ = picked_ref.shape
    mine = lax.axis_index("lo")
    here = lax.axis_index("hi") * SPLIT + mine
    chosen = one_hot(points_ref, lax.axis_index("half"), here, slab_size, npoints)
    for k, slab_ref in ((mine, mine_ref), (1 - mine, other_ref)):
        picked_ref[k] = pick(chosen, slab_ref[...]).astype(jnp.bfloat16)


def make_front(mine, other, points):
    vmem = pl.BlockSpec(memory_space=pltpu.VMEM)
    return pl.pallas_call(
        front_kernel,
        in_specs=[vmem] * 3,
        out_specs=vmem,
        out_shape=jax.ShapeDtypeStruct(
            (SPLIT, points.shape[1] // 2, mine.shape[1]), jnp.bfloat16
        ),
        compiler_params=pltpu.CompilerParams(vmem_limit_bytes=VMEM_LIMIT),
        name="front",
    )(points, mine, other)


def near_kernel(orbitals_ref, *refs):
    *picked_refs, out_ref = refs
    groups = out_ref.shape[0]
    rows = sum(picked_ref[0].astype(jnp.float32) for picked_ref in picked_refs)
    for part, turned in enumerate((rows, rotate(rows))):
        out_ref[:, 0, part] = product(turned.astype(jnp.bfloat16), orbitals_ref[0], groups)


def make_near(orbitals, shares, groups):
    kdevice, slab_size, channels = orbitals.shape
    npoints = shares[0].shape[1]
    length = npoints // groups
    return pl.pallas_call(
        near_kernel,
        grid=(kdevice,),
        in_specs=[pl.BlockSpec((1, slab_size, channels), lambda k: (k, 0, 0))]
        + [pl.BlockSpec((1, npoints, channels), lambda k: (k, 0, 0)) for _ in shares],
        out_specs=pl.BlockSpec((groups, 1, 2, length, slab_size), lambda k: (0, k, 0, 0, 0)),
        out_shape=jax.ShapeDtypeStruct((groups, kdevice, 2, length, slab_size), jnp.bfloat16),
        cost_estimate=pl.CostEstimate(
            flops=1_000_000_000, bytes_accessed=3_000_000, transcendentals=0
        ),
        compiler_params=pltpu.CompilerParams(vmem_limit_bytes=VMEM_LIMIT),
        name="near",
    )(orbitals, *shares)


def ahead_kernel(rows_ref, slab_ref, picked_ref, chosen_ref):
    npoints, slabs = rows_ref.shape
    spot = lax.broadcasted_iota(jnp.int32, (npoints, slab_ref.shape[0]), 1)
    for number in range(slabs):
        chosen = (rows_ref[:, number : number + 1] == spot).astype(jnp.float32)
        chosen = chosen.astype(jnp.bfloat16)
        if number:
            chosen_ref[number - 1] = chosen
        else:
            picked = jnp.dot(chosen, slab_ref[...], preferred_element_type=jnp.float32)
            picked_ref[...] = picked.astype(jnp.bfloat16)


def far_kernel(picked_ref, chosen_ref, *refs):
    *slab_refs, out_ref, parts_ref, sems = refs
    _, groups, _, length, slab_size = out_ref.shape
    picked = picked_ref[...].astype(jnp.float32)
    for number, slab_ref in enumerate(slab_refs[1:]):
        picked += jnp.dot(chosen_ref[number], slab_ref[...], preferred_element_type=jnp.float32)
    turned = [rows.astype(jnp.bfloat16) for rows in (picked, rotate(picked))]
    copies = []
    for number in range(SPLIT):
        for part in range(2):
            place = len(copies)
            pieces = product(turned[part], slab_refs[number][...], groups)
            for member in range(groups):
                parts_ref[place, crossed(member, groups)] = pieces[member]
            target = out_ref.at[lax.axis_index("lo") ^ number, :, part]
            copies.append(pltpu.make_async_copy(parts_ref.at[place], target, sems.at[place]))
            copies[-1].start()
    for copy in copies:
        copy.wait()


def make_far(rows, slabs, groups):
    slab_size, channels = slabs[0].shape
    npoints, _ = rows.shape
    length = npoints // groups
    vmem = pl.BlockSpec(memory_space=pltpu.VMEM)
    picked, chosen = pl.pallas_call(
        ahead_kernel,
        in_specs=[vmem] * 2,
        out_specs=[vmem] * 2,
        out_shape=[
            jax.ShapeDtypeStruct((npoints, channels), jnp.bfloat16),
            jax.ShapeDtypeStruct((len(slabs) - 1, npoints, slab_size), jnp.bfloat16),
        ],
        cost_estimate=pl.CostEstimate(flops=1_000_000, bytes_accessed=3_000, transcendentals=0),
        compiler_params=pltpu.CompilerParams(vmem_limit_bytes=VMEM_LIMIT),
        name="ahead",
    )(rows, slabs[0])
    return pl.pallas_call(
        far_kernel,
        in_specs=[vmem] * (2 + len(slabs)),
        out_specs=pl.BlockSpec(memory_space=pl.ANY),
        out_shape=jax.ShapeDtypeStruct((SPLIT, groups, 2, length, slab_size), jnp.bfloat16),
        scratch_shapes=[
            pltpu.VMEM((2 * SPLIT, groups, length, slab_size), jnp.bfloat16),
            pltpu.SemaphoreType.DMA((2 * SPLIT,)),
        ],
        cost_estimate=pl.CostEstimate(
            flops=60_000_000_000, bytes_accessed=180_000_000, transcendentals=0
        ),
        compiler_params=pltpu.CompilerParams(vmem_limit_bytes=VMEM_LIMIT),
        name="far",
    )(picked, chosen, *slabs)


def pair_kernel(scale, table_ref, near_ref, far_ref, out_ref, held_ref, sums_ref, sems):
    total_k, _, length, width = held_ref.shape
    transfers = table_ref.shape[0]
    table = table_ref[...]
    shifts = []
    for transfer in range(transfers):
        place = table[transfer, 0]
        far_place_of = total_k // 2 + lax.rem(place + total_k // 4, total_k // 2)
        shifts.append(total_k - jnp.where(place < total_k // 2, place, far_place_of))
    groups = near_ref.shape[0] // SPLIT
    held_ref[: total_k // 2] = near_ref[...].astype(jnp.float32)
    for member in range(groups):
        for k in range(SPLIT):
            far = far_ref[far_place(member, k, groups)]
            place = (member * SPLIT + k + total_k // 4) % (total_k // 2)
            held_ref[total_k // 2 + place] = far.astype(jnp.float32)

    count, columns = min(16, length), min(256, width)
    copies = []
    for start in range(0, length, count):
        rows = pl.ds(start, count)
        for column in range(0, width, columns):
            lanes = pl.ds(column, columns)

            def step(k, sums):
                real, imag = held_ref[k, 0, rows, lanes], held_ref[k, 1, rows, lanes]
                after = []
                for transfer in range(transfers):
                    other = lax.rem(k + total_k - shifts[transfer], total_k)
                    other_real = held_ref[other, 0, rows, lanes]
                    other_imag = held_ref[other, 1, rows, lanes]
                    after.append(sums[2 * transfer] + (real * other_real + imag * other_imag))
                    after.append(sums[2 * transfer + 1] + (imag * other_real - real * other_imag))
                return tuple(after)

            zero = jnp.zeros((count, columns), jnp.float32)
            sums = lax.fori_loop(0, total_k, step, (zero,) * (2 * transfers), unroll=32)
            for place, value in enumerate(sums):
                sums_ref[rows, place // 2, place % 2, lanes] = value * scale
        copies.append(
            pltpu.make_async_copy(sums_ref.at[rows], out_ref.at[rows], sems.at[start // count])
        )
        copies[-1].start()
    for copy in copies:
        copy.wait()


def make_pairs(near, far, table):
    half_k, _, length, slab_size = near.shape
    transfers = table.shape[0]
    out = jax.ShapeDtypeStruct((length, transfers, 2, slab_size), jnp.float32)
    vmem = pl.BlockSpec(memory_space=pltpu.VMEM)
    return pl.pallas_call(
        functools.partial(pair_kernel, 1.0 / math.sqrt(2 * half_k)),
        in_specs=[vmem, vmem, vmem],
        out_specs=pl.BlockSpec(memory_space=pl.ANY),
        out_shape=out,
        scratch_shapes=[
            pltpu.VMEM((2 * half_k, 2, length, slab_size), jnp.float32),
            pltpu.VMEM(out.shape, jnp.float32),
            pltpu.SemaphoreType.DMA((length // min(16, length),)),
        ],
        compiler_params=pltpu.CompilerParams(vmem_limit_bytes=VMEM_LIMIT),
        name="pairs",
    )(table, near, far)


def on_device(orbitals, minus_table, points):
    kdevice, slab_size, channels = orbitals.shape
    half = lax.axis_index("half")
    groups = lax.axis_size("quarter") * lax.axis_size("inner")
    slabs = lax.axis_size("hi") * lax.axis_size("lo")
    total_k = 2 * groups * kdevice
    points = points.reshape(1, -1)
    here = lax.axis_index("hi") * SPLIT + lax.axis_index("lo")

    lo = lax.axis_index("lo")
    mine = lax.dynamic_index_in_dim(orbitals, lo, 0, keepdims=False)
    other = lax.dynamic_index_in_dim(orbitals, 1 - lo, 0, keepdims=False)
    share = make_front(mine, other, points)
    share, mine, other = lax.optimization_barrier((share, mine, other))
    shares = [share] + [swap(share, False, x) for x in range(1, slabs)]
    far = [swap(other if x & 1 else mine, True, x) for x in range(slabs)]

    def send(fields, around):
        fields = fields.reshape((-1,) + fields.shape[-3:])
        return lax.all_to_all(fields, around, split_axis=0, concat_axis=0, tiled=True)

    near_fields = make_near(orbitals, shares, groups)
    npoints = points.shape[1] // 2
    wanted = lax.dynamic_slice_in_dim(points[0], half * npoints, npoints)
    starts = jnp.stack([(here ^ x) * slab_size for x in range(slabs)])
    rows = wanted[:, None] - starts[None, :]
    near_fields, rows = lax.optimization_barrier((near_fields, rows))
    far_fields = make_far(rows, far, groups)
    near_fields = send(near_fields, ("quarter", "inner"))
    near_fields, far_fields = lax.optimization_barrier((near_fields, far_fields))
    far_fields = send(far_fields, ("lo", "inner", "quarter"))

    def mirrored(kpoints):
        return total_k // 2 + (kpoints + total_k // 4) % (total_k // 2)

    turn = half * (total_k // 2)
    table = (jnp.roll(minus_table, -turn, axis=1) - turn) % total_k
    table = jnp.where(table < total_k // 2, table, mirrored(table))
    first, third, fourth = jnp.split(table, (total_k // 2, 3 * total_k // 4), axis=1)
    return make_pairs(near_fields, far_fields, jnp.concatenate([first, fourth, third], axis=1))


def solution(mesh):
    kplaces, slabs = mesh.shape["ka"], mesh.shape["ga"]
    devices = mesh.devices.reshape(2, 2, kplaces // 4, slabs // SPLIT, SPLIT)
    finer = Mesh(devices, KA + GA)
    return jax.shard_map(
        on_device,
        mesh=finer,
        in_specs=(P(KA, GA, None), P(), P()),
        out_specs=P(KA, None, None, GA),
        check_vma=False,
    )
```

```python
import functools
import math

import jax
import jax.numpy as jnp
from jax import lax
from jax.experimental import pallas as pl
from jax.experimental.pallas import tpu as pltpu
from jax.sharding import Mesh
from jax.sharding import PartitionSpec as P

VMEM_LIMIT = 40 * 1024 * 1024
SPLIT = 2
KA, GA = ("half", "quarter", "inner"), ("hi", "lo")


def swap(block, mirror, other):
    half, quarter, inner, hi, lo = (lax.axis_size(name) for name in KA + GA)
    slabs = hi * lo
    route = []
    for place in range(half * quarter * inner * slabs):
        kplace, slab = divmod(place, slabs)
        part, within = divmod(kplace, inner)
        part = half * quarter - 1 - part if mirror else part
        route.append((place, (part * inner + within) * slabs + (slab ^ other)))
    return lax.ppermute(block, KA + GA, route)


def one_hot(points_ref, half, slab, slab_size, npoints):
    first = pl.multiple_of(half * npoints, npoints)
    wanted = points_ref[:, pl.ds(first, npoints)] - slab * slab_size
    spot = lax.broadcasted_iota(jnp.int32, (slab_size, npoints), 0)
    return (spot == wanted).astype(jnp.float32).astype(jnp.bfloat16)


def pick(chosen, slab):
    return lax.dot_general(
        chosen, slab, (((0,), (0,)), ((), ())), preferred_element_type=jnp.float32
    )


def crossed(member, groups):
    quarter, inner = divmod(member, groups // 2)
    return inner * 2 + quarter


def far_place(member, lo, groups):
    return lo * groups + crossed(member, groups)


def rotate(picked):
    middle = picked.shape[1] // 2
    return jnp.concatenate([-picked[:, middle:], picked[:, :middle]], axis=1)


def product(rows, slab, groups):
    out = lax.dot_general(
        rows, slab, (((1,), (1,)), ((), ())), preferred_element_type=jnp.float32
    )
    return out.reshape(groups, -1, out.shape[1]).astype(jnp.bfloat16)


def front_kernel(points_ref, mine_ref, other_ref, picked_ref):
    slab_size, _ = mine_ref.shape
    _, npoints, _ = picked_ref.shape
    mine = lax.axis_index("lo")
    here = lax.axis_index("hi") * SPLIT + mine
    chosen = one_hot(points_ref, lax.axis_index("half"), here, slab_size, npoints)
    for k, slab_ref in ((mine, mine_ref), (1 - mine, other_ref)):
        picked_ref[k] = pick(chosen, slab_ref[...]).astype(jnp.bfloat16)


def make_front(mine, other, points):
    vmem = pl.BlockSpec(memory_space=pltpu.VMEM)
    return pl.pallas_call(
        front_kernel,
        in_specs=[vmem] * 3,
        out_specs=vmem,
        out_shape=jax.ShapeDtypeStruct(
            (SPLIT, points.shape[1] // 2, mine.shape[1]), jnp.bfloat16
        ),
        compiler_params=pltpu.CompilerParams(vmem_limit_bytes=VMEM_LIMIT),
        name="front",
    )(points, mine, other)


def near_kernel(orbitals_ref, *refs):
    *picked_refs, out_ref = refs
    groups = out_ref.shape[0]
    rows = sum(picked_ref[0].astype(jnp.float32) for picked_ref in picked_refs)
    for part, turned in enumerate((rows, rotate(rows))):
        out_ref[:, 0, part] = product(turned.astype(jnp.bfloat16), orbitals_ref[0], groups)


def make_near(orbitals, shares, groups):
    kdevice, slab_size, channels = orbitals.shape
    npoints = shares[0].shape[1]
    length = npoints // groups
    return pl.pallas_call(
        near_kernel,
        grid=(kdevice,),
        in_specs=[pl.BlockSpec((1, slab_size, channels), lambda k: (k, 0, 0))]
        + [pl.BlockSpec((1, npoints, channels), lambda k: (k, 0, 0)) for _ in shares],
        out_specs=pl.BlockSpec((groups, 1, 2, length, slab_size), lambda k: (0, k, 0, 0, 0)),
        out_shape=jax.ShapeDtypeStruct((groups, kdevice, 2, length, slab_size), jnp.bfloat16),
        cost_estimate=pl.CostEstimate(
            flops=3_000_000_000, bytes_accessed=9_000_000, transcendentals=0
        ),
        compiler_params=pltpu.CompilerParams(vmem_limit_bytes=VMEM_LIMIT),
        name="near",
    )(orbitals, *shares)


def ahead_kernel(rows_ref, slab_ref, picked_ref, chosen_ref):
    npoints, slabs = rows_ref.shape
    spot = lax.broadcasted_iota(jnp.int32, (npoints, slab_ref.shape[0]), 1)
    for number in range(slabs):
        chosen = (rows_ref[:, number : number + 1] == spot).astype(jnp.float32)
        chosen = chosen.astype(jnp.bfloat16)
        if number:
            chosen_ref[number - 1] = chosen
        else:
            picked = jnp.dot(chosen, slab_ref[...], preferred_element_type=jnp.float32)
            picked_ref[...] = picked.astype(jnp.bfloat16)


def far_kernel(picked_ref, chosen_ref, *refs):
    *slab_refs, out_ref, parts_ref, sems = refs
    _, groups, _, length, slab_size = out_ref.shape
    picked = picked_ref[...].astype(jnp.float32)
    for number, slab_ref in enumerate(slab_refs[1:]):
        picked += jnp.dot(chosen_ref[number], slab_ref[...], preferred_element_type=jnp.float32)
    turned = [rows.astype(jnp.bfloat16) for rows in (picked, rotate(picked))]
    copies = []
    for number in range(SPLIT):
        for part in range(2):
            place = len(copies)
            pieces = product(turned[part], slab_refs[number][...], groups)
            for member in range(groups):
                parts_ref[place, crossed(member, groups)] = pieces[member]
            target = out_ref.at[lax.axis_index("lo") ^ number, :, part]
            copies.append(pltpu.make_async_copy(parts_ref.at[place], target, sems.at[place]))
            copies[-1].start()
    for copy in copies:
        copy.wait()


def make_far(rows, slabs, groups):
    slab_size, channels = slabs[0].shape
    npoints, _ = rows.shape
    length = npoints // groups
    vmem = pl.BlockSpec(memory_space=pltpu.VMEM)
    picked, chosen = pl.pallas_call(
        ahead_kernel,
        in_specs=[vmem] * 2,
        out_specs=[vmem] * 2,
        out_shape=[
            jax.ShapeDtypeStruct((npoints, channels), jnp.bfloat16),
            jax.ShapeDtypeStruct((len(slabs) - 1, npoints, slab_size), jnp.bfloat16),
        ],
        cost_estimate=pl.CostEstimate(flops=1_000_000, bytes_accessed=3_000, transcendentals=0),
        compiler_params=pltpu.CompilerParams(vmem_limit_bytes=VMEM_LIMIT),
        name="ahead",
    )(rows, slabs[0])
    return pl.pallas_call(
        far_kernel,
        in_specs=[vmem] * (2 + len(slabs)),
        out_specs=pl.BlockSpec(memory_space=pl.ANY),
        out_shape=jax.ShapeDtypeStruct((SPLIT, groups, 2, length, slab_size), jnp.bfloat16),
        scratch_shapes=[
            pltpu.VMEM((2 * SPLIT, groups, length, slab_size), jnp.bfloat16),
            pltpu.SemaphoreType.DMA((2 * SPLIT,)),
        ],
        cost_estimate=pl.CostEstimate(
            flops=60_000_000_000, bytes_accessed=180_000_000, transcendentals=0
        ),
        compiler_params=pltpu.CompilerParams(vmem_limit_bytes=VMEM_LIMIT),
        name="far",
    )(picked, chosen, *slabs)


def pair_kernel(scale, table_ref, near_ref, far_ref, out_ref, held_ref, sums_ref, sems):
    total_k, _, length, width = held_ref.shape
    transfers = table_ref.shape[0]
    table = table_ref[...]
    shifts = [lax.rem(total_k - table[transfer, 0], total_k) for transfer in range(transfers)]
    groups = near_ref.shape[0] // SPLIT
    held_ref[: total_k // 2] = near_ref[...].astype(jnp.float32)
    for member in range(groups):
        for k in range(SPLIT):
            far = far_ref[far_place(member, k, groups)]
            place = (member * SPLIT + k + total_k // 4) % (total_k // 2)
            held_ref[total_k // 2 + place] = far.astype(jnp.float32)

    count, columns = min(16, length), min(256, width)
    copies = []
    for start in range(0, length, count):
        rows = pl.ds(start, count)
        for column in range(0, width, columns):
            lanes = pl.ds(column, columns)

            def step(k, sums):
                real, imag = held_ref[k, 0, rows, lanes], held_ref[k, 1, rows, lanes]
                after = []
                for transfer in range(transfers):
                    other = lax.rem(k + total_k - shifts[transfer], total_k)
                    other_real = held_ref[other, 0, rows, lanes]
                    other_imag = held_ref[other, 1, rows, lanes]
                    after.append(sums[2 * transfer] + (real * other_real + imag * other_imag))
                    after.append(sums[2 * transfer + 1] + (imag * other_real - real * other_imag))
                return tuple(after)

            zero = jnp.zeros((count, columns), jnp.float32)
            sums = lax.fori_loop(0, total_k, step, (zero,) * (2 * transfers), unroll=32)
            for place, value in enumerate(sums):
                sums_ref[rows, place // 2, place % 2, lanes] = value * scale
        copies.append(
            pltpu.make_async_copy(sums_ref.at[rows], out_ref.at[rows], sems.at[start // count])
        )
        copies[-1].start()
    for copy in copies:
        copy.wait()


def make_pairs(near, far, table):
    half_k, _, length, slab_size = near.shape
    transfers = table.shape[0]
    out = jax.ShapeDtypeStruct((length, transfers, 2, slab_size), jnp.float32)
    vmem = pl.BlockSpec(memory_space=pltpu.VMEM)
    return pl.pallas_call(
        functools.partial(pair_kernel, 1.0 / math.sqrt(2 * half_k)),
        in_specs=[vmem, vmem, vmem],
        out_specs=pl.BlockSpec(memory_space=pl.ANY),
        out_shape=out,
        scratch_shapes=[
            pltpu.VMEM((2 * half_k, 2, length, slab_size), jnp.float32),
            pltpu.VMEM(out.shape, jnp.float32),
            pltpu.SemaphoreType.DMA((length // min(16, length),)),
        ],
        compiler_params=pltpu.CompilerParams(vmem_limit_bytes=VMEM_LIMIT),
        name="pairs",
    )(table, near, far)


def on_device(orbitals, minus_table, points):
    kdevice, slab_size, channels = orbitals.shape
    half = lax.axis_index("half")
    groups = lax.axis_size("quarter") * lax.axis_size("inner")
    slabs = lax.axis_size("hi") * lax.axis_size("lo")
    total_k = 2 * groups * kdevice
    points = points.reshape(1, -1)
    here = lax.axis_index("hi") * SPLIT + lax.axis_index("lo")

    lo = lax.axis_index("lo")
    mine = lax.dynamic_index_in_dim(orbitals, lo, 0, keepdims=False)
    other = lax.dynamic_index_in_dim(orbitals, 1 - lo, 0, keepdims=False)
    share = make_front(mine, other, points)
    share, mine, other = lax.optimization_barrier((share, mine, other))
    shares = [share] + [swap(share, False, x) for x in range(1, slabs)]
    far = [swap(other if x & 1 else mine, True, x) for x in range(slabs)]

    def send(fields, around):
        fields = fields.reshape((-1,) + fields.shape[-3:])
        return lax.all_to_all(fields, around, split_axis=0, concat_axis=0, tiled=True)

    near_fields = make_near(orbitals, shares, groups)
    npoints = points.shape[1] // 2
    wanted = lax.dynamic_slice_in_dim(points[0], half * npoints, npoints)
    starts = jnp.stack([(here ^ x) * slab_size for x in range(slabs)])
    rows = wanted[:, None] - starts[None, :]
    near_fields, rows = lax.optimization_barrier((near_fields, rows))
    far_fields = make_far(rows, far, groups)
    near_fields = send(near_fields, ("quarter", "inner"))
    near_fields, far_fields = lax.optimization_barrier((near_fields, far_fields))
    far_fields = send(far_fields, ("lo", "inner", "quarter"))
    return make_pairs(near_fields, far_fields, minus_table)


def solution(mesh):
    kplaces, slabs = mesh.shape["ka"], mesh.shape["ga"]
    devices = mesh.devices.reshape(2, 2, kplaces // 4, slabs // SPLIT, SPLIT)
    finer = Mesh(devices, KA + GA)
    return jax.shard_map(
        on_device,
        mesh=finer,
        in_specs=(P(KA, GA, None), P(), P()),
        out_specs=P(KA, None, None, GA),
        check_vma=False,
    )
```

```python
import functools
import math

import jax
import jax.numpy as jnp
from jax import lax
from jax.experimental import pallas as pl
from jax.experimental.pallas import tpu as pltpu
from jax.sharding import Mesh
from jax.sharding import PartitionSpec as P

VMEM_LIMIT = 40 * 1024 * 1024
SPLIT = 2
KA, GA = ("half", "quarter", "inner"), ("hi", "lo")


def swap(block, mirror, other):
    half, quarter, inner, hi, lo = (lax.axis_size(name) for name in KA + GA)
    slabs = hi * lo
    route = []
    for place in range(half * quarter * inner * slabs):
        kplace, slab = divmod(place, slabs)
        part, within = divmod(kplace, inner)
        part = half * quarter - 1 - part if mirror else part
        route.append((place, (part * inner + within) * slabs + (slab ^ other)))
    return lax.ppermute(block, KA + GA, route)


def one_hot(points_ref, half, slab, slab_size, npoints):
    first = pl.multiple_of(half * npoints, npoints)
    wanted = points_ref[:, pl.ds(first, npoints)] - slab * slab_size
    spot = lax.broadcasted_iota(jnp.int32, (slab_size, npoints), 0)
    return (spot == wanted).astype(jnp.float32).astype(jnp.bfloat16)


def pick(chosen, slab):
    return lax.dot_general(
        chosen, slab, (((0,), (0,)), ((), ())), preferred_element_type=jnp.float32
    )


def crossed(member, groups):
    quarter, inner = divmod(member, groups // 2)
    return inner * 2 + quarter


def far_place(member, lo, groups):
    return lo * groups + crossed(member, groups)


def rotate(picked):
    middle = picked.shape[1] // 2
    return jnp.concatenate([-picked[:, middle:], picked[:, :middle]], axis=1)


def product(rows, slab, groups):
    out = lax.dot_general(
        rows, slab, (((1,), (1,)), ((), ())), preferred_element_type=jnp.float32
    )
    return out.reshape(groups, -1, out.shape[1]).astype(jnp.bfloat16)


def front_kernel(points_ref, mine_ref, other_ref, picked_ref):
    slab_size, _ = mine_ref.shape
    _, npoints, _ = picked_ref.shape
    mine = lax.axis_index("lo")
    here = lax.axis_index("hi") * SPLIT + mine
    chosen = one_hot(points_ref, lax.axis_index("half"), here, slab_size, npoints)
    for k, slab_ref in ((mine, mine_ref), (1 - mine, other_ref)):
        picked_ref[k] = pick(chosen, slab_ref[...]).astype(jnp.bfloat16)


def make_front(mine, other, points):
    vmem = pl.BlockSpec(memory_space=pltpu.VMEM)
    return pl.pallas_call(
        front_kernel,
        in_specs=[vmem] * 3,
        out_specs=vmem,
        out_shape=jax.ShapeDtypeStruct(
            (SPLIT, points.shape[1] // 2, mine.shape[1]), jnp.bfloat16
        ),
        compiler_params=pltpu.CompilerParams(vmem_limit_bytes=VMEM_LIMIT),
        name="front",
    )(points, mine, other)


def near_kernel(orbitals_ref, *refs):
    *picked_refs, out_ref = refs
    groups = out_ref.shape[0]
    rows = sum(picked_ref[0].astype(jnp.float32) for picked_ref in picked_refs)
    for part, turned in enumerate((rows, rotate(rows))):
        out_ref[:, 0, part] = product(turned.astype(jnp.bfloat16), orbitals_ref[0], groups)


def make_near(orbitals, shares, groups):
    kdevice, slab_size, channels = orbitals.shape
    npoints = shares[0].shape[1]
    length = npoints // groups
    return pl.pallas_call(
        near_kernel,
        grid=(kdevice,),
        in_specs=[pl.BlockSpec((1, slab_size, channels), lambda k: (k, 0, 0))]
        + [pl.BlockSpec((1, npoints, channels), lambda k: (k, 0, 0)) for _ in shares],
        out_specs=pl.BlockSpec((groups, 1, 2, length, slab_size), lambda k: (0, k, 0, 0, 0)),
        out_shape=jax.ShapeDtypeStruct((groups, kdevice, 2, length, slab_size), jnp.bfloat16),
        cost_estimate=pl.CostEstimate(
            flops=1_000_000_000, bytes_accessed=3_000_000, transcendentals=0
        ),
        compiler_params=pltpu.CompilerParams(vmem_limit_bytes=VMEM_LIMIT),
        name="near",
    )(orbitals, *shares)


def ahead_kernel(rows_ref, slab_ref, picked_ref, chosen_ref):
    npoints, slabs = rows_ref.shape
    spot = lax.broadcasted_iota(jnp.int32, (npoints, slab_ref.shape[0]), 1)
    for number in range(slabs):
        chosen = (rows_ref[:, number : number + 1] == spot).astype(jnp.float32)
        chosen = chosen.astype(jnp.bfloat16)
        if number:
            chosen_ref[number - 1] = chosen
        else:
            picked = jnp.dot(chosen, slab_ref[...], preferred_element_type=jnp.float32)
            picked_ref[...] = picked.astype(jnp.bfloat16)


def far_kernel(picked_ref, chosen_ref, *refs):
    *slab_refs, out_ref, parts_ref, sems = refs
    _, groups, _, length, slab_size = out_ref.shape
    picked = picked_ref[...].astype(jnp.float32)
    for number, slab_ref in enumerate(slab_refs[1:]):
        picked += jnp.dot(chosen_ref[number], slab_ref[...], preferred_element_type=jnp.float32)
    turned = [rows.astype(jnp.bfloat16) for rows in (picked, rotate(picked))]
    copies = []
    for number in range(SPLIT):
        for part in range(2):
            place = len(copies)
            pieces = product(turned[part], slab_refs[number][...], groups)
            for member in range(groups):
                parts_ref[place, crossed(member, groups)] = pieces[member]
            target = out_ref.at[lax.axis_index("lo") ^ number, :, part]
            copies.append(pltpu.make_async_copy(parts_ref.at[place], target, sems.at[place]))
            copies[-1].start()
    for copy in copies:
        copy.wait()


def make_far(rows, slabs, groups):
    slab_size, channels = slabs[0].shape
    npoints, _ = rows.shape
    length = npoints // groups
    vmem = pl.BlockSpec(memory_space=pltpu.VMEM)
    picked, chosen = pl.pallas_call(
        ahead_kernel,
        in_specs=[vmem] * 2,
        out_specs=[vmem] * 2,
        out_shape=[
            jax.ShapeDtypeStruct((npoints, channels), jnp.bfloat16),
            jax.ShapeDtypeStruct((len(slabs) - 1, npoints, slab_size), jnp.bfloat16),
        ],
        cost_estimate=pl.CostEstimate(flops=1_000_000, bytes_accessed=3_000, transcendentals=0),
        compiler_params=pltpu.CompilerParams(vmem_limit_bytes=VMEM_LIMIT),
        name="ahead",
    )(rows, slabs[0])
    return pl.pallas_call(
        far_kernel,
        in_specs=[vmem] * (2 + len(slabs)),
        out_specs=pl.BlockSpec(memory_space=pl.ANY),
        out_shape=jax.ShapeDtypeStruct((SPLIT, groups, 2, length, slab_size), jnp.bfloat16),
        scratch_shapes=[
            pltpu.VMEM((2 * SPLIT, groups, length, slab_size), jnp.bfloat16),
            pltpu.SemaphoreType.DMA((2 * SPLIT,)),
        ],
        cost_estimate=pl.CostEstimate(
            flops=60_000_000_000, bytes_accessed=180_000_000, transcendentals=0
        ),
        compiler_params=pltpu.CompilerParams(vmem_limit_bytes=VMEM_LIMIT),
        name="far",
    )(picked, chosen, *slabs)


def pair_kernel(scale, table_ref, near_ref, far_ref, out_ref, held_ref, sums_ref, sems):
    total_k, _, length, width = held_ref.shape
    transfers = table_ref.shape[0]
    table = table_ref[...]
    shifts = []
    for transfer in range(transfers):
        place = table[transfer, 0]
        far_place_of = total_k // 2 + lax.rem(place + total_k // 4, total_k // 2)
        shifts.append(total_k - jnp.where(place < total_k // 2, place, far_place_of))
    groups = near_ref.shape[0] // SPLIT
    held_ref[: total_k // 2] = near_ref[...].astype(jnp.float32)
    for member in range(groups):
        for k in range(SPLIT):
            far = far_ref[far_place(member, k, groups)]
            place = (member * SPLIT + k + total_k // 4) % (total_k // 2)
            held_ref[total_k // 2 + place] = far.astype(jnp.float32)

    count, columns = min(16, length), min(256, width)
    copies = []
    for start in range(0, length, count):
        rows = pl.ds(start, count)
        for column in range(0, width, columns):
            lanes = pl.ds(column, columns)

            def step(k, sums):
                real, imag = held_ref[k, 0, rows, lanes], held_ref[k, 1, rows, lanes]
                after = []
                for transfer in range(transfers):
                    other = lax.rem(k + total_k - shifts[transfer], total_k)
                    other_real = held_ref[other, 0, rows, lanes]
                    other_imag = held_ref[other, 1, rows, lanes]
                    after.append(sums[2 * transfer] + (real * other_real + imag * other_imag))
                    after.append(sums[2 * transfer + 1] + (imag * other_real - real * other_imag))
                return tuple(after)

            zero = jnp.zeros((count, columns), jnp.float32)
            sums = lax.fori_loop(0, total_k, step, (zero,) * (2 * transfers), unroll=32)
            for place, value in enumerate(sums):
                sums_ref[rows, place // 2, place % 2, lanes] = value * scale
        copies.append(
            pltpu.make_async_copy(sums_ref.at[rows], out_ref.at[rows], sems.at[start // count])
        )
        copies[-1].start()
    for copy in copies:
        copy.wait()


def make_pairs(near, far, table):
    half_k, _, length, slab_size = near.shape
    transfers = table.shape[0]
    out = jax.ShapeDtypeStruct((length, transfers, 2, slab_size), jnp.float32)
    vmem = pl.BlockSpec(memory_space=pltpu.VMEM)
    return pl.pallas_call(
        functools.partial(pair_kernel, 1.0 / math.sqrt(2 * half_k)),
        in_specs=[vmem, vmem, vmem],
        out_specs=pl.BlockSpec(memory_space=pl.ANY),
        out_shape=out,
        scratch_shapes=[
            pltpu.VMEM((2 * half_k, 2, length, slab_size), jnp.float32),
            pltpu.VMEM(out.shape, jnp.float32),
            pltpu.SemaphoreType.DMA((length // min(16, length),)),
        ],
        compiler_params=pltpu.CompilerParams(vmem_limit_bytes=VMEM_LIMIT),
        name="pairs",
    )(table, near, far)


def on_device(orbitals, minus_table, points):
    kdevice, slab_size, channels = orbitals.shape
    half = lax.axis_index("half")
    groups = lax.axis_size("quarter") * lax.axis_size("inner")
    slabs = lax.axis_size("hi") * lax.axis_size("lo")
    total_k = 2 * groups * kdevice
    points = points.reshape(1, -1)
    here = lax.axis_index("hi") * SPLIT + lax.axis_index("lo")

    lo = lax.axis_index("lo")
    mine = lax.dynamic_index_in_dim(orbitals, lo, 0, keepdims=False)
    other = lax.dynamic_index_in_dim(orbitals, 1 - lo, 0, keepdims=False)
    share = make_front(mine, other, points)
    share, mine, other = lax.optimization_barrier((share, mine, other))
    shares = [share] + [swap(share, False, x) for x in range(1, slabs)]
    far = [swap(other if x & 1 else mine, True, x) for x in range(slabs)]

    def send(fields, around):
        fields = fields.reshape((-1,) + fields.shape[-3:])
        return lax.all_to_all(fields, around, split_axis=0, concat_axis=0, tiled=True)

    near_fields = make_near(orbitals, shares, groups)
    npoints = points.shape[1] // 2
    wanted = lax.dynamic_slice_in_dim(points[0], half * npoints, npoints)
    starts = jnp.stack([(here ^ x) * slab_size for x in range(slabs)])
    rows = wanted[:, None] - starts[None, :]
    near_fields, rows = lax.optimization_barrier((near_fields, rows))
    far_fields = make_far(rows, far, groups)
    def mirrored(kpoints):
        return total_k // 2 + (kpoints + total_k // 4) % (total_k // 2)

    turn = half * (total_k // 2)
    table = (jnp.roll(minus_table, -turn, axis=1) - turn) % total_k
    table = jnp.where(table < total_k // 2, table, mirrored(table))
    first, third, fourth = jnp.split(table, (total_k // 2, 3 * total_k // 4), axis=1)
    table = jnp.concatenate([first, fourth, third], axis=1)

    near_fields = send(near_fields, ("quarter", "inner"))
    near_fields, far_fields, table = lax.optimization_barrier((near_fields, far_fields, table))
    far_fields = send(far_fields, ("lo", "inner", "quarter"))
    return make_pairs(near_fields, far_fields, table)


def solution(mesh):
    kplaces, slabs = mesh.shape["ka"], mesh.shape["ga"]
    devices = mesh.devices.reshape(2, 2, kplaces // 4, slabs // SPLIT, SPLIT)
    finer = Mesh(devices, KA + GA)
    return jax.shard_map(
        on_device,
        mesh=finer,
        in_specs=(P(KA, GA, None), P(), P()),
        out_specs=P(KA, None, None, GA),
        check_vma=False,
    )
```

```python
import functools
import math

import jax
import jax.numpy as jnp
from jax import lax
from jax.experimental import pallas as pl
from jax.experimental.pallas import tpu as pltpu
from jax.sharding import Mesh
from jax.sharding import PartitionSpec as P

VMEM_LIMIT = 40 * 1024 * 1024
SPLIT = 2
KA, GA = ("half", "quarter", "inner"), ("hi", "lo")


def swap(block, mirror, other):
    half, quarter, inner, hi, lo = (lax.axis_size(name) for name in KA + GA)
    slabs = hi * lo
    route = []
    for place in range(half * quarter * inner * slabs):
        kplace, slab = divmod(place, slabs)
        part, within = divmod(kplace, inner)
        part = half * quarter - 1 - part if mirror else part
        route.append((place, (part * inner + within) * slabs + (slab ^ other)))
    return lax.ppermute(block, KA + GA, route)


def one_hot(points_ref, half, slab, slab_size, npoints):
    first = pl.multiple_of(half * npoints, npoints)
    wanted = points_ref[:, pl.ds(first, npoints)] - slab * slab_size
    spot = lax.broadcasted_iota(jnp.int32, (slab_size, npoints), 0)
    return (spot == wanted).astype(jnp.float32).astype(jnp.bfloat16)


def pick(chosen, slab):
    return lax.dot_general(
        chosen, slab, (((0,), (0,)), ((), ())), preferred_element_type=jnp.float32
    )


def crossed(member, groups):
    quarter, inner = divmod(member, groups // 2)
    return inner * 2 + quarter


def far_place(member, lo, groups):
    return lo * groups + crossed(member, groups)


def rotate(picked):
    middle = picked.shape[1] // 2
    return jnp.concatenate([-picked[:, middle:], picked[:, :middle]], axis=1)


def product(rows, slab, groups):
    out = lax.dot_general(
        rows, slab, (((1,), (1,)), ((), ())), preferred_element_type=jnp.float32
    )
    return out.reshape(groups, -1, out.shape[1]).astype(jnp.bfloat16)


def front_kernel(points_ref, mine_ref, other_ref, picked_ref):
    slab_size, _ = mine_ref.shape
    _, npoints, _ = picked_ref.shape
    mine = lax.axis_index("lo")
    here = lax.axis_index("hi") * SPLIT + mine
    chosen = one_hot(points_ref, lax.axis_index("half"), here, slab_size, npoints)
    for k, slab_ref in ((mine, mine_ref), (1 - mine, other_ref)):
        picked_ref[k] = pick(chosen, slab_ref[...]).astype(jnp.bfloat16)


def make_front(mine, other, points):
    vmem = pl.BlockSpec(memory_space=pltpu.VMEM)
    return pl.pallas_call(
        front_kernel,
        in_specs=[vmem] * 3,
        out_specs=vmem,
        out_shape=jax.ShapeDtypeStruct(
            (SPLIT, points.shape[1] // 2, mine.shape[1]), jnp.bfloat16
        ),
        compiler_params=pltpu.CompilerParams(vmem_limit_bytes=VMEM_LIMIT),
        name="front",
    )(points, mine, other)


def near_kernel(orbitals_ref, *refs):
    *picked_refs, out_ref = refs
    groups = out_ref.shape[0]
    rows = sum(picked_ref[0].astype(jnp.float32) for picked_ref in picked_refs)
    for part, turned in enumerate((rows, rotate(rows))):
        out_ref[:, 0, part] = product(turned.astype(jnp.bfloat16), orbitals_ref[0], groups)


def make_near(orbitals, shares, groups):
    kdevice, slab_size, channels = orbitals.shape
    npoints = shares[0].shape[1]
    length = npoints // groups
    return pl.pallas_call(
        near_kernel,
        grid=(kdevice,),
        in_specs=[pl.BlockSpec((1, slab_size, channels), lambda k: (k, 0, 0))]
        + [pl.BlockSpec((1, npoints, channels), lambda k: (k, 0, 0)) for _ in shares],
        out_specs=pl.BlockSpec((groups, 1, 2, length, slab_size), lambda k: (0, k, 0, 0, 0)),
        out_shape=jax.ShapeDtypeStruct((groups, kdevice, 2, length, slab_size), jnp.bfloat16),
        cost_estimate=pl.CostEstimate(
            flops=10_000_000_000, bytes_accessed=30_000_000, transcendentals=0
        ),
        compiler_params=pltpu.CompilerParams(vmem_limit_bytes=VMEM_LIMIT),
        name="near",
    )(orbitals, *shares)


def ahead_kernel(rows_ref, slab_ref, picked_ref, chosen_ref):
    npoints, slabs = rows_ref.shape
    spot = lax.broadcasted_iota(jnp.int32, (npoints, slab_ref.shape[0]), 1)
    for number in range(slabs):
        chosen = (rows_ref[:, number : number + 1] == spot).astype(jnp.float32)
        chosen = chosen.astype(jnp.bfloat16)
        if number:
            chosen_ref[number - 1] = chosen
        else:
            picked = jnp.dot(chosen, slab_ref[...], preferred_element_type=jnp.float32)
            picked_ref[...] = picked.astype(jnp.bfloat16)


def far_kernel(picked_ref, chosen_ref, *refs):
    *slab_refs, out_ref, parts_ref, sems = refs
    _, groups, _, length, slab_size = out_ref.shape
    picked = picked_ref[...].astype(jnp.float32)
    for number, slab_ref in enumerate(slab_refs[1:]):
        picked += jnp.dot(chosen_ref[number], slab_ref[...], preferred_element_type=jnp.float32)
    turned = [rows.astype(jnp.bfloat16) for rows in (picked, rotate(picked))]
    copies = []
    for number in range(SPLIT):
        for part in range(2):
            place = len(copies)
            pieces = product(turned[part], slab_refs[number][...], groups)
            for member in range(groups):
                parts_ref[place, crossed(member, groups)] = pieces[member]
            target = out_ref.at[lax.axis_index("lo") ^ number, :, part]
            copies.append(pltpu.make_async_copy(parts_ref.at[place], target, sems.at[place]))
            copies[-1].start()
    for copy in copies:
        copy.wait()


def make_far(rows, slabs, groups):
    slab_size, channels = slabs[0].shape
    npoints, _ = rows.shape
    length = npoints // groups
    vmem = pl.BlockSpec(memory_space=pltpu.VMEM)
    picked, chosen = pl.pallas_call(
        ahead_kernel,
        in_specs=[vmem] * 2,
        out_specs=[vmem] * 2,
        out_shape=[
            jax.ShapeDtypeStruct((npoints, channels), jnp.bfloat16),
            jax.ShapeDtypeStruct((len(slabs) - 1, npoints, slab_size), jnp.bfloat16),
        ],
        cost_estimate=pl.CostEstimate(flops=1_000_000, bytes_accessed=3_000, transcendentals=0),
        compiler_params=pltpu.CompilerParams(vmem_limit_bytes=VMEM_LIMIT),
        name="ahead",
    )(rows, slabs[0])
    return pl.pallas_call(
        far_kernel,
        in_specs=[vmem] * (2 + len(slabs)),
        out_specs=pl.BlockSpec(memory_space=pl.ANY),
        out_shape=jax.ShapeDtypeStruct((SPLIT, groups, 2, length, slab_size), jnp.bfloat16),
        scratch_shapes=[
            pltpu.VMEM((2 * SPLIT, groups, length, slab_size), jnp.bfloat16),
            pltpu.SemaphoreType.DMA((2 * SPLIT,)),
        ],
        cost_estimate=pl.CostEstimate(
            flops=60_000_000_000, bytes_accessed=180_000_000, transcendentals=0
        ),
        compiler_params=pltpu.CompilerParams(vmem_limit_bytes=VMEM_LIMIT),
        name="far",
    )(picked, chosen, *slabs)


def pair_kernel(scale, table_ref, near_ref, far_ref, out_ref, held_ref, sums_ref, sems):
    total_k, _, length, width = held_ref.shape
    transfers = table_ref.shape[0]
    table = table_ref[...]
    shifts = [lax.rem(total_k - table[transfer, 0], total_k) for transfer in range(transfers)]
    groups = near_ref.shape[0] // SPLIT
    held_ref[: total_k // 2] = near_ref[...].astype(jnp.float32)
    for member in range(groups):
        for k in range(SPLIT):
            far = far_ref[far_place(member, k, groups)]
            place = (member * SPLIT + k + total_k // 4) % (total_k // 2)
            held_ref[total_k // 2 + place] = far.astype(jnp.float32)

    count, columns = min(16, length), min(256, width)
    copies = []
    for start in range(0, length, count):
        rows = pl.ds(start, count)
        for column in range(0, width, columns):
            lanes = pl.ds(column, columns)

            def step(k, sums):
                real, imag = held_ref[k, 0, rows, lanes], held_ref[k, 1, rows, lanes]
                after = []
                for transfer in range(transfers):
                    other = lax.rem(k + total_k - shifts[transfer], total_k)
                    other_real = held_ref[other, 0, rows, lanes]
                    other_imag = held_ref[other, 1, rows, lanes]
                    after.append(sums[2 * transfer] + (real * other_real + imag * other_imag))
                    after.append(sums[2 * transfer + 1] + (imag * other_real - real * other_imag))
                return tuple(after)

            zero = jnp.zeros((count, columns), jnp.float32)
            sums = lax.fori_loop(0, total_k, step, (zero,) * (2 * transfers), unroll=32)
            for place, value in enumerate(sums):
                sums_ref[rows, place // 2, place % 2, lanes] = value * scale
        copies.append(
            pltpu.make_async_copy(sums_ref.at[rows], out_ref.at[rows], sems.at[start // count])
        )
        copies[-1].start()
    for copy in copies:
        copy.wait()


def make_pairs(near, far, table):
    half_k, _, length, slab_size = near.shape
    transfers = table.shape[0]
    out = jax.ShapeDtypeStruct((length, transfers, 2, slab_size), jnp.float32)
    vmem = pl.BlockSpec(memory_space=pltpu.VMEM)
    return pl.pallas_call(
        functools.partial(pair_kernel, 1.0 / math.sqrt(2 * half_k)),
        in_specs=[vmem, vmem, vmem],
        out_specs=pl.BlockSpec(memory_space=pl.ANY),
        out_shape=out,
        scratch_shapes=[
            pltpu.VMEM((2 * half_k, 2, length, slab_size), jnp.float32),
            pltpu.VMEM(out.shape, jnp.float32),
            pltpu.SemaphoreType.DMA((length // min(16, length),)),
        ],
        compiler_params=pltpu.CompilerParams(vmem_limit_bytes=VMEM_LIMIT),
        name="pairs",
    )(table, near, far)


def on_device(orbitals, minus_table, points):
    kdevice, slab_size, channels = orbitals.shape
    half = lax.axis_index("half")
    groups = lax.axis_size("quarter") * lax.axis_size("inner")
    slabs = lax.axis_size("hi") * lax.axis_size("lo")
    total_k = 2 * groups * kdevice
    points = points.reshape(1, -1)
    here = lax.axis_index("hi") * SPLIT + lax.axis_index("lo")

    lo = lax.axis_index("lo")
    mine = lax.dynamic_index_in_dim(orbitals, lo, 0, keepdims=False)
    other = lax.dynamic_index_in_dim(orbitals, 1 - lo, 0, keepdims=False)
    share = make_front(mine, other, points)
    share, mine, other = lax.optimization_barrier((share, mine, other))
    shares = [share] + [swap(share, False, x) for x in range(1, slabs)]
    far = [swap(other if x & 1 else mine, True, x) for x in range(slabs)]

    def send(fields, around):
        fields = fields.reshape((-1,) + fields.shape[-3:])
        return lax.all_to_all(fields, around, split_axis=0, concat_axis=0, tiled=True)

    near_fields = make_near(orbitals, shares, groups)
    npoints = points.shape[1] // 2
    wanted = lax.dynamic_slice_in_dim(points[0], half * npoints, npoints)
    starts = jnp.stack([(here ^ x) * slab_size for x in range(slabs)])
    rows = wanted[:, None] - starts[None, :]
    near_fields, rows = lax.optimization_barrier((near_fields, rows))
    far_fields = make_far(rows, far, groups)
    near_fields = send(near_fields, ("quarter", "inner"))
    near_fields, far_fields = lax.optimization_barrier((near_fields, far_fields))
    far_fields = send(far_fields, ("lo", "inner", "quarter"))
    return make_pairs(near_fields, far_fields, minus_table)


def solution(mesh):
    kplaces, slabs = mesh.shape["ka"], mesh.shape["ga"]
    devices = mesh.devices.reshape(2, 2, kplaces // 4, slabs // SPLIT, SPLIT)
    finer = Mesh(devices, KA + GA)
    return jax.shard_map(
        on_device,
        mesh=finer,
        in_specs=(P(KA, GA, None), P(), P()),
        out_specs=P(KA, None, None, GA),
        check_vma=False,
    )
```

```python
import functools
import math

import jax
import jax.numpy as jnp
from jax import lax
from jax.experimental import pallas as pl
from jax.experimental.pallas import tpu as pltpu
from jax.sharding import Mesh
from jax.sharding import PartitionSpec as P

VMEM_LIMIT = 40 * 1024 * 1024
SPLIT = 2
KA, GA = ("half", "quarter", "inner"), ("hi", "lo")


def swap(block, mirror, other):
    half, quarter, inner, hi, lo = (lax.axis_size(name) for name in KA + GA)
    slabs = hi * lo
    route = []
    for place in range(half * quarter * inner * slabs):
        kplace, slab = divmod(place, slabs)
        part, within = divmod(kplace, inner)
        part = half * quarter - 1 - part if mirror else part
        route.append((place, (part * inner + within) * slabs + (slab ^ other)))
    return lax.ppermute(block, KA + GA, route)


def one_hot(points_ref, half, slab, slab_size, npoints):
    first = pl.multiple_of(half * npoints, npoints)
    wanted = points_ref[:, pl.ds(first, npoints)] - slab * slab_size
    spot = lax.broadcasted_iota(jnp.int32, (slab_size, npoints), 0)
    return (spot == wanted).astype(jnp.float32).astype(jnp.bfloat16)


def pick(chosen, slab):
    return lax.dot_general(
        chosen, slab, (((0,), (0,)), ((), ())), preferred_element_type=jnp.float32
    )


def crossed(member, groups):
    quarter, inner = divmod(member, groups // 2)
    return inner * 2 + quarter


def far_place(member, lo, groups):
    return lo * groups + crossed(member, groups)


def rotate(picked):
    middle = picked.shape[1] // 2
    return jnp.concatenate([-picked[:, middle:], picked[:, :middle]], axis=1)


def product(rows, slab, groups):
    out = lax.dot_general(
        rows, slab, (((1,), (1,)), ((), ())), preferred_element_type=jnp.float32
    )
    return out.reshape(groups, -1, out.shape[1]).astype(jnp.bfloat16)


def front_kernel(points_ref, mine_ref, other_ref, picked_ref):
    slab_size, _ = mine_ref.shape
    _, npoints, _ = picked_ref.shape
    mine = lax.axis_index("lo")
    here = lax.axis_index("hi") * SPLIT + mine
    chosen = one_hot(points_ref, lax.axis_index("half"), here, slab_size, npoints)
    for k, slab_ref in ((mine, mine_ref), (1 - mine, other_ref)):
        picked_ref[k] = pick(chosen, slab_ref[...]).astype(jnp.bfloat16)


def make_front(mine, other, points):
    vmem = pl.BlockSpec(memory_space=pltpu.VMEM)
    return pl.pallas_call(
        front_kernel,
        in_specs=[vmem] * 3,
        out_specs=vmem,
        out_shape=jax.ShapeDtypeStruct(
            (SPLIT, points.shape[1] // 2, mine.shape[1]), jnp.bfloat16
        ),
        compiler_params=pltpu.CompilerParams(vmem_limit_bytes=VMEM_LIMIT),
        name="front",
    )(points, mine, other)


def near_kernel(orbitals_ref, *refs):
    *picked_refs, out_ref = refs
    groups = out_ref.shape[0]
    rows = sum(picked_ref[0].astype(jnp.float32) for picked_ref in picked_refs)
    for part, turned in enumerate((rows, rotate(rows))):
        out_ref[:, 0, part] = product(turned.astype(jnp.bfloat16), orbitals_ref[0], groups)


def make_near(orbitals, shares, groups):
    kdevice, slab_size, channels = orbitals.shape
    npoints = shares[0].shape[1]
    length = npoints // groups
    return pl.pallas_call(
        near_kernel,
        grid=(kdevice,),
        in_specs=[pl.BlockSpec((1, slab_size, channels), lambda k: (k, 0, 0))]
        + [pl.BlockSpec((1, npoints, channels), lambda k: (k, 0, 0)) for _ in shares],
        out_specs=pl.BlockSpec((groups, 1, 2, length, slab_size), lambda k: (0, k, 0, 0, 0)),
        out_shape=jax.ShapeDtypeStruct((groups, kdevice, 2, length, slab_size), jnp.bfloat16),
        cost_estimate=pl.CostEstimate(
            flops=1_000_000_000, bytes_accessed=3_000_000, transcendentals=0
        ),
        compiler_params=pltpu.CompilerParams(vmem_limit_bytes=VMEM_LIMIT),
        name="near",
    )(orbitals, *shares)


def ahead_kernel(rows_ref, slab_ref, picked_ref, chosen_ref):
    npoints, slabs = rows_ref.shape
    spot = lax.broadcasted_iota(jnp.int32, (npoints, slab_ref.shape[0]), 1)
    for number in range(slabs):
        chosen = (rows_ref[:, number : number + 1] == spot).astype(jnp.float32)
        chosen = chosen.astype(jnp.bfloat16)
        if number:
            chosen_ref[number - 1] = chosen
        else:
            picked = jnp.dot(chosen, slab_ref[...], preferred_element_type=jnp.float32)
            picked_ref[...] = picked.astype(jnp.bfloat16)


def far_kernel(picked_ref, chosen_ref, *refs):
    *slab_refs, out_ref, parts_ref, sems = refs
    _, groups, _, length, slab_size = out_ref.shape
    picked = picked_ref[...].astype(jnp.float32)
    for number, slab_ref in enumerate(slab_refs[1:]):
        picked += jnp.dot(chosen_ref[number], slab_ref[...], preferred_element_type=jnp.float32)
    turned = [rows.astype(jnp.bfloat16) for rows in (picked, rotate(picked))]
    copies = []
    for number in range(SPLIT):
        for part in range(2):
            place = len(copies)
            pieces = product(turned[part], slab_refs[number][...], groups)
            for member in range(groups):
                parts_ref[place, crossed(member, groups)] = pieces[member]
            target = out_ref.at[lax.axis_index("lo") ^ number, :, part]
            copies.append(pltpu.make_async_copy(parts_ref.at[place], target, sems.at[place]))
            copies[-1].start()
    for copy in copies:
        copy.wait()


def make_far(rows, slabs, groups):
    slab_size, channels = slabs[0].shape
    npoints, _ = rows.shape
    length = npoints // groups
    vmem = pl.BlockSpec(memory_space=pltpu.VMEM)
    picked, chosen = pl.pallas_call(
        ahead_kernel,
        in_specs=[vmem] * 2,
        out_specs=[vmem] * 2,
        out_shape=[
            jax.ShapeDtypeStruct((npoints, channels), jnp.bfloat16),
            jax.ShapeDtypeStruct((len(slabs) - 1, npoints, slab_size), jnp.bfloat16),
        ],
        cost_estimate=pl.CostEstimate(flops=1_000_000, bytes_accessed=3_000, transcendentals=0),
        compiler_params=pltpu.CompilerParams(vmem_limit_bytes=VMEM_LIMIT),
        name="ahead",
    )(rows, slabs[0])
    return pl.pallas_call(
        far_kernel,
        in_specs=[vmem] * (2 + len(slabs)),
        out_specs=pl.BlockSpec(memory_space=pl.ANY),
        out_shape=jax.ShapeDtypeStruct((SPLIT, groups, 2, length, slab_size), jnp.bfloat16),
        scratch_shapes=[
            pltpu.VMEM((2 * SPLIT, groups, length, slab_size), jnp.bfloat16),
            pltpu.SemaphoreType.DMA((2 * SPLIT,)),
        ],
        cost_estimate=pl.CostEstimate(
            flops=60_000_000_000, bytes_accessed=180_000_000, transcendentals=0
        ),
        compiler_params=pltpu.CompilerParams(vmem_limit_bytes=VMEM_LIMIT),
        name="far",
    )(picked, chosen, *slabs)


def pair_kernel(scale, table_ref, near_ref, far_ref, out_ref, held_ref, sums_ref, sems):
    total_k, _, length, width = held_ref.shape
    transfers = table_ref.shape[0]
    table = table_ref[...]
    shifts = [lax.rem(total_k - table[transfer, 0], total_k) for transfer in range(transfers)]
    groups = near_ref.shape[0] // SPLIT
    held_ref[: total_k // 2] = near_ref[...].astype(jnp.float32)
    for member in range(groups):
        for k in range(SPLIT):
            far = far_ref[far_place(member, k, groups)]
            place = (member * SPLIT + k + total_k // 4) % (total_k // 2)
            held_ref[total_k // 2 + place] = far.astype(jnp.float32)

    count, columns = min(16, length), min(256, width)
    copies = []
    for start in range(0, length, count):
        rows = pl.ds(start, count)
        for column in range(0, width, columns):
            lanes = pl.ds(column, columns)

            def step(k, sums):
                real, imag = held_ref[k, 0, rows, lanes], held_ref[k, 1, rows, lanes]
                after = []
                for transfer in range(transfers):
                    other = lax.rem(k + total_k - shifts[transfer], total_k)
                    other_real = held_ref[other, 0, rows, lanes]
                    other_imag = held_ref[other, 1, rows, lanes]
                    after.append(sums[2 * transfer] + (real * other_real + imag * other_imag))
                    after.append(sums[2 * transfer + 1] + (imag * other_real - real * other_imag))
                return tuple(after)

            zero = jnp.zeros((count, columns), jnp.float32)
            sums = lax.fori_loop(0, total_k, step, (zero,) * (2 * transfers), unroll=32)
            for place, value in enumerate(sums):
                sums_ref[rows, place // 2, place % 2, lanes] = value * scale
        copies.append(
            pltpu.make_async_copy(sums_ref.at[rows], out_ref.at[rows], sems.at[start // count])
        )
        copies[-1].start()
    for copy in copies:
        copy.wait()


def make_pairs(near, far, table):
    half_k, _, length, slab_size = near.shape
    transfers = table.shape[0]
    out = jax.ShapeDtypeStruct((length, transfers, 2, slab_size), jnp.float32)
    vmem = pl.BlockSpec(memory_space=pltpu.VMEM)
    return pl.pallas_call(
        functools.partial(pair_kernel, 1.0 / math.sqrt(2 * half_k)),
        in_specs=[vmem, vmem, vmem],
        out_specs=pl.BlockSpec(memory_space=pl.ANY),
        out_shape=out,
        scratch_shapes=[
            pltpu.VMEM((2 * half_k, 2, length, slab_size), jnp.float32),
            pltpu.VMEM(out.shape, jnp.float32),
            pltpu.SemaphoreType.DMA((length // min(16, length),)),
        ],
        compiler_params=pltpu.CompilerParams(vmem_limit_bytes=VMEM_LIMIT),
        name="pairs",
    )(table, near, far)


def on_device(orbitals, minus_table, points):
    kdevice, slab_size, channels = orbitals.shape
    half = lax.axis_index("half")
    groups = lax.axis_size("quarter") * lax.axis_size("inner")
    slabs = lax.axis_size("hi") * lax.axis_size("lo")
    total_k = 2 * groups * kdevice
    points = points.reshape(1, -1)
    here = lax.axis_index("hi") * SPLIT + lax.axis_index("lo")

    lo = lax.axis_index("lo")
    mine = lax.dynamic_index_in_dim(orbitals, lo, 0, keepdims=False)
    other = lax.dynamic_index_in_dim(orbitals, 1 - lo, 0, keepdims=False)
    share = make_front(mine, other, points)
    share, mine, other = lax.optimization_barrier((share, mine, other))
    far = [swap(other if x & 1 else mine, True, x) for x in range(slabs)]
    shares = [share] + [swap(share, False, x) for x in range(1, slabs)]

    def send(fields, around):
        fields = fields.reshape((-1,) + fields.shape[-3:])
        return lax.all_to_all(fields, around, split_axis=0, concat_axis=0, tiled=True)

    near_fields = make_near(orbitals, shares, groups)
    npoints = points.shape[1] // 2
    wanted = lax.dynamic_slice_in_dim(points[0], half * npoints, npoints)
    starts = jnp.stack([(here ^ x) * slab_size for x in range(slabs)])
    rows = wanted[:, None] - starts[None, :]
    near_fields, rows = lax.optimization_barrier((near_fields, rows))
    far_fields = make_far(rows, far, groups)
    near_fields = send(near_fields, ("quarter", "inner"))
    near_fields, far_fields = lax.optimization_barrier((near_fields, far_fields))
    far_fields = send(far_fields, ("lo", "inner", "quarter"))
    return make_pairs(near_fields, far_fields, minus_table)


def solution(mesh):
    kplaces, slabs = mesh.shape["ka"], mesh.shape["ga"]
    devices = mesh.devices.reshape(2, 2, kplaces // 4, slabs // SPLIT, SPLIT)
    finer = Mesh(devices, KA + GA)
    return jax.shard_map(
        on_device,
        mesh=finer,
        in_specs=(P(KA, GA, None), P(), P()),
        out_specs=P(KA, None, None, GA),
        check_vma=False,
    )
```
